128 devices in a mesh: dp: 16 (over y, z_hi, core), tm: 8 (over x, z_lo).
Axes of the slice: x: 4, y: 4, z: 4 (z_hi: 2, z_lo: 2; z = z_hi * 2 + z_lo), core: 2. Of those that a mesh axis runs over, the one named last changes fastest.
Arguments:
- code_ids: int32 [16, 1024, 2], P('dp', 'tm'), may hold values from 0 to 1023
- code_table: bfloat16 [2048, 768], replicated, may hold values from -6 to 6
- kernel: float32 [7, 768], replicated, may hold values from -2 to 2
- up_weight: bfloat16 [768, 2304], replicated, may hold values from -0.21875 to 0.21875
- down_weight: bfloat16 [2304, 768], replicated, may hold values from -0.125 to 0.125
- layer_scale: float32 [768], replicated, may hold values from 0.3 to 1
- head_weight: bfloat16 [768, 1026], replicated, may hold values from -0.21875 to 0.21875
- target: float32 [16, 262144], P('dp', 'tm'), may hold values from -0.75 to 0.75, as said below
- loss_scale: float32 [], replicated, may hold values from 30000 to 100000
Outputs:
- spectral_loss: float32 [], replicated
- table_grad: float32 [2048, 768], P(('dp', 'tm'))
- kernel_grad: float32 [7, 768], P(None, ('dp', 'tm'))
- up_grad: float32 [768, 2304], P(('dp', 'tm'))
- down_grad: float32 [2304, 768], P(('dp', 'tm'))
- scale_grad: float32 [768], P(('dp', 'tm'))
- head_grad: float32 [768, 1026], P(('dp', 'tm'))
The draws below stay inside these ranges and needn't reach their ends.
Inputs may be any that keep to these rules, and one draw needn't show every extreme that they name: target waveform samples.
All inputs are finite; a program needn't handle non-finite values.
Results may differ from the reference program's by a relative error of at most 0.02.
Values sent between devices are 32-bit elements; how exact they have to be, the bound alone decides.
A program may use at most 128 MiB of HBM per device.

```python
import math
import jax
import jax.numpy as jnp
from jax import lax

D = 768
FF = 2304
CODES = 1024
NQ = 2
KSIZE = 7
NFFT = 1024
HOP = 256
BINS = 513
FRAMES = 1024
SAMPLES = 262144
CLIPS = 16


def draw_target(key, part):
    key = jax.random.fold_in(key, 7)
    first_key = jax.random.fold_in(key, 0)
    position = jnp.arange(SAMPLES, dtype=jnp.float32) / SAMPLES
    clip_place = jnp.arange(CLIPS, dtype=jnp.float32) / max(CLIPS - 1, 1)
    rising = 0.01 * jnp.exp(jnp.log(3.0) * position)
    clip_rise = jnp.exp(jnp.log(6.0) * clip_place)[:, None]
    noise = jnp.clip(jax.random.normal(first_key, (CLIPS, SAMPLES), jnp.float32), -4.0, 4.0)
    return (rising[None, :] * clip_rise * noise).astype(jnp.float32)


def place_ends(array, rng, low, top_value):
    longest = array.shape.index(max(array.shape))
    spots = []
    for shift in (0, 1):
        where = [jax.random.randint(jax.random.fold_in(rng, axis), (), 0, length) for axis, length in enumerate(array.shape)]
        where[longest] = (where[longest] + shift) % array.shape[longest]
        spots.append(tuple(where))
    return array.at[spots[0]].set(low).at[spots[1]].set(top_value)


def normal_values(rng, shape, scale, most, kind=jnp.bfloat16):
    entries = scale * jax.random.normal(rng, shape, jnp.float32)
    return jnp.clip(entries, min=-most, max=most).astype(kind)


def setup_inputs(seed: int = 0) -> dict:
    key_of = jax.random.split(jax.random.key(seed), 10)
    return {
        "code_ids": place_ends(jax.random.randint(key_of[0], (CLIPS, FRAMES, NQ), 0, CODES), jax.random.fold_in(key_of[0], 1), 0, CODES - 1).astype(jnp.int32),
        "code_table": normal_values(key_of[1], (NQ * CODES, D), 1.0, 6.0),
        "kernel": normal_values(key_of[2], (KSIZE, D), KSIZE ** -0.5, 2.0, jnp.float32),
        "up_weight": normal_values(key_of[3], (D, FF), D ** -0.5, 0.21875),
        "down_weight": normal_values(key_of[4], (FF, D), FF ** -0.5, 0.125),
        "layer_scale": jnp.clip(jnp.exp(jax.random.uniform(key_of[5], (D,), jnp.float32, math.log(0.3), math.log(1.0))), 0.3, 1.0),
        "head_weight": normal_values(key_of[6], (D, 2 * BINS), D ** -0.5, 0.21875),
        "target": draw_target(jax.random.fold_in(key_of[9], 71), 0),
        "loss_scale": jnp.clip(jnp.exp(jax.random.uniform(key_of[8], (), jnp.float32, math.log(30000.0), math.log(100000.0))), 30000.0, 100000.0),
    }


def layer_norm(values):
    centre = values - lax.optimization_barrier(jnp.mean(values, axis=-1, keepdims=True))
    spread = lax.optimization_barrier(jnp.mean(centre * centre, axis=-1, keepdims=True))
    return centre * lax.rsqrt(spread + 1e-06)

def hann_window(length):
    places = jnp.arange(length, dtype=jnp.float32)
    return 0.5 - 0.5 * jnp.cos(2.0 * jnp.pi * places / length)

def fourier_angles(length):
    frequency = jnp.arange(length // 2 + 1, dtype=jnp.int32)
    places = jnp.arange(length, dtype=jnp.int32)
    product = frequency[:, None] * places[None, :] % length
    return 2.0 * jnp.pi * product.astype(jnp.float32) / length

def synthesis_table(length):
    angles = fourier_angles(length)
    frequency = jnp.arange(length // 2 + 1, dtype=jnp.int32)
    factor = jnp.where((frequency == 0) | (frequency == length // 2), 1.0, 2.0).astype(jnp.float32) / length
    window = hann_window(length)
    cosine_part = factor[:, None] * jnp.cos(angles) * window[None, :]
    sine_part = -factor[:, None] * jnp.sin(angles) * window[None, :]
    return jnp.concatenate([cosine_part, sine_part], axis=0).astype(jnp.bfloat16)

def analysis_table(length):
    angles = fourier_angles(length)
    return jnp.concatenate([jnp.cos(angles).T, -jnp.sin(angles).T], axis=1).astype(jnp.bfloat16)

def envelope(first_sample, samples, frame_total):
    places = first_sample + jnp.arange(samples, dtype=jnp.int32)
    blocks = places // HOP
    summed = jnp.zeros((samples,), jnp.float32)
    for offset in (-1, 0, 1, 2):
        frame_index = blocks + offset
        inside = places - frame_index * HOP + NFFT // 2
        weight = 0.5 - 0.5 * jnp.cos(2.0 * jnp.pi * inside.astype(jnp.float32) / NFFT)
        within = (frame_index >= 0) & (frame_index < frame_total)
        summed = summed + jnp.where(within, weight * weight, 0.0)
    return summed

def frame_sum(frames_out):
    lead_rows, frame_count = (frames_out.shape[0], frames_out.shape[1])
    stride = frames_out.shape[2] // 4
    pieces = frames_out.reshape(lead_rows, frame_count, 4, stride)
    buffer = jnp.zeros((lead_rows, frame_count + 4, stride), jnp.float32)
    for offset in range(4):
        buffer = buffer + jnp.pad(pieces[:, :, offset], ((0, 0), (offset, 4 - offset), (0, 0)))
    return buffer.reshape(lead_rows, (frame_count + 4) * stride)

def framed(padded, stride):
    lead_rows = padded.shape[0]
    block_total = padded.shape[1] // stride
    blocks = padded.reshape(lead_rows, block_total, stride)
    number = block_total - 4
    return jnp.concatenate([blocks[:, offset:offset + number] for offset in range(4)], axis=-1)

def code_matrix(code_ids, vocab_total):
    codebooks = code_ids.shape[-1]
    shifted = code_ids + jnp.arange(codebooks, dtype=jnp.int32) * (vocab_total // codebooks)
    columns = jnp.arange(vocab_total, dtype=jnp.int32)
    matches = (shifted[..., :, None] == columns).astype(jnp.float32)
    return lax.optimization_barrier(jnp.sum(matches, axis=-2)).astype(jnp.bfloat16)

def embed_forward(code_ids, code_table, probe_embed):
    onehot = code_matrix(code_ids, code_table.shape[0])
    return layer_norm(jnp.dot(onehot, code_table, preferred_element_type=jnp.float32) + probe_embed)

def block_forward(extended, kernel, layer_scale, probe_up, probe_down, probe_head, up_weight, down_weight, head_weight):
    margin = kernel.shape[0] // 2
    frame_rows = extended.shape[1] - 2 * margin
    mixture = kernel[0] * extended[:, 0:frame_rows]
    for offset in range(1, kernel.shape[0]):
        mixture = mixture + kernel[offset] * extended[:, offset:offset + frame_rows]
    normed = layer_norm(mixture).astype(jnp.bfloat16)
    up_out = jnp.dot(normed, up_weight, preferred_element_type=jnp.float32) + probe_up
    hidden = jax.nn.gelu(up_out, approximate=False).astype(jnp.bfloat16)
    down_out = jnp.dot(hidden, down_weight, preferred_element_type=jnp.float32) + probe_down
    stream = extended[:, margin:margin + frame_rows] + layer_scale * down_out
    output_norm = layer_norm(stream).astype(jnp.bfloat16)
    head_out = jnp.dot(output_norm, head_weight, preferred_element_type=jnp.float32) + probe_head
    bin_count = head_out.shape[-1] // 2
    magnitude = jnp.exp(head_out[..., :bin_count])
    phases = head_out[..., bin_count:]
    spectrum = jnp.concatenate([magnitude * jnp.cos(phases), magnitude * jnp.sin(phases)], axis=-1).astype(jnp.bfloat16)
    frames_out = jnp.dot(spectrum, synthesis_table(2 * (bin_count - 1)), preferred_element_type=jnp.float32)
    buffer = frame_sum(frames_out)
    half_frame = frames_out.shape[-1] // 2
    rim_parts = jnp.concatenate([buffer[:, :half_frame], buffer[:, -half_frame:]], axis=1)
    return ((rim_parts, buffer[:, half_frame:-half_frame]), (normed, hidden, output_norm))

def spectral_stats(predicted, goal):
    columns = []
    for length, stride, margin in ((NFFT, NFFT // 4, 0), (NFFT // 2, NFFT // 8, NFFT // 4)):
        window = hann_window(length)
        dft_table = analysis_table(length)
        extent = predicted.shape[1] - margin
        results = []
        for signal in (predicted, goal):
            segment = framed(signal[:, margin:extent], stride) * window
            results.append(jnp.dot(segment.astype(jnp.bfloat16), dft_table, preferred_element_type=jnp.float32))
        bin_count = length // 2 + 1
        pred_spec, goal_spec = results
        differ = pred_spec - goal_spec
        pred_power = pred_spec[..., :bin_count] * pred_spec[..., :bin_count] + pred_spec[..., bin_count:] * pred_spec[..., bin_count:]
        goal_power = goal_spec[..., :bin_count] * goal_spec[..., :bin_count] + goal_spec[..., bin_count:] * goal_spec[..., bin_count:]
        log_gap = jnp.log1p(pred_power) - jnp.log1p(goal_power)
        columns.extend([lax.optimization_barrier(jnp.sum(differ * differ, axis=(1, 2))), lax.optimization_barrier(jnp.sum(goal_spec * goal_spec, axis=(1, 2))), lax.optimization_barrier(jnp.sum(log_gap * log_gap, axis=(1, 2)))])
    return jnp.stack(columns, axis=-1)

def per_clip_loss(statistics, frame_total):
    counts = (frame_total * (NFFT // 2 + 1), 2 * frame_total * (NFFT // 4 + 1))
    summed = jnp.zeros(statistics.shape[:1], jnp.float32)
    for level in range(2):
        convergence = jnp.sqrt(statistics[:, 3 * level] + 1e-06) / jnp.sqrt(statistics[:, 3 * level + 1] + 1e-06)
        summed = summed + convergence + statistics[:, 3 * level + 2] / counts[level]
    return summed

def stat_cotangent(statistics, frame_total, factor):
    counts = (frame_total * (NFFT // 2 + 1), 2 * frame_total * (NFFT // 4 + 1))
    columns = []
    for level in range(2):
        first_sum = statistics[:, 3 * level]
        second_sum = statistics[:, 3 * level + 1]
        columns.append(factor * 0.5 / (jnp.sqrt(first_sum + 1e-06) * jnp.sqrt(second_sum + 1e-06)))
        columns.append(jnp.zeros_like(first_sum))
        columns.append(jnp.zeros_like(first_sum) + factor / counts[level])
    return jnp.stack(columns, axis=-1)

def weight_grad(inputs, cotangent):
    left_side = inputs.reshape(-1, inputs.shape[-1])
    right_side = cotangent.reshape(-1, cotangent.shape[-1]).astype(jnp.bfloat16)
    return jnp.dot(left_side.T, right_side, preferred_element_type=jnp.float32)

def reference(code_ids, code_table, kernel, up_weight, down_weight, layer_scale, head_weight, target, loss_scale):
    clip_total, frame_total = (code_ids.shape[0], code_ids.shape[1])
    sample_total = frame_total * HOP
    half_frame = NFFT // 2
    margin = KSIZE // 2
    factor = loss_scale / (2.0 * clip_total)
    divisor = envelope(0, sample_total, frame_total)
    model_width = code_table.shape[1]
    inner_width = up_weight.shape[1]
    head_width = head_weight.shape[1]

    def one_clip(carry, inputs):
        clip_codes = inputs[0][None]
        goal_padded = jnp.pad(inputs[1][None], ((0, 0), (half_frame, half_frame)))

        def forward(kernel_in, scale_in, probe_embed, probe_up, probe_down, probe_head):
            stream_in = embed_forward(clip_codes, code_table, probe_embed)
            extended = jnp.pad(stream_in, ((0, 0), (margin, margin), (0, 0)))
            outputs, saved = block_forward(extended, kernel_in, scale_in, probe_up, probe_down, probe_head, up_weight, down_weight, head_weight)
            predicted = outputs[1] / divisor
            padded = jnp.pad(predicted, ((0, 0), (half_frame, half_frame)))
            return (spectral_stats(padded, goal_padded), saved)
        statistics, pullback, saved = jax.vjp(forward, kernel, layer_scale, jnp.zeros((1, frame_total, model_width), jnp.float32), jnp.zeros((1, frame_total, inner_width), jnp.float32), jnp.zeros((1, frame_total, model_width), jnp.float32), jnp.zeros((1, frame_total, head_width), jnp.float32), has_aux=True)
        cotangents = pullback(stat_cotangent(statistics, frame_total, factor))
        normed, hidden, output_norm = saved
        onehot = code_matrix(clip_codes, code_table.shape[0])
        updated = (carry[0] + per_clip_loss(statistics, frame_total)[0], carry[1] + weight_grad(onehot, cotangents[2]), carry[2] + cotangents[0], carry[3] + weight_grad(normed, cotangents[3]), carry[4] + weight_grad(hidden, cotangents[4]), carry[5] + cotangents[1], carry[6] + weight_grad(output_norm, cotangents[5]))
        return (updated, None)
    initial = (jnp.zeros((), jnp.float32), jnp.zeros(code_table.shape, jnp.float32), jnp.zeros(kernel.shape, jnp.float32), jnp.zeros(up_weight.shape, jnp.float32), jnp.zeros(down_weight.shape, jnp.float32), jnp.zeros(layer_scale.shape, jnp.float32), jnp.zeros(head_weight.shape, jnp.float32))
    final_carry, unused = lax.scan(one_clip, initial, (code_ids, target))
    return (final_carry[0] / (2.0 * clip_total), final_carry[1], final_carry[2], final_carry[3], final_carry[4], final_carry[5], final_carry[6])
```

```python
import jax
import jax.numpy as jnp
import ml_dtypes
import numpy as np
from jax import lax
from jax.experimental import pallas as pl
from jax.experimental.pallas import tpu as pltpu
from jax.sharding import PartitionSpec as P

F32, BF16 = jnp.float32, jnp.bfloat16
MESH = pl.DeviceIdType.MESH
D, FF = 768, 2304
HOP, NFFT = 256, 1024
FRAMES, OWN, HALO = 1024, 128, 16
ROWS = OWN + 2 * HALO
CHUNKS1, CHUNKS2 = 5, 3
WIDE1, WIDE2 = CHUNKS1 * 256, CHUNKS2 * 256
CLIPS = 16
MB = 1 << 20
ORDERS = ("xyz", "yzx", "zxy")
HEAD_BLOCKS = ((0, 2), (2, 3), (5, 4))
PART_ROWS = (18 * 24 + 2 * 24, 6 * 72 + 3 * 24, 6 * 64 + 4 * 24)


def bf(array):
    return np.asarray(array, np.float32).astype(ml_dtypes.bfloat16)


def hann(length):
    return 0.5 - 0.5 * np.cos(2.0 * np.pi * np.arange(length) / length)


def angles(length):
    product = np.arange(length // 2 + 1)[:, None] * np.arange(length)[None, :] % length
    return 2.0 * np.pi * product / length


def interleave(real, imag, chunks):
    bins, width = real.shape
    out = np.zeros((chunks, 2, 128, width), np.float64)
    for half, part in enumerate((real, imag)):
        padded = np.zeros((chunks * 128, width), np.float64)
        padded[:bins] = part
        out[:, half] = padded.reshape(chunks, 128, width)
    return out.reshape(chunks * 256, width)


def make_constants():
    ang = angles(NFFT)
    bins = np.arange(NFFT // 2 + 1)
    factor = np.where((bins == 0) | (bins == NFFT // 2), 1.0, 2.0)[:, None] / NFFT
    window = hann(NFFT)[None, :]
    synthesis = bf(interleave(factor * np.cos(ang) * window, -factor * np.sin(ang) * window, CHUNKS1))
    analysis1 = bf(interleave(np.cos(ang), -np.sin(ang), CHUNKS1).T)
    ang = angles(NFFT // 2)
    analysis2 = bf(interleave(np.cos(ang), -np.sin(ang), CHUNKS2).T)
    win = np.zeros((8, NFFT), np.float32)
    win[0] = hann(NFFT)
    win[1] = hann(NFFT) ** 2
    win[2, : NFFT // 2] = hann(NFFT // 2)
    return synthesis, analysis1, analysis2, win


def device_index(x, y, z, core):
    return ((y * 2 + z // 2) * 2 + core) * 8 + x * 2 + z % 2


def shard_order(order, core):
    places = []
    for a in range(4):
        for b in range(4):
            for c in range(4):
                at = dict(zip(order, (a, b, c)))
                places.append(device_index(at["x"], at["y"], at["z"], core))
    return np.array(places)


def columns_of(order, core, each):
    return (shard_order(order, core)[:, None] * each + np.arange(each)[None, :]).reshape(-1)


def one_hot_columns(sources, size):
    out = np.zeros((size, sources.size), np.float32)
    out[sources, np.arange(sources.size)] = 1.0
    return bf(out)


def make_orders():
    pick_n = np.stack([one_hot_columns(columns_of(ORDERS[0], c, 6), D) for c in (0, 1)])
    half = [columns_of(ORDERS[1], c, 18)[: 4 * 4 * 2 * 18] for c in (0, 1)]
    pick_h = np.stack([one_hot_columns(h, FF // 2) for h in half])
    pick_k = np.stack([one_hot_columns(columns_of(ORDERS[2], c, 6), D) for c in (0, 1)])
    first = columns_of(ORDERS[0], 0, 6)
    where = {col: i for i, col in enumerate(first)}
    turns = []
    for k in (1, 2):
        sources = np.array([where[col] for col in columns_of(ORDERS[k], 0, 6)])
        turns.append(one_hot_columns(sources, 384))
    row_id = columns_of(ORDERS[2], 0, 16).astype(np.float32)[None, :]
    return pick_n, pick_h, pick_k, turns[0], turns[1], row_id


def mm(a, b):
    return jnp.dot(a, b, preferred_element_type=F32)


def mm_bt(a, b):
    return lax.dot_general(a, b, (((1,), (1,)), ((), ())), preferred_element_type=F32)


def mm_at(a, b):
    return lax.dot_general(a, b, (((0,), (0,)), ((), ())), preferred_element_type=F32)


def shift(values, by):
    by = by % values.shape[0]
    return values if by == 0 else pltpu.roll(values, by, 0)


def norm(values):
    centre = values - jnp.mean(values, axis=-1, keepdims=True)
    rstd = lax.rsqrt(jnp.mean(centre * centre, axis=-1, keepdims=True) + 1e-6)
    return centre * rstd, rstd


def norm_back(grad, y, rstd):
    mean_g = jnp.mean(grad, axis=-1, keepdims=True)
    mean_gy = jnp.mean(grad * y, axis=-1, keepdims=True)
    return rstd * (grad - mean_g - y * mean_gy)


def frame_places(comb):
    first = comb[HALO : HALO + 1, 258:259]
    rows = lax.broadcasted_iota(jnp.int32, (ROWS, 1), 0).astype(F32)
    return first + rows - float(HALO)


def inside(places):
    return (places >= 0.0) & (places < float(FRAMES))


def envelope(places, win):
    total = jnp.zeros((ROWS, HOP), F32)
    for p in range(4):
        total = total + jnp.where(inside(places + float(2 - p)), win[1:2, HOP * p : HOP * (p + 1)], 0.0)
    return jnp.where(inside(places), total, 1.0)


def spec(space):
    return pl.BlockSpec(memory_space=space)


def full(*shape, dtype=F32):
    return jax.ShapeDtypeStruct(shape, dtype)


def halo_kernel(comb, out, send, recv):
    tm = lax.axis_index("tm")
    right, left = lax.rem(tm + 1, 8), lax.rem(tm + 7, 8)
    barrier = pltpu.get_barrier_semaphore()
    for there in (left, right):
        pl.semaphore_signal(barrier, inc=1, device_id={"tm": there}, device_id_type=MESH)
    pl.semaphore_wait(barrier, 2)
    copies = []
    for i, (src, dst, there) in enumerate(
        ((OWN - HALO, 0, right), (0, OWN + HALO, left))
    ):
        copies.append(
            pltpu.make_async_remote_copy(
                src_ref=comb.at[pl.ds(src, HALO)],
                dst_ref=out.at[pl.ds(dst, HALO)],
                send_sem=send.at[i],
                recv_sem=recv.at[i],
                device_id={"tm": there},
                device_id_type=MESH,
            )
        )
    for copy in copies:
        copy.start()
    out[HALO : HALO + OWN, :] = comb[...]
    for copy in copies:
        copy.wait()


def halo_call(comb):
    return pl.pallas_call(
        halo_kernel,
        out_shape=full(ROWS, 384),
        in_specs=[spec(pltpu.VMEM)],
        out_specs=spec(pltpu.VMEM),
        scratch_shapes=[pltpu.SemaphoreType.DMA((2,)), pltpu.SemaphoreType.DMA((2,))],
        compiler_params=pltpu.CompilerParams(collective_id=0, has_side_effects=True),
        name="halo",
    )(comb)


def forward_kernel(
    comb, kern, scale, win, table_h, up_h, down_h, head_h, syn_h, a1_h, a2_h,
    sin_o, rstd_o, y1_o, gp_o, hid_o, down_o, y2_o, re_o, im_o, d1_o, q1_o, d2_o, q2_o, stat_o,
    table_v, up_v, down_v, head_v, syn_v, a1_v, a2_v, hid_v, spec_v, seg1, seg2, sems,
):
    pairs = (
        (table_h, table_v), (up_h, up_v), (down_h, down_v), (head_h, head_v),
        (syn_h, syn_v), (a1_h, a1_v), (a2_h, a2_v),
    )
    copies = [pltpu.make_async_copy(h, v, sems.at[i]) for i, (h, v) in enumerate(pairs)]
    for copy in copies:
        copy.start()
    places = frame_places(comb)
    valid = inside(places)
    lane = lax.broadcasted_iota(jnp.int32, (ROWS, 2 * FRAMES), 1).astype(F32)
    hot = (lane == comb[:, 256:257]) | (lane == comb[:, 257:258] + 1024.0)
    hot = jnp.where(hot, 1.0, 0.0).astype(BF16)
    copies[0].wait()
    y0, rstd0 = norm(mm(hot, table_v[...]))
    y0 = jnp.where(valid, y0, 0.0)
    sin_o[...] = y0
    mixture = kern[0:1, :] * shift(y0, 3)
    for k in range(1, 7):
        mixture = mixture + kern[k : k + 1, :] * shift(y0, 3 - k)
    y1, rstd1 = norm(mixture)
    y1_o[...] = y1
    normed = y1.astype(BF16)
    copies[1].wait()
    for c in range(FF // 256):
        at = slice(256 * c, 256 * (c + 1))
        up = mm(normed, up_v[:, at])
        cdf = 0.5 * (1.0 + lax.erf(up * 0.7071067811865476))
        hid_v[:, at] = (up * cdf).astype(BF16)
        gp_o[:, at] = cdf + up * (0.3989422804014327 * jnp.exp(-0.5 * up * up))
    hid_o[...] = hid_v[HALO : HALO + OWN, :]
    copies[2].wait()
    down = mm(hid_v[...], down_v[...])
    down_o[...] = down
    y2, rstd2 = norm(sin_o[...] + scale[...] * down)
    y2_o[...] = y2
    places128 = lax.broadcasted_iota(jnp.int32, (ROWS, 128), 1)
    rstd_o[...] = jnp.where(places128 == 0, rstd0, jnp.where(places128 == 1, rstd1, rstd2))
    onorm = y2.astype(BF16)
    copies[3].wait()
    for c in range(CHUNKS1):
        head = mm(onorm, head_v[:, 256 * c : 256 * (c + 1)])
        mag = jnp.exp(head[:, :128])
        phase = head[:, 128:]
        re, im = mag * jnp.cos(phase), mag * jnp.sin(phase)
        re_o[:, 128 * c : 128 * (c + 1)] = re
        im_o[:, 128 * c : 128 * (c + 1)] = im
        spec_v[:, 256 * c : 256 * c + 128] = re.astype(BF16)
        spec_v[:, 256 * c + 128 : 256 * (c + 1)] = im.astype(BF16)
    copies[4].wait()
    pred = jnp.zeros((ROWS, HOP), F32)
    for p in range(4):
        piece = jnp.where(valid, mm(spec_v[...], syn_v[:, HOP * p : HOP * (p + 1)]), 0.0)
        pred = pred + shift(piece, p - 2)
    pred = jnp.where(valid, pred / envelope(places, win), 0.0)
    goal = jnp.where(valid, comb[:, :HOP], 0.0)
    for s, x in enumerate((pred, goal)):
        r1 = slice(ROWS * s, ROWS * (s + 1))
        for p in range(4):
            at = slice(HOP * p, HOP * (p + 1))
            seg1[r1, at] = (shift(x, 2 - p) * win[0:1, at]).astype(BF16)
        even = slice(2 * ROWS * s, 2 * ROWS * s + ROWS)
        odd = slice(2 * ROWS * s + ROWS, 2 * ROWS * (s + 1))
        before, after = shift(x, 1), shift(x, -1)
        seg2[even, 0:256] = (before * win[2:3, 0:256]).astype(BF16)
        seg2[even, 256:512] = (x * win[2:3, 256:512]).astype(BF16)
        seg2[odd, 0:128] = (before[:, 128:] * win[2:3, 0:128]).astype(BF16)
        seg2[odd, 128:384] = (x * win[2:3, 128:384]).astype(BF16)
        seg2[odd, 384:512] = (after[:, :128] * win[2:3, 384:512]).astype(BF16)
    own = slice(HALO, HALO + OWN)
    for level in range(2):
        seg, table, chunks = ((seg1, a1_v, CHUNKS1), (seg2, a2_v, CHUNKS2))[level]
        d_o, q_o = ((d1_o, q1_o), (d2_o, q2_o))[level]
        copies[5 + level].wait()
        sums = [jnp.zeros((OWN, 128), F32) for _ in range(3)]
        for c in range(chunks):
            for sub in range(level + 1):
                rows_p = slice(ROWS * sub, ROWS * (sub + 1))
                base = ROWS * (level + 1)
                rows_g = slice(base + ROWS * sub, base + ROWS * (sub + 1))
                weights = table[:, 256 * c : 256 * (c + 1)]
                sp, sg = mm(seg[rows_p, :], weights), mm(seg[rows_g, :], weights)
                diff = sp - sg
                pr, pi, gr, gi = sp[:, :128], sp[:, 128:], sg[:, :128], sg[:, 128:]
                power_p, power_g = pr * pr + pi * pi, gr * gr + gi * gi
                gap = jnp.log1p(power_p) - jnp.log1p(power_g)
                slope = jnp.where(valid, 4.0 * gap / (1.0 + power_p), 0.0)
                d_o[rows_p, 256 * c : 256 * (c + 1)] = jnp.where(valid, diff, 0.0)
                q_o[rows_p, 256 * c : 256 * c + 128] = slope * pr
                q_o[rows_p, 256 * c + 128 : 256 * (c + 1)] = slope * pi
                dr, di = diff[own, :128], diff[own, 128:]
                sums[0] = sums[0] + dr * dr + di * di
                sums[1] = sums[1] + power_g[own]
                sums[2] = sums[2] + gap[own] * gap[own]
        for i in range(3):
            total = jnp.sum(jnp.sum(sums[i], axis=0, keepdims=True), axis=1, keepdims=True)
            stat_o[3 * level + i : 3 * level + i + 1, :] = jnp.broadcast_to(total, (1, 128))
    stat_o[6:8, :] = jnp.zeros((2, 128), F32)


def forward_call(comb, kern, scale, win, table, up_w, down_w, head_w, syn, a1, a2):
    outs = [
        full(ROWS, D), full(ROWS, 128), full(ROWS, D), full(ROWS, FF), full(OWN, FF, dtype=BF16),
        full(ROWS, D), full(ROWS, D), full(ROWS, CHUNKS1 * 128), full(ROWS, CHUNKS1 * 128),
        full(ROWS, WIDE1), full(ROWS, WIDE1), full(2 * ROWS, WIDE2), full(2 * ROWS, WIDE2),
        full(8, 128),
    ]
    big = (table, up_w, down_w, head_w, syn, a1, a2)
    return pl.pallas_call(
        forward_kernel,
        out_shape=outs,
        in_specs=[spec(pltpu.VMEM)] * 4 + [spec(pl.ANY)] * len(big),
        out_specs=[spec(pltpu.VMEM)] * len(outs),
        scratch_shapes=[pltpu.VMEM(a.shape, BF16) for a in big]
        + [
            pltpu.VMEM((ROWS, FF), BF16),
            pltpu.VMEM((ROWS, WIDE1), BF16),
            pltpu.VMEM((2 * ROWS, NFFT), BF16),
            pltpu.VMEM((4 * ROWS, NFFT // 2), BF16),
            pltpu.SemaphoreType.DMA((len(big),)),
        ],
        compiler_params=pltpu.CompilerParams(vmem_limit_bytes=56 * MB),
        name="forward",
    )(comb, kern, scale, win, *big)


def stat_kernel(stat, out, slots, send, recv):
    tm = lax.axis_index("tm")
    barrier = pltpu.get_barrier_semaphore()
    others = [lax.rem(tm + j, 8) for j in range(1, 8)]
    for there in others:
        pl.semaphore_signal(barrier, inc=1, device_id={"tm": there}, device_id_type=MESH)
    pl.semaphore_wait(barrier, 7)
    copies = []
    for j, there in enumerate(others):
        copies.append(
            pltpu.make_async_remote_copy(
                src_ref=stat,
                dst_ref=slots.at[tm],
                send_sem=send.at[j],
                recv_sem=recv.at[j],
                device_id={"tm": there},
                device_id_type=MESH,
            )
        )
    for copy in copies:
        copy.start()
    slots[tm] = stat[...]
    for copy in copies:
        copy.wait()
    total = slots[0]
    for j in range(1, 8):
        total = total + slots[j]
    out[...] = total


def stat_call(stat):
    return pl.pallas_call(
        stat_kernel,
        out_shape=full(8, 128),
        in_specs=[spec(pltpu.VMEM)],
        out_specs=spec(pltpu.VMEM),
        scratch_shapes=[
            pltpu.VMEM((8, 8, 128), F32),
            pltpu.SemaphoreType.DMA((7,)),
            pltpu.SemaphoreType.DMA((7,)),
        ],
        compiler_params=pltpu.CompilerParams(collective_id=1, has_side_effects=True),
        name="clip_sums",
    )(stat)


def backward_kernel(
    comb, kern, scale, win, stat, loss_scale,
    sin_i, rstd_i, y1_i, gp_i, hid_i, down_i, y2_i, re_i, im_i, d1_i, q1_i, d2_i, q2_i,
    a1_h, a2_h, syn_h, head_h, down_h, up_h, pick_n_h, pick_h_h, pick_k_h,
    nrm_o, hid_o, onm_o, dup_o, ddn_o, dhd_o, dem_o, ids_o, kg_o,
    a1_v, a2_v, syn_v, head_v, down_v, up_v, pick_n, pick_h, pick_k,
    dfr, dhead, dup, small, sems,
):
    pairs = (
        (a1_h, a1_v), (a2_h, a2_v), (syn_h, syn_v), (head_h, head_v), (down_h, down_v),
        (up_h, up_v), (pick_n_h, pick_n), (pick_h_h, pick_h), (pick_k_h, pick_k),
    )
    copies = [pltpu.make_async_copy(h, v, sems.at[i]) for i, (h, v) in enumerate(pairs)]
    for copy in copies:
        copy.start()
    own = slice(HALO, HALO + OWN)
    places = frame_places(comb)
    valid = inside(places)
    ids_o[...] = comb[own, 256:384]

    factor = loss_scale[...] * (0.5 / CLIPS)
    loss = jnp.zeros((1, 1), F32)
    cots = []
    for level in range(2):
        count = ((FRAMES * 513), (2 * FRAMES * 257))[level]
        sum_a = stat[3 * level : 3 * level + 1, 0:1]
        sum_b = stat[3 * level + 1 : 3 * level + 2, 0:1]
        sum_g = stat[3 * level + 2 : 3 * level + 3, 0:1]
        root_a, root_b = jnp.sqrt(sum_a + 1e-6), jnp.sqrt(sum_b + 1e-6)
        loss = loss + root_a / root_b + sum_g * (1.0 / count)
        cots.append((factor / (root_a * root_b), factor * (1.0 / count)))
    loss = jnp.where(comb[HALO : HALO + 1, 258:259] == 0.0, loss, 0.0)

    dx = jnp.zeros((ROWS, HOP), F32)
    copies[0].wait()
    ds1 = (cots[0][0] * d1_i[...] + cots[0][1] * q1_i[...]).astype(BF16)
    for p in range(4):
        at = slice(HOP * p, HOP * (p + 1))
        piece = mm_bt(ds1, a1_v[at, :]).astype(BF16).astype(F32) * win[0:1, at]
        dx = dx + shift(piece, p - 2)
    copies[1].wait()
    ds2 = (cots[1][0] * d2_i[...] + cots[1][1] * q2_i[...]).astype(BF16)
    dseg = mm_bt(ds2, a2_v[...]).astype(BF16).astype(F32) * win[2:3, : NFFT // 2]
    even, odd = dseg[:ROWS], dseg[ROWS:]
    dx = dx + shift(even[:, :256], -1) + even[:, 256:] + odd[:, 128:384]
    dx = dx + jnp.concatenate([shift(odd[:, 384:], 1), shift(odd[:, :128], -1)], axis=1)
    dx = jnp.where(valid, dx / envelope(places, win), 0.0)
    for p in range(4):
        piece = jnp.where(valid, shift(dx, 2 - p), 0.0)
        dfr[:, HOP * p : HOP * (p + 1)] = piece.astype(BF16)

    copies[2].wait()
    for c in range(CHUNKS1):
        dsp = mm_bt(dfr[...], syn_v[256 * c : 256 * (c + 1), :]).astype(BF16).astype(F32)
        dre, dim = dsp[:, :128], dsp[:, 128:]
        re, im = re_i[:, 128 * c : 128 * (c + 1)], im_i[:, 128 * c : 128 * (c + 1)]
        dlog, dph = dre * re + dim * im, dim * re - dre * im
        dhead[:, 256 * c : 256 * c + 128] = dlog.astype(BF16)
        dhead[:, 256 * c + 128 : 256 * (c + 1)] = dph.astype(BF16)
    dhd_o[:, :1024] = dhead[own, :1024].astype(F32)
    tail = dhead[own, 1024:1152].astype(F32) + pltpu.roll(dhead[own, 1152:1280].astype(F32), 1, 1)
    dhd_o[:, 1024:] = tail
    copies[3].wait()
    don = mm_bt(dhead[...], head_v[...]).astype(BF16).astype(F32)
    dstream = norm_back(don, y2_i[...], rstd_i[:, 2:3])

    scale_grad = jnp.sum(dstream[own] * down_i[own, :], axis=0, keepdims=True)
    ddn = (scale[...] * dstream).astype(BF16)
    ddn_o[...] = ddn[own].astype(F32)
    copies[4].wait()
    for c in range(FF // 256):
        at = slice(256 * c, 256 * (c + 1))
        dh = mm_bt(ddn, down_v[at, :]).astype(BF16).astype(F32)
        dup[:, at] = (dh * gp_i[:, at]).astype(BF16)
    dup_o[...] = dup[own, :].astype(F32)
    copies[5].wait()
    dnorm = mm_bt(dup[...], up_v[...]).astype(BF16).astype(F32)
    dmix = norm_back(dnorm, y1_i[...], rstd_i[:, 1:2])
    dmix = jnp.where(valid, dmix, 0.0)
    y0 = sin_i[...]
    dsin = dstream
    small[...] = jnp.zeros((128, D), F32)
    for k in range(7):
        dsin = dsin + kern[k : k + 1, :] * shift(dmix, k - 3)
        taps = dmix * shift(y0, 3 - k)
        small[2 + k : 3 + k, :] = jnp.sum(taps[own], axis=0, keepdims=True)
    demb = norm_back(dsin, y0, rstd_i[:, 0:1])
    dem_o[...] = demb[own].astype(BF16).astype(F32)

    small[9:10, :] = scale_grad
    rest = loss
    for i, grid in enumerate((65536.0, 1.0, 1.0 / 65536.0, 1.0 / 65536.0 / 65536.0)):
        piece = jnp.floor(rest * (1.0 / grid)) * grid
        rest = rest - piece
        small[10 + i : 11 + i, :] = jnp.broadcast_to(piece, (1, D))

    for i in (6, 7, 8):
        copies[i].wait()
    normed = y1_i[own, :].astype(BF16)
    onorm = y2_i[own, :].astype(BF16)
    small0 = small[...].astype(BF16)
    left = small[...] - small0.astype(F32)
    small1 = left.astype(BF16)
    small2 = (left - small1.astype(F32)).astype(BF16)
    for c in range(2):
        nrm_o[c] = mm(normed, pick_n[c])
        onm_o[c] = mm(onorm, pick_n[c])
        for h in range(2):
            out = slice(576 * h, 576 * (h + 1))
            hid_o[c, :, out] = mm(hid_i[:, 1152 * h : 1152 * (h + 1)], pick_h[c])
        kg_o[c] = sum(
            lax.dot_general(pick_k[c], s, (((0,), (1,)), ((), ())), preferred_element_type=F32)
            for s in (small0, small1, small2)
        )


def backward_call(comb, kern, scale, win, stat, loss_scale, saved, big):
    outs = [
        full(2, OWN, 384), full(2, OWN, 1152), full(2, OWN, 384), full(OWN, FF), full(OWN, D),
        full(OWN, 1152), full(OWN, D), full(OWN, 128), full(2, 384, 128),
    ]
    return pl.pallas_call(
        backward_kernel,
        out_shape=outs,
        in_specs=[spec(pltpu.VMEM)] * (6 + len(saved)) + [spec(pl.ANY)] * len(big),
        out_specs=[spec(pltpu.VMEM)] * len(outs),
        scratch_shapes=[pltpu.VMEM(a.shape, BF16) for a in big]
        + [
            pltpu.VMEM((ROWS, NFFT), BF16),
            pltpu.VMEM((ROWS, WIDE1), BF16),
            pltpu.VMEM((ROWS, FF), BF16),
            pltpu.VMEM((128, D), F32),
            pltpu.SemaphoreType.DMA((len(big),)),
        ],
        compiler_params=pltpu.CompilerParams(vmem_limit_bytes=56 * MB),
        name="backward",
    )(comb, kern, scale, win, stat, loss_scale, *saved, *big)


PICKED = (True, True, True, False, False, False, False, False, True)


def pair_kernel(*refs):
    count = len(PICKED)
    ins, outs = refs[:count], refs[count : 2 * count]
    send, recv, local = refs[2 * count :]
    dp = lax.axis_index("dp")
    core = lax.rem(dp, 2)
    partner = dp + 1 - 2 * core
    barrier = pltpu.get_barrier_semaphore()
    pl.semaphore_signal(barrier, inc=1, device_id={"dp": partner}, device_id_type=MESH)
    pl.semaphore_wait(barrier, 1)
    copies = []
    for i, picked in enumerate(PICKED):
        rows = outs[i].shape[0] // 2
        copy = pltpu.make_async_remote_copy(
            src_ref=ins[i].at[1 - core] if picked else ins[i],
            dst_ref=outs[i].at[pl.ds(rows, rows)],
            send_sem=send.at[i],
            recv_sem=recv.at[i],
            device_id={"dp": partner},
            device_id_type=MESH,
        )
        copy.start()
        copies.append(copy)
    for i, picked in enumerate(PICKED):
        rows = outs[i].shape[0] // 2
        copy = pltpu.make_async_copy(
            ins[i].at[core] if picked else ins[i], outs[i].at[pl.ds(0, rows)], local.at[i]
        )
        copy.start()
        copies.append(copy)
    for copy in copies:
        copy.wait()


def pair_call(arrays):
    count = len(arrays)
    outs = [full(2 * a.shape[-2], a.shape[-1]) for a in arrays]
    return pl.pallas_call(
        pair_kernel,
        out_shape=outs,
        in_specs=[spec(pl.ANY)] * count,
        out_specs=[spec(pl.ANY)] * count,
        scratch_shapes=[pltpu.SemaphoreType.DMA((count,))] * 3,
        compiler_params=pltpu.CompilerParams(collective_id=2, has_side_effects=True),
        name="core_pair",
    )(*arrays)


def put(out, first, values, rows):
    for block in range(values.shape[1] // 128):
        part = values[:, 128 * block : 128 * (block + 1)].reshape(4, 4, rows, 128)
        out[:, :, first + rows * block : first + rows * (block + 1), :] = part


def weight_kernel(nrm, hid, onm, dup, ddn, dhd, dem, ids, kg, turn1, turn2, row_id, p0, p1, p2):
    onorm = [onm[...].astype(BF16)]
    for turn in (turn1, turn2):
        onorm.append(mm(onorm[0], turn[...]).astype(BF16))
    normed = nrm[...].astype(BF16)
    for c in range(FF // 256):
        put(p0, 48 * c, mm_at(normed, dup[:, 256 * c : 256 * (c + 1)].astype(BF16)), 24)
    hidden = hid[...].astype(BF16)
    for c in range(3):
        put(p1, 144 * c, mm_at(hidden, ddn[:, 256 * c : 256 * (c + 1)].astype(BF16)), 72)
    core = ids[0:1, 3:4]
    rows = row_id[...] + 128.0 * core
    hot = (rows == ids[:, 0:1]) | (rows == ids[:, 1:2] + 1024.0)
    hot = jnp.where(hot, 1.0, 0.0).astype(BF16)
    for c in range(3):
        put(p2, 128 * c, mm_at(hot, dem[:, 256 * c : 256 * (c + 1)].astype(BF16)), 64)
    for k, (out, first) in enumerate(((p0, 432), (p1, 432), (p2, 384))):
        start, blocks = HEAD_BLOCKS[k]
        for b in range(blocks):
            at = slice(128 * (start + b), 128 * (start + b + 1))
            values = mm_at(onorm[k], dhd[:, at].astype(BF16))
            if start + b == 8:
                values = values + kg[:384, :] + kg[384:, :]
            put(out, first + 24 * b, values, 24)


def weight_call(arrays, turn1, turn2, row_id):
    outs = [full(4, 4, n, 128) for n in PART_ROWS]
    return pl.pallas_call(
        weight_kernel,
        out_shape=outs,
        in_specs=[spec(pltpu.VMEM)] * (len(arrays) + 3),
        out_specs=[spec(pltpu.VMEM)] * 3,
        compiler_params=pltpu.CompilerParams(vmem_limit_bytes=56 * MB),
        name="weight_grads",
    )(*arrays, turn1, turn2, row_id)


LAST_ROWS = (120, 128, 120)


def scatter_kernel(*refs):
    parts, (up_o, down_o, table_o, head_o) = refs[0:3], refs[3:7]
    scratch = refs[7:]
    mine, to_right, to_left = scratch[0:3], scratch[3:6], scratch[6:9]
    got1, got2a, got2b = scratch[9:12], scratch[12:15], scratch[15:18]
    last, got3 = scratch[18:21], scratch[21:24]
    send, recv, local = scratch[24:]

    dp, tm = lax.axis_index("dp"), lax.axis_index("tm")
    at = {"x": tm // 2, "y": dp // 4, "z": lax.rem(dp // 2, 2) * 2 + lax.rem(tm, 2)}
    core = lax.rem(dp, 2)

    def device(axis, by):
        to = dict(at)
        to[axis] = lax.rem(at[axis] + by, 4)
        return {
            "dp": (to["y"] * 2 + to["z"] // 2) * 2 + core,
            "tm": to["x"] * 2 + lax.rem(to["z"], 2),
        }

    barrier = pltpu.get_barrier_semaphore()
    for axis in "xyz":
        for by in (1, 2, 3):
            pl.semaphore_signal(barrier, inc=1, device_id=device(axis, by), device_id_type=MESH)
    pl.semaphore_wait(barrier, 9)

    def remote(src, dst, k, slot, axis, by):
        return pltpu.make_async_remote_copy(
            src_ref=src,
            dst_ref=dst,
            send_sem=send.at[k, slot],
            recv_sem=recv.at[k, slot],
            device_id=device(axis, by),
            device_id_type=MESH,
        )

    first, second = pl.ds(0, 2), pl.ds(2, 2)
    sent = []
    loads = []
    for k in range(3):
        axis, p, g = ORDERS[k][0], parts[k], got1[k]
        i = at[axis]
        right, opposite, left = lax.rem(i + 1, 4), lax.rem(i + 2, 4), lax.rem(i + 3, 4)
        copies = [
            remote(p.at[opposite, first], g.at[0], k, 0, axis, 1),
            remote(p.at[opposite, second], g.at[1], k, 1, axis, 3),
            remote(p.at[right, second], g.at[3], k, 3, axis, 1),
            remote(p.at[left, first], g.at[4], k, 4, axis, 3),
        ]
        here = [
            pltpu.make_async_copy(p.at[right, first], to_right[k], local.at[k, 0]),
            pltpu.make_async_copy(p.at[left, second], to_left[k], local.at[k, 1]),
            pltpu.make_async_copy(p.at[i], mine[k], local.at[k, 2]),
        ]
        for copy in copies + here:
            copy.start()
        sent.append(copies)
        loads.append(here)
    for k in range(3):
        axis, g = ORDERS[k][0], got1[k]
        loads[k][0].wait()
        sent[k][0].wait_recv()
        to_right[k][...] += g[0]
        sent[k].append(remote(to_right[k], g.at[2], k, 2, axis, 1))
        sent[k][-1].start()
        loads[k][1].wait()
        sent[k][1].wait_recv()
        to_left[k][...] += g[1]
        sent[k].append(remote(to_left[k], g.at[5], k, 5, axis, 3))
        sent[k][-1].start()
    for k in range(3):
        g, m = got1[k], mine[k]
        loads[k][2].wait()
        sent[k][2].wait_recv()
        sent[k][3].wait_recv()
        sent[k][4].wait_recv()
        sent[k][5].wait_recv()
        m[0:2] += g[2] + g[4]
        m[2:4] += g[3] + g[5]
        axis = ORDERS[k][1]
        i = at[axis]
        right, opposite, left = lax.rem(i + 1, 4), lax.rem(i + 2, 4), lax.rem(i + 3, 4)
        n = PART_ROWS[k]
        cut = (n // 2 + 7) // 8 * 8
        upper, lower = pl.ds(0, cut), pl.ds(cut, n - cut)
        a, b = got2a[k], got2b[k]
        copies = [
            remote(m.at[opposite, upper], a.at[0], k, 6, axis, 1),
            remote(m.at[opposite, lower], b.at[0], k, 7, axis, 3),
            remote(m.at[right, lower], b.at[1], k, 8, axis, 1),
            remote(m.at[left, upper], a.at[1], k, 9, axis, 3),
        ]
        for copy in copies:
            copy.start()
        sent[k] = sent[k] + copies
    for k in range(3):
        axis = ORDERS[k][1]
        i = at[axis]
        right, left = lax.rem(i + 1, 4), lax.rem(i + 3, 4)
        n = PART_ROWS[k]
        cut = (n // 2 + 7) // 8 * 8
        upper, lower = pl.ds(0, cut), pl.ds(cut, n - cut)
        m, a, b = mine[k], got2a[k], got2b[k]
        sent[k][6].wait_recv()
        m[right, upper] += a[0]
        sent[k].append(remote(m.at[right, upper], a.at[2], k, 10, axis, 1))
        sent[k][-1].start()
        sent[k][7].wait_recv()
        m[left, lower] += b[0]
        sent[k].append(remote(m.at[left, lower], b.at[2], k, 11, axis, 3))
        sent[k][-1].start()
    for k in range(3):
        axis = ORDERS[k][1]
        i = at[axis]
        n = PART_ROWS[k]
        cut = (n // 2 + 7) // 8 * 8
        upper, lower = pl.ds(0, cut), pl.ds(cut, n - cut)
        m, a, b, out = mine[k], got2a[k], got2b[k], last[k]
        for j in (8, 9, 10, 11):
            sent[k][j].wait_recv()
        m[i, upper] += a[1] + a[2]
        m[i, lower] += b[1] + b[2]
        blocks = (((18, 24), (2, 24)), ((6, 72), (3, 24)), ((6, 64), (4, 24)))[k]
        start, place = 0, 0
        for count, rows in blocks:
            each = rows // 4
            for _ in range(count):
                for d in range(4):
                    out[d, pl.ds(place, each)] = m[i, pl.ds(start + d * each, each)]
                start += rows
                place += each
        if place < LAST_ROWS[k]:
            for d in range(4):
                out[d, pl.ds(place, LAST_ROWS[k] - place)] = jnp.zeros(
                    (LAST_ROWS[k] - place, 128), F32
                )
        axis = ORDERS[k][2]
        i = at[axis]
        for by in (1, 2, 3):
            copy = remote(
                out.at[lax.rem(i + by, 4)], got3[k].at[by - 1], k, 11 + by, axis, by
            )
            copy.start()
            sent[k].append(copy)
    for k in range(3):
        for j in (12, 13, 14):
            sent[k][j].wait_recv()
        total = last[k][at[ORDERS[k][2]]] + got3[k][0] + got3[k][1] + got3[k][2]
        out, count, each = ((up_o, 18, 6), (down_o, 6, 18), (table_o, 6, 16))[k]
        for c in range(count):
            out[:, 128 * c : 128 * (c + 1)] = total[each * c : each * (c + 1)]
        start, blocks = HEAD_BLOCKS[k]
        for c in range(blocks):
            rows = count * each + 6 * c
            head_o[:, 128 * (start + c) : 128 * (start + c + 1)] = total[rows : rows + 6]
    for k in range(3):
        for copy in sent[k]:
            copy.wait_send()


def scatter_call(parts):
    def each(make):
        return [make(k) for k in range(3)]

    rows = PART_ROWS
    cuts = [(n // 2 + 7) // 8 * 8 for n in rows]
    return pl.pallas_call(
        scatter_kernel,
        out_shape=[full(6, FF), full(18, D), full(16, D), full(6, 1152)],
        in_specs=[spec(pl.ANY)] * 3,
        out_specs=[spec(pltpu.VMEM)] * 4,
        scratch_shapes=each(lambda k: pltpu.VMEM((4, rows[k], 128), F32))
        + each(lambda k: pltpu.VMEM((2, rows[k], 128), F32))
        + each(lambda k: pltpu.VMEM((2, rows[k], 128), F32))
        + each(lambda k: pltpu.VMEM((6, 2, rows[k], 128), F32))
        + each(lambda k: pltpu.VMEM((3, cuts[k], 128), F32))
        + each(lambda k: pltpu.VMEM((3, rows[k] - cuts[k], 128), F32))
        + each(lambda k: pltpu.VMEM((4, LAST_ROWS[k], 128), F32))
        + each(lambda k: pltpu.VMEM((3, LAST_ROWS[k], 128), F32))
        + [
            pltpu.SemaphoreType.DMA((3, 15)),
            pltpu.SemaphoreType.DMA((3, 15)),
            pltpu.SemaphoreType.DMA((3, 3)),
        ],
        compiler_params=pltpu.CompilerParams(
            collective_id=3, has_side_effects=True, vmem_limit_bytes=48 * MB
        ),
        name="reduce_scatter",
    )(*parts)


def lay_out_head(head_weight):
    def halves(part):
        padded = jnp.pad(part, ((0, 0), (0, CHUNKS1 * 128 - part.shape[1])))
        return padded.reshape(D, CHUNKS1, 128)

    both = jnp.stack([halves(head_weight[:, :513]), halves(head_weight[:, 513:])], axis=2)
    return both.reshape(D, WIDE1)


def assemble(up, down, table, head):
    mags = [head[:, 256 * c : 256 * c + 128] for c in range(4)] + [head[:, 1024:1025]]
    phases = [head[:, 256 * c + 128 : 256 * (c + 1)] for c in range(4)] + [head[:, 1025:1026]]
    head_grad = jnp.concatenate(mags + phases, axis=1)
    loss = (head[0, 1034] + head[0, 1035] + (head[0, 1036] + head[0, 1037])) * (0.5 / CLIPS)
    return loss, table, head[:, 1026:1033].T, up, down, head[:, 1033], head_grad


def body(
    code_ids, code_table, kernel, up_weight, down_weight, layer_scale, head_weight, target, loss_scale
):
    syn, a1, a2, win = make_constants()
    pick_n, pick_h, pick_k, turn1, turn2, row_id = make_orders()
    place = jnp.stack(
        [
            (lax.axis_index("tm") * OWN).astype(F32),
            lax.rem(lax.axis_index("dp"), 2).astype(F32),
        ]
    )
    comb = jnp.concatenate(
        [
            target.reshape(OWN, HOP),
            code_ids.reshape(OWN, 2).astype(F32),
            jnp.broadcast_to(place[None, :], (OWN, 2)),
            jnp.zeros((OWN, 124), F32),
        ],
        axis=1,
    )
    comb = halo_call(comb)
    kern = jnp.pad(kernel, ((0, 1), (0, 0)))
    scale = layer_scale.reshape(1, D)
    head_w = lay_out_head(head_weight)
    saved = forward_call(
        comb, kern, scale, win, code_table, up_weight, down_weight, head_w, syn, a1, a2
    )
    stat = stat_call(saved[-1])
    operands = backward_call(
        comb, kern, scale, win, stat, loss_scale.reshape(1, 1), saved[:-1],
        (a1, a2, syn, head_w, down_weight, up_weight, pick_n, pick_h, pick_k),
    )
    parts = weight_call(pair_call(operands), turn1, turn2, row_id)
    return assemble(*scatter_call(parts))


def solution(mesh):
    in_specs = (P("dp", "tm", None), P(), P(), P(), P(), P(), P(), P("dp", "tm"), P())
    out_specs = (
        P(),
        P(("dp", "tm"), None),
        P(None, ("dp", "tm")),
        P(("dp", "tm"), None),
        P(("dp", "tm"), None),
        P(("dp", "tm")),
        P(("dp", "tm"), None),
    )
    return jax.shard_map(body, mesh=mesh, in_specs=in_specs, out_specs=out_specs, check_vma=False)
```

```python
import jax
import jax.numpy as jnp
import ml_dtypes
import numpy as np
from jax import lax
from jax.experimental import pallas as pl
from jax.experimental.pallas import tpu as pltpu
from jax.sharding import PartitionSpec as P

F32, BF16 = jnp.float32, jnp.bfloat16
MESH = pl.DeviceIdType.MESH
D, FF = 768, 2304
HOP, NFFT = 256, 1024
FRAMES, OWN, HALO = 1024, 128, 16
ROWS = OWN + 2 * HALO
CHUNKS1, CHUNKS2 = 5, 3
WIDE1, WIDE2 = CHUNKS1 * 256, CHUNKS2 * 256
CLIPS = 16
MB = 1 << 20
ORDERS = ("xyz", "yzx", "zxy")
HEAD_BLOCKS = ((0, 2), (2, 3), (5, 4))
PART_ROWS = (18 * 24 + 2 * 24, 6 * 72 + 3 * 24, 6 * 64 + 4 * 24)


def bf(array):
    return np.asarray(array, np.float32).astype(ml_dtypes.bfloat16)


def hann(length):
    return 0.5 - 0.5 * np.cos(2.0 * np.pi * np.arange(length) / length)


def angles(length):
    product = np.arange(length // 2 + 1)[:, None] * np.arange(length)[None, :] % length
    return 2.0 * np.pi * product / length


def interleave(real, imag, chunks):
    bins, width = real.shape
    out = np.zeros((chunks, 2, 128, width), np.float64)
    for half, part in enumerate((real, imag)):
        padded = np.zeros((chunks * 128, width), np.float64)
        padded[:bins] = part
        out[:, half] = padded.reshape(chunks, 128, width)
    return out.reshape(chunks * 256, width)


def make_constants():
    ang = angles(NFFT)
    bins = np.arange(NFFT // 2 + 1)
    factor = np.where((bins == 0) | (bins == NFFT // 2), 1.0, 2.0)[:, None] / NFFT
    window = hann(NFFT)[None, :]
    synthesis = bf(interleave(factor * np.cos(ang) * window, -factor * np.sin(ang) * window, CHUNKS1))
    analysis1 = bf(interleave(np.cos(ang), -np.sin(ang), CHUNKS1).T)
    ang = angles(NFFT // 2)
    analysis2 = bf(interleave(np.cos(ang), -np.sin(ang), CHUNKS2).T)
    win = np.zeros((8, NFFT), np.float32)
    win[0] = hann(NFFT)
    win[1] = hann(NFFT) ** 2
    win[2, : NFFT // 2] = hann(NFFT // 2)
    return synthesis, analysis1, analysis2, win


def device_index(x, y, z, core):
    return ((y * 2 + z // 2) * 2 + core) * 8 + x * 2 + z % 2


def shard_order(order, core):
    places = []
    for a in range(4):
        for b in range(4):
            for c in range(4):
                at = dict(zip(order, (a, b, c)))
                places.append(device_index(at["x"], at["y"], at["z"], core))
    return np.array(places)


def columns_of(order, core, each):
    return (shard_order(order, core)[:, None] * each + np.arange(each)[None, :]).reshape(-1)


def one_hot_columns(sources, size):
    out = np.zeros((size, sources.size), np.float32)
    out[sources, np.arange(sources.size)] = 1.0
    return bf(out)


def make_orders():
    pick_n = np.stack([one_hot_columns(columns_of(ORDERS[0], c, 6), D) for c in (0, 1)])
    half = [columns_of(ORDERS[1], c, 18)[: 4 * 4 * 2 * 18] for c in (0, 1)]
    pick_h = np.stack([one_hot_columns(h, FF // 2) for h in half])
    pick_k = np.stack([one_hot_columns(columns_of(ORDERS[2], c, 6), D) for c in (0, 1)])
    first = columns_of(ORDERS[0], 0, 6)
    where = {col: i for i, col in enumerate(first)}
    turns = []
    for k in (1, 2):
        sources = np.array([where[col] for col in columns_of(ORDERS[k], 0, 6)])
        turns.append(one_hot_columns(sources, 384))
    row_id = columns_of(ORDERS[2], 0, 16).astype(np.float32)[None, :]
    return pick_n, pick_h, pick_k, turns[0], turns[1], row_id


def mm(a, b):
    return jnp.dot(a, b, preferred_element_type=F32)


def mm_bt(a, b):
    return lax.dot_general(a, b, (((1,), (1,)), ((), ())), preferred_element_type=F32)


def mm_at(a, b):
    return lax.dot_general(a, b, (((0,), (0,)), ((), ())), preferred_element_type=F32)


def shift(values, by):
    by = by % values.shape[0]
    return values if by == 0 else pltpu.roll(values, by, 0)


def norm(values):
    centre = values - jnp.mean(values, axis=-1, keepdims=True)
    rstd = lax.rsqrt(jnp.mean(centre * centre, axis=-1, keepdims=True) + 1e-6)
    return centre * rstd, rstd


def norm_back(grad, y, rstd):
    mean_g = jnp.mean(grad, axis=-1, keepdims=True)
    mean_gy = jnp.mean(grad * y, axis=-1, keepdims=True)
    return rstd * (grad - mean_g - y * mean_gy)


def frame_places(comb):
    first = comb[HALO : HALO + 1, 258:259]
    rows = lax.broadcasted_iota(jnp.int32, (ROWS, 1), 0).astype(F32)
    return first + rows - float(HALO)


def inside(places):
    return (places >= 0.0) & (places < float(FRAMES))


def envelope(places, win):
    total = jnp.zeros((ROWS, HOP), F32)
    for p in range(4):
        total = total + jnp.where(inside(places + float(2 - p)), win[1:2, HOP * p : HOP * (p + 1)], 0.0)
    return jnp.where(inside(places), total, 1.0)


def spec(space):
    return pl.BlockSpec(memory_space=space)


def full(*shape, dtype=F32):
    return jax.ShapeDtypeStruct(shape, dtype)


def halo_kernel(target, ids, out, comb, send, recv):
    tm = lax.axis_index("tm")
    lane = lax.broadcasted_iota(jnp.int32, (OWN, 128), 1)
    marks = jnp.where(lane == 2, tm * OWN, lax.rem(lax.axis_index("dp"), 2))
    marks = jnp.where(lane == 0, ids[:, 0:1], jnp.where(lane == 1, ids[:, 1:2], marks))
    comb[:, :HOP] = target[...]
    comb[:, HOP:] = marks.astype(F32)
    right, left = lax.rem(tm + 1, 8), lax.rem(tm + 7, 8)
    barrier = pltpu.get_barrier_semaphore()
    for there in (left, right):
        pl.semaphore_signal(barrier, inc=1, device_id={"tm": there}, device_id_type=MESH)
    pl.semaphore_wait(barrier, 2)
    copies = []
    for i, (src, dst, there) in enumerate(
        ((OWN - HALO, 0, right), (0, OWN + HALO, left))
    ):
        copies.append(
            pltpu.make_async_remote_copy(
                src_ref=comb.at[pl.ds(src, HALO)],
                dst_ref=out.at[pl.ds(dst, HALO)],
                send_sem=send.at[i],
                recv_sem=recv.at[i],
                device_id={"tm": there},
                device_id_type=MESH,
            )
        )
    for copy in copies:
        copy.start()
    out[HALO : HALO + OWN, :] = comb[...]
    for copy in copies:
        copy.wait()


def halo_call(target, ids):
    return pl.pallas_call(
        halo_kernel,
        out_shape=full(ROWS, 384),
        in_specs=[spec(pltpu.VMEM)] * 2,
        out_specs=spec(pltpu.VMEM),
        scratch_shapes=[
            pltpu.VMEM((OWN, 384), F32),
            pltpu.SemaphoreType.DMA((2,)),
            pltpu.SemaphoreType.DMA((2,)),
        ],
        compiler_params=pltpu.CompilerParams(collective_id=0, has_side_effects=True),
        name="halo",
    )(target, ids)


def forward_kernel(
    comb, kern, scale, win, table_h, up_h, down_h, head_h, syn_h, a1_h, a2_h,
    sin_o, rstd_o, y1_o, gp_o, hid_o, down_o, y2_o, re_o, im_o, d1_o, q1_o, d2_o, q2_o, stat_o,
    table_v, up_v, down_v, head_v, syn_v, a1_v, a2_v, hid_v, head_s, spec_v, seg1, seg2, sems,
):
    pairs = (
        (table_h, table_v), (up_h, up_v), (down_h, down_v), (head_h, head_v),
        (syn_h, syn_v), (a1_h, a1_v), (a2_h, a2_v),
    )
    copies = [pltpu.make_async_copy(h, v, sems.at[i]) for i, (h, v) in enumerate(pairs)]
    for copy in copies:
        copy.start()
    places = frame_places(comb)
    valid = inside(places)
    lane = lax.broadcasted_iota(jnp.int32, (ROWS, 2 * FRAMES), 1).astype(F32)
    hot = (lane == comb[:, 256:257]) | (lane == comb[:, 257:258] + 1024.0)
    hot = jnp.where(hot, 1.0, 0.0).astype(BF16)
    copies[0].wait()
    y0, rstd0 = norm(mm(hot, table_v[...]))
    y0 = jnp.where(valid, y0, 0.0)
    sin_o[...] = y0
    mixture = kern[0:1, :] * shift(y0, 3)
    for k in range(1, 7):
        mixture = mixture + kern[k : k + 1, :] * shift(y0, 3 - k)
    y1, rstd1 = norm(mixture)
    y1_o[...] = y1
    normed = y1.astype(BF16)
    copies[1].wait()
    for c in range(FF // 256):
        at = slice(256 * c, 256 * (c + 1))
        up = mm(normed, up_v[:, at])
        cdf = 0.5 * (1.0 + lax.erf(up * 0.7071067811865476))
        hid_v[:, at] = (up * cdf).astype(BF16)
        gp_o[:, at] = cdf + up * (0.3989422804014327 * jnp.exp(-0.5 * up * up))
    hid_o[...] = hid_v[HALO : HALO + OWN, :]
    copies[2].wait()
    down = mm(hid_v[...], down_v[...])
    down_o[...] = down
    y2, rstd2 = norm(sin_o[...] + scale[...] * down)
    y2_o[...] = y2
    places128 = lax.broadcasted_iota(jnp.int32, (ROWS, 128), 1)
    rstd_o[...] = jnp.where(places128 == 0, rstd0, jnp.where(places128 == 1, rstd1, rstd2))
    onorm = y2.astype(BF16)
    copies[3].wait()
    head_s[:, 1024:] = jnp.zeros((ROWS, 128), F32)
    for c in range(4):
        head_s[:, 256 * c : 256 * (c + 1)] = mm(onorm, head_v[:, 256 * c : 256 * (c + 1)])
    head_s[:, 1024:1026] = mm(onorm, head_v[:, 1024:1026])
    phases = pltpu.roll(head_s[:, 512:], CHUNKS1 * 128 - 1, 1)
    for c in range(CHUNKS1):
        logmag = head_s[:, 128 * c : 128 * (c + 1)]
        if c == 4:
            logmag = jnp.where(places128 == 0, logmag, 0.0)
        mag = jnp.exp(logmag)
        phase = phases[:, 128 * c : 128 * (c + 1)]
        re, im = mag * jnp.cos(phase), mag * jnp.sin(phase)
        re_o[:, 128 * c : 128 * (c + 1)] = re
        im_o[:, 128 * c : 128 * (c + 1)] = im
        spec_v[:, 256 * c : 256 * c + 128] = re.astype(BF16)
        spec_v[:, 256 * c + 128 : 256 * (c + 1)] = im.astype(BF16)
    copies[4].wait()
    pred = jnp.zeros((ROWS, HOP), F32)
    for p in range(4):
        piece = jnp.where(valid, mm(spec_v[...], syn_v[:, HOP * p : HOP * (p + 1)]), 0.0)
        pred = pred + shift(piece, p - 2)
    pred = jnp.where(valid, pred / envelope(places, win), 0.0)
    goal = jnp.where(valid, comb[:, :HOP], 0.0)
    for s, x in enumerate((pred, goal)):
        r1 = slice(ROWS * s, ROWS * (s + 1))
        for p in range(4):
            at = slice(HOP * p, HOP * (p + 1))
            seg1[r1, at] = (shift(x, 2 - p) * win[0:1, at]).astype(BF16)
        even = slice(2 * ROWS * s, 2 * ROWS * s + ROWS)
        odd = slice(2 * ROWS * s + ROWS, 2 * ROWS * (s + 1))
        before, after = shift(x, 1), shift(x, -1)
        seg2[even, 0:256] = (before * win[2:3, 0:256]).astype(BF16)
        seg2[even, 256:512] = (x * win[2:3, 256:512]).astype(BF16)
        seg2[odd, 0:128] = (before[:, 128:] * win[2:3, 0:128]).astype(BF16)
        seg2[odd, 128:384] = (x * win[2:3, 128:384]).astype(BF16)
        seg2[odd, 384:512] = (after[:, :128] * win[2:3, 384:512]).astype(BF16)
    own = slice(HALO, HALO + OWN)
    for level in range(2):
        seg, table, chunks = ((seg1, a1_v, CHUNKS1), (seg2, a2_v, CHUNKS2))[level]
        d_o, q_o = ((d1_o, q1_o), (d2_o, q2_o))[level]
        copies[5 + level].wait()
        sums = [jnp.zeros((OWN, 128), F32) for _ in range(3)]
        for c in range(chunks):
            for sub in range(level + 1):
                rows_p = slice(ROWS * sub, ROWS * (sub + 1))
                base = ROWS * (level + 1)
                rows_g = slice(base + ROWS * sub, base + ROWS * (sub + 1))
                weights = table[:, 256 * c : 256 * (c + 1)]
                sp, sg = mm(seg[rows_p, :], weights), mm(seg[rows_g, :], weights)
                diff = sp - sg
                pr, pi, gr, gi = sp[:, :128], sp[:, 128:], sg[:, :128], sg[:, 128:]
                power_p, power_g = pr * pr + pi * pi, gr * gr + gi * gi
                gap = jnp.log1p(power_p) - jnp.log1p(power_g)
                slope = jnp.where(valid, 4.0 * gap / (1.0 + power_p), 0.0)
                d_o[rows_p, 256 * c : 256 * (c + 1)] = jnp.where(valid, diff, 0.0)
                q_o[rows_p, 256 * c : 256 * c + 128] = slope * pr
                q_o[rows_p, 256 * c + 128 : 256 * (c + 1)] = slope * pi
                dr, di = diff[own, :128], diff[own, 128:]
                sums[0] = sums[0] + dr * dr + di * di
                sums[1] = sums[1] + power_g[own]
                sums[2] = sums[2] + gap[own] * gap[own]
        for i in range(3):
            total = jnp.sum(jnp.sum(sums[i], axis=0, keepdims=True), axis=1, keepdims=True)
            stat_o[3 * level + i : 3 * level + i + 1, :] = jnp.broadcast_to(total, (1, 128))
    stat_o[6:8, :] = jnp.zeros((2, 128), F32)


def forward_call(comb, kern, scale, win, table, up_w, down_w, head_w, syn, a1, a2):
    outs = [
        full(ROWS, D), full(ROWS, 128), full(ROWS, D), full(ROWS, FF), full(OWN, FF, dtype=BF16),
        full(ROWS, D), full(ROWS, D), full(ROWS, CHUNKS1 * 128), full(ROWS, CHUNKS1 * 128),
        full(ROWS, WIDE1), full(ROWS, WIDE1), full(2 * ROWS, WIDE2), full(2 * ROWS, WIDE2),
        full(8, 128),
    ]
    big = (table, up_w, down_w, head_w, syn, a1, a2)
    return pl.pallas_call(
        forward_kernel,
        out_shape=outs,
        in_specs=[spec(pltpu.VMEM)] * 4 + [spec(pl.ANY)] * len(big),
        out_specs=[spec(pltpu.VMEM)] * len(outs),
        scratch_shapes=[pltpu.VMEM(a.shape, BF16) for a in big]
        + [
            pltpu.VMEM((ROWS, FF), BF16),
            pltpu.VMEM((ROWS, 1152), F32),
            pltpu.VMEM((ROWS, WIDE1), BF16),
            pltpu.VMEM((2 * ROWS, NFFT), BF16),
            pltpu.VMEM((4 * ROWS, NFFT // 2), BF16),
            pltpu.SemaphoreType.DMA((len(big),)),
        ],
        compiler_params=pltpu.CompilerParams(vmem_limit_bytes=56 * MB),
        name="forward",
    )(comb, kern, scale, win, *big)


def stat_kernel(stat, out, slots, send, recv):
    tm = lax.axis_index("tm")
    barrier = pltpu.get_barrier_semaphore()
    others = [lax.rem(tm + j, 8) for j in range(1, 8)]
    for there in others:
        pl.semaphore_signal(barrier, inc=1, device_id={"tm": there}, device_id_type=MESH)
    pl.semaphore_wait(barrier, 7)
    copies = []
    for j, there in enumerate(others):
        copies.append(
            pltpu.make_async_remote_copy(
                src_ref=stat,
                dst_ref=slots.at[tm],
                send_sem=send.at[j],
                recv_sem=recv.at[j],
                device_id={"tm": there},
                device_id_type=MESH,
            )
        )
    for copy in copies:
        copy.start()
    slots[tm] = stat[...]
    for copy in copies:
        copy.wait()
    total = slots[0]
    for j in range(1, 8):
        total = total + slots[j]
    out[...] = total


def stat_call(stat):
    return pl.pallas_call(
        stat_kernel,
        out_shape=full(8, 128),
        in_specs=[spec(pltpu.VMEM)],
        out_specs=spec(pltpu.VMEM),
        scratch_shapes=[
            pltpu.VMEM((8, 8, 128), F32),
            pltpu.SemaphoreType.DMA((7,)),
            pltpu.SemaphoreType.DMA((7,)),
        ],
        compiler_params=pltpu.CompilerParams(collective_id=1, has_side_effects=True),
        name="clip_sums",
    )(stat)


def backward_kernel(
    comb, kern, scale, win, stat, loss_scale,
    sin_i, rstd_i, y1_i, gp_i, hid_i, down_i, y2_i, re_i, im_i, d1_i, q1_i, d2_i, q2_i,
    a1_h, a2_h, syn_h, head_h, down_h, up_h, pick_n_h, pick_h_h, pick_k_h,
    nrm_o, hid_o, onm_o, dup_o, ddn_o, dhd_o, dem_o, ids_o, kg_o,
    a1_v, a2_v, syn_v, head_v, down_v, up_v, pick_n, pick_h, pick_k,
    dfr, dphase, dhead, dup, small, sems,
):
    pairs = (
        (a1_h, a1_v), (a2_h, a2_v), (syn_h, syn_v), (head_h, head_v), (down_h, down_v),
        (up_h, up_v), (pick_n_h, pick_n), (pick_h_h, pick_h), (pick_k_h, pick_k),
    )
    copies = [pltpu.make_async_copy(h, v, sems.at[i]) for i, (h, v) in enumerate(pairs)]
    for copy in copies:
        copy.start()
    own = slice(HALO, HALO + OWN)
    places = frame_places(comb)
    valid = inside(places)
    ids_o[...] = comb[own, 256:384]

    factor = loss_scale[...] * (0.5 / CLIPS)
    loss = jnp.zeros((1, 1), F32)
    cots = []
    for level in range(2):
        count = ((FRAMES * 513), (2 * FRAMES * 257))[level]
        sum_a = stat[3 * level : 3 * level + 1, 0:1]
        sum_b = stat[3 * level + 1 : 3 * level + 2, 0:1]
        sum_g = stat[3 * level + 2 : 3 * level + 3, 0:1]
        root_a, root_b = jnp.sqrt(sum_a + 1e-6), jnp.sqrt(sum_b + 1e-6)
        loss = loss + root_a / root_b + sum_g * (1.0 / count)
        cots.append((factor / (root_a * root_b), factor * (1.0 / count)))
    loss = jnp.where(comb[HALO : HALO + 1, 258:259] == 0.0, loss, 0.0)

    dx = jnp.zeros((ROWS, HOP), F32)
    copies[0].wait()
    ds1 = (cots[0][0] * d1_i[...] + cots[0][1] * q1_i[...]).astype(BF16)
    for p in range(4):
        at = slice(HOP * p, HOP * (p + 1))
        piece = mm_bt(ds1, a1_v[at, :]).astype(BF16).astype(F32) * win[0:1, at]
        dx = dx + shift(piece, p - 2)
    copies[1].wait()
    ds2 = (cots[1][0] * d2_i[...] + cots[1][1] * q2_i[...]).astype(BF16)
    dseg = mm_bt(ds2, a2_v[...]).astype(BF16).astype(F32) * win[2:3, : NFFT // 2]
    even, odd = dseg[:ROWS], dseg[ROWS:]
    dx = dx + shift(even[:, :256], -1) + even[:, 256:] + odd[:, 128:384]
    dx = dx + jnp.concatenate([shift(odd[:, 384:], 1), shift(odd[:, :128], -1)], axis=1)
    dx = jnp.where(valid, dx / envelope(places, win), 0.0)
    for p in range(4):
        piece = jnp.where(valid, shift(dx, 2 - p), 0.0)
        dfr[:, HOP * p : HOP * (p + 1)] = piece.astype(BF16)

    copies[2].wait()
    for c in range(CHUNKS1):
        dsp = mm_bt(dfr[...], syn_v[256 * c : 256 * (c + 1), :]).astype(BF16).astype(F32)
        dre, dim = dsp[:, :128], dsp[:, 128:]
        re, im = re_i[:, 128 * c : 128 * (c + 1)], im_i[:, 128 * c : 128 * (c + 1)]
        dlog, dph = dre * re + dim * im, dim * re - dre * im
        if c < 4:
            dhead[:, 128 * c : 128 * (c + 1)] = dlog.astype(BF16)
        dphase[:, 128 * c : 128 * (c + 1)] = dph
    moved = pltpu.roll(dphase[...], 1, 1)
    dhead[:, 512:640] = (moved[:, :128] + dlog).astype(BF16)
    dhead[:, 640:] = moved[:, 128:].astype(BF16)
    dhd_o[...] = dhead[own, :].astype(F32)
    copies[3].wait()
    don = mm_bt(dhead[:, :1026], head_v[...]).astype(BF16).astype(F32)
    dstream = norm_back(don, y2_i[...], rstd_i[:, 2:3])

    scale_grad = jnp.sum(dstream[own] * down_i[own, :], axis=0, keepdims=True)
    ddn = (scale[...] * dstream).astype(BF16)
    ddn_o[...] = ddn[own].astype(F32)
    copies[4].wait()
    for c in range(FF // 256):
        at = slice(256 * c, 256 * (c + 1))
        dh = mm_bt(ddn, down_v[at, :]).astype(BF16).astype(F32)
        dup[:, at] = (dh * gp_i[:, at]).astype(BF16)
    dup_o[...] = dup[own, :].astype(F32)
    copies[5].wait()
    dnorm = mm_bt(dup[...], up_v[...]).astype(BF16).astype(F32)
    dmix = norm_back(dnorm, y1_i[...], rstd_i[:, 1:2])
    dmix = jnp.where(valid, dmix, 0.0)
    y0 = sin_i[...]
    dsin = dstream
    small[...] = jnp.zeros((128, D), F32)
    for k in range(7):
        dsin = dsin + kern[k : k + 1, :] * shift(dmix, k - 3)
        taps = dmix * shift(y0, 3 - k)
        small[2 + k : 3 + k, :] = jnp.sum(taps[own], axis=0, keepdims=True)
    demb = norm_back(dsin, y0, rstd_i[:, 0:1])
    dem_o[...] = demb[own].astype(BF16).astype(F32)

    small[9:10, :] = scale_grad
    rest = loss
    for i, grid in enumerate((65536.0, 1.0, 1.0 / 65536.0, 1.0 / 65536.0 / 65536.0)):
        piece = jnp.floor(rest * (1.0 / grid)) * grid
        rest = rest - piece
        small[10 + i : 11 + i, :] = jnp.broadcast_to(piece, (1, D))

    for i in (6, 7, 8):
        copies[i].wait()
    normed = y1_i[own, :].astype(BF16)
    onorm = y2_i[own, :].astype(BF16)
    small0 = small[...].astype(BF16)
    left = small[...] - small0.astype(F32)
    small1 = left.astype(BF16)
    small2 = (left - small1.astype(F32)).astype(BF16)
    for c in range(2):
        nrm_o[c] = mm(normed, pick_n[c])
        onm_o[c] = mm(onorm, pick_n[c])
        for h in range(2):
            out = slice(576 * h, 576 * (h + 1))
            hid_o[c, :, out] = mm(hid_i[:, 1152 * h : 1152 * (h + 1)], pick_h[c])
        kg_o[c] = sum(
            lax.dot_general(pick_k[c], s, (((0,), (1,)), ((), ())), preferred_element_type=F32)
            for s in (small0, small1, small2)
        )


def backward_call(comb, kern, scale, win, stat, loss_scale, saved, big):
    outs = [
        full(2, OWN, 384), full(2, OWN, 1152), full(2, OWN, 384), full(OWN, FF), full(OWN, D),
        full(OWN, 1152), full(OWN, D), full(OWN, 128), full(2, 384, 128),
    ]
    return pl.pallas_call(
        backward_kernel,
        out_shape=outs,
        in_specs=[spec(pltpu.VMEM)] * (6 + len(saved)) + [spec(pl.ANY)] * len(big),
        out_specs=[spec(pltpu.VMEM)] * len(outs),
        scratch_shapes=[pltpu.VMEM(a.shape, BF16) for a in big]
        + [
            pltpu.VMEM((ROWS, NFFT), BF16),
            pltpu.VMEM((ROWS, CHUNKS1 * 128), F32),
            pltpu.VMEM((ROWS, 1152), BF16),
            pltpu.VMEM((ROWS, FF), BF16),
            pltpu.VMEM((128, D), F32),
            pltpu.SemaphoreType.DMA((len(big),)),
        ],
        compiler_params=pltpu.CompilerParams(vmem_limit_bytes=56 * MB),
        name="backward",
    )(comb, kern, scale, win, stat, loss_scale, *saved, *big)


def pair_kernel(*refs):
    count = len(refs) // 2 - 1
    ins, outs = refs[:count], refs[count : 2 * count]
    send, recv = refs[2 * count :]
    dp = lax.axis_index("dp")
    core = lax.rem(dp, 2)
    partner = dp + 1 - 2 * core
    barrier = pltpu.get_barrier_semaphore()
    pl.semaphore_signal(barrier, inc=1, device_id={"dp": partner}, device_id_type=MESH)
    pl.semaphore_wait(barrier, 1)
    copies = []
    for i in range(count):
        copy = pltpu.make_async_remote_copy(
            src_ref=ins[i].at[1 - core] if len(ins[i].shape) == 3 else ins[i],
            dst_ref=outs[i],
            send_sem=send.at[i],
            recv_sem=recv.at[i],
            device_id={"dp": partner},
            device_id_type=MESH,
        )
        copy.start()
        copies.append(copy)
    for copy in copies:
        copy.wait()


def pair_call(arrays):
    count = len(arrays)
    return pl.pallas_call(
        pair_kernel,
        out_shape=[full(*a.shape[-2:]) for a in arrays],
        in_specs=[spec(pl.ANY)] * count,
        out_specs=[spec(pl.ANY)] * count,
        scratch_shapes=[pltpu.SemaphoreType.DMA((count,))] * 2,
        compiler_params=pltpu.CompilerParams(collective_id=2, has_side_effects=True),
        name="core_pair",
    )(*arrays)


def put(out, first, values, rows):
    for block in range(values.shape[1] // 128):
        part = values[:, 128 * block : 128 * (block + 1)].reshape(4, 4, rows, 128)
        out[:, :, first + rows * block : first + rows * (block + 1), :] = part


def weight_kernel(*refs):
    here, there = refs[0:9], refs[9:18]
    turn1, turn2, row_id, p0, p1, p2 = refs[18:]
    core = lax.rem(lax.axis_index("dp"), 2)

    def both(i, cols=slice(None)):
        mine = here[i][core, :, cols] if len(here[i].shape) == 3 else here[i][:, cols]
        return jnp.concatenate([mine, there[i][:, cols]], axis=0)

    onorm = [both(2).astype(BF16)]
    for turn in (turn1, turn2):
        onorm.append(mm(onorm[0], turn[...]).astype(BF16))
    normed = both(0).astype(BF16)
    for c in range(FF // 256):
        put(p0, 48 * c, mm_at(normed, both(3, slice(256 * c, 256 * (c + 1))).astype(BF16)), 24)
    hidden = both(1).astype(BF16)
    for c in range(3):
        put(p1, 144 * c, mm_at(hidden, both(4, slice(256 * c, 256 * (c + 1))).astype(BF16)), 72)
    ids = both(7)
    rows = row_id[...] + 128.0 * ids[0:1, 3:4]
    hot = (rows == ids[:, 0:1]) | (rows == ids[:, 1:2] + 1024.0)
    hot = jnp.where(hot, 1.0, 0.0).astype(BF16)
    for c in range(3):
        put(p2, 128 * c, mm_at(hot, both(6, slice(256 * c, 256 * (c + 1))).astype(BF16)), 64)
    for k, (out, first) in enumerate(((p0, 432), (p1, 432), (p2, 384))):
        start, blocks = HEAD_BLOCKS[k]
        for b in range(blocks):
            at = slice(128 * (start + b), 128 * (start + b + 1))
            values = mm_at(onorm[k], both(5, at).astype(BF16))
            if start + b == 8:
                values = values + here[8][core] + there[8][...]
            put(out, first + 24 * b, values, 24)


def weight_call(here, there, turn1, turn2, row_id):
    outs = [full(4, 4, n, 128) for n in PART_ROWS]
    return pl.pallas_call(
        weight_kernel,
        out_shape=outs,
        in_specs=[spec(pltpu.VMEM)] * 21,
        out_specs=[spec(pltpu.VMEM)] * 3,
        compiler_params=pltpu.CompilerParams(vmem_limit_bytes=56 * MB),
        name="weight_grads",
    )(*here, *there, turn1, turn2, row_id)


LAST_ROWS = (120, 128, 120)


def scatter_kernel(*refs):
    parts, (up_o, down_o, table_o, head_o) = refs[0:3], refs[3:7]
    scratch = refs[7:]
    mine, to_right, to_left = scratch[0:3], scratch[3:6], scratch[6:9]
    got1, got2a, got2b = scratch[9:12], scratch[12:15], scratch[15:18]
    last, got3 = scratch[18:21], scratch[21:24]
    send, recv, local = scratch[24:]

    dp, tm = lax.axis_index("dp"), lax.axis_index("tm")
    at = {"x": tm // 2, "y": dp // 4, "z": lax.rem(dp // 2, 2) * 2 + lax.rem(tm, 2)}
    core = lax.rem(dp, 2)

    def device(axis, by):
        to = dict(at)
        to[axis] = lax.rem(at[axis] + by, 4)
        return {
            "dp": (to["y"] * 2 + to["z"] // 2) * 2 + core,
            "tm": to["x"] * 2 + lax.rem(to["z"], 2),
        }

    barrier = pltpu.get_barrier_semaphore()
    for axis in "xyz":
        for by in (1, 2, 3):
            pl.semaphore_signal(barrier, inc=1, device_id=device(axis, by), device_id_type=MESH)
    pl.semaphore_wait(barrier, 9)

    def remote(src, dst, k, slot, axis, by):
        return pltpu.make_async_remote_copy(
            src_ref=src,
            dst_ref=dst,
            send_sem=send.at[k, slot],
            recv_sem=recv.at[k, slot],
            device_id=device(axis, by),
            device_id_type=MESH,
        )

    first, second = pl.ds(0, 2), pl.ds(2, 2)
    sent = []
    loads = []
    for k in range(3):
        axis, p, g = ORDERS[k][0], parts[k], got1[k]
        i = at[axis]
        right, opposite, left = lax.rem(i + 1, 4), lax.rem(i + 2, 4), lax.rem(i + 3, 4)
        copies = [
            remote(p.at[opposite, first], g.at[0], k, 0, axis, 1),
            remote(p.at[opposite, second], g.at[1], k, 1, axis, 3),
            remote(p.at[right, second], g.at[3], k, 3, axis, 1),
            remote(p.at[left, first], g.at[4], k, 4, axis, 3),
        ]
        here = [
            pltpu.make_async_copy(p.at[right, first], to_right[k], local.at[k, 0]),
            pltpu.make_async_copy(p.at[left, second], to_left[k], local.at[k, 1]),
            pltpu.make_async_copy(p.at[i], mine[k], local.at[k, 2]),
        ]
        for copy in copies + here:
            copy.start()
        sent.append(copies)
        loads.append(here)
    for k in range(3):
        axis, g = ORDERS[k][0], got1[k]
        loads[k][0].wait()
        sent[k][0].wait_recv()
        to_right[k][...] += g[0]
        sent[k].append(remote(to_right[k], g.at[2], k, 2, axis, 1))
        sent[k][-1].start()
        loads[k][1].wait()
        sent[k][1].wait_recv()
        to_left[k][...] += g[1]
        sent[k].append(remote(to_left[k], g.at[5], k, 5, axis, 3))
        sent[k][-1].start()
    for k in range(3):
        g, m = got1[k], mine[k]
        loads[k][2].wait()
        sent[k][2].wait_recv()
        sent[k][3].wait_recv()
        sent[k][4].wait_recv()
        sent[k][5].wait_recv()
        m[0:2] += g[2] + g[4]
        m[2:4] += g[3] + g[5]
        axis = ORDERS[k][1]
        i = at[axis]
        right, opposite, left = lax.rem(i + 1, 4), lax.rem(i + 2, 4), lax.rem(i + 3, 4)
        n = PART_ROWS[k]
        cut = (n // 2 + 7) // 8 * 8
        upper, lower = pl.ds(0, cut), pl.ds(cut, n - cut)
        a, b = got2a[k], got2b[k]
        copies = [
            remote(m.at[opposite, upper], a.at[0], k, 6, axis, 1),
            remote(m.at[opposite, lower], b.at[0], k, 7, axis, 3),
            remote(m.at[right, lower], b.at[1], k, 8, axis, 1),
            remote(m.at[left, upper], a.at[1], k, 9, axis, 3),
        ]
        for copy in copies:
            copy.start()
        sent[k] = sent[k] + copies
    for k in range(3):
        axis = ORDERS[k][1]
        i = at[axis]
        right, left = lax.rem(i + 1, 4), lax.rem(i + 3, 4)
        n = PART_ROWS[k]
        cut = (n // 2 + 7) // 8 * 8
        upper, lower = pl.ds(0, cut), pl.ds(cut, n - cut)
        m, a, b = mine[k], got2a[k], got2b[k]
        sent[k][6].wait_recv()
        m[right, upper] += a[0]
        sent[k].append(remote(m.at[right, upper], a.at[2], k, 10, axis, 1))
        sent[k][-1].start()
        sent[k][7].wait_recv()
        m[left, lower] += b[0]
        sent[k].append(remote(m.at[left, lower], b.at[2], k, 11, axis, 3))
        sent[k][-1].start()
    for k in range(3):
        axis = ORDERS[k][1]
        i = at[axis]
        n = PART_ROWS[k]
        cut = (n // 2 + 7) // 8 * 8
        upper, lower = pl.ds(0, cut), pl.ds(cut, n - cut)
        m, a, b, out = mine[k], got2a[k], got2b[k], last[k]
        for j in (8, 9, 10, 11):
            sent[k][j].wait_recv()
        m[i, upper] += a[1] + a[2]
        m[i, lower] += b[1] + b[2]
        blocks = (((18, 24), (2, 24)), ((6, 72), (3, 24)), ((6, 64), (4, 24)))[k]
        start, place = 0, 0
        for count, rows in blocks:
            each = rows // 4
            for _ in range(count):
                for d in range(4):
                    out[d, pl.ds(place, each)] = m[i, pl.ds(start + d * each, each)]
                start += rows
                place += each
        if place < LAST_ROWS[k]:
            for d in range(4):
                out[d, pl.ds(place, LAST_ROWS[k] - place)] = jnp.zeros(
                    (LAST_ROWS[k] - place, 128), F32
                )
        axis = ORDERS[k][2]
        i = at[axis]
        for by in (1, 2, 3):
            copy = remote(
                out.at[lax.rem(i + by, 4)], got3[k].at[by - 1], k, 11 + by, axis, by
            )
            copy.start()
            sent[k].append(copy)
    for k in range(3):
        for j in (12, 13, 14):
            sent[k][j].wait_recv()
        total = last[k][at[ORDERS[k][2]]] + got3[k][0] + got3[k][1] + got3[k][2]
        out, count, each = ((up_o, 18, 6), (down_o, 6, 18), (table_o, 6, 16))[k]
        for c in range(count):
            out[:, 128 * c : 128 * (c + 1)] = total[each * c : each * (c + 1)]
        start, blocks = HEAD_BLOCKS[k]
        for c in range(blocks):
            rows = count * each + 6 * c
            head_o[:, 128 * (start + c) : 128 * (start + c + 1)] = total[rows : rows + 6]
    for k in range(3):
        for copy in sent[k]:
            copy.wait_send()


def scatter_call(parts):
    def each(make):
        return [make(k) for k in range(3)]

    rows = PART_ROWS
    cuts = [(n // 2 + 7) // 8 * 8 for n in rows]
    return pl.pallas_call(
        scatter_kernel,
        out_shape=[full(6, FF), full(18, D), full(16, D), full(6, 1152)],
        in_specs=[spec(pl.ANY)] * 3,
        out_specs=[spec(pltpu.VMEM)] * 4,
        scratch_shapes=each(lambda k: pltpu.VMEM((4, rows[k], 128), F32))
        + each(lambda k: pltpu.VMEM((2, rows[k], 128), F32))
        + each(lambda k: pltpu.VMEM((2, rows[k], 128), F32))
        + each(lambda k: pltpu.VMEM((6, 2, rows[k], 128), F32))
        + each(lambda k: pltpu.VMEM((3, cuts[k], 128), F32))
        + each(lambda k: pltpu.VMEM((3, rows[k] - cuts[k], 128), F32))
        + each(lambda k: pltpu.VMEM((4, LAST_ROWS[k], 128), F32))
        + each(lambda k: pltpu.VMEM((3, LAST_ROWS[k], 128), F32))
        + [
            pltpu.SemaphoreType.DMA((3, 15)),
            pltpu.SemaphoreType.DMA((3, 15)),
            pltpu.SemaphoreType.DMA((3, 3)),
        ],
        compiler_params=pltpu.CompilerParams(
            collective_id=3, has_side_effects=True, vmem_limit_bytes=48 * MB
        ),
        name="reduce_scatter",
    )(*parts)


def assemble(up, down, table, head):
    loss = (head[0, 1034] + head[0, 1035] + (head[0, 1036] + head[0, 1037])) * (0.5 / CLIPS)
    return loss, table, head[:, 1026:1033].T, up, down, head[:, 1033], head[:, :1026]


def body(
    code_ids, code_table, kernel, up_weight, down_weight, layer_scale, head_weight, target, loss_scale
):
    syn, a1, a2, win = make_constants()
    pick_n, pick_h, pick_k, turn1, turn2, row_id = make_orders()
    comb = halo_call(target.reshape(OWN, HOP), code_ids.reshape(OWN, 2))
    scale = layer_scale.reshape(1, D)
    saved = forward_call(
        comb, kernel, scale, win, code_table, up_weight, down_weight, head_weight, syn, a1, a2
    )
    stat = stat_call(saved[-1])
    operands = backward_call(
        comb, kernel, scale, win, stat, loss_scale.reshape(1, 1), saved[:-1],
        (a1, a2, syn, head_weight, down_weight, up_weight, pick_n, pick_h, pick_k),
    )
    parts = weight_call(operands, pair_call(operands), turn1, turn2, row_id)
    return assemble(*scatter_call(parts))


def solution(mesh):
    in_specs = (P("dp", "tm", None), P(), P(), P(), P(), P(), P(), P("dp", "tm"), P())
    out_specs = (
        P(),
        P(("dp", "tm"), None),
        P(None, ("dp", "tm")),
        P(("dp", "tm"), None),
        P(("dp", "tm"), None),
        P(("dp", "tm")),
        P(("dp", "tm"), None),
    )
    return jax.shard_map(body, mesh=mesh, in_specs=in_specs, out_specs=out_specs, check_vma=False)
```

```python
import jax
import jax.numpy as jnp
import ml_dtypes
import numpy as np
from jax import lax
from jax.experimental import pallas as pl
from jax.experimental.pallas import tpu as pltpu
from jax.sharding import PartitionSpec as P

F32, BF16 = jnp.float32, jnp.bfloat16
MESH = pl.DeviceIdType.MESH
D, FF = 768, 2304
HOP, NFFT = 256, 1024
FRAMES, OWN, HALO = 1024, 128, 16
ROWS = OWN + 2 * HALO
CHUNKS1, CHUNKS2 = 5, 3
WIDE1, WIDE2 = CHUNKS1 * 256, CHUNKS2 * 256
CLIPS = 16
MB = 1 << 20
ORDERS = ("xyz", "yzx", "zxy")
HEAD_BLOCKS = ((0, 2), (2, 3), (5, 4))
PART_ROWS = (18 * 24 + 2 * 24, 6 * 72 + 3 * 24, 6 * 64 + 4 * 24)


def bf(array):
    return np.asarray(array, np.float32).astype(ml_dtypes.bfloat16)


def hann(length):
    return 0.5 - 0.5 * np.cos(2.0 * np.pi * np.arange(length) / length)


def angles(length):
    product = np.arange(length // 2 + 1)[:, None] * np.arange(length)[None, :] % length
    return 2.0 * np.pi * product / length


def interleave(real, imag, chunks):
    bins, width = real.shape
    out = np.zeros((chunks, 2, 128, width), np.float64)
    for half, part in enumerate((real, imag)):
        padded = np.zeros((chunks * 128, width), np.float64)
        padded[:bins] = part
        out[:, half] = padded.reshape(chunks, 128, width)
    return out.reshape(chunks * 256, width)


def make_constants():
    ang = angles(NFFT)
    bins = np.arange(NFFT // 2 + 1)
    factor = np.where((bins == 0) | (bins == NFFT // 2), 1.0, 2.0)[:, None] / NFFT
    window = hann(NFFT)[None, :]
    synthesis = bf(interleave(factor * np.cos(ang) * window, -factor * np.sin(ang) * window, CHUNKS1))
    analysis1 = bf(interleave(np.cos(ang), -np.sin(ang), CHUNKS1).T)
    ang = angles(NFFT // 2)
    analysis2 = bf(interleave(np.cos(ang), -np.sin(ang), CHUNKS2).T)
    win = np.zeros((8, NFFT), np.float32)
    win[0] = hann(NFFT)
    win[1] = hann(NFFT) ** 2
    win[2, : NFFT // 2] = hann(NFFT // 2)
    return synthesis, analysis1, analysis2, win


def device_index(x, y, z, core):
    return ((y * 2 + z // 2) * 2 + core) * 8 + x * 2 + z % 2


def shard_order(order, core):
    places = []
    for a in range(4):
        for b in range(4):
            for c in range(4):
                at = dict(zip(order, (a, b, c)))
                places.append(device_index(at["x"], at["y"], at["z"], core))
    return np.array(places)


def columns_of(order, core, each):
    return (shard_order(order, core)[:, None] * each + np.arange(each)[None, :]).reshape(-1)


def one_hot_columns(sources, size):
    out = np.zeros((size, sources.size), np.float32)
    out[sources, np.arange(sources.size)] = 1.0
    return bf(out)


def make_orders():
    pick_n = np.stack([one_hot_columns(columns_of(ORDERS[0], c, 6), D) for c in (0, 1)])
    half = [columns_of(ORDERS[1], c, 18)[: 4 * 4 * 2 * 18] for c in (0, 1)]
    pick_h = np.stack([one_hot_columns(h, FF // 2) for h in half])
    pick_k = np.stack([one_hot_columns(columns_of(ORDERS[2], c, 6), D) for c in (0, 1)])
    first = columns_of(ORDERS[0], 0, 6)
    where = {col: i for i, col in enumerate(first)}
    turns = []
    for k in (1, 2):
        sources = np.array([where[col] for col in columns_of(ORDERS[k], 0, 6)])
        turns.append(one_hot_columns(sources, 384))
    row_id = columns_of(ORDERS[2], 0, 16).astype(np.int32)[:, None]
    return pick_n, pick_h, pick_k, turns[0], turns[1], row_id


def mm(a, b):
    return jnp.dot(a, b, preferred_element_type=F32)


def mm_bt(a, b):
    return lax.dot_general(a, b, (((1,), (1,)), ((), ())), preferred_element_type=F32)


def mm_at(a, b):
    return lax.dot_general(a, b, (((0,), (0,)), ((), ())), preferred_element_type=F32)


def shift(values, by):
    by = by % values.shape[0]
    return values if by == 0 else pltpu.roll(values, by, 0)


def norm(values):
    centre = values - jnp.mean(values, axis=-1, keepdims=True)
    rstd = lax.rsqrt(jnp.mean(centre * centre, axis=-1, keepdims=True) + 1e-6)
    return centre * rstd, rstd


def norm_back(grad, y, rstd):
    mean_g = jnp.mean(grad, axis=-1, keepdims=True)
    mean_gy = jnp.mean(grad * y, axis=-1, keepdims=True)
    return rstd * (grad - mean_g - y * mean_gy)


def frame_places():
    first = lax.axis_index("tm") * OWN - HALO
    return (lax.broadcasted_iota(jnp.int32, (ROWS, 1), 0) + first).astype(F32)


def inside(places):
    return (places >= 0.0) & (places < float(FRAMES))


def envelope(places, win):
    total = jnp.zeros((ROWS, HOP), F32)
    for p in range(4):
        total = total + jnp.where(inside(places + float(2 - p)), win[1:2, HOP * p : HOP * (p + 1)], 0.0)
    return jnp.where(inside(places), total, 1.0)


def spec(space):
    return pl.BlockSpec(memory_space=space)


def full(*shape, dtype=F32):
    return jax.ShapeDtypeStruct(shape, dtype)


def halo_kernel(target, ids, left_t, right_t, left_i, right_i, send, recv):
    tm = lax.axis_index("tm")
    right, left = lax.rem(tm + 1, 8), lax.rem(tm + 7, 8)
    barrier = pltpu.get_barrier_semaphore()
    for there in (left, right):
        pl.semaphore_signal(barrier, inc=1, device_id={"tm": there}, device_id_type=MESH)
    pl.semaphore_wait(barrier, 2)
    edge = HALO * HOP
    copies = []
    for i, (src, dst, there) in enumerate(
        (
            (target.at[:, pl.ds(OWN * HOP - edge, edge)], left_t, right),
            (target.at[:, pl.ds(0, edge)], right_t, left),
            (ids, left_i, right),
            (ids, right_i, left),
        )
    ):
        copies.append(
            pltpu.make_async_remote_copy(
                src_ref=src,
                dst_ref=dst,
                send_sem=send.at[i],
                recv_sem=recv.at[i],
                device_id={"tm": there},
                device_id_type=MESH,
            )
        )
    for copy in copies:
        copy.start()
    for copy in copies:
        copy.wait()


def halo_call(target, ids):
    edge = full(1, HALO * HOP)
    around = full(2, OWN, dtype=jnp.int32)
    return pl.pallas_call(
        halo_kernel,
        out_shape=[edge, edge, around, around],
        in_specs=[spec(pltpu.VMEM)] * 2,
        out_specs=[spec(pltpu.VMEM)] * 4,
        scratch_shapes=[pltpu.SemaphoreType.DMA((4,)), pltpu.SemaphoreType.DMA((4,))],
        compiler_params=pltpu.CompilerParams(collective_id=0, has_side_effects=True),
        name="halo",
    )(target, ids)


def ids_column(ids):
    padded = jnp.concatenate([ids.astype(F32), jnp.zeros((126, OWN), F32)], axis=0)
    return jnp.transpose(padded)[:, :2]


def forward_kernel(
    target, left_t, right_t, ids, left_i, right_i, kern, scale_i, win,
    table_h, up_h, down_h, head_h, syn_h, a1_h, a2_h, *refs,
):
    outs, stat_o, refs = refs[: len(SAVED)], refs[len(SAVED)], refs[len(SAVED) + 1 :]
    (sin_o, rstd_o, y1_o, gp_o, hid_o, down_o, y2_o, re_o, im_o, d1_o, q1_o, d2_o, q2_o) = refs[
        : len(SAVED)
    ]
    kept = refs[: len(SAVED)]
    refs = refs[len(SAVED) :]
    (table_v, up_v, down_v, head_v, syn_v, a1_v, a2_v) = refs[:7]
    goal, codes, hid_v, head_s, spec_v, seg1, seg2, sems, out_sems = refs[7:]
    pairs = (
        (table_h, table_v), (up_h, up_v), (down_h, down_v), (head_h, head_v),
        (syn_h, syn_v), (a1_h, a1_v), (a2_h, a2_v),
    )
    copies = [pltpu.make_async_copy(h, v, sems.at[i]) for i, (h, v) in enumerate(pairs)]
    for copy in copies:
        copy.start()
    saves = [pltpu.make_async_copy(v, h, out_sems.at[i]) for i, (v, h) in enumerate(zip(kept, outs))]
    scale = scale_i[...].reshape(1, D)
    for source, first, count, skip in (
        (left_t, 0, HALO, 0), (target, HALO, OWN, 0), (right_t, HALO + OWN, HALO, 0),
    ):
        for r in range(count):
            goal[first + r : first + r + 1, :] = source[:, HOP * r : HOP * (r + 1)]
    codes[0:HALO, :] = ids_column(left_i[...])[OWN - HALO :]
    codes[HALO : HALO + OWN, :] = ids_column(ids[...])
    codes[HALO + OWN :, :] = ids_column(right_i[...])[:HALO]
    places = frame_places()
    valid = inside(places)
    lane = lax.broadcasted_iota(jnp.int32, (ROWS, 2 * FRAMES), 1).astype(F32)
    hot = (lane == codes[:, 0:1]) | (lane == codes[:, 1:2] + 1024.0)
    hot = jnp.where(hot, 1.0, 0.0).astype(BF16)
    copies[0].wait()
    y0, rstd0 = norm(mm(hot, table_v[...]))
    y0 = jnp.where(valid, y0, 0.0)
    sin_o[...] = y0
    saves[0].start()
    mixture = kern[0:1, :] * shift(y0, 3)
    for k in range(1, 7):
        mixture = mixture + kern[k : k + 1, :] * shift(y0, 3 - k)
    y1, rstd1 = norm(mixture)
    y1_o[...] = y1
    saves[2].start()
    normed = y1.astype(BF16)
    copies[1].wait()
    for c in range(FF // 256):
        at = slice(256 * c, 256 * (c + 1))
        up = mm(normed, up_v[:, at])
        cdf = 0.5 * (1.0 + lax.erf(up * 0.7071067811865476))
        hid_v[:, at] = (up * cdf).astype(BF16)
        gp_o[:, at] = cdf + up * (0.3989422804014327 * jnp.exp(-0.5 * up * up))
    hid_o[...] = hid_v[HALO : HALO + OWN, :]
    saves[3].start()
    saves[4].start()
    copies[2].wait()
    down = mm(hid_v[...], down_v[...])
    down_o[...] = down
    saves[5].start()
    y2, rstd2 = norm(y0 + scale * down)
    y2_o[...] = y2
    saves[6].start()
    places128 = lax.broadcasted_iota(jnp.int32, (ROWS, 128), 1)
    rstd_o[...] = jnp.where(places128 == 0, rstd0, jnp.where(places128 == 1, rstd1, rstd2))
    saves[1].start()
    onorm = y2.astype(BF16)
    copies[3].wait()
    head_s[:, 1024:] = jnp.zeros((ROWS, 128), F32)
    for c in range(4):
        head_s[:, 256 * c : 256 * (c + 1)] = mm_bt(onorm, head_v[256 * c : 256 * (c + 1), :])
    head_s[:, 1024:1026] = mm_bt(onorm, head_v[1024:1026, :])
    phases = pltpu.roll(head_s[:, 512:], CHUNKS1 * 128 - 1, 1)
    for c in range(CHUNKS1):
        logmag = head_s[:, 128 * c : 128 * (c + 1)]
        if c == 4:
            logmag = jnp.where(places128 == 0, logmag, 0.0)
        mag = jnp.exp(logmag)
        phase = phases[:, 128 * c : 128 * (c + 1)]
        re, im = mag * jnp.cos(phase), mag * jnp.sin(phase)
        re_o[:, 128 * c : 128 * (c + 1)] = re
        im_o[:, 128 * c : 128 * (c + 1)] = im
        spec_v[:, 256 * c : 256 * c + 128] = re.astype(BF16)
        spec_v[:, 256 * c + 128 : 256 * (c + 1)] = im.astype(BF16)
    saves[7].start()
    saves[8].start()
    copies[4].wait()
    pred = jnp.zeros((ROWS, HOP), F32)
    for p in range(4):
        piece = jnp.where(valid, mm(spec_v[...], syn_v[:, HOP * p : HOP * (p + 1)]), 0.0)
        pred = pred + shift(piece, p - 2)
    pred = jnp.where(valid, pred / envelope(places, win), 0.0)
    for s, x in enumerate((pred, jnp.where(valid, goal[...], 0.0))):
        r1 = slice(ROWS * s, ROWS * (s + 1))
        for p in range(4):
            at = slice(HOP * p, HOP * (p + 1))
            seg1[r1, at] = (shift(x, 2 - p) * win[0:1, at]).astype(BF16)
        even = slice(2 * ROWS * s, 2 * ROWS * s + ROWS)
        odd = slice(2 * ROWS * s + ROWS, 2 * ROWS * (s + 1))
        before, after = shift(x, 1), shift(x, -1)
        seg2[even, 0:256] = (before * win[2:3, 0:256]).astype(BF16)
        seg2[even, 256:512] = (x * win[2:3, 256:512]).astype(BF16)
        seg2[odd, 0:128] = (before[:, 128:] * win[2:3, 0:128]).astype(BF16)
        seg2[odd, 128:384] = (x * win[2:3, 128:384]).astype(BF16)
        seg2[odd, 384:512] = (after[:, :128] * win[2:3, 384:512]).astype(BF16)
    own = slice(HALO, HALO + OWN)
    for level in range(2):
        seg, table, chunks = ((seg1, a1_v, CHUNKS1), (seg2, a2_v, CHUNKS2))[level]
        d_o, q_o = ((d1_o, q1_o), (d2_o, q2_o))[level]
        copies[5 + level].wait()
        sums = [jnp.zeros((OWN, 128), F32) for _ in range(3)]
        for c in range(chunks):
            for sub in range(level + 1):
                rows_p = slice(ROWS * sub, ROWS * (sub + 1))
                base = ROWS * (level + 1)
                rows_g = slice(base + ROWS * sub, base + ROWS * (sub + 1))
                weights = table[:, 256 * c : 256 * (c + 1)]
                sp, sg = mm(seg[rows_p, :], weights), mm(seg[rows_g, :], weights)
                diff = sp - sg
                pr, pi, gr, gi = sp[:, :128], sp[:, 128:], sg[:, :128], sg[:, 128:]
                power_p, power_g = pr * pr + pi * pi, gr * gr + gi * gi
                gap = jnp.log1p(power_p) - jnp.log1p(power_g)
                slope = jnp.where(valid, 4.0 * gap / (1.0 + power_p), 0.0)
                d_o[rows_p, 256 * c : 256 * (c + 1)] = jnp.where(valid, diff, 0.0)
                q_o[rows_p, 256 * c : 256 * c + 128] = slope * pr
                q_o[rows_p, 256 * c + 128 : 256 * (c + 1)] = slope * pi
                dr, di = diff[own, :128], diff[own, 128:]
                sums[0] = sums[0] + dr * dr + di * di
                sums[1] = sums[1] + power_g[own]
                sums[2] = sums[2] + gap[own] * gap[own]
        saves[9 + 2 * level].start()
        saves[10 + 2 * level].start()
        for i in range(3):
            total = jnp.sum(jnp.sum(sums[i], axis=0, keepdims=True), axis=1, keepdims=True)
            stat_o[3 * level + i : 3 * level + i + 1, :] = jnp.broadcast_to(total, (1, 128))
    stat_o[6:8, :] = jnp.zeros((2, 128), F32)
    for save in saves:
        save.wait()


SAVED = (
    full(ROWS, D), full(ROWS, 128), full(ROWS, D), full(ROWS, FF), full(OWN, FF, dtype=BF16),
    full(ROWS, D), full(ROWS, D), full(ROWS, CHUNKS1 * 128), full(ROWS, CHUNKS1 * 128),
    full(ROWS, WIDE1), full(ROWS, WIDE1), full(2 * ROWS, WIDE2), full(2 * ROWS, WIDE2),
)


def vmem(shapes):
    return [pltpu.VMEM(a.shape, a.dtype) for a in shapes]


def forward_call(small, big):
    outs = list(SAVED) + [full(8, 128)]
    return pl.pallas_call(
        forward_kernel,
        out_shape=outs,
        in_specs=[spec(pltpu.VMEM)] * len(small) + [spec(pl.ANY)] * len(big),
        out_specs=[spec(pl.ANY)] * len(SAVED) + [spec(pltpu.VMEM)],
        scratch_shapes=vmem(SAVED)
        + vmem(big)
        + [
            pltpu.VMEM((ROWS, HOP), F32),
            pltpu.VMEM((ROWS, 2), F32),
            pltpu.VMEM((ROWS, FF), BF16),
            pltpu.VMEM((ROWS, 1152), F32),
            pltpu.VMEM((ROWS, WIDE1), BF16),
            pltpu.VMEM((2 * ROWS, NFFT), BF16),
            pltpu.VMEM((4 * ROWS, NFFT // 2), BF16),
            pltpu.SemaphoreType.DMA((len(big),)),
            pltpu.SemaphoreType.DMA((len(SAVED),)),
        ],
        compiler_params=pltpu.CompilerParams(vmem_limit_bytes=60 * MB),
        name="forward",
    )(*small, *big)


def stat_kernel(stat, out, slots, send, recv):
    tm = lax.axis_index("tm")
    barrier = pltpu.get_barrier_semaphore()
    others = [lax.rem(tm + j, 8) for j in range(1, 8)]
    for there in others:
        pl.semaphore_signal(barrier, inc=1, device_id={"tm": there}, device_id_type=MESH)
    pl.semaphore_wait(barrier, 7)
    copies = []
    for j, there in enumerate(others):
        copies.append(
            pltpu.make_async_remote_copy(
                src_ref=stat,
                dst_ref=slots.at[tm],
                send_sem=send.at[j],
                recv_sem=recv.at[j],
                device_id={"tm": there},
                device_id_type=MESH,
            )
        )
    for copy in copies:
        copy.start()
    slots[tm] = stat[...]
    for copy in copies:
        copy.wait()
    total = slots[0]
    for j in range(1, 8):
        total = total + slots[j]
    out[...] = total


def stat_call(stat):
    return pl.pallas_call(
        stat_kernel,
        out_shape=full(8, 128),
        in_specs=[spec(pltpu.VMEM)],
        out_specs=spec(pltpu.VMEM),
        scratch_shapes=[
            pltpu.VMEM((8, 8, 128), F32),
            pltpu.SemaphoreType.DMA((7,)),
            pltpu.SemaphoreType.DMA((7,)),
        ],
        compiler_params=pltpu.CompilerParams(collective_id=1, has_side_effects=True),
        name="clip_sums",
    )(stat)


def backward_kernel(kern, scale_i, win, stat, loss_scale, *refs):
    count = len(SAVED)
    saved_h, refs = refs[:count], refs[count:]
    big_h, refs = refs[:9], refs[9:]
    outs, refs = refs[:8], refs[8:]
    saved, refs = refs[:count], refs[count:]
    (sin_i, rstd_i, y1_i, gp_i, hid_i, down_i, y2_i, re_i, im_i, d1_i, q1_i, d2_i, q2_i) = saved
    (a1_v, a2_v, syn_v, head_v, down_v, up_v, pick_n, pick_h, pick_k), refs = refs[:9], refs[9:]
    (nrm_o, hid_o, onm_o, dup_o, ddn_o, dhd_o, dem_o, kg_o), refs = refs[:8], refs[8:]
    kept = (nrm_o, hid_o, onm_o, dup_o, ddn_o, dhd_o, dem_o, kg_o)
    dfr, dphase, dhead, dup, small, sems, saved_sems, out_sems = refs
    loads = [
        pltpu.make_async_copy(h, v, saved_sems.at[i]) for i, (h, v) in enumerate(zip(saved_h, saved))
    ]
    copies = [
        pltpu.make_async_copy(h, v, sems.at[i])
        for i, (h, v) in enumerate(
            zip(big_h, (a1_v, a2_v, syn_v, head_v, down_v, up_v, pick_n, pick_h, pick_k))
        )
    ]
    saves = [pltpu.make_async_copy(v, h, out_sems.at[i]) for i, (v, h) in enumerate(zip(kept, outs))]
    for copy in (
        loads[9], loads[10], copies[0], loads[11], loads[12], copies[1], copies[2], loads[7],
        loads[8], copies[3], loads[1], loads[6], loads[5], copies[4], loads[3], copies[5],
        loads[2], loads[0], copies[6], loads[4], copies[7], copies[8],
    ):
        copy.start()
    scale = scale_i[...].reshape(1, D)
    own = slice(HALO, HALO + OWN)
    places = frame_places()
    valid = inside(places)

    factor = loss_scale[...] * (0.5 / CLIPS)
    loss = jnp.zeros((1, 1), F32)
    cots = []
    for level in range(2):
        count = ((FRAMES * 513), (2 * FRAMES * 257))[level]
        sum_a = stat[3 * level : 3 * level + 1, 0:1]
        sum_b = stat[3 * level + 1 : 3 * level + 2, 0:1]
        sum_g = stat[3 * level + 2 : 3 * level + 3, 0:1]
        root_a, root_b = jnp.sqrt(sum_a + 1e-6), jnp.sqrt(sum_b + 1e-6)
        loss = loss + root_a / root_b + sum_g * (1.0 / count)
        cots.append((factor / (root_a * root_b), factor * (1.0 / count)))
    loss = jnp.where(lax.axis_index("tm") == 0, loss, 0.0)

    dx = jnp.zeros((ROWS, HOP), F32)
    loads[9].wait()
    loads[10].wait()
    copies[0].wait()
    ds1 = (cots[0][0] * d1_i[...] + cots[0][1] * q1_i[...]).astype(BF16)
    for p in range(4):
        at = slice(HOP * p, HOP * (p + 1))
        piece = mm_bt(ds1, a1_v[at, :]).astype(BF16).astype(F32) * win[0:1, at]
        dx = dx + shift(piece, p - 2)
    loads[11].wait()
    loads[12].wait()
    copies[1].wait()
    ds2 = (cots[1][0] * d2_i[...] + cots[1][1] * q2_i[...]).astype(BF16)
    dseg = mm_bt(ds2, a2_v[...]).astype(BF16).astype(F32) * win[2:3, : NFFT // 2]
    even, odd = dseg[:ROWS], dseg[ROWS:]
    dx = dx + shift(even[:, :256], -1) + even[:, 256:] + odd[:, 128:384]
    dx = dx + jnp.concatenate([shift(odd[:, 384:], 1), shift(odd[:, :128], -1)], axis=1)
    dx = jnp.where(valid, dx / envelope(places, win), 0.0)
    for p in range(4):
        piece = jnp.where(valid, shift(dx, 2 - p), 0.0)
        dfr[:, HOP * p : HOP * (p + 1)] = piece.astype(BF16)

    copies[2].wait()
    loads[7].wait()
    loads[8].wait()
    for c in range(CHUNKS1):
        dsp = mm_bt(dfr[...], syn_v[256 * c : 256 * (c + 1), :]).astype(BF16).astype(F32)
        dre, dim = dsp[:, :128], dsp[:, 128:]
        re, im = re_i[:, 128 * c : 128 * (c + 1)], im_i[:, 128 * c : 128 * (c + 1)]
        dlog, dph = dre * re + dim * im, dim * re - dre * im
        if c < 4:
            dhead[:, 128 * c : 128 * (c + 1)] = dlog.astype(BF16)
        dphase[:, 128 * c : 128 * (c + 1)] = dph
    moved = pltpu.roll(dphase[...], 1, 1)
    dhead[:, 512:640] = (moved[:, :128] + dlog).astype(BF16)
    dhead[:, 640:] = moved[:, 128:].astype(BF16)
    dhd_o[...] = dhead[own, :].astype(F32)
    saves[5].start()
    copies[3].wait()
    don = mm(dhead[:, :1026], head_v[...]).astype(BF16).astype(F32)
    for i in (1, 6, 5):
        loads[i].wait()
    dstream = norm_back(don, y2_i[...], rstd_i[:, 2:3])

    scale_grad = jnp.sum(dstream[own] * down_i[own, :], axis=0, keepdims=True)
    ddn = (scale * dstream).astype(BF16)
    ddn_o[...] = ddn[own].astype(F32)
    saves[4].start()
    copies[4].wait()
    loads[3].wait()
    for c in range(FF // 256):
        at = slice(256 * c, 256 * (c + 1))
        dh = mm_bt(ddn, down_v[at, :]).astype(BF16).astype(F32)
        dup[:, at] = (dh * gp_i[:, at]).astype(BF16)
    dup_o[...] = dup[own, :].astype(F32)
    saves[3].start()
    copies[5].wait()
    loads[2].wait()
    loads[0].wait()
    dnorm = mm_bt(dup[...], up_v[...]).astype(BF16).astype(F32)
    dmix = norm_back(dnorm, y1_i[...], rstd_i[:, 1:2])
    dmix = jnp.where(valid, dmix, 0.0)
    y0 = sin_i[...]
    dsin = dstream
    small[...] = jnp.zeros((128, D), F32)
    for k in range(7):
        dsin = dsin + kern[k : k + 1, :] * shift(dmix, k - 3)
        taps = dmix * shift(y0, 3 - k)
        small[2 + k : 3 + k, :] = jnp.sum(taps[own], axis=0, keepdims=True)
    demb = norm_back(dsin, y0, rstd_i[:, 0:1])
    dem_o[...] = demb[own].astype(BF16).astype(F32)
    saves[6].start()

    small[9:10, :] = scale_grad
    rest = loss
    for i, grid in enumerate((65536.0, 1.0, 1.0 / 65536.0, 1.0 / 65536.0 / 65536.0)):
        piece = jnp.floor(rest * (1.0 / grid)) * grid
        rest = rest - piece
        small[10 + i : 11 + i, :] = jnp.broadcast_to(piece, (1, D))

    for copy in (copies[6], copies[7], copies[8], loads[4]):
        copy.wait()
    normed = y1_i[own, :].astype(BF16)
    onorm = y2_i[own, :].astype(BF16)
    small0 = small[...].astype(BF16)
    left = small[...] - small0.astype(F32)
    small1 = left.astype(BF16)
    small2 = (left - small1.astype(F32)).astype(BF16)
    for c in range(2):
        nrm_o[c] = mm(normed, pick_n[c])
        onm_o[c] = mm(onorm, pick_n[c])
        for h in range(2):
            out = slice(576 * h, 576 * (h + 1))
            hid_o[c, :, out] = mm(hid_i[:, 1152 * h : 1152 * (h + 1)], pick_h[c])
        kg_o[c] = sum(
            lax.dot_general(pick_k[c], s, (((0,), (1,)), ((), ())), preferred_element_type=F32)
            for s in (small0, small1, small2)
        )
    for i in (0, 1, 2, 7):
        saves[i].start()
    for save in saves:
        save.wait()


def backward_call(small, saved, big):
    outs = [
        full(2, OWN, 384), full(2, OWN, 1152), full(2, OWN, 384), full(OWN, FF), full(OWN, D),
        full(OWN, 1152), full(OWN, D), full(2, 384, 128),
    ]
    return pl.pallas_call(
        backward_kernel,
        out_shape=outs,
        in_specs=[spec(pltpu.VMEM)] * len(small) + [spec(pl.ANY)] * (len(saved) + len(big)),
        out_specs=[spec(pl.ANY)] * len(outs),
        scratch_shapes=vmem(saved)
        + vmem(big)
        + vmem(outs)
        + [
            pltpu.VMEM((ROWS, NFFT), BF16),
            pltpu.VMEM((ROWS, CHUNKS1 * 128), F32),
            pltpu.VMEM((ROWS, 1152), BF16),
            pltpu.VMEM((ROWS, FF), BF16),
            pltpu.VMEM((128, D), F32),
            pltpu.SemaphoreType.DMA((len(big),)),
            pltpu.SemaphoreType.DMA((len(saved),)),
            pltpu.SemaphoreType.DMA((len(outs),)),
        ],
        compiler_params=pltpu.CompilerParams(vmem_limit_bytes=60 * MB),
        name="backward",
    )(*small, *saved, *big)


def pair_kernel(*refs):
    count = len(refs) // 2 - 1
    ins, outs = refs[:count], refs[count : 2 * count]
    send, recv = refs[2 * count :]
    dp = lax.axis_index("dp")
    core = lax.rem(dp, 2)
    partner = dp + 1 - 2 * core
    barrier = pltpu.get_barrier_semaphore()
    pl.semaphore_signal(barrier, inc=1, device_id={"dp": partner}, device_id_type=MESH)
    pl.semaphore_wait(barrier, 1)
    copies = []
    for i in range(count):
        copy = pltpu.make_async_remote_copy(
            src_ref=ins[i].at[1 - core] if len(ins[i].shape) == 3 else ins[i],
            dst_ref=outs[i],
            send_sem=send.at[i],
            recv_sem=recv.at[i],
            device_id={"dp": partner},
            device_id_type=MESH,
        )
        copy.start()
        copies.append(copy)
    for copy in copies:
        copy.wait()


def pair_call(arrays):
    count = len(arrays)
    return pl.pallas_call(
        pair_kernel,
        out_shape=[full(*a.shape[-2:], dtype=a.dtype) for a in arrays],
        in_specs=[spec(pl.ANY)] * count,
        out_specs=[spec(pl.ANY)] * count,
        scratch_shapes=[pltpu.SemaphoreType.DMA((count,))] * 2,
        compiler_params=pltpu.CompilerParams(collective_id=2, has_side_effects=True),
        name="core_pair",
    )(*arrays)


def put(out, first, values, rows):
    for block in range(values.shape[1] // 128):
        part = values[:, 128 * block : 128 * (block + 1)].reshape(4, 4, rows, 128)
        out[:, :, first + rows * block : first + rows * (block + 1), :] = part


def weight_kernel(*refs):
    here, there = refs[0:9], refs[9:18]
    turn1, turn2, row_id, p0, p1, p2 = refs[18:]
    core = lax.rem(lax.axis_index("dp"), 2)

    def both(i, cols=slice(None)):
        mine = here[i][core, :, cols] if len(here[i].shape) == 3 else here[i][:, cols]
        return jnp.concatenate([mine, there[i][:, cols]], axis=0)

    onorm = [both(2).astype(BF16)]
    for turn in (turn1, turn2):
        onorm.append(mm(onorm[0], turn[...]).astype(BF16))
    normed = both(0).astype(BF16)
    for c in range(FF // 256):
        put(p0, 48 * c, mm_at(normed, both(3, slice(256 * c, 256 * (c + 1))).astype(BF16)), 24)
    hidden = both(1).astype(BF16)
    for c in range(3):
        put(p1, 144 * c, mm_at(hidden, both(4, slice(256 * c, 256 * (c + 1))).astype(BF16)), 72)
    ids = jnp.concatenate([here[8][...], there[8][...]], axis=1)
    rows = row_id[...] + OWN * core
    hot = (rows == ids[0:1, :]) | (rows == ids[1:2, :] + 1024)
    hot = jnp.where(hot, 1.0, 0.0).astype(BF16)
    for c in range(3):
        put(p2, 128 * c, mm(hot, both(6, slice(256 * c, 256 * (c + 1))).astype(BF16)), 64)
    for k, (out, first) in enumerate(((p0, 432), (p1, 432), (p2, 384))):
        start, blocks = HEAD_BLOCKS[k]
        for b in range(blocks):
            at = slice(128 * (start + b), 128 * (start + b + 1))
            values = mm_at(onorm[k], both(5, at).astype(BF16))
            if start + b == 8:
                values = values + here[7][core] + there[7][...]
            put(out, first + 24 * b, values, 24)


def weight_call(here, there, turn1, turn2, row_id):
    outs = [full(4, 4, n, 128) for n in PART_ROWS]
    return pl.pallas_call(
        weight_kernel,
        out_shape=outs,
        in_specs=[spec(pltpu.VMEM)] * 21,
        out_specs=[spec(pltpu.VMEM)] * 3,
        compiler_params=pltpu.CompilerParams(vmem_limit_bytes=56 * MB),
        name="weight_grads",
    )(*here, *there, turn1, turn2, row_id)


LAST_ROWS = (120, 128, 120)


def scatter_kernel(*refs):
    parts, outs = refs[0:3], refs[3:6]
    scratch = refs[6:]
    mine, to_right, to_left = scratch[0:3], scratch[3:6], scratch[6:9]
    got1, got2a, got2b = scratch[9:12], scratch[12:15], scratch[15:18]
    last, got3 = scratch[18:21], scratch[21:24]
    send, recv, local = scratch[24:]

    dp, tm = lax.axis_index("dp"), lax.axis_index("tm")
    at = {"x": tm // 2, "y": dp // 4, "z": lax.rem(dp // 2, 2) * 2 + lax.rem(tm, 2)}
    core = lax.rem(dp, 2)

    def device(axis, by):
        to = dict(at)
        to[axis] = lax.rem(at[axis] + by, 4)
        return {
            "dp": (to["y"] * 2 + to["z"] // 2) * 2 + core,
            "tm": to["x"] * 2 + lax.rem(to["z"], 2),
        }

    barrier = pltpu.get_barrier_semaphore()
    for axis in "xyz":
        for by in (1, 2, 3):
            pl.semaphore_signal(barrier, inc=1, device_id=device(axis, by), device_id_type=MESH)
    pl.semaphore_wait(barrier, 9)

    def remote(src, dst, k, slot, axis, by):
        return pltpu.make_async_remote_copy(
            src_ref=src,
            dst_ref=dst,
            send_sem=send.at[k, slot],
            recv_sem=recv.at[k, slot],
            device_id=device(axis, by),
            device_id_type=MESH,
        )

    first, second = pl.ds(0, 2), pl.ds(2, 2)
    sent = []
    loads = []
    for k in range(3):
        axis, p, g = ORDERS[k][0], parts[k], got1[k]
        i = at[axis]
        right, opposite, left = lax.rem(i + 1, 4), lax.rem(i + 2, 4), lax.rem(i + 3, 4)
        copies = [
            remote(p.at[opposite, first], g.at[0], k, 0, axis, 1),
            remote(p.at[opposite, second], g.at[1], k, 1, axis, 3),
            remote(p.at[right, second], g.at[3], k, 3, axis, 1),
            remote(p.at[left, first], g.at[4], k, 4, axis, 3),
        ]
        here = [
            pltpu.make_async_copy(p.at[right, first], to_right[k], local.at[k, 0]),
            pltpu.make_async_copy(p.at[left, second], to_left[k], local.at[k, 1]),
            pltpu.make_async_copy(p.at[i], mine[k], local.at[k, 2]),
        ]
        for copy in copies + here:
            copy.start()
        sent.append(copies)
        loads.append(here)
    for k in range(3):
        axis, g = ORDERS[k][0], got1[k]
        loads[k][0].wait()
        sent[k][0].wait_recv()
        to_right[k][...] += g[0]
        sent[k].append(remote(to_right[k], g.at[2], k, 2, axis, 1))
        sent[k][-1].start()
        loads[k][1].wait()
        sent[k][1].wait_recv()
        to_left[k][...] += g[1]
        sent[k].append(remote(to_left[k], g.at[5], k, 5, axis, 3))
        sent[k][-1].start()
    for k in range(3):
        g, m = got1[k], mine[k]
        loads[k][2].wait()
        sent[k][2].wait_recv()
        sent[k][3].wait_recv()
        sent[k][4].wait_recv()
        sent[k][5].wait_recv()
        m[0:2] += g[2] + g[4]
        m[2:4] += g[3] + g[5]
        axis = ORDERS[k][1]
        i = at[axis]
        right, opposite, left = lax.rem(i + 1, 4), lax.rem(i + 2, 4), lax.rem(i + 3, 4)
        n = PART_ROWS[k]
        cut = (n // 2 + 7) // 8 * 8
        upper, lower = pl.ds(0, cut), pl.ds(cut, n - cut)
        a, b = got2a[k], got2b[k]
        copies = [
            remote(m.at[opposite, upper], a.at[0], k, 6, axis, 1),
            remote(m.at[opposite, lower], b.at[0], k, 7, axis, 3),
            remote(m.at[right, lower], b.at[1], k, 8, axis, 1),
            remote(m.at[left, upper], a.at[1], k, 9, axis, 3),
        ]
        for copy in copies:
            copy.start()
        sent[k] = sent[k] + copies
    for k in range(3):
        axis = ORDERS[k][1]
        i = at[axis]
        right, left = lax.rem(i + 1, 4), lax.rem(i + 3, 4)
        n = PART_ROWS[k]
        cut = (n // 2 + 7) // 8 * 8
        upper, lower = pl.ds(0, cut), pl.ds(cut, n - cut)
        m, a, b = mine[k], got2a[k], got2b[k]
        sent[k][6].wait_recv()
        m[right, upper] += a[0]
        sent[k].append(remote(m.at[right, upper], a.at[2], k, 10, axis, 1))
        sent[k][-1].start()
        sent[k][7].wait_recv()
        m[left, lower] += b[0]
        sent[k].append(remote(m.at[left, lower], b.at[2], k, 11, axis, 3))
        sent[k][-1].start()
    for k in range(3):
        axis = ORDERS[k][1]
        i = at[axis]
        n = PART_ROWS[k]
        cut = (n // 2 + 7) // 8 * 8
        upper, lower = pl.ds(0, cut), pl.ds(cut, n - cut)
        m, a, b, out = mine[k], got2a[k], got2b[k], last[k]
        for j in (8, 9, 10, 11):
            sent[k][j].wait_recv()
        m[i, upper] += a[1] + a[2]
        m[i, lower] += b[1] + b[2]
        blocks = (((18, 24), (2, 24)), ((6, 72), (3, 24)), ((6, 64), (4, 24)))[k]
        start, place = 0, 0
        for count, rows in blocks:
            each = rows // 4
            for _ in range(count):
                for d in range(4):
                    out[d, pl.ds(place, each)] = m[i, pl.ds(start + d * each, each)]
                start += rows
                place += each
        if place < LAST_ROWS[k]:
            for d in range(4):
                out[d, pl.ds(place, LAST_ROWS[k] - place)] = jnp.zeros(
                    (LAST_ROWS[k] - place, 128), F32
                )
        axis = ORDERS[k][2]
        i = at[axis]
        for by in (1, 2, 3):
            copy = remote(
                out.at[lax.rem(i + by, 4)], got3[k].at[by - 1], k, 11 + by, axis, by
            )
            copy.start()
            sent[k].append(copy)
    for k in range(3):
        for j in (12, 13, 14):
            sent[k][j].wait_recv()
        outs[k][...] = last[k][at[ORDERS[k][2]]] + got3[k][0] + got3[k][1] + got3[k][2]
    for k in range(3):
        for copy in sent[k]:
            copy.wait_send()


def scatter_call(parts):
    def each(make):
        return [make(k) for k in range(3)]

    rows = PART_ROWS
    cuts = [(n // 2 + 7) // 8 * 8 for n in rows]
    return pl.pallas_call(
        scatter_kernel,
        out_shape=[full(n, 128) for n in LAST_ROWS],
        in_specs=[spec(pl.ANY)] * 3,
        out_specs=[spec(pltpu.VMEM)] * 3,
        scratch_shapes=each(lambda k: pltpu.VMEM((4, rows[k], 128), F32))
        + each(lambda k: pltpu.VMEM((2, rows[k], 128), F32))
        + each(lambda k: pltpu.VMEM((2, rows[k], 128), F32))
        + each(lambda k: pltpu.VMEM((6, 2, rows[k], 128), F32))
        + each(lambda k: pltpu.VMEM((3, cuts[k], 128), F32))
        + each(lambda k: pltpu.VMEM((3, rows[k] - cuts[k], 128), F32))
        + each(lambda k: pltpu.VMEM((4, LAST_ROWS[k], 128), F32))
        + each(lambda k: pltpu.VMEM((3, LAST_ROWS[k], 128), F32))
        + [
            pltpu.SemaphoreType.DMA((3, 15)),
            pltpu.SemaphoreType.DMA((3, 15)),
            pltpu.SemaphoreType.DMA((3, 3)),
        ],
        compiler_params=pltpu.CompilerParams(
            collective_id=3, has_side_effects=True, vmem_limit_bytes=48 * MB
        ),
        name="reduce_scatter",
    )(*parts)


def finish_kernel(s0, s1, s2, loss_o, table_o, kern_o, up_o, down_o, scale_o, head_o):
    sources = (s0, s1, s2)
    for k, (out, count, each) in enumerate(((up_o, 18, 6), (down_o, 6, 18), (table_o, 6, 16))):
        for c in range(count):
            out[:, 128 * c : 128 * (c + 1)] = sources[k][each * c : each * (c + 1), :]
        start, blocks = HEAD_BLOCKS[k]
        for c in range(blocks):
            rows = count * each + 6 * c
            values = sources[k][rows : rows + 6, :]
            if start + c < 8:
                head_o[:, 128 * (start + c) : 128 * (start + c + 1)] = values
            else:
                head_o[:, 1024:1026] = values[:, 0:2]
                tail = jnp.transpose(jnp.concatenate([values, jnp.zeros((122, 128), F32)], axis=0))
                kern_o[...] = tail[2:9, 0:6]
                scale_o[...] = tail[9:10, 0:6]
                pieces = values[0:1, 10:14]
                loss_o[...] = jnp.sum(pieces, axis=1, keepdims=True) * (0.5 / CLIPS)


def finish_call(sums):
    loss, table, kern, up, down, scale, head = pl.pallas_call(
        finish_kernel,
        out_shape=[
            full(1, 1), full(16, D), full(7, 6), full(6, FF), full(18, D), full(1, 6), full(6, 1026),
        ],
        in_specs=[spec(pltpu.VMEM)] * 3,
        out_specs=[spec(pltpu.VMEM)] * 7,
        name="finish",
    )(*sums)
    return loss.reshape(()), table, kern, up, down, scale.reshape(6), head


def body(
    code_ids, code_table, kernel, up_weight, down_weight, layer_scale, head_weight, target, loss_scale
):
    syn, a1, a2, win = make_constants()
    pick_n, pick_h, pick_k, turn1, turn2, row_id = make_orders()
    ids = jnp.swapaxes(code_ids, 1, 2).reshape(2, OWN)
    head_t = head_weight.T
    left_t, right_t, left_i, right_i = halo_call(target, ids)
    *saved, stat = forward_call(
        (target, left_t, right_t, ids, left_i, right_i, kernel, layer_scale, win),
        (code_table, up_weight, down_weight, head_t, syn, a1, a2),
    )
    operands = backward_call(
        (kernel, layer_scale, win, stat_call(stat), loss_scale.reshape(1, 1)),
        saved,
        (a1, a2, syn, head_t, down_weight, up_weight, pick_n, pick_h, pick_k),
    )
    here = [*operands, ids]
    parts = weight_call(here, pair_call(here), turn1, turn2, row_id)
    return finish_call(scatter_call(parts))


def solution(mesh):
    in_specs = (P("dp", "tm", None), P(), P(), P(), P(), P(), P(), P("dp", "tm"), P())
    out_specs = (
        P(),
        P(("dp", "tm"), None),
        P(None, ("dp", "tm")),
        P(("dp", "tm"), None),
        P(("dp", "tm"), None),
        P(("dp", "tm")),
        P(("dp", "tm"), None),
    )
    return jax.shard_map(body, mesh=mesh, in_specs=in_specs, out_specs=out_specs, check_vma=False)
```

```python
import jax
import jax.numpy as jnp
import ml_dtypes
import numpy as np
from jax import lax
from jax.experimental import pallas as pl
from jax.experimental.pallas import tpu as pltpu
from jax.sharding import PartitionSpec as P

F32, BF16 = jnp.float32, jnp.bfloat16
MESH = pl.DeviceIdType.MESH
D, FF = 768, 2304
HOP, NFFT = 256, 1024
FRAMES, OWN, HALO = 1024, 128, 16
ROWS = OWN + 2 * HALO
CHUNKS1, CHUNKS2 = 5, 3
WIDE1, WIDE2 = CHUNKS1 * 256, CHUNKS2 * 256
CLIPS = 16
MB = 1 << 20
ORDERS = ("xyz", "yzx", "zxy")
HEAD_BLOCKS = ((0, 2), (2, 3), (5, 4))
PART_ROWS = (18 * 24 + 2 * 24, 6 * 72 + 3 * 24, 6 * 64 + 4 * 24)


def bf(array):
    return np.asarray(array, np.float32).astype(ml_dtypes.bfloat16)


def hann(length):
    return 0.5 - 0.5 * np.cos(2.0 * np.pi * np.arange(length) / length)


def angles(length):
    product = np.arange(length // 2 + 1)[:, None] * np.arange(length)[None, :] % length
    return 2.0 * np.pi * product / length


def interleave(real, imag, chunks):
    bins, width = real.shape
    out = np.zeros((chunks, 2, 128, width), np.float64)
    for half, part in enumerate((real, imag)):
        padded = np.zeros((chunks * 128, width), np.float64)
        padded[:bins] = part
        out[:, half] = padded.reshape(chunks, 128, width)
    return out.reshape(chunks * 256, width)


def make_constants():
    ang = angles(NFFT)
    bins = np.arange(NFFT // 2 + 1)
    factor = np.where((bins == 0) | (bins == NFFT // 2), 1.0, 2.0)[:, None] / NFFT
    window = hann(NFFT)[None, :]
    synthesis = bf(interleave(factor * np.cos(ang) * window, -factor * np.sin(ang) * window, CHUNKS1))
    analysis1 = bf(interleave(np.cos(ang), -np.sin(ang), CHUNKS1).T)
    ang = angles(NFFT // 2)
    analysis2 = bf(interleave(np.cos(ang), -np.sin(ang), CHUNKS2).T)
    win = np.zeros((8, NFFT), np.float32)
    win[0] = hann(NFFT)
    win[1] = hann(NFFT) ** 2
    win[2, : NFFT // 2] = hann(NFFT // 2)
    return synthesis, analysis1, analysis2, win


def device_index(x, y, z, core):
    return ((y * 2 + z // 2) * 2 + core) * 8 + x * 2 + z % 2


def shard_order(order, core):
    places = []
    for a in range(4):
        for b in range(4):
            for c in range(4):
                at = dict(zip(order, (a, b, c)))
                places.append(device_index(at["x"], at["y"], at["z"], core))
    return np.array(places)


def columns_of(order, core, each):
    return (shard_order(order, core)[:, None] * each + np.arange(each)[None, :]).reshape(-1)


def one_hot_columns(sources, size):
    out = np.zeros((size, sources.size), np.float32)
    out[sources, np.arange(sources.size)] = 1.0
    return bf(out)


def make_orders():
    pick_n = np.stack([one_hot_columns(columns_of(ORDERS[0], c, 6), D) for c in (0, 1)])
    half = [columns_of(ORDERS[1], c, 18)[: 4 * 4 * 2 * 18] for c in (0, 1)]
    pick_h = np.stack([one_hot_columns(h, FF // 2) for h in half])
    pick_k = np.stack([one_hot_columns(columns_of(ORDERS[2], c, 6), D) for c in (0, 1)])
    first = columns_of(ORDERS[0], 0, 6)
    where = {col: i for i, col in enumerate(first)}
    turns = []
    for k in (1, 2):
        sources = np.array([where[col] for col in columns_of(ORDERS[k], 0, 6)])
        turns.append(one_hot_columns(sources, 384))
    row_id = columns_of(ORDERS[2], 0, 16).astype(np.int32)[:, None]
    return pick_n, pick_h, pick_k, turns[0], turns[1], row_id


def mm(a, b):
    return jnp.dot(a, b, preferred_element_type=F32)


def mm_bt(a, b):
    return lax.dot_general(a, b, (((1,), (1,)), ((), ())), preferred_element_type=F32)


def mm_at(a, b):
    return lax.dot_general(a, b, (((0,), (0,)), ((), ())), preferred_element_type=F32)


def shift(values, by):
    by = by % values.shape[0]
    return values if by == 0 else pltpu.roll(values, by, 0)


def norm(values):
    centre = values - jnp.mean(values, axis=-1, keepdims=True)
    rstd = lax.rsqrt(jnp.mean(centre * centre, axis=-1, keepdims=True) + 1e-6)
    return centre * rstd, rstd


def norm_back(grad, y, rstd):
    mean_g = jnp.mean(grad, axis=-1, keepdims=True)
    mean_gy = jnp.mean(grad * y, axis=-1, keepdims=True)
    return rstd * (grad - mean_g - y * mean_gy)


def frame_places():
    first = lax.axis_index("tm") * OWN - HALO
    return (lax.broadcasted_iota(jnp.int32, (ROWS, 1), 0) + first).astype(F32)


def sin_cos(x):
    turns = jnp.round(x * 0.6366197723675814)
    r = x - turns * 1.5703125
    r = r - turns * 4.837512969970703125e-4
    r = r - turns * 7.549789954891882e-8
    z = r * r
    sine = r + r * z * (-1.6666654611e-1 + z * (8.3321608736e-3 + z * -1.9515295891e-4))
    cosine = (4.166664568298827e-2 + z * (-1.388731625493765e-3 + z * 2.443315711809948e-5)) * (z * z)
    cosine = cosine - 0.5 * z + 1.0
    quarter = turns.astype(jnp.int32)
    odd = (quarter & 1) == 1
    first, second = jnp.where(odd, cosine, sine), jnp.where(odd, sine, cosine)
    first = jnp.where((quarter & 2) == 2, -first, first)
    second = jnp.where(((quarter + 1) & 2) == 2, -second, second)
    return first, second


def inside(places):
    return (places >= 0.0) & (places < float(FRAMES))


def envelope(places, win):
    total = jnp.zeros((ROWS, HOP), F32)
    for p in range(4):
        total = total + jnp.where(inside(places + float(2 - p)), win[1:2, HOP * p : HOP * (p + 1)], 0.0)
    return jnp.where(inside(places), total, 1.0)


def spec(space):
    return pl.BlockSpec(memory_space=space)


def full(*shape, dtype=F32):
    return jax.ShapeDtypeStruct(shape, dtype)


def halo_kernel(target, ids, left_t, right_t, left_i, right_i, send, recv):
    tm = lax.axis_index("tm")
    right, left = lax.rem(tm + 1, 8), lax.rem(tm + 7, 8)
    barrier = pltpu.get_barrier_semaphore()
    for there in (left, right):
        pl.semaphore_signal(barrier, inc=1, device_id={"tm": there}, device_id_type=MESH)
    pl.semaphore_wait(barrier, 2)
    edge = HALO * HOP
    copies = []
    for i, (src, dst, there) in enumerate(
        (
            (target.at[:, pl.ds(OWN * HOP - edge, edge)], left_t, right),
            (target.at[:, pl.ds(0, edge)], right_t, left),
            (ids, left_i, right),
            (ids, right_i, left),
        )
    ):
        copies.append(
            pltpu.make_async_remote_copy(
                src_ref=src,
                dst_ref=dst,
                send_sem=send.at[i],
                recv_sem=recv.at[i],
                device_id={"tm": there},
                device_id_type=MESH,
            )
        )
    for copy in copies:
        copy.start()
    for copy in copies:
        copy.wait()


def halo_call(target, ids):
    edge = full(1, HALO * HOP)
    around = full(2, OWN, dtype=jnp.int32)
    return pl.pallas_call(
        halo_kernel,
        out_shape=[edge, edge, around, around],
        in_specs=[spec(pltpu.VMEM)] * 2,
        out_specs=[spec(pltpu.VMEM)] * 4,
        scratch_shapes=[pltpu.SemaphoreType.DMA((4,)), pltpu.SemaphoreType.DMA((4,))],
        compiler_params=pltpu.CompilerParams(collective_id=0, has_side_effects=True),
        name="halo",
    )(target, ids)


def ids_column(ids):
    padded = jnp.concatenate([ids.astype(F32), jnp.zeros((126, OWN), F32)], axis=0)
    return jnp.transpose(padded)[:, :2]


def forward_kernel(
    target, left_t, right_t, ids, left_i, right_i, kern, scale_i, win,
    table_h, up_h, down_h, head_h, syn_h, a1_h, a2_h, *refs,
):
    outs, stat_o, refs = refs[: len(SAVED)], refs[len(SAVED)], refs[len(SAVED) + 1 :]
    (sin_o, rstd_o, y1_o, gp_o, hid_o, down_o, y2_o, re_o, im_o, d1_o, q1_o, d2_o, q2_o) = refs[
        : len(SAVED)
    ]
    kept = refs[: len(SAVED)]
    refs = refs[len(SAVED) :]
    (table_v, up_v, down_v, head_v, syn_v, a1_v, a2_v) = refs[:7]
    goal, codes, hid_v, head_s, spec_v, seg1, seg2, sems, out_sems = refs[7:]
    pairs = (
        (table_h, table_v), (up_h, up_v), (down_h, down_v), (head_h, head_v),
        (syn_h, syn_v), (a1_h, a1_v), (a2_h, a2_v),
    )
    copies = [pltpu.make_async_copy(h, v, sems.at[i]) for i, (h, v) in enumerate(pairs)]
    copies[0].start()
    copies[1].start()
    saves = [pltpu.make_async_copy(v, h, out_sems.at[i]) for i, (v, h) in enumerate(zip(kept, outs))]
    scale = scale_i[...].reshape(1, D)
    for source, first, count, skip in (
        (left_t, 0, HALO, 0), (target, HALO, OWN, 0), (right_t, HALO + OWN, HALO, 0),
    ):
        for r in range(count):
            goal[first + r : first + r + 1, :] = source[:, HOP * r : HOP * (r + 1)]
    codes[0:HALO, :] = ids_column(left_i[...])[OWN - HALO :]
    codes[HALO : HALO + OWN, :] = ids_column(ids[...])
    codes[HALO + OWN :, :] = ids_column(right_i[...])[:HALO]
    places = frame_places()
    valid = inside(places)
    lane = lax.broadcasted_iota(jnp.int32, (ROWS, 2 * FRAMES), 1).astype(F32)
    hot = (lane == codes[:, 0:1]) | (lane == codes[:, 1:2] + 1024.0)
    hot = jnp.where(hot, 1.0, 0.0).astype(BF16)
    copies[0].wait()
    copies[2].start()
    y0, rstd0 = norm(mm(hot, table_v[...]))
    y0 = jnp.where(valid, y0, 0.0)
    sin_o[...] = y0
    saves[0].start()
    mixture = kern[0:1, :] * shift(y0, 3)
    for k in range(1, 7):
        mixture = mixture + kern[k : k + 1, :] * shift(y0, 3 - k)
    y1, rstd1 = norm(mixture)
    y1_o[...] = y1
    saves[2].start()
    normed = y1.astype(BF16)
    copies[1].wait()
    copies[3].start()
    copies[4].start()
    for c in range(FF // 256):
        at = slice(256 * c, 256 * (c + 1))
        up = mm(normed, up_v[:, at])
        cdf = 0.5 * (1.0 + lax.erf(up * 0.7071067811865476))
        hid_v[:, at] = (up * cdf).astype(BF16)
        gp_o[:, at] = cdf + up * (0.3989422804014327 * jnp.exp(-0.5 * up * up))
    hid_o[...] = hid_v[HALO : HALO + OWN, :]
    saves[3].start()
    saves[4].start()
    copies[2].wait()
    copies[5].start()
    copies[6].start()
    down = mm(hid_v[...], down_v[...])
    down_o[...] = down
    saves[5].start()
    y2, rstd2 = norm(y0 + scale * down)
    y2_o[...] = y2
    saves[6].start()
    places128 = lax.broadcasted_iota(jnp.int32, (ROWS, 128), 1)
    rstd_o[...] = jnp.where(places128 == 0, rstd0, jnp.where(places128 == 1, rstd1, rstd2))
    saves[1].start()
    onorm = y2.astype(BF16)
    copies[3].wait()
    head_s[:, 1024:] = jnp.zeros((ROWS, 128), F32)
    for c in range(4):
        head_s[:, 256 * c : 256 * (c + 1)] = mm_bt(onorm, head_v[256 * c : 256 * (c + 1), :])
    head_s[:, 1024:1026] = mm_bt(onorm, head_v[1024:1026, :])
    phases = pltpu.roll(head_s[:, 512:], CHUNKS1 * 128 - 1, 1)
    for c in range(CHUNKS1):
        logmag = head_s[:, 128 * c : 128 * (c + 1)]
        if c == 4:
            logmag = jnp.where(places128 == 0, logmag, 0.0)
        mag = jnp.exp(logmag)
        phase = phases[:, 128 * c : 128 * (c + 1)]
        sine, cosine = sin_cos(phase)
        re, im = mag * cosine, mag * sine
        re_o[:, 128 * c : 128 * (c + 1)] = re
        im_o[:, 128 * c : 128 * (c + 1)] = im
        spec_v[:, 256 * c : 256 * c + 128] = re.astype(BF16)
        spec_v[:, 256 * c + 128 : 256 * (c + 1)] = im.astype(BF16)
    saves[7].start()
    saves[8].start()
    copies[4].wait()
    pred = jnp.zeros((ROWS, HOP), F32)
    for p in range(4):
        piece = jnp.where(valid, mm(spec_v[...], syn_v[:, HOP * p : HOP * (p + 1)]), 0.0)
        pred = pred + shift(piece, p - 2)
    pred = jnp.where(valid, pred / envelope(places, win), 0.0)
    for s, x in enumerate((pred, jnp.where(valid, goal[...], 0.0))):
        r1 = slice(ROWS * s, ROWS * (s + 1))
        for p in range(4):
            at = slice(HOP * p, HOP * (p + 1))
            seg1[r1, at] = (shift(x, 2 - p) * win[0:1, at]).astype(BF16)
        even = slice(2 * ROWS * s, 2 * ROWS * s + ROWS)
        odd = slice(2 * ROWS * s + ROWS, 2 * ROWS * (s + 1))
        before, after = shift(x, 1), shift(x, -1)
        seg2[even, 0:256] = (before * win[2:3, 0:256]).astype(BF16)
        seg2[even, 256:512] = (x * win[2:3, 256:512]).astype(BF16)
        seg2[odd, 0:128] = (before[:, 128:] * win[2:3, 0:128]).astype(BF16)
        seg2[odd, 128:384] = (x * win[2:3, 128:384]).astype(BF16)
        seg2[odd, 384:512] = (after[:, :128] * win[2:3, 384:512]).astype(BF16)
    own = slice(HALO, HALO + OWN)
    for level in range(2):
        seg, table, chunks = ((seg1, a1_v, CHUNKS1), (seg2, a2_v, CHUNKS2))[level]
        d_o, q_o = ((d1_o, q1_o), (d2_o, q2_o))[level]
        copies[5 + level].wait()
        sums = [jnp.zeros((OWN, 128), F32) for _ in range(3)]
        for c in range(chunks):
            for sub in range(level + 1):
                rows_p = slice(ROWS * sub, ROWS * (sub + 1))
                base = ROWS * (level + 1)
                rows_g = slice(base + ROWS * sub, base + ROWS * (sub + 1))
                weights = table[:, 256 * c : 256 * (c + 1)]
                sp, sg = mm(seg[rows_p, :], weights), mm(seg[rows_g, :], weights)
                diff = sp - sg
                pr, pi, gr, gi = sp[:, :128], sp[:, 128:], sg[:, :128], sg[:, 128:]
                power_p, power_g = pr * pr + pi * pi, gr * gr + gi * gi
                gap = jnp.log1p(power_p) - jnp.log1p(power_g)
                slope = jnp.where(valid, 4.0 * gap / (1.0 + power_p), 0.0)
                d_o[rows_p, 256 * c : 256 * (c + 1)] = jnp.where(valid, diff, 0.0)
                q_o[rows_p, 256 * c : 256 * c + 128] = slope * pr
                q_o[rows_p, 256 * c + 128 : 256 * (c + 1)] = slope * pi
                dr, di = diff[own, :128], diff[own, 128:]
                sums[0] = sums[0] + dr * dr + di * di
                sums[1] = sums[1] + power_g[own]
                sums[2] = sums[2] + gap[own] * gap[own]
        saves[9 + 2 * level].start()
        saves[10 + 2 * level].start()
        for i in range(3):
            total = jnp.sum(jnp.sum(sums[i], axis=0, keepdims=True), axis=1, keepdims=True)
            stat_o[3 * level + i : 3 * level + i + 1, :] = jnp.broadcast_to(total, (1, 128))
    stat_o[6:8, :] = jnp.zeros((2, 128), F32)
    for save in saves:
        save.wait()


SAVED = (
    full(ROWS, D), full(ROWS, 128), full(ROWS, D), full(ROWS, FF), full(OWN, FF, dtype=BF16),
    full(ROWS, D), full(ROWS, D), full(ROWS, CHUNKS1 * 128), full(ROWS, CHUNKS1 * 128),
    full(ROWS, WIDE1), full(ROWS, WIDE1), full(2 * ROWS, WIDE2), full(2 * ROWS, WIDE2),
)


def vmem(shapes):
    return [pltpu.VMEM(a.shape, a.dtype) for a in shapes]


def forward_call(small, big):
    outs = list(SAVED) + [full(8, 128)]
    return pl.pallas_call(
        forward_kernel,
        out_shape=outs,
        in_specs=[spec(pltpu.VMEM)] * len(small) + [spec(pl.ANY)] * len(big),
        out_specs=[spec(pl.ANY)] * len(SAVED) + [spec(pltpu.VMEM)],
        scratch_shapes=vmem(SAVED)
        + vmem(big)
        + [
            pltpu.VMEM((ROWS, HOP), F32),
            pltpu.VMEM((ROWS, 2), F32),
            pltpu.VMEM((ROWS, FF), BF16),
            pltpu.VMEM((ROWS, 1152), F32),
            pltpu.VMEM((ROWS, WIDE1), BF16),
            pltpu.VMEM((2 * ROWS, NFFT), BF16),
            pltpu.VMEM((4 * ROWS, NFFT // 2), BF16),
            pltpu.SemaphoreType.DMA((len(big),)),
            pltpu.SemaphoreType.DMA((len(SAVED),)),
        ],
        compiler_params=pltpu.CompilerParams(vmem_limit_bytes=60 * MB),
        name="forward",
    )(*small, *big)


def stat_kernel(stat, out, slots, send, recv):
    tm = lax.axis_index("tm")
    barrier = pltpu.get_barrier_semaphore()
    others = [lax.rem(tm + j, 8) for j in range(1, 8)]
    for there in others:
        pl.semaphore_signal(barrier, inc=1, device_id={"tm": there}, device_id_type=MESH)
    pl.semaphore_wait(barrier, 7)
    copies = []
    for j, there in enumerate(others):
        copies.append(
            pltpu.make_async_remote_copy(
                src_ref=stat,
                dst_ref=slots.at[tm],
                send_sem=send.at[j],
                recv_sem=recv.at[j],
                device_id={"tm": there},
                device_id_type=MESH,
            )
        )
    for copy in copies:
        copy.start()
    slots[tm] = stat[...]
    for copy in copies:
        copy.wait()
    total = slots[0]
    for j in range(1, 8):
        total = total + slots[j]
    out[...] = total


def stat_call(stat):
    return pl.pallas_call(
        stat_kernel,
        out_shape=full(8, 128),
        in_specs=[spec(pltpu.VMEM)],
        out_specs=spec(pltpu.VMEM),
        scratch_shapes=[
            pltpu.VMEM((8, 8, 128), F32),
            pltpu.SemaphoreType.DMA((7,)),
            pltpu.SemaphoreType.DMA((7,)),
        ],
        compiler_params=pltpu.CompilerParams(collective_id=1, has_side_effects=True),
        name="clip_sums",
    )(stat)


def backward_kernel(kern, scale_i, win, stat, loss_scale, *refs):
    count = len(SAVED)
    saved_h, refs = refs[:count], refs[count:]
    big_h, refs = refs[:9], refs[9:]
    outs, refs = refs[:8], refs[8:]
    saved, refs = refs[:count], refs[count:]
    (sin_i, rstd_i, y1_i, gp_i, hid_i, down_i, y2_i, re_i, im_i, d1_i, q1_i, d2_i, q2_i) = saved
    (a1_v, a2_v, syn_v, head_v, down_v, up_v, pick_n, pick_h, pick_k), refs = refs[:9], refs[9:]
    (nrm_o, hid_o, onm_o, dup_o, ddn_o, dhd_o, dem_o, kg_o), refs = refs[:8], refs[8:]
    kept = (nrm_o, hid_o, onm_o, dup_o, ddn_o, dhd_o, dem_o, kg_o)
    dfr, dphase, dhead, dup, small, sems, saved_sems, out_sems = refs
    loads = [
        pltpu.make_async_copy(h, v, saved_sems.at[i]) for i, (h, v) in enumerate(zip(saved_h, saved))
    ]
    copies = [
        pltpu.make_async_copy(h, v, sems.at[i])
        for i, (h, v) in enumerate(
            zip(big_h, (a1_v, a2_v, syn_v, head_v, down_v, up_v, pick_n, pick_h, pick_k))
        )
    ]
    saves = [pltpu.make_async_copy(v, h, out_sems.at[i]) for i, (v, h) in enumerate(zip(kept, outs))]
    for copy in (loads[9], loads[10], copies[0]):
        copy.start()
    scale = scale_i[...].reshape(1, D)
    own = slice(HALO, HALO + OWN)
    places = frame_places()
    valid = inside(places)

    factor = loss_scale[...] * (0.5 / CLIPS)
    loss = jnp.zeros((1, 1), F32)
    cots = []
    for level in range(2):
        count = ((FRAMES * 513), (2 * FRAMES * 257))[level]
        sum_a = stat[3 * level : 3 * level + 1, 0:1]
        sum_b = stat[3 * level + 1 : 3 * level + 2, 0:1]
        sum_g = stat[3 * level + 2 : 3 * level + 3, 0:1]
        root_a, root_b = jnp.sqrt(sum_a + 1e-6), jnp.sqrt(sum_b + 1e-6)
        loss = loss + root_a / root_b + sum_g * (1.0 / count)
        cots.append((factor / (root_a * root_b), factor * (1.0 / count)))
    loss = jnp.where(lax.axis_index("tm") == 0, loss, 0.0)

    dx = jnp.zeros((ROWS, HOP), F32)
    loads[9].wait()
    loads[10].wait()
    copies[0].wait()
    for copy in (loads[11], loads[12], copies[1], copies[2], loads[7], loads[8]):
        copy.start()
    ds1 = (cots[0][0] * d1_i[...] + cots[0][1] * q1_i[...]).astype(BF16)
    for p in range(4):
        at = slice(HOP * p, HOP * (p + 1))
        piece = mm_bt(ds1, a1_v[at, :]).astype(BF16).astype(F32) * win[0:1, at]
        dx = dx + shift(piece, p - 2)
    loads[11].wait()
    loads[12].wait()
    copies[1].wait()
    for copy in (copies[3], loads[1], loads[6], loads[5]):
        copy.start()
    ds2 = (cots[1][0] * d2_i[...] + cots[1][1] * q2_i[...]).astype(BF16)
    dseg = mm_bt(ds2, a2_v[...]).astype(BF16).astype(F32) * win[2:3, : NFFT // 2]
    even, odd = dseg[:ROWS], dseg[ROWS:]
    dx = dx + shift(even[:, :256], -1) + even[:, 256:] + odd[:, 128:384]
    dx = dx + jnp.concatenate([shift(odd[:, 384:], 1), shift(odd[:, :128], -1)], axis=1)
    dx = jnp.where(valid, dx / envelope(places, win), 0.0)
    for p in range(4):
        piece = jnp.where(valid, shift(dx, 2 - p), 0.0)
        dfr[:, HOP * p : HOP * (p + 1)] = piece.astype(BF16)

    copies[2].wait()
    loads[7].wait()
    loads[8].wait()
    copies[4].start()
    loads[3].start()
    for c in range(CHUNKS1):
        dsp = mm_bt(dfr[...], syn_v[256 * c : 256 * (c + 1), :]).astype(BF16).astype(F32)
        dre, dim = dsp[:, :128], dsp[:, 128:]
        re, im = re_i[:, 128 * c : 128 * (c + 1)], im_i[:, 128 * c : 128 * (c + 1)]
        dlog, dph = dre * re + dim * im, dim * re - dre * im
        if c < 4:
            dhead[:, 128 * c : 128 * (c + 1)] = dlog.astype(BF16)
        dphase[:, 128 * c : 128 * (c + 1)] = dph
    moved = pltpu.roll(dphase[...], 1, 1)
    dhead[:, 512:640] = (moved[:, :128] + dlog).astype(BF16)
    dhead[:, 640:] = moved[:, 128:].astype(BF16)
    dhd_o[...] = dhead[own, :].astype(F32)
    saves[5].start()
    copies[3].wait()
    for copy in (copies[5], loads[2], loads[0]):
        copy.start()
    don = mm(dhead[:, :1026], head_v[...]).astype(BF16).astype(F32)
    for i in (1, 6, 5):
        loads[i].wait()
    dstream = norm_back(don, y2_i[...], rstd_i[:, 2:3])

    scale_grad = jnp.sum(dstream[own] * down_i[own, :], axis=0, keepdims=True)
    ddn = (scale * dstream).astype(BF16)
    ddn_o[...] = ddn[own].astype(F32)
    saves[4].start()
    copies[4].wait()
    loads[3].wait()
    for copy in (copies[6], loads[4], copies[7], copies[8]):
        copy.start()
    for c in range(FF // 256):
        at = slice(256 * c, 256 * (c + 1))
        dh = mm_bt(ddn, down_v[at, :]).astype(BF16).astype(F32)
        dup[:, at] = (dh * gp_i[:, at]).astype(BF16)
    dup_o[...] = dup[own, :].astype(F32)
    saves[3].start()
    copies[5].wait()
    loads[2].wait()
    loads[0].wait()
    dnorm = mm_bt(dup[...], up_v[...]).astype(BF16).astype(F32)
    dmix = norm_back(dnorm, y1_i[...], rstd_i[:, 1:2])
    dmix = jnp.where(valid, dmix, 0.0)
    y0 = sin_i[...]
    dsin = dstream
    small[...] = jnp.zeros((128, D), F32)
    for k in range(7):
        dsin = dsin + kern[k : k + 1, :] * shift(dmix, k - 3)
        taps = dmix * shift(y0, 3 - k)
        small[2 + k : 3 + k, :] = jnp.sum(taps[own], axis=0, keepdims=True)
    demb = norm_back(dsin, y0, rstd_i[:, 0:1])
    dem_o[...] = demb[own].astype(BF16).astype(F32)
    saves[6].start()

    small[9:10, :] = scale_grad
    rest = loss
    for i, grid in enumerate((65536.0, 1.0, 1.0 / 65536.0, 1.0 / 65536.0 / 65536.0)):
        piece = jnp.floor(rest * (1.0 / grid)) * grid
        rest = rest - piece
        small[10 + i : 11 + i, :] = jnp.broadcast_to(piece, (1, D))

    for copy in (copies[6], copies[7], copies[8], loads[4]):
        copy.wait()
    normed = y1_i[own, :].astype(BF16)
    onorm = y2_i[own, :].astype(BF16)
    small0 = small[...].astype(BF16)
    left = small[...] - small0.astype(F32)
    small1 = left.astype(BF16)
    small2 = (left - small1.astype(F32)).astype(BF16)
    for c in range(2):
        nrm_o[c] = mm(normed, pick_n[c])
        onm_o[c] = mm(onorm, pick_n[c])
        for h in range(2):
            out = slice(576 * h, 576 * (h + 1))
            hid_o[c, :, out] = mm(hid_i[:, 1152 * h : 1152 * (h + 1)], pick_h[c])
        kg_o[c] = sum(
            lax.dot_general(pick_k[c], s, (((0,), (1,)), ((), ())), preferred_element_type=F32)
            for s in (small0, small1, small2)
        )
    for i in (0, 1, 2, 7):
        saves[i].start()
    for save in saves:
        save.wait()


def backward_call(small, saved, big):
    outs = [
        full(2, OWN, 384), full(2, OWN, 1152), full(2, OWN, 384), full(OWN, FF), full(OWN, D),
        full(OWN, 1152), full(OWN, D), full(2, 384, 128),
    ]
    return pl.pallas_call(
        backward_kernel,
        out_shape=outs,
        in_specs=[spec(pltpu.VMEM)] * len(small) + [spec(pl.ANY)] * (len(saved) + len(big)),
        out_specs=[spec(pl.ANY)] * len(outs),
        scratch_shapes=vmem(saved)
        + vmem(big)
        + vmem(outs)
        + [
            pltpu.VMEM((ROWS, NFFT), BF16),
            pltpu.VMEM((ROWS, CHUNKS1 * 128), F32),
            pltpu.VMEM((ROWS, 1152), BF16),
            pltpu.VMEM((ROWS, FF), BF16),
            pltpu.VMEM((128, D), F32),
            pltpu.SemaphoreType.DMA((len(big),)),
            pltpu.SemaphoreType.DMA((len(saved),)),
            pltpu.SemaphoreType.DMA((len(outs),)),
        ],
        compiler_params=pltpu.CompilerParams(vmem_limit_bytes=60 * MB),
        name="backward",
    )(*small, *saved, *big)


LAST_ROWS = (120, 128, 120)
FIRST_ROWS = (0, 120, 248)
OPERANDS = (
    full(OWN, 384), full(OWN, 1152), full(OWN, 384), full(OWN, FF), full(OWN, D),
    full(OWN, 1152), full(OWN, D), full(384, 128), full(2, OWN, dtype=jnp.int32),
)


def put(out, first, values, rows):
    for block in range(values.shape[1] // 128):
        part = values[:, 128 * block : 128 * (block + 1)].reshape(4, 4, rows, 128)
        out[:, :, first + rows * block : first + rows * (block + 1), :] = part


def halves_of(rows):
    upper = (rows // 2 + 7) // 8 * 8
    return pl.ds(0, upper), pl.ds(upper, rows - upper)


def scatter_kernel(*refs):
    here_h, (turn1, turn2, row_id), out_o, scratch = refs[0:9], refs[9:12], refs[12], refs[13:]
    here, there = scratch[0:9], scratch[9:18]
    parts, through, from_left, from_right = (scratch[18 + 3 * i : 21 + 3 * i] for i in range(4))
    got2a, got2b, last, got3 = (scratch[30 + 3 * i : 33 + 3 * i] for i in range(4))
    send, recv, pair_send, pair_recv, load = scratch[42:]

    dp, tm = lax.axis_index("dp"), lax.axis_index("tm")
    at = {"x": tm // 2, "y": dp // 4, "z": lax.rem(dp // 2, 2) * 2 + lax.rem(tm, 2)}
    core = lax.rem(dp, 2)
    partner = {"dp": dp + 1 - 2 * core, "tm": tm}

    def device(axis, by):
        to = dict(at)
        to[axis] = lax.rem(at[axis] + by, 4)
        return {
            "dp": (to["y"] * 2 + to["z"] // 2) * 2 + core,
            "tm": to["x"] * 2 + lax.rem(to["z"], 2),
        }

    barrier = pltpu.get_barrier_semaphore()
    pl.semaphore_signal(barrier, inc=1, device_id=partner, device_id_type=MESH)
    for axis in "xyz":
        for by in (1, 2, 3):
            pl.semaphore_signal(barrier, inc=1, device_id=device(axis, by), device_id_type=MESH)
    order = (0, 3, 2, 5, 1, 4, 8, 6, 7)
    loads, pairs = {}, {}
    for i in order:
        picked = len(here_h[i].shape) == 3
        loads[i] = pltpu.make_async_copy(
            here_h[i].at[core] if picked else here_h[i], here[i], load.at[i]
        )
        pairs[i] = pltpu.make_async_remote_copy(
            src_ref=here_h[i].at[1 - core] if picked else here_h[i],
            dst_ref=there[i],
            send_sem=pair_send.at[i],
            recv_sem=pair_recv.at[i],
            device_id=partner,
            device_id_type=MESH,
        )
        loads[i].start()
    pl.semaphore_wait(barrier, 10)
    for i in order:
        pairs[i].start()

    def need(*which):
        for i in which:
            loads[i].wait()
            pairs[i].wait_recv()

    def both(i, cols=slice(None)):
        return jnp.concatenate([here[i][:, cols], there[i][:, cols]], axis=0).astype(BF16)

    def remote(src, dst, k, slot, axis, by):
        copy = pltpu.make_async_remote_copy(
            src_ref=src,
            dst_ref=dst,
            send_sem=send.at[k, slot],
            recv_sem=recv.at[k, slot],
            device_id=device(axis, by),
            device_id_type=MESH,
        )
        copy.start()
        return copy

    def around(axis):
        i = at[axis]
        return i, lax.rem(i + 1, 4), lax.rem(i + 2, 4), lax.rem(i + 3, 4)

    def head_part(k, first, onorm):
        start, blocks = HEAD_BLOCKS[k]
        for b in range(blocks):
            cols = slice(128 * (start + b), 128 * (start + b + 1))
            values = mm_at(onorm, both(5, cols))
            if start + b == 8:
                values = values + here[7][...] + there[7][...]
            put(parts[k], first + 24 * b, values, 24)

    low, high = pl.ds(0, 2), pl.ds(2, 2)
    sent = []

    def phase1(k):
        axis, p = ORDERS[k][0], parts[k]
        i, right, opposite, left = around(axis)
        sent.append(
            [
                remote(p.at[opposite, low], through[k].at[0], k, 0, axis, 1),
                remote(p.at[opposite, high], through[k].at[1], k, 1, axis, 3),
                remote(p.at[right, high], from_left[k].at[high], k, 2, axis, 1),
                remote(p.at[left, low], from_right[k].at[low], k, 3, axis, 3),
            ]
        )

    need(0, 3)
    normed = both(0)
    for c in range(FF // 256):
        put(parts[0], 48 * c, mm_at(normed, both(3, slice(256 * c, 256 * (c + 1)))), 24)
    need(2, 5)
    onorm = both(2)
    head_part(0, 432, onorm)
    phase1(0)
    need(1, 4)
    hidden = both(1)
    for c in range(3):
        put(parts[1], 144 * c, mm_at(hidden, both(4, slice(256 * c, 256 * (c + 1)))), 72)
    head_part(1, 432, mm(onorm, turn1[...]).astype(BF16))
    phase1(1)
    need(8, 6, 7)
    ids = jnp.concatenate([here[8][...], there[8][...]], axis=1)
    rows = row_id[...] + OWN * core
    hot = (rows == ids[0:1, :]) | (rows == ids[1:2, :] + 1024)
    hot = jnp.where(hot, 1.0, 0.0).astype(BF16)
    for c in range(3):
        put(parts[2], 128 * c, mm(hot, both(6, slice(256 * c, 256 * (c + 1)))), 64)
    head_part(2, 384, mm(onorm, turn2[...]).astype(BF16))
    phase1(2)

    for k in range(3):
        axis, p = ORDERS[k][0], parts[k]
        i, right, opposite, left = around(axis)
        sent[k][0].wait_recv()
        p[right, low] += through[k][0]
        sent[k].append(remote(p.at[right, low], from_left[k].at[low], k, 4, axis, 1))
        sent[k][1].wait_recv()
        p[left, high] += through[k][1]
        sent[k].append(remote(p.at[left, high], from_right[k].at[high], k, 5, axis, 3))
    for k in range(3):
        mine = at[ORDERS[k][0]]
        axis, p, a, b = ORDERS[k][1], parts[k], got2a[k], got2b[k]
        i, right, opposite, left = around(axis)
        upper, lower = halves_of(PART_ROWS[k])
        for j in (2, 3, 4, 5):
            sent[k][j].wait_recv()
        p[mine, opposite] += from_left[k][opposite] + from_right[k][opposite]
        sent[k].append(remote(p.at[mine, opposite, upper], a.at[0], k, 6, axis, 1))
        sent[k].append(remote(p.at[mine, opposite, lower], b.at[0], k, 7, axis, 3))
        p[mine, right] += from_left[k][right] + from_right[k][right]
        sent[k].append(remote(p.at[mine, right, lower], b.at[1], k, 8, axis, 1))
        p[mine, left] += from_left[k][left] + from_right[k][left]
        sent[k].append(remote(p.at[mine, left, upper], a.at[1], k, 9, axis, 3))
        p[mine, i] += from_left[k][i] + from_right[k][i]
    for k in range(3):
        mine = at[ORDERS[k][0]]
        axis, p, a, b = ORDERS[k][1], parts[k], got2a[k], got2b[k]
        i, right, opposite, left = around(axis)
        upper, lower = halves_of(PART_ROWS[k])
        sent[k][6].wait_recv()
        p[mine, right, upper] += a[0]
        sent[k].append(remote(p.at[mine, right, upper], a.at[2], k, 10, axis, 1))
        sent[k][7].wait_recv()
        p[mine, left, lower] += b[0]
        sent[k].append(remote(p.at[mine, left, lower], b.at[2], k, 11, axis, 3))
    for k in range(3):
        mine = at[ORDERS[k][0]]
        i = at[ORDERS[k][1]]
        p, a, b, out = parts[k], got2a[k], got2b[k], last[k]
        upper, lower = halves_of(PART_ROWS[k])
        for j in (8, 9, 10, 11):
            sent[k][j].wait_recv()
        p[mine, i, upper] += a[1] + a[2]
        p[mine, i, lower] += b[1] + b[2]
        blocks = (((18, 24), (2, 24)), ((6, 72), (3, 24)), ((6, 64), (4, 24)))[k]
        start, place = 0, 0
        for count, rows in blocks:
            each = rows // 4
            for _ in range(count):
                for d in range(4):
                    out[d, pl.ds(place, each)] = p[mine, i, pl.ds(start + d * each, each)]
                start += rows
                place += each
        if place < LAST_ROWS[k]:
            for d in range(4):
                out[d, pl.ds(place, LAST_ROWS[k] - place)] = jnp.zeros(
                    (LAST_ROWS[k] - place, 128), F32
                )
        axis = ORDERS[k][2]
        for by in (1, 2, 3):
            to = lax.rem(at[axis] + by, 4)
            sent[k].append(remote(out.at[to], got3[k].at[by - 1], k, 11 + by, axis, by))
    for k in range(3):
        for j in (12, 13, 14):
            sent[k][j].wait_recv()
        total = last[k][at[ORDERS[k][2]]] + got3[k][0] + got3[k][1] + got3[k][2]
        out_o[pl.ds(FIRST_ROWS[k], LAST_ROWS[k]), :] = total
    for i in order:
        pairs[i].wait_send()
    for k in range(3):
        for copy in sent[k]:
            copy.wait_send()


def scatter_call(operands, turn1, turn2, row_id):
    def each(make):
        return [pltpu.VMEM(make(k), F32) for k in range(3)]

    rows = PART_ROWS
    cuts = [halves_of(n)[0].size for n in rows]
    return pl.pallas_call(
        scatter_kernel,
        out_shape=full(sum(LAST_ROWS), 128),
        in_specs=[spec(pl.ANY)] * 9 + [spec(pltpu.VMEM)] * 3,
        out_specs=spec(pltpu.VMEM),
        scratch_shapes=vmem(OPERANDS)
        + vmem(OPERANDS)
        + each(lambda k: (4, 4, rows[k], 128))
        + each(lambda k: (2, 2, rows[k], 128))
        + each(lambda k: (4, rows[k], 128))
        + each(lambda k: (4, rows[k], 128))
        + each(lambda k: (3, cuts[k], 128))
        + each(lambda k: (3, rows[k] - cuts[k], 128))
        + each(lambda k: (4, LAST_ROWS[k], 128))
        + each(lambda k: (3, LAST_ROWS[k], 128))
        + [
            pltpu.SemaphoreType.DMA((3, 15)),
            pltpu.SemaphoreType.DMA((3, 15)),
            pltpu.SemaphoreType.DMA((9,)),
            pltpu.SemaphoreType.DMA((9,)),
            pltpu.SemaphoreType.DMA((9,)),
        ],
        compiler_params=pltpu.CompilerParams(
            collective_id=3, has_side_effects=True, vmem_limit_bytes=60 * MB
        ),
        name="weight_grads_scatter",
    )(*operands, turn1, turn2, row_id)


def finish_kernel(sums, loss_o, table_o, kern_o, up_o, down_o, scale_o, head_o):
    sources = [sums.at[pl.ds(FIRST_ROWS[k], LAST_ROWS[k])] for k in range(3)]
    for k, (out, count, each) in enumerate(((up_o, 18, 6), (down_o, 6, 18), (table_o, 6, 16))):
        for c in range(count):
            out[:, 128 * c : 128 * (c + 1)] = sources[k][each * c : each * (c + 1), :]
        start, blocks = HEAD_BLOCKS[k]
        for c in range(blocks):
            rows = count * each + 6 * c
            values = sources[k][rows : rows + 6, :]
            if start + c < 8:
                head_o[:, 128 * (start + c) : 128 * (start + c + 1)] = values
            else:
                head_o[:, 1024:1026] = values[:, 0:2]
                tail = jnp.transpose(jnp.concatenate([values, jnp.zeros((122, 128), F32)], axis=0))
                kern_o[...] = tail[2:9, 0:6]
                scale_o[...] = tail[9:10, 0:6]
                pieces = values[0:1, 10:14]
                loss_o[...] = jnp.sum(pieces, axis=1, keepdims=True) * (0.5 / CLIPS)


def finish_call(sums):
    loss, table, kern, up, down, scale, head = pl.pallas_call(
        finish_kernel,
        out_shape=[
            full(1, 1), full(16, D), full(7, 6), full(6, FF), full(18, D), full(1, 6), full(6, 1026),
        ],
        in_specs=[spec(pltpu.VMEM)],
        out_specs=[spec(pltpu.VMEM)] * 7,
        name="finish",
    )(sums)
    return loss.reshape(()), table, kern, up, down, scale.reshape(6), head


def body(
    code_ids, code_table, kernel, up_weight, down_weight, layer_scale, head_weight, target, loss_scale
):
    syn, a1, a2, win = make_constants()
    pick_n, pick_h, pick_k, turn1, turn2, row_id = make_orders()
    ids = jnp.swapaxes(code_ids, 1, 2).reshape(2, OWN)
    head_t = head_weight.T
    left_t, right_t, left_i, right_i = halo_call(target, ids)
    *saved, stat = forward_call(
        (target, left_t, right_t, ids, left_i, right_i, kernel, layer_scale, win),
        (code_table, up_weight, down_weight, head_t, syn, a1, a2),
    )
    operands = backward_call(
        (kernel, layer_scale, win, stat_call(stat), loss_scale.reshape(1, 1)),
        saved,
        (a1, a2, syn, head_t, down_weight, up_weight, pick_n, pick_h, pick_k),
    )
    return finish_call(scatter_call([*operands, ids], turn1, turn2, row_id))


def solution(mesh):
    in_specs = (P("dp", "tm", None), P(), P(), P(), P(), P(), P(), P("dp", "tm"), P())
    out_specs = (
        P(),
        P(("dp", "tm"), None),
        P(None, ("dp", "tm")),
        P(("dp", "tm"), None),
        P(("dp", "tm"), None),
        P(("dp", "tm")),
        P(("dp", "tm"), None),
    )
    return jax.shard_map(body, mesh=mesh, in_specs=in_specs, out_specs=out_specs, check_vma=False)
```

```python
import jax
import jax.numpy as jnp
import ml_dtypes
import numpy as np
from jax import lax
from jax.experimental import pallas as pl
from jax.experimental.pallas import tpu as pltpu
from jax.sharding import PartitionSpec as P

F32, BF16 = jnp.float32, jnp.bfloat16
MESH = pl.DeviceIdType.MESH
D, FF = 768, 2304
HOP, NFFT = 256, 1024
FRAMES, OWN, HALO = 1024, 128, 16
ROWS = OWN + 2 * HALO
CHUNKS1, CHUNKS2 = 5, 3
WIDE1, WIDE2 = CHUNKS1 * 256, CHUNKS2 * 256
CLIPS = 16
MB = 1 << 20
ORDERS = ("xyz", "yzx", "zxy")
HEAD_BLOCKS = ((0, 2), (2, 3), (5, 4))
PART_ROWS = (18 * 24 + 2 * 24, 6 * 72 + 3 * 24, 6 * 64 + 4 * 24)


def bf(array):
    return np.asarray(array, np.float32).astype(ml_dtypes.bfloat16)


def hann(length):
    return 0.5 - 0.5 * np.cos(2.0 * np.pi * np.arange(length) / length)


def angles(length):
    product = np.arange(length // 2 + 1)[:, None] * np.arange(length)[None, :] % length
    return 2.0 * np.pi * product / length


def interleave(real, imag, chunks):
    bins, width = real.shape
    out = np.zeros((chunks, 2, 128, width), np.float64)
    for half, part in enumerate((real, imag)):
        padded = np.zeros((chunks * 128, width), np.float64)
        padded[:bins] = part
        out[:, half] = padded.reshape(chunks, 128, width)
    return out.reshape(chunks * 256, width)


def make_constants():
    ang = angles(NFFT)
    bins = np.arange(NFFT // 2 + 1)
    factor = np.where((bins == 0) | (bins == NFFT // 2), 1.0, 2.0)[:, None] / NFFT
    window = hann(NFFT)[None, :]
    synthesis = bf(interleave(factor * np.cos(ang) * window, -factor * np.sin(ang) * window, CHUNKS1))
    analysis1 = bf(interleave(np.cos(ang), -np.sin(ang), CHUNKS1).T)
    ang = angles(NFFT // 2)
    analysis2 = bf(interleave(np.cos(ang), -np.sin(ang), CHUNKS2).T)
    win = np.zeros((8, NFFT), np.float32)
    win[0] = hann(NFFT)
    win[1] = hann(NFFT) ** 2
    win[2, : NFFT // 2] = hann(NFFT // 2)
    return synthesis, analysis1, analysis2, win


def device_index(x, y, z, core):
    return ((y * 2 + z // 2) * 2 + core) * 8 + x * 2 + z % 2


def shard_order(order, core):
    places = []
    for a in range(4):
        for b in range(4):
            for c in range(4):
                at = dict(zip(order, (a, b, c)))
                places.append(device_index(at["x"], at["y"], at["z"], core))
    return np.array(places)


def columns_of(order, core, each):
    return (shard_order(order, core)[:, None] * each + np.arange(each)[None, :]).reshape(-1)


def one_hot_columns(sources, size):
    out = np.zeros((size, sources.size), np.float32)
    out[sources, np.arange(sources.size)] = 1.0
    return bf(out)


def make_orders():
    pick_n = np.stack([one_hot_columns(columns_of(ORDERS[0], c, 6), D) for c in (0, 1)])
    half = [columns_of(ORDERS[1], c, 18)[: 4 * 4 * 2 * 18] for c in (0, 1)]
    pick_h = np.stack([one_hot_columns(h, FF // 2) for h in half])
    pick_k = np.stack([one_hot_columns(columns_of(ORDERS[2], c, 6), D) for c in (0, 1)])
    first = columns_of(ORDERS[0], 0, 6)
    where = {col: i for i, col in enumerate(first)}
    turns = []
    for k in (1, 2):
        sources = np.array([where[col] for col in columns_of(ORDERS[k], 0, 6)])
        turns.append(one_hot_columns(sources, 384))
    row_id = columns_of(ORDERS[2], 0, 16).astype(np.int32)[:, None]
    return pick_n, pick_h, pick_k, turns[0], turns[1], row_id


def mm(a, b):
    return jnp.dot(a, b, preferred_element_type=F32)


def mm_bt(a, b):
    return lax.dot_general(a, b, (((1,), (1,)), ((), ())), preferred_element_type=F32)


def mm_at(a, b):
    return lax.dot_general(a, b, (((0,), (0,)), ((), ())), preferred_element_type=F32)


def shift(values, by):
    by = by % values.shape[0]
    return values if by == 0 else pltpu.roll(values, by, 0)


def norm(values):
    centre = values - jnp.mean(values, axis=-1, keepdims=True)
    rstd = lax.rsqrt(jnp.mean(centre * centre, axis=-1, keepdims=True) + 1e-6)
    return centre * rstd, rstd


def norm_back(grad, y, rstd):
    mean_g = jnp.mean(grad, axis=-1, keepdims=True)
    mean_gy = jnp.mean(grad * y, axis=-1, keepdims=True)
    return rstd * (grad - mean_g - y * mean_gy)


def frame_places():
    first = lax.axis_index("tm") * OWN - HALO
    return (lax.broadcasted_iota(jnp.int32, (ROWS, 1), 0) + first).astype(F32)


def sin_cos(x):
    turns = jnp.round(x * 0.6366197723675814)
    r = x - turns * 1.5703125
    r = r - turns * 4.837512969970703125e-4
    r = r - turns * 7.549789954891882e-8
    z = r * r
    sine = r + r * z * (-1.6666654611e-1 + z * (8.3321608736e-3 + z * -1.9515295891e-4))
    cosine = (4.166664568298827e-2 + z * (-1.388731625493765e-3 + z * 2.443315711809948e-5)) * (z * z)
    cosine = cosine - 0.5 * z + 1.0
    quarter = turns.astype(jnp.int32)
    odd = (quarter & 1) == 1
    first, second = jnp.where(odd, cosine, sine), jnp.where(odd, sine, cosine)
    first = jnp.where((quarter & 2) == 2, -first, first)
    second = jnp.where(((quarter + 1) & 2) == 2, -second, second)
    return first, second


def inside(places):
    return (places >= 0.0) & (places < float(FRAMES))


def envelope(places, win):
    total = jnp.zeros((ROWS, HOP), F32)
    for p in range(4):
        total = total + jnp.where(inside(places + float(2 - p)), win[1:2, HOP * p : HOP * (p + 1)], 0.0)
    return jnp.where(inside(places), total, 1.0)


def spec(space):
    return pl.BlockSpec(memory_space=space)


def full(*shape, dtype=F32):
    return jax.ShapeDtypeStruct(shape, dtype)


def ids_column(ids):
    padded = jnp.concatenate([ids.astype(F32), jnp.zeros((126, OWN), F32)], axis=0)
    return jnp.transpose(padded)[:, :2]


OPERANDS = (
    full(OWN, 384), full(OWN, 1152), full(OWN, 384), full(OWN, FF), full(OWN, D),
    full(OWN, 1152), full(OWN, D), full(384, 128),
)
PICKED = (True, True, True, False, False, False, False, True)
IDS = full(2, OWN, dtype=jnp.int32)
SAVED = (
    full(ROWS, D), full(ROWS, 128), full(ROWS, D), full(ROWS, FF),
    full(ROWS, D), full(ROWS, D), full(ROWS, CHUNKS1 * 128), full(ROWS, CHUNKS1 * 128),
    full(ROWS, WIDE1), full(ROWS, WIDE1), full(2 * ROWS, WIDE2), full(2 * ROWS, WIDE2),
)


def vmem(shapes):
    return [pltpu.VMEM(a.shape, a.dtype) for a in shapes]


def step_kernel(target, ids, kern, scale_i, win, loss_scale, *refs):
    big_h, refs = refs[:10], refs[10:]
    here_h, refs = refs[:8], refs[8:]
    there_h, refs = refs[:9], refs[9:]
    big_v, refs = refs[:10], refs[10:]
    (table_v, up_v, down_v, head_v, syn_v, a1_v, a2_v, pick_n, pick_h, pick_k) = big_v
    (sin_o, rstd_o, y1_o, gp_o, down_o, y2_o, re_o, im_o, d1_o, q1_o, d2_o, q2_o) = refs[:12]
    refs = refs[12:]
    kept, refs = refs[:8], refs[8:]
    (nrm_o, hid_o, onm_o, dup_o, ddn_o, dhd_o, dem_o, kg_o) = kept
    (left_t, right_t, left_i, right_i, goal, codes, hid_v, head_s, spec_v, seg1, seg2), refs = (
        refs[:11], refs[11:],
    )
    (stat_o, slots, dfr, dphase, dhead, dup, small), refs = refs[:7], refs[7:]
    sems, halo_send, halo_recv, stat_send, stat_recv, pair_send, pair_recv, save_sems = refs

    dp, tm = lax.axis_index("dp"), lax.axis_index("tm")
    core = lax.rem(dp, 2)
    partner = {"dp": dp + 1 - 2 * core, "tm": tm}
    others = [{"dp": dp, "tm": lax.rem(tm + j, 8)} for j in range(1, 8)]
    barrier = pltpu.get_barrier_semaphore()
    for there in others + [partner]:
        pl.semaphore_signal(barrier, inc=1, device_id=there, device_id_type=MESH)
    copies = [pltpu.make_async_copy(h, v, sems.at[i]) for i, (h, v) in enumerate(zip(big_h, big_v))]
    for copy in copies:
        copy.start()

    def remote(src, dst, send, recv, there):
        copy = pltpu.make_async_remote_copy(
            src_ref=src, dst_ref=dst, send_sem=send, recv_sem=recv,
            device_id=there, device_id_type=MESH,
        )
        copy.start()
        return copy

    edge = HALO * HOP
    right, left = others[0], others[6]
    pl.semaphore_wait(barrier, 8)
    halo = [
        remote(src, dst, halo_send.at[i], halo_recv.at[i], there)
        for i, (src, dst, there) in enumerate(
            (
                (ids, left_i, right),
                (ids, right_i, left),
                (target.at[:, pl.ds(OWN * HOP - edge, edge)], left_t, right),
                (target.at[:, pl.ds(0, edge)], right_t, left),
            )
        )
    ]
    pairs = [remote(ids, there_h[8], pair_send.at[8], pair_recv.at[8], partner)]
    saves = [
        pltpu.make_async_copy(v.at[core] if p else v, h, save_sems.at[i])
        for i, (v, h, p) in enumerate(zip(kept, here_h, PICKED))
    ]

    def give(i):
        saves[i].start()
        source = kept[i].at[1 - core] if PICKED[i] else kept[i]
        pairs.append(remote(source, there_h[i], pair_send.at[i], pair_recv.at[i], partner))

    scale = scale_i[...].reshape(1, D)
    codes[HALO : HALO + OWN, :] = ids_column(ids[...])
    for source, first, count in (
        (target, HALO, OWN), (left_t, 0, HALO), (right_t, HALO + OWN, HALO),
    ):
        if source is left_t:
            for copy in halo:
                copy.wait_recv()
        for r in range(count):
            goal[first + r : first + r + 1, :] = source[:, HOP * r : HOP * (r + 1)]
    codes[0:HALO, :] = ids_column(left_i[...])[OWN - HALO :]
    codes[HALO + OWN :, :] = ids_column(right_i[...])[:HALO]
    places = frame_places()
    valid = inside(places)
    lane = lax.broadcasted_iota(jnp.int32, (ROWS, 2 * FRAMES), 1).astype(F32)
    hot = (lane == codes[:, 0:1]) | (lane == codes[:, 1:2] + 1024.0)
    hot = jnp.where(hot, 1.0, 0.0).astype(BF16)
    copies[0].wait()
    y0, rstd0 = norm(mm(hot, table_v[...]))
    y0 = jnp.where(valid, y0, 0.0)
    sin_o[...] = y0
    mixture = kern[0:1, :] * shift(y0, 3)
    for k in range(1, 7):
        mixture = mixture + kern[k : k + 1, :] * shift(y0, 3 - k)
    y1, rstd1 = norm(mixture)
    y1_o[...] = y1
    normed = y1.astype(BF16)
    copies[1].wait()
    for c in range(FF // 256):
        at = slice(256 * c, 256 * (c + 1))
        up = mm(normed, up_v[:, at])
        cdf = 0.5 * (1.0 + lax.erf(up * 0.7071067811865476))
        hid_v[:, at] = (up * cdf).astype(BF16)
        gp_o[:, at] = cdf + up * (0.3989422804014327 * jnp.exp(-0.5 * up * up))
    copies[2].wait()
    down = mm(hid_v[...], down_v[...])
    down_o[...] = down
    y2, rstd2 = norm(y0 + scale * down)
    y2_o[...] = y2
    places128 = lax.broadcasted_iota(jnp.int32, (ROWS, 128), 1)
    rstd_o[...] = jnp.where(places128 == 0, rstd0, jnp.where(places128 == 1, rstd1, rstd2))
    onorm = y2.astype(BF16)
    copies[3].wait()
    head_s[:, 1024:] = jnp.zeros((ROWS, 128), F32)
    for c in range(4):
        head_s[:, 256 * c : 256 * (c + 1)] = mm_bt(onorm, head_v[256 * c : 256 * (c + 1), :])
    head_s[:, 1024:1026] = mm_bt(onorm, head_v[1024:1026, :])
    phases = pltpu.roll(head_s[:, 512:], CHUNKS1 * 128 - 1, 1)
    for c in range(CHUNKS1):
        logmag = head_s[:, 128 * c : 128 * (c + 1)]
        if c == 4:
            logmag = jnp.where(places128 == 0, logmag, 0.0)
        mag = jnp.exp(logmag)
        phase = phases[:, 128 * c : 128 * (c + 1)]
        sine, cosine = sin_cos(phase)
        re, im = mag * cosine, mag * sine
        re_o[:, 128 * c : 128 * (c + 1)] = re
        im_o[:, 128 * c : 128 * (c + 1)] = im
        spec_v[:, 256 * c : 256 * c + 128] = re.astype(BF16)
        spec_v[:, 256 * c + 128 : 256 * (c + 1)] = im.astype(BF16)
    copies[4].wait()
    pred = jnp.zeros((ROWS, HOP), F32)
    for p in range(4):
        piece = jnp.where(valid, mm(spec_v[...], syn_v[:, HOP * p : HOP * (p + 1)]), 0.0)
        pred = pred + shift(piece, p - 2)
    pred = jnp.where(valid, pred / envelope(places, win), 0.0)
    for s, x in enumerate((pred, jnp.where(valid, goal[...], 0.0))):
        r1 = slice(ROWS * s, ROWS * (s + 1))
        for p in range(4):
            at = slice(HOP * p, HOP * (p + 1))
            seg1[r1, at] = (shift(x, 2 - p) * win[0:1, at]).astype(BF16)
        even = slice(2 * ROWS * s, 2 * ROWS * s + ROWS)
        odd = slice(2 * ROWS * s + ROWS, 2 * ROWS * (s + 1))
        before, after = shift(x, 1), shift(x, -1)
        seg2[even, 0:256] = (before * win[2:3, 0:256]).astype(BF16)
        seg2[even, 256:512] = (x * win[2:3, 256:512]).astype(BF16)
        seg2[odd, 0:128] = (before[:, 128:] * win[2:3, 0:128]).astype(BF16)
        seg2[odd, 128:384] = (x * win[2:3, 128:384]).astype(BF16)
        seg2[odd, 384:512] = (after[:, :128] * win[2:3, 384:512]).astype(BF16)
    own = slice(HALO, HALO + OWN)
    for level in range(2):
        seg, table, chunks = ((seg1, a1_v, CHUNKS1), (seg2, a2_v, CHUNKS2))[level]
        d_o, q_o = ((d1_o, q1_o), (d2_o, q2_o))[level]
        copies[5 + level].wait()
        sums = [jnp.zeros((OWN, 128), F32) for _ in range(3)]
        for c in range(chunks):
            for sub in range(level + 1):
                rows_p = slice(ROWS * sub, ROWS * (sub + 1))
                base = ROWS * (level + 1)
                rows_g = slice(base + ROWS * sub, base + ROWS * (sub + 1))
                weights = table[:, 256 * c : 256 * (c + 1)]
                sp, sg = mm(seg[rows_p, :], weights), mm(seg[rows_g, :], weights)
                diff = sp - sg
                pr, pi, gr, gi = sp[:, :128], sp[:, 128:], sg[:, :128], sg[:, 128:]
                power_p, power_g = pr * pr + pi * pi, gr * gr + gi * gi
                gap = jnp.log1p(power_p) - jnp.log1p(power_g)
                slope = jnp.where(valid, 4.0 * gap / (1.0 + power_p), 0.0)
                d_o[rows_p, 256 * c : 256 * (c + 1)] = jnp.where(valid, diff, 0.0)
                q_o[rows_p, 256 * c : 256 * c + 128] = slope * pr
                q_o[rows_p, 256 * c + 128 : 256 * (c + 1)] = slope * pi
                dr, di = diff[own, :128], diff[own, 128:]
                sums[0] = sums[0] + dr * dr + di * di
                sums[1] = sums[1] + power_g[own]
                sums[2] = sums[2] + gap[own] * gap[own]
        for i in range(3):
            total = jnp.sum(jnp.sum(sums[i], axis=0, keepdims=True), axis=1, keepdims=True)
            stat_o[3 * level + i : 3 * level + i + 1, :] = jnp.broadcast_to(total, (1, 128))
    stat_o[6:8, :] = jnp.zeros((2, 128), F32)
    shares = [
        remote(stat_o, slots.at[tm], stat_send.at[j], stat_recv.at[j], there)
        for j, there in enumerate(others)
    ]
    slots[tm] = stat_o[...]

    copies[7].wait()
    copies[8].wait()
    normed = y1_o[own, :].astype(BF16)
    onorm = y2_o[own, :].astype(BF16)
    for c in range(2):
        nrm_o[c] = mm(normed, pick_n[c])
        onm_o[c] = mm(onorm, pick_n[c])
        for h in range(2):
            out = slice(576 * h, 576 * (h + 1))
            hid_o[c, :, out] = mm(hid_v[own, 1152 * h : 1152 * (h + 1)], pick_h[c])
    for i in (0, 2, 1):
        give(i)

    for share in shares:
        share.wait_recv()
    total = slots[0]
    for j in range(1, 8):
        total = total + slots[j]

    factor = loss_scale[...] * (0.5 / CLIPS)
    loss = jnp.zeros((1, 1), F32)
    cots = []
    for level in range(2):
        count = ((FRAMES * 513), (2 * FRAMES * 257))[level]
        sum_a = total[3 * level : 3 * level + 1, 0:1]
        sum_b = total[3 * level + 1 : 3 * level + 2, 0:1]
        sum_g = total[3 * level + 2 : 3 * level + 3, 0:1]
        root_a, root_b = jnp.sqrt(sum_a + 1e-6), jnp.sqrt(sum_b + 1e-6)
        loss = loss + root_a / root_b + sum_g * (1.0 / count)
        cots.append((factor / (root_a * root_b), factor * (1.0 / count)))
    loss = jnp.where(lax.axis_index("tm") == 0, loss, 0.0)

    dx = jnp.zeros((ROWS, HOP), F32)
    ds1 = (cots[0][0] * d1_o[...] + cots[0][1] * q1_o[...]).astype(BF16)
    for p in range(4):
        at = slice(HOP * p, HOP * (p + 1))
        piece = mm_bt(ds1, a1_v[at, :]).astype(BF16).astype(F32) * win[0:1, at]
        dx = dx + shift(piece, p - 2)
    ds2 = (cots[1][0] * d2_o[...] + cots[1][1] * q2_o[...]).astype(BF16)
    dseg = mm_bt(ds2, a2_v[...]).astype(BF16).astype(F32) * win[2:3, : NFFT // 2]
    even, odd = dseg[:ROWS], dseg[ROWS:]
    dx = dx + shift(even[:, :256], -1) + even[:, 256:] + odd[:, 128:384]
    dx = dx + jnp.concatenate([shift(odd[:, 384:], 1), shift(odd[:, :128], -1)], axis=1)
    dx = jnp.where(valid, dx / envelope(places, win), 0.0)
    for p in range(4):
        piece = jnp.where(valid, shift(dx, 2 - p), 0.0)
        dfr[:, HOP * p : HOP * (p + 1)] = piece.astype(BF16)

    for c in range(CHUNKS1):
        dsp = mm_bt(dfr[...], syn_v[256 * c : 256 * (c + 1), :]).astype(BF16).astype(F32)
        dre, dim = dsp[:, :128], dsp[:, 128:]
        re, im = re_o[:, 128 * c : 128 * (c + 1)], im_o[:, 128 * c : 128 * (c + 1)]
        dlog, dph = dre * re + dim * im, dim * re - dre * im
        if c < 4:
            dhead[:, 128 * c : 128 * (c + 1)] = dlog.astype(BF16)
        dphase[:, 128 * c : 128 * (c + 1)] = dph
    moved = pltpu.roll(dphase[...], 1, 1)
    dhead[:, 512:640] = (moved[:, :128] + dlog).astype(BF16)
    dhead[:, 640:] = moved[:, 128:].astype(BF16)
    dhd_o[...] = dhead[own, :].astype(F32)
    give(5)
    don = mm(dhead[:, :1026], head_v[...]).astype(BF16).astype(F32)
    dstream = norm_back(don, y2_o[...], rstd_o[:, 2:3])

    scale_grad = jnp.sum(dstream[own] * down_o[own, :], axis=0, keepdims=True)
    ddn = (scale * dstream).astype(BF16)
    ddn_o[...] = ddn[own].astype(F32)
    give(4)
    for c in range(FF // 256):
        at = slice(256 * c, 256 * (c + 1))
        dh = mm_bt(ddn, down_v[at, :]).astype(BF16).astype(F32)
        dup[:, at] = (dh * gp_o[:, at]).astype(BF16)
    dup_o[...] = dup[own, :].astype(F32)
    give(3)
    dnorm = mm_bt(dup[...], up_v[...]).astype(BF16).astype(F32)
    dmix = norm_back(dnorm, y1_o[...], rstd_o[:, 1:2])
    dmix = jnp.where(valid, dmix, 0.0)
    y0 = sin_o[...]
    dsin = dstream
    small[...] = jnp.zeros((128, D), F32)
    for k in range(7):
        dsin = dsin + kern[k : k + 1, :] * shift(dmix, k - 3)
        taps = dmix * shift(y0, 3 - k)
        small[2 + k : 3 + k, :] = jnp.sum(taps[own], axis=0, keepdims=True)
    demb = norm_back(dsin, y0, rstd_o[:, 0:1])
    dem_o[...] = demb[own].astype(BF16).astype(F32)
    give(6)

    small[9:10, :] = scale_grad
    rest = loss
    for i, grid in enumerate((65536.0, 1.0, 1.0 / 65536.0, 1.0 / 65536.0 / 65536.0)):
        piece = jnp.floor(rest * (1.0 / grid)) * grid
        rest = rest - piece
        small[10 + i : 11 + i, :] = jnp.broadcast_to(piece, (1, D))

    copies[9].wait()
    small0 = small[...].astype(BF16)
    left = small[...] - small0.astype(F32)
    small1 = left.astype(BF16)
    small2 = (left - small1.astype(F32)).astype(BF16)
    for c in range(2):
        kg_o[c] = sum(
            lax.dot_general(pick_k[c], s, (((0,), (1,)), ((), ())), preferred_element_type=F32)
            for s in (small0, small1, small2)
        )
    give(7)
    for i in range(8):
        saves[i].wait()
    for copy in pairs:
        copy.wait()
    for copy in halo + shares:
        copy.wait_send()


def step_call(small, big):
    wide = [full(*((2,) if p else ()), *a.shape) for a, p in zip(OPERANDS, PICKED)]
    edge = full(1, HALO * HOP)
    return pl.pallas_call(
        step_kernel,
        out_shape=[*OPERANDS, *OPERANDS, IDS],
        in_specs=[spec(pltpu.VMEM)] * len(small) + [spec(pl.ANY)] * len(big),
        out_specs=[spec(pl.ANY)] * 17,
        scratch_shapes=vmem(big)
        + vmem(SAVED)
        + vmem(wide)
        + vmem([edge, edge, IDS, IDS])
        + [
            pltpu.VMEM((ROWS, HOP), F32),
            pltpu.VMEM((ROWS, 2), F32),
            pltpu.VMEM((ROWS, FF), BF16),
            pltpu.VMEM((ROWS, 1152), F32),
            pltpu.VMEM((ROWS, WIDE1), BF16),
            pltpu.VMEM((2 * ROWS, NFFT), BF16),
            pltpu.VMEM((4 * ROWS, NFFT // 2), BF16),
            pltpu.VMEM((8, 128), F32),
            pltpu.VMEM((8, 8, 128), F32),
            pltpu.VMEM((ROWS, NFFT), BF16),
            pltpu.VMEM((ROWS, CHUNKS1 * 128), F32),
            pltpu.VMEM((ROWS, 1152), BF16),
            pltpu.VMEM((ROWS, FF), BF16),
            pltpu.VMEM((128, D), F32),
        ]
        + [pltpu.SemaphoreType.DMA((n,)) for n in (len(big), 4, 4, 7, 7, 9, 9, 8)],
        compiler_params=pltpu.CompilerParams(
            collective_id=0, has_side_effects=True, vmem_limit_bytes=60 * MB
        ),
        name="forward_backward",
    )(*small, *big)


LAST_ROWS = (120, 128, 120)
FIRST_ROWS = (0, 120, 248)

def put(out, first, values, rows):
    for block in range(values.shape[1] // 128):
        part = values[:, 128 * block : 128 * (block + 1)].reshape(4, 4, rows, 128)
        out[:, :, first + rows * block : first + rows * (block + 1), :] = part


def halves_of(rows):
    upper = (rows // 2 + 7) // 8 * 8
    return pl.ds(0, upper), pl.ds(upper, rows - upper)


def scatter_kernel(*refs):
    ins, (turn1, turn2, row_id), out_o, scratch = refs[0:18], refs[18:21], refs[21], refs[22:]
    here, there = scratch[0:9], scratch[9:18]
    parts, through, from_left, from_right = (scratch[18 + 3 * i : 21 + 3 * i] for i in range(4))
    got2a, got2b, last, got3 = (scratch[30 + 3 * i : 33 + 3 * i] for i in range(4))
    send, recv, load = scratch[42:]

    dp, tm = lax.axis_index("dp"), lax.axis_index("tm")
    at = {"x": tm // 2, "y": dp // 4, "z": lax.rem(dp // 2, 2) * 2 + lax.rem(tm, 2)}
    core = lax.rem(dp, 2)

    def device(axis, by):
        to = dict(at)
        to[axis] = lax.rem(at[axis] + by, 4)
        return {
            "dp": (to["y"] * 2 + to["z"] // 2) * 2 + core,
            "tm": to["x"] * 2 + lax.rem(to["z"], 2),
        }

    barrier = pltpu.get_barrier_semaphore()
    for axis in "xyz":
        for by in (1, 2, 3):
            pl.semaphore_signal(barrier, inc=1, device_id=device(axis, by), device_id_type=MESH)
    loads = [
        pltpu.make_async_copy(h, v, load.at[i])
        for i, (h, v) in enumerate(zip(ins, (*here, *there)))
    ]
    for i in (0, 3, 2, 5, 1, 4, 8, 6, 7):
        loads[i].start()
        loads[i + 9].start()

    def need(*which):
        for i in which:
            loads[i].wait()
            loads[i + 9].wait()

    def both(i, cols=slice(None)):
        return jnp.concatenate([here[i][:, cols], there[i][:, cols]], axis=0).astype(BF16)

    def remote(src, dst, k, slot, axis, by):
        copy = pltpu.make_async_remote_copy(
            src_ref=src,
            dst_ref=dst,
            send_sem=send.at[k, slot],
            recv_sem=recv.at[k, slot],
            device_id=device(axis, by),
            device_id_type=MESH,
        )
        copy.start()
        return copy

    def around(axis):
        i = at[axis]
        return i, lax.rem(i + 1, 4), lax.rem(i + 2, 4), lax.rem(i + 3, 4)

    def head_part(k, first, onorm):
        start, blocks = HEAD_BLOCKS[k]
        for b in range(blocks):
            cols = slice(128 * (start + b), 128 * (start + b + 1))
            values = mm_at(onorm, both(5, cols))
            if start + b == 8:
                values = values + here[7][...] + there[7][...]
            put(parts[k], first + 24 * b, values, 24)

    low, high = pl.ds(0, 2), pl.ds(2, 2)
    sent = []

    def phase1(k):
        axis, p = ORDERS[k][0], parts[k]
        i, right, opposite, left = around(axis)
        sent.append(
            [
                remote(p.at[opposite, low], through[k].at[0], k, 0, axis, 1),
                remote(p.at[opposite, high], through[k].at[1], k, 1, axis, 3),
                remote(p.at[right, high], from_left[k].at[high], k, 2, axis, 1),
                remote(p.at[left, low], from_right[k].at[low], k, 3, axis, 3),
            ]
        )

    need(0, 3)
    normed = both(0)
    for c in range(FF // 256):
        put(parts[0], 48 * c, mm_at(normed, both(3, slice(256 * c, 256 * (c + 1)))), 24)
    need(2, 5)
    onorm = both(2)
    head_part(0, 432, onorm)
    pl.semaphore_wait(barrier, 9)
    phase1(0)
    need(1, 4)
    hidden = both(1)
    for c in range(3):
        put(parts[1], 144 * c, mm_at(hidden, both(4, slice(256 * c, 256 * (c + 1)))), 72)
    head_part(1, 432, mm(onorm, turn1[...]).astype(BF16))
    phase1(1)
    need(8, 6, 7)
    ids = jnp.concatenate([here[8][...], there[8][...]], axis=1)
    rows = row_id[...] + OWN * core
    hot = (rows == ids[0:1, :]) | (rows == ids[1:2, :] + 1024)
    hot = jnp.where(hot, 1.0, 0.0).astype(BF16)
    for c in range(3):
        put(parts[2], 128 * c, mm(hot, both(6, slice(256 * c, 256 * (c + 1)))), 64)
    head_part(2, 384, mm(onorm, turn2[...]).astype(BF16))
    phase1(2)

    for k in range(3):
        axis, p = ORDERS[k][0], parts[k]
        i, right, opposite, left = around(axis)
        sent[k][0].wait_recv()
        p[right, low] += through[k][0]
        sent[k].append(remote(p.at[right, low], from_left[k].at[low], k, 4, axis, 1))
        sent[k][1].wait_recv()
        p[left, high] += through[k][1]
        sent[k].append(remote(p.at[left, high], from_right[k].at[high], k, 5, axis, 3))
    for k in range(3):
        mine = at[ORDERS[k][0]]
        axis, p, a, b = ORDERS[k][1], parts[k], got2a[k], got2b[k]
        i, right, opposite, left = around(axis)
        upper, lower = halves_of(PART_ROWS[k])
        for j in (2, 3, 4, 5):
            sent[k][j].wait_recv()
        p[mine, opposite] += from_left[k][opposite] + from_right[k][opposite]
        sent[k].append(remote(p.at[mine, opposite, upper], a.at[0], k, 6, axis, 1))
        sent[k].append(remote(p.at[mine, opposite, lower], b.at[0], k, 7, axis, 3))
        p[mine, right] += from_left[k][right] + from_right[k][right]
        sent[k].append(remote(p.at[mine, right, lower], b.at[1], k, 8, axis, 1))
        p[mine, left] += from_left[k][left] + from_right[k][left]
        sent[k].append(remote(p.at[mine, left, upper], a.at[1], k, 9, axis, 3))
        p[mine, i] += from_left[k][i] + from_right[k][i]
    for k in range(3):
        mine = at[ORDERS[k][0]]
        axis, p, a, b = ORDERS[k][1], parts[k], got2a[k], got2b[k]
        i, right, opposite, left = around(axis)
        upper, lower = halves_of(PART_ROWS[k])
        sent[k][6].wait_recv()
        p[mine, right, upper] += a[0]
        sent[k].append(remote(p.at[mine, right, upper], a.at[2], k, 10, axis, 1))
        sent[k][7].wait_recv()
        p[mine, left, lower] += b[0]
        sent[k].append(remote(p.at[mine, left, lower], b.at[2], k, 11, axis, 3))
    for k in range(3):
        mine = at[ORDERS[k][0]]
        i = at[ORDERS[k][1]]
        p, a, b, out = parts[k], got2a[k], got2b[k], last[k]
        upper, lower = halves_of(PART_ROWS[k])
        for j in (8, 9, 10, 11):
            sent[k][j].wait_recv()
        p[mine, i, upper] += a[1] + a[2]
        p[mine, i, lower] += b[1] + b[2]
        blocks = (((18, 24), (2, 24)), ((6, 72), (3, 24)), ((6, 64), (4, 24)))[k]
        start, place = 0, 0
        for count, rows in blocks:
            each = rows // 4
            for _ in range(count):
                for d in range(4):
                    out[d, pl.ds(place, each)] = p[mine, i, pl.ds(start + d * each, each)]
                start += rows
                place += each
        if place < LAST_ROWS[k]:
            for d in range(4):
                out[d, pl.ds(place, LAST_ROWS[k] - place)] = jnp.zeros(
                    (LAST_ROWS[k] - place, 128), F32
                )
        axis = ORDERS[k][2]
        for by in (1, 2, 3):
            to = lax.rem(at[axis] + by, 4)
            sent[k].append(remote(out.at[to], got3[k].at[by - 1], k, 11 + by, axis, by))
    for k in range(3):
        for j in (12, 13, 14):
            sent[k][j].wait_recv()
        total = last[k][at[ORDERS[k][2]]] + got3[k][0] + got3[k][1] + got3[k][2]
        out_o[pl.ds(FIRST_ROWS[k], LAST_ROWS[k]), :] = total
    for k in range(3):
        for copy in sent[k]:
            copy.wait_send()


def scatter_call(operands, turn1, turn2, row_id):
    def each(make):
        return [pltpu.VMEM(make(k), F32) for k in range(3)]

    rows = PART_ROWS
    cuts = [halves_of(n)[0].size for n in rows]
    return pl.pallas_call(
        scatter_kernel,
        out_shape=full(sum(LAST_ROWS), 128),
        in_specs=[spec(pl.ANY)] * 18 + [spec(pltpu.VMEM)] * 3,
        out_specs=spec(pltpu.VMEM),
        scratch_shapes=vmem([*OPERANDS, IDS]) * 2
        + each(lambda k: (4, 4, rows[k], 128))
        + each(lambda k: (2, 2, rows[k], 128))
        + each(lambda k: (4, rows[k], 128))
        + each(lambda k: (4, rows[k], 128))
        + each(lambda k: (3, cuts[k], 128))
        + each(lambda k: (3, rows[k] - cuts[k], 128))
        + each(lambda k: (4, LAST_ROWS[k], 128))
        + each(lambda k: (3, LAST_ROWS[k], 128))
        + [
            pltpu.SemaphoreType.DMA((3, 15)),
            pltpu.SemaphoreType.DMA((3, 15)),
            pltpu.SemaphoreType.DMA((18,)),
        ],
        compiler_params=pltpu.CompilerParams(
            collective_id=3, has_side_effects=True, vmem_limit_bytes=60 * MB
        ),
        name="weight_grads_scatter",
    )(*operands, turn1, turn2, row_id)


def finish_kernel(sums, loss_o, table_o, kern_o, up_o, down_o, scale_o, head_o):
    sources = [sums.at[pl.ds(FIRST_ROWS[k], LAST_ROWS[k])] for k in range(3)]
    for k, (out, count, each) in enumerate(((up_o, 18, 6), (down_o, 6, 18), (table_o, 6, 16))):
        for c in range(count):
            out[:, 128 * c : 128 * (c + 1)] = sources[k][each * c : each * (c + 1), :]
        start, blocks = HEAD_BLOCKS[k]
        for c in range(blocks):
            rows = count * each + 6 * c
            values = sources[k][rows : rows + 6, :]
            if start + c < 8:
                head_o[:, 128 * (start + c) : 128 * (start + c + 1)] = values
            else:
                head_o[:, 1024:1026] = values[:, 0:2]
                tail = jnp.transpose(jnp.concatenate([values, jnp.zeros((122, 128), F32)], axis=0))
                kern_o[...] = tail[2:9, 0:6]
                scale_o[...] = tail[9:10, 0:6]
                pieces = values[0:1, 10:14]
                loss_o[...] = jnp.sum(pieces, axis=1, keepdims=True) * (0.5 / CLIPS)


def finish_call(sums):
    loss, table, kern, up, down, scale, head = pl.pallas_call(
        finish_kernel,
        out_shape=[
            full(1, 1), full(16, D), full(7, 6), full(6, FF), full(18, D), full(1, 6), full(6, 1026),
        ],
        in_specs=[spec(pltpu.VMEM)],
        out_specs=[spec(pltpu.VMEM)] * 7,
        name="finish",
    )(sums)
    return loss.reshape(()), table, kern, up, down, scale.reshape(6), head


def body(
    code_ids, code_table, kernel, up_weight, down_weight, layer_scale, head_weight, target, loss_scale
):
    syn, a1, a2, win = make_constants()
    pick_n, pick_h, pick_k, turn1, turn2, row_id = make_orders()
    ids = jnp.swapaxes(code_ids, 1, 2).reshape(2, OWN)
    head_t = head_weight.T
    operands = step_call(
        (target, ids, kernel, layer_scale, win, loss_scale.reshape(1, 1)),
        (
            code_table, up_weight, down_weight, head_t, syn, a1, a2, pick_n, pick_h, pick_k,
        ),
    )
    operands = [*operands[:8], ids, *operands[8:]]
    return finish_call(scatter_call(operands, turn1, turn2, row_id))


def solution(mesh):
    in_specs = (P("dp", "tm", None), P(), P(), P(), P(), P(), P(), P("dp", "tm"), P())
    out_specs = (
        P(),
        P(("dp", "tm"), None),
        P(None, ("dp", "tm")),
        P(("dp", "tm"), None),
        P(("dp", "tm"), None),
        P(("dp", "tm")),
        P(("dp", "tm"), None),
    )
    return jax.shard_map(body, mesh=mesh, in_specs=in_specs, out_specs=out_specs, check_vma=False)
```

```python
import jax
import jax.numpy as jnp
import ml_dtypes
import numpy as np
from jax import lax
from jax.experimental import pallas as pl
from jax.experimental.pallas import tpu as pltpu
from jax.sharding import PartitionSpec as P

F32, BF16 = jnp.float32, jnp.bfloat16
MESH = pl.DeviceIdType.MESH
D, FF = 768, 2304
HOP, NFFT = 256, 1024
FRAMES, OWN, HALO = 1024, 128, 16
ROWS = OWN + 2 * HALO
CHUNKS1, CHUNKS2 = 5, 3
WIDE1, WIDE2 = CHUNKS1 * 256, CHUNKS2 * 256
CLIPS = 16
MB = 1 << 20
ORDERS = ("xyz", "yzx", "zxy")
HEAD_BLOCKS = ((0, 3), (3, 2), (5, 4))
MAIN_BLOCKS = ((18, 24), (6, 72), (6, 64))
RANGES = (((0, 72), (72, 504)), ((0, 480),), ((0, 72), (72, 480)))
PART_ROWS = (504, 480, 480)
LAST_ROWS = (128, 120, 120)
FIRST_ROWS = (0, 128, 248)


def bf(array):
    return np.asarray(array, np.float32).astype(ml_dtypes.bfloat16)


def hann(length):
    return 0.5 - 0.5 * np.cos(2.0 * np.pi * np.arange(length) / length)


def angles(length):
    product = np.arange(length // 2 + 1)[:, None] * np.arange(length)[None, :] % length
    return 2.0 * np.pi * product / length


def interleave(real, imag, chunks):
    bins, width = real.shape
    out = np.zeros((chunks, 2, 128, width), np.float64)
    for half, part in enumerate((real, imag)):
        padded = np.zeros((chunks * 128, width), np.float64)
        padded[:bins] = part
        out[:, half] = padded.reshape(chunks, 128, width)
    return out.reshape(chunks * 256, width)


def make_constants():
    ang = angles(NFFT)
    bins = np.arange(NFFT // 2 + 1)
    factor = np.where((bins == 0) | (bins == NFFT // 2), 1.0, 2.0)[:, None] / NFFT
    window = hann(NFFT)[None, :]
    synthesis = bf(interleave(factor * np.cos(ang) * window, -factor * np.sin(ang) * window, CHUNKS1))
    analysis1 = bf(interleave(np.cos(ang), -np.sin(ang), CHUNKS1).T)
    ang = angles(NFFT // 2)
    analysis2 = bf(interleave(np.cos(ang), -np.sin(ang), CHUNKS2).T)
    win = np.zeros((8, NFFT), np.float32)
    win[0] = hann(NFFT)
    win[1] = hann(NFFT) ** 2
    win[2, : NFFT // 2] = hann(NFFT // 2)
    return synthesis, analysis1, analysis2, win


def device_index(x, y, z, core):
    return ((y * 2 + z // 2) * 2 + core) * 8 + x * 2 + z % 2


def shard_order(order, core):
    places = []
    for a in range(4):
        for b in range(4):
            for c in range(4):
                at = dict(zip(order, (a, b, c)))
                places.append(device_index(at["x"], at["y"], at["z"], core))
    return np.array(places)


def columns_of(order, core, each):
    return (shard_order(order, core)[:, None] * each + np.arange(each)[None, :]).reshape(-1)


def one_hot_columns(sources, size):
    out = np.zeros((size, sources.size), np.float32)
    out[sources, np.arange(sources.size)] = 1.0
    return bf(out)


def make_orders():
    pick_n = np.stack([one_hot_columns(columns_of(ORDERS[0], c, 6), D).T for c in (0, 1)])
    half = [columns_of(ORDERS[1], c, 18)[: 4 * 4 * 2 * 18] for c in (0, 1)]
    pick_h = np.stack([one_hot_columns(h, FF // 2).T for h in half])
    pick_k = np.stack([one_hot_columns(columns_of(ORDERS[2], c, 6), D).T for c in (0, 1)])
    first = columns_of(ORDERS[0], 0, 6)
    where = {col: i for i, col in enumerate(first)}
    turns = []
    for k in (1, 2):
        sources = np.array([where[col] for col in columns_of(ORDERS[k], 0, 6)])
        turns.append(one_hot_columns(sources, 384).T)
    row_id = columns_of(ORDERS[2], 0, 16).astype(np.int32)[:, None]
    return pick_n, pick_h, pick_k, turns[0], turns[1], row_id


def mm(a, b):
    return jnp.dot(a, b, preferred_element_type=F32)


def mm_bt(a, b):
    return lax.dot_general(a, b, (((1,), (1,)), ((), ())), preferred_element_type=F32)


def mm_at(a, b):
    return lax.dot_general(a, b, (((0,), (0,)), ((), ())), preferred_element_type=F32)


def shift(values, by):
    by = by % values.shape[0]
    return values if by == 0 else pltpu.roll(values, by, 0)


def norm(values):
    centre = values - jnp.mean(values, axis=-1, keepdims=True)
    rstd = lax.rsqrt(jnp.mean(centre * centre, axis=-1, keepdims=True) + 1e-6)
    return centre * rstd, rstd


def norm_back(grad, y, rstd):
    mean_g = jnp.mean(grad, axis=-1, keepdims=True)
    mean_gy = jnp.mean(grad * y, axis=-1, keepdims=True)
    return rstd * (grad - mean_g - y * mean_gy)


def frame_places():
    first = lax.axis_index("tm") * OWN - HALO
    return (lax.broadcasted_iota(jnp.int32, (ROWS, 1), 0) + first).astype(F32)


def sin_cos(x):
    turns = jnp.round(x * 0.6366197723675814)
    r = x - turns * 1.5703125
    r = r - turns * 4.837512969970703125e-4
    r = r - turns * 7.549789954891882e-8
    z = r * r
    sine = r + r * z * (-1.6666654611e-1 + z * (8.3321608736e-3 + z * -1.9515295891e-4))
    cosine = (4.166664568298827e-2 + z * (-1.388731625493765e-3 + z * 2.443315711809948e-5)) * (z * z)
    cosine = cosine - 0.5 * z + 1.0
    quarter = turns.astype(jnp.int32)
    odd = (quarter & 1) == 1
    first, second = jnp.where(odd, cosine, sine), jnp.where(odd, sine, cosine)
    first = jnp.where((quarter & 2) == 2, -first, first)
    second = jnp.where(((quarter + 1) & 2) == 2, -second, second)
    return first, second


def inside(places):
    return (places >= 0.0) & (places < float(FRAMES))


def envelope(places, win):
    total = jnp.zeros((ROWS, HOP), F32)
    for p in range(4):
        total = total + jnp.where(inside(places + float(2 - p)), win[1:2, HOP * p : HOP * (p + 1)], 0.0)
    return jnp.where(inside(places), total, 1.0)


def spec(space):
    return pl.BlockSpec(memory_space=space)


def full(*shape, dtype=F32):
    return jax.ShapeDtypeStruct(shape, dtype)


def ids_column(ids):
    padded = jnp.concatenate([ids.astype(F32), jnp.zeros((126, OWN), F32)], axis=0)
    return jnp.transpose(padded)[:, :2]


OPERANDS = (
    full(384, OWN), full(1152, OWN), full(384, OWN), full(OWN, FF), full(OWN, D),
    full(OWN, 1152), full(OWN, D), full(384, 128),
)
PICKED = (True, True, True, False, False, False, False, True)
IDS = full(2, OWN, dtype=jnp.int32)
SAVED = (
    full(ROWS, D), full(ROWS, 128), full(ROWS, D), full(ROWS, FF),
    full(ROWS, D), full(ROWS, D), full(ROWS, CHUNKS1 * 128), full(ROWS, CHUNKS1 * 128),
    full(ROWS, WIDE1), full(ROWS, WIDE1), full(2 * ROWS, WIDE2), full(2 * ROWS, WIDE2),
)


def vmem(shapes):
    return [pltpu.VMEM(a.shape, a.dtype) for a in shapes]


def put(out, first, values, rows):
    for block in range(values.shape[1] // 128):
        part = values[:, 128 * block : 128 * (block + 1)].reshape(4, 4, rows, 128)
        out[:, :, first + rows * block : first + rows * (block + 1), :] = part


def halves_of(rows):
    upper = (rows // 2 + 7) // 8 * 8
    return pl.ds(0, upper), pl.ds(upper, rows - upper)


def step_kernel(target, ids, kern, scale_i, win, loss_scale, turn1, turn2, row_id, *refs):
    big_h, out_o, refs = refs[:10], refs[10], refs[11:]
    (up_v, down_v, head_v, syn_v, a1_v, a2_v, pick_k), refs = refs[:7], refs[7:]
    (sin_o, rstd_o, y1_o, gp_o, down_o, y2_o, re_o, im_o, d1_o, q1_o, d2_o, q2_o) = refs[:12]
    refs = refs[12:]
    here, there, refs = refs[:8], refs[8:17], refs[17:]
    (nrm_o, hid_o, onm_o, dup_o, ddn_o, dhd_o, dem_o, kg_o) = here
    (left_t, right_t, left_i, right_i, hid_v, stat_o, slots), refs = refs[:7], refs[7:]
    (dfr, dphase, dhead, dup, small), refs = refs[:5], refs[5:]
    through, from_left, from_right, got2a, got2b, last, got3 = (
        refs[3 * i : 3 * i + 3] for i in range(7)
    )
    (
        sems, halo_send, halo_recv, stat_send, stat_recv, pair_send, pair_recv, send, recv,
    ) = refs[21:]

    dp, tm = lax.axis_index("dp"), lax.axis_index("tm")
    core = lax.rem(dp, 2)
    other = 1 - core
    partner = {"dp": dp + 1 - 2 * core, "tm": tm}
    others = [{"dp": dp, "tm": lax.rem(tm + j, 8)} for j in range(1, 8)]
    spot = {"x": tm // 2, "y": dp // 4, "z": lax.rem(dp // 2, 2) * 2 + lax.rem(tm, 2)}

    def device(axis, by):
        to = dict(spot)
        to[axis] = lax.rem(spot[axis] + by, 4)
        return {
            "dp": (to["y"] * 2 + to["z"] // 2) * 2 + core,
            "tm": to["x"] * 2 + lax.rem(to["z"], 2),
        }

    barrier = pltpu.get_barrier_semaphore()
    around_me = [device(axis, by) for axis in "xyz" for by in (1, 2, 3)]
    for place in others + [partner] + around_me:
        pl.semaphore_signal(barrier, inc=1, device_id=place, device_id_type=MESH)

    def remote(src, dst, send, recv, place):
        return pltpu.make_async_remote_copy(
            src_ref=src, dst_ref=dst, send_sem=send, recv_sem=recv,
            device_id=place, device_id_type=MESH,
        )

    edge = HALO * HOP
    right, left = others[0], others[6]
    halo = [
        remote(src, dst, halo_send.at[i], halo_recv.at[i], place)
        for i, (src, dst, place) in enumerate(
            (
                (ids, left_i, right),
                (ids, right_i, left),
                (target.at[:, pl.ds(OWN * HOP - edge, edge)], left_t, right),
                (target.at[:, pl.ds(0, edge)], right_t, left),
            )
        )
    ]
    shares = [
        remote(stat_o, slots.at[tm], stat_send.at[j], stat_recv.at[j], place)
        for j, place in enumerate(others)
    ]
    pairs = [
        remote(ref.at[other] if picked else ref, there[i], pair_send.at[i], pair_recv.at[i], partner)
        for i, (ref, picked) in enumerate(zip((*here, ids), (*PICKED, False)))
    ]

    def give(i):
        pairs[i].start()

    own = slice(HALO, HALO + OWN)
    scale = scale_i[...].reshape(1, D)
    places = frame_places()
    valid = inside(places)

    def forward(table_v, pick_n, pick_h, goal, codes, head_s, spec_v, seg1, seg2):
        big_v = (table_v, up_v, down_v, head_v, syn_v, a1_v, a2_v, pick_n, pick_h, pick_k)
        copies = [
            pltpu.make_async_copy(h, v, sems.at[i]) for i, (h, v) in enumerate(zip(big_h, big_v))
        ]
        for copy in copies:
            copy.start()
        pl.semaphore_wait(barrier, 17)
        for copy in halo:
            copy.start()
        give(8)
        codes[HALO : HALO + OWN, :] = ids_column(ids[...])
        for source, first, count in (
            (target, HALO, OWN), (left_t, 0, HALO), (right_t, HALO + OWN, HALO),
        ):
            if source is left_t:
                for copy in halo:
                    copy.wait_recv()
            for r in range(count):
                goal[first + r : first + r + 1, :] = source[:, HOP * r : HOP * (r + 1)]
        codes[0:HALO, :] = ids_column(left_i[...])[OWN - HALO :]
        codes[HALO + OWN :, :] = ids_column(right_i[...])[:HALO]
        lane = lax.broadcasted_iota(jnp.int32, (ROWS, 2 * FRAMES), 1).astype(F32)
        hot = (lane == codes[:, 0:1]) | (lane == codes[:, 1:2] + 1024.0)
        hot = jnp.where(hot, 1.0, 0.0).astype(BF16)
        copies[0].wait()
        y0, rstd0 = norm(mm(hot, table_v[...]))
        y0 = jnp.where(valid, y0, 0.0)
        sin_o[...] = y0
        mixture = kern[0:1, :] * shift(y0, 3)
        for k in range(1, 7):
            mixture = mixture + kern[k : k + 1, :] * shift(y0, 3 - k)
        y1, rstd1 = norm(mixture)
        y1_o[...] = y1
        normed = y1.astype(BF16)
        copies[1].wait()
        for c in range(FF // 256):
            at = slice(256 * c, 256 * (c + 1))
            up = mm(normed, up_v[:, at])
            cdf = 0.5 * (1.0 + lax.erf(up * 0.7071067811865476))
            hid_v[:, at] = (up * cdf).astype(BF16)
            gp_o[:, at] = cdf + up * (0.3989422804014327 * jnp.exp(-0.5 * up * up))
        copies[2].wait()
        down = mm(hid_v[...], down_v[...])
        down_o[...] = down
        y2, rstd2 = norm(y0 + scale * down)
        y2_o[...] = y2
        places128 = lax.broadcasted_iota(jnp.int32, (ROWS, 128), 1)
        rstd_o[...] = jnp.where(places128 == 0, rstd0, jnp.where(places128 == 1, rstd1, rstd2))
        onorm = y2.astype(BF16)
        copies[3].wait()
        head_s[:, 1024:] = jnp.zeros((ROWS, 128), F32)
        for c in range(4):
            head_s[:, 256 * c : 256 * (c + 1)] = mm_bt(onorm, head_v[256 * c : 256 * (c + 1), :])
        head_s[:, 1024:1026] = mm_bt(onorm, head_v[1024:1026, :])
        phases = pltpu.roll(head_s[:, 512:], CHUNKS1 * 128 - 1, 1)
        for c in range(CHUNKS1):
            logmag = head_s[:, 128 * c : 128 * (c + 1)]
            if c == 4:
                logmag = jnp.where(places128 == 0, logmag, 0.0)
            mag = jnp.exp(logmag)
            phase = phases[:, 128 * c : 128 * (c + 1)]
            sine, cosine = sin_cos(phase)
            re, im = mag * cosine, mag * sine
            re_o[:, 128 * c : 128 * (c + 1)] = re
            im_o[:, 128 * c : 128 * (c + 1)] = im
            spec_v[:, 256 * c : 256 * c + 128] = re.astype(BF16)
            spec_v[:, 256 * c + 128 : 256 * (c + 1)] = im.astype(BF16)
        copies[4].wait()
        pred = jnp.zeros((ROWS, HOP), F32)
        for p in range(4):
            piece = jnp.where(valid, mm(spec_v[...], syn_v[:, HOP * p : HOP * (p + 1)]), 0.0)
            pred = pred + shift(piece, p - 2)
        pred = jnp.where(valid, pred / envelope(places, win), 0.0)
        for s, x in enumerate((pred, jnp.where(valid, goal[...], 0.0))):
            r1 = slice(ROWS * s, ROWS * (s + 1))
            for p in range(4):
                at = slice(HOP * p, HOP * (p + 1))
                seg1[r1, at] = (shift(x, 2 - p) * win[0:1, at]).astype(BF16)
            even = slice(2 * ROWS * s, 2 * ROWS * s + ROWS)
            odd = slice(2 * ROWS * s + ROWS, 2 * ROWS * (s + 1))
            before, after = shift(x, 1), shift(x, -1)
            seg2[even, 0:256] = (before * win[2:3, 0:256]).astype(BF16)
            seg2[even, 256:512] = (x * win[2:3, 256:512]).astype(BF16)
            seg2[odd, 0:128] = (before[:, 128:] * win[2:3, 0:128]).astype(BF16)
            seg2[odd, 128:384] = (x * win[2:3, 128:384]).astype(BF16)
            seg2[odd, 384:512] = (after[:, :128] * win[2:3, 384:512]).astype(BF16)
        for level in range(2):
            seg, table, chunks = ((seg1, a1_v, CHUNKS1), (seg2, a2_v, CHUNKS2))[level]
            d_o, q_o = ((d1_o, q1_o), (d2_o, q2_o))[level]
            copies[5 + level].wait()
            sums = [jnp.zeros((OWN, 128), F32) for _ in range(3)]
            for c in range(chunks):
                for sub in range(level + 1):
                    rows_p = slice(ROWS * sub, ROWS * (sub + 1))
                    base = ROWS * (level + 1)
                    rows_g = slice(base + ROWS * sub, base + ROWS * (sub + 1))
                    weights = table[:, 256 * c : 256 * (c + 1)]
                    sp, sg = mm(seg[rows_p, :], weights), mm(seg[rows_g, :], weights)
                    diff = sp - sg
                    pr, pi, gr, gi = sp[:, :128], sp[:, 128:], sg[:, :128], sg[:, 128:]
                    power_p, power_g = pr * pr + pi * pi, gr * gr + gi * gi
                    gap = jnp.log1p(power_p) - jnp.log1p(power_g)
                    slope = jnp.where(valid, 4.0 * gap / (1.0 + power_p), 0.0)
                    d_o[rows_p, 256 * c : 256 * (c + 1)] = jnp.where(valid, diff, 0.0)
                    q_o[rows_p, 256 * c : 256 * c + 128] = slope * pr
                    q_o[rows_p, 256 * c + 128 : 256 * (c + 1)] = slope * pi
                    dr, di = diff[own, :128], diff[own, 128:]
                    sums[0] = sums[0] + dr * dr + di * di
                    sums[1] = sums[1] + power_g[own]
                    sums[2] = sums[2] + gap[own] * gap[own]
            for i in range(3):
                total = jnp.sum(jnp.sum(sums[i], axis=0, keepdims=True), axis=1, keepdims=True)
                stat_o[3 * level + i : 3 * level + i + 1, :] = jnp.broadcast_to(total, (1, 128))
        stat_o[6:8, :] = jnp.zeros((2, 128), F32)
        for share in shares:
            share.start()
        slots[tm] = stat_o[...]

        copies[7].wait()
        copies[8].wait()
        normed = y1_o[own, :].astype(BF16)
        onorm = y2_o[own, :].astype(BF16)
        for c in range(2):
            nrm_o[c] = mm_bt(pick_n[c], normed)
            onm_o[c] = mm_bt(pick_n[c], onorm)
            for h in range(2):
                out = slice(576 * h, 576 * (h + 1))
                hid_o[c, out, :] = mm_bt(pick_h[c], hid_v[own, 1152 * h : 1152 * (h + 1)])
        for i in (0, 2, 1):
            give(i)
        copies[9].wait()

    pl.run_scoped(
        forward,
        *vmem([full(*shape, dtype=BF16) for shape in (BIG[0], BIG[7], BIG[8])]),
        pltpu.VMEM((ROWS, HOP), F32),
        pltpu.VMEM((ROWS, 2), F32),
        pltpu.VMEM((ROWS, 1152), F32),
        pltpu.VMEM((ROWS, WIDE1), BF16),
        pltpu.VMEM((2 * ROWS, NFFT), BF16),
        pltpu.VMEM((4 * ROWS, NFFT // 2), BF16),
    )

    def need(*which):
        for i in which:
            pairs[i].wait_recv()

    def lhs(i):
        return jnp.concatenate([here[i][core], there[i][...]], axis=1).astype(BF16)

    def rhs(i, cols):
        return jnp.concatenate([here[i][:, cols], there[i][:, cols]], axis=0).astype(BF16)

    def head_block(onorm, block):
        return mm(onorm, rhs(5, slice(128 * block, 128 * (block + 1))))

    def around(axis):
        i = spot[axis]
        return i, lax.rem(i + 1, 4), lax.rem(i + 2, 4), lax.rem(i + 3, 4)

    def backward(*parts):
        sent = [{}, {}, {}]

        def go(src, dst, k, slot, axis, by):
            sent[k][slot] = remote(src, dst, send.at[k, slot], recv.at[k, slot], device(axis, by))
            sent[k][slot].start()

        low, high = pl.ds(0, 2), pl.ds(2, 2)

        def phase1(k, s):
            axis, p = ORDERS[k][0], parts[k]
            i, right, opposite, left = around(axis)
            first, end = RANGES[k][s]
            rows = pl.ds(first, end - first)
            go(p.at[opposite, low, rows], through[k].at[0, :, rows], k, 6 * s, axis, 1)
            go(p.at[opposite, high, rows], through[k].at[1, :, rows], k, 6 * s + 1, axis, 3)
            go(p.at[right, high, rows], from_left[k].at[high, rows], k, 6 * s + 2, axis, 1)
            go(p.at[left, low, rows], from_right[k].at[low, rows], k, 6 * s + 3, axis, 3)

        def combine(k, s):
            axis, p = ORDERS[k][0], parts[k]
            i, right, opposite, left = around(axis)
            first, end = RANGES[k][s]
            rows = pl.ds(first, end - first)
            sent[k][6 * s].wait_recv()
            p[right, low, rows] += through[k][0, :, rows]
            go(p.at[right, low, rows], from_left[k].at[low, rows], k, 6 * s + 4, axis, 1)
            sent[k][6 * s + 1].wait_recv()
            p[left, high, rows] += through[k][1, :, rows]
            go(p.at[left, high, rows], from_right[k].at[high, rows], k, 6 * s + 5, axis, 3)

        for share in shares:
            share.wait_recv()
        total = slots[0]
        for j in range(1, 8):
            total = total + slots[j]

        factor = loss_scale[...] * (0.5 / CLIPS)
        loss = jnp.zeros((1, 1), F32)
        cots = []
        for level in range(2):
            count = ((FRAMES * 513), (2 * FRAMES * 257))[level]
            sum_a = total[3 * level : 3 * level + 1, 0:1]
            sum_b = total[3 * level + 1 : 3 * level + 2, 0:1]
            sum_g = total[3 * level + 2 : 3 * level + 3, 0:1]
            root_a, root_b = jnp.sqrt(sum_a + 1e-6), jnp.sqrt(sum_b + 1e-6)
            loss = loss + root_a / root_b + sum_g * (1.0 / count)
            cots.append((factor / (root_a * root_b), factor * (1.0 / count)))
        loss = jnp.where(lax.axis_index("tm") == 0, loss, 0.0)

        dx = jnp.zeros((ROWS, HOP), F32)
        ds1 = (cots[0][0] * d1_o[...] + cots[0][1] * q1_o[...]).astype(BF16)
        for p in range(4):
            at = slice(HOP * p, HOP * (p + 1))
            piece = mm_bt(ds1, a1_v[at, :]).astype(BF16).astype(F32) * win[0:1, at]
            dx = dx + shift(piece, p - 2)
        ds2 = (cots[1][0] * d2_o[...] + cots[1][1] * q2_o[...]).astype(BF16)
        dseg = mm_bt(ds2, a2_v[...]).astype(BF16).astype(F32) * win[2:3, : NFFT // 2]
        even, odd = dseg[:ROWS], dseg[ROWS:]
        dx = dx + shift(even[:, :256], -1) + even[:, 256:] + odd[:, 128:384]
        dx = dx + jnp.concatenate([shift(odd[:, 384:], 1), shift(odd[:, :128], -1)], axis=1)
        dx = jnp.where(valid, dx / envelope(places, win), 0.0)
        for p in range(4):
            piece = jnp.where(valid, shift(dx, 2 - p), 0.0)
            dfr[:, HOP * p : HOP * (p + 1)] = piece.astype(BF16)

        for c in range(CHUNKS1):
            dsp = mm_bt(dfr[...], syn_v[256 * c : 256 * (c + 1), :]).astype(BF16).astype(F32)
            dre, dim = dsp[:, :128], dsp[:, 128:]
            re, im = re_o[:, 128 * c : 128 * (c + 1)], im_o[:, 128 * c : 128 * (c + 1)]
            dlog, dph = dre * re + dim * im, dim * re - dre * im
            if c < 4:
                dhead[:, 128 * c : 128 * (c + 1)] = dlog.astype(BF16)
            dphase[:, 128 * c : 128 * (c + 1)] = dph
        moved = pltpu.roll(dphase[...], 1, 1)
        dhead[:, 512:640] = (moved[:, :128] + dlog).astype(BF16)
        dhead[:, 640:] = moved[:, 128:].astype(BF16)
        dhd_o[...] = dhead[own, :].astype(F32)
        give(5)
        don = mm(dhead[:, :1026], head_v[...]).astype(BF16).astype(F32)
        dstream = norm_back(don, y2_o[...], rstd_o[:, 2:3])

        scale_grad = jnp.sum(dstream[own] * down_o[own, :], axis=0, keepdims=True)
        ddn = (scale * dstream).astype(BF16)
        ddn_o[...] = ddn[own].astype(F32)
        give(4)
        for c in range(FF // 256):
            at = slice(256 * c, 256 * (c + 1))
            dh = mm_bt(ddn, down_v[at, :]).astype(BF16).astype(F32)
            dup[:, at] = (dh * gp_o[:, at]).astype(BF16)
        dup_o[...] = dup[own, :].astype(F32)
        give(3)

        need(2, 5)
        onorm = [lhs(2)]
        onorm += [mm(turn[...], onorm[0]).astype(BF16) for turn in (turn1, turn2)]
        for k in range(3):
            start, blocks = HEAD_BLOCKS[k]
            for b in range(min(blocks, 8 - start)):
                put(parts[k], 24 * b, head_block(onorm[k], start + b), 24)
        phase1(0, 0)
        phase1(2, 0)
        need(1, 4)
        hidden = lhs(1)
        for c in range(3):
            put(parts[1], 48 + 144 * c, mm(hidden, rhs(4, slice(256 * c, 256 * (c + 1)))), 72)
        phase1(1, 0)

        dnorm = mm_bt(dup[...], up_v[...]).astype(BF16).astype(F32)
        dmix = norm_back(dnorm, y1_o[...], rstd_o[:, 1:2])
        dmix = jnp.where(valid, dmix, 0.0)
        y0 = sin_o[...]
        dsin = dstream
        small[...] = jnp.zeros((128, D), F32)
        for k in range(7):
            dsin = dsin + kern[k : k + 1, :] * shift(dmix, k - 3)
            taps = dmix * shift(y0, 3 - k)
            small[2 + k : 3 + k, :] = jnp.sum(taps[own], axis=0, keepdims=True)
        demb = norm_back(dsin, y0, rstd_o[:, 0:1])
        dem_o[...] = demb[own].astype(BF16).astype(F32)
        give(6)

        small[9:10, :] = scale_grad
        rest = loss
        for i, grid in enumerate((65536.0, 1.0, 1.0 / 65536.0, 1.0 / 65536.0 / 65536.0)):
            piece = jnp.floor(rest * (1.0 / grid)) * grid
            rest = rest - piece
            small[10 + i : 11 + i, :] = jnp.broadcast_to(piece, (1, D))

        small0 = small[...].astype(BF16)
        rest = small[...] - small0.astype(F32)
        small1 = rest.astype(BF16)
        small2 = (rest - small1.astype(F32)).astype(BF16)
        for c in range(2):
            kg_o[c] = sum(mm_bt(pick_k[c], part) for part in (small0, small1, small2))
        give(7)

        combine(0, 0)
        combine(2, 0)
        need(0, 3)
        normed = lhs(0)
        for c in range(FF // 256):
            put(parts[0], 72 + 48 * c, mm(normed, rhs(3, slice(256 * c, 256 * (c + 1)))), 24)
        phase1(0, 1)
        need(8, 6, 7)
        put(parts[2], 72, head_block(onorm[2], 8) + here[7][core] + there[7][...], 24)
        both_ids = jnp.concatenate([ids[...], there[8][...]], axis=1)
        code_rows = row_id[...] + OWN * core
        hot = (code_rows == both_ids[0:1, :]) | (code_rows == both_ids[1:2, :] + 1024)
        hot = jnp.where(hot, 1.0, 0.0).astype(BF16)
        for c in range(3):
            put(parts[2], 96 + 128 * c, mm(hot, rhs(6, slice(256 * c, 256 * (c + 1)))), 64)
        phase1(2, 1)
        combine(1, 0)
        combine(0, 1)
        combine(2, 1)

        for k in (1, 0, 2):
            mine = spot[ORDERS[k][0]]
            axis, p, a, b = ORDERS[k][1], parts[k], got2a[k], got2b[k]
            i, right, opposite, left = around(axis)
            upper, lower = halves_of(PART_ROWS[k])
            for s in range(len(RANGES[k])):
                for j in (2, 3, 4, 5):
                    sent[k][6 * s + j].wait_recv()
            p[mine, opposite] += from_left[k][opposite] + from_right[k][opposite]
            go(p.at[mine, opposite, upper], a.at[0], k, 12, axis, 1)
            go(p.at[mine, opposite, lower], b.at[0], k, 13, axis, 3)
            p[mine, right] += from_left[k][right] + from_right[k][right]
            go(p.at[mine, right, lower], b.at[1], k, 14, axis, 1)
            p[mine, left] += from_left[k][left] + from_right[k][left]
            go(p.at[mine, left, upper], a.at[1], k, 15, axis, 3)
            p[mine, i] += from_left[k][i] + from_right[k][i]
        for k in (1, 0, 2):
            mine = spot[ORDERS[k][0]]
            axis, p, a, b = ORDERS[k][1], parts[k], got2a[k], got2b[k]
            i, right, opposite, left = around(axis)
            upper, lower = halves_of(PART_ROWS[k])
            sent[k][12].wait_recv()
            p[mine, right, upper] += a[0]
            go(p.at[mine, right, upper], a.at[2], k, 16, axis, 1)
            sent[k][13].wait_recv()
            p[mine, left, lower] += b[0]
            go(p.at[mine, left, lower], b.at[2], k, 17, axis, 3)
        for k in (1, 0, 2):
            mine = spot[ORDERS[k][0]]
            i = spot[ORDERS[k][1]]
            p, a, b, out = parts[k], got2a[k], got2b[k], last[k]
            upper, lower = halves_of(PART_ROWS[k])
            for j in (14, 15, 16, 17):
                sent[k][j].wait_recv()
            p[mine, i, upper] += a[1] + a[2]
            p[mine, i, lower] += b[1] + b[2]
            start, place = 0, 0
            for count, rows in ((HEAD_BLOCKS[k][1], 24), MAIN_BLOCKS[k]):
                each = rows // 4
                for _ in range(count):
                    for d in range(4):
                        out[d, pl.ds(place, each)] = p[mine, i, pl.ds(start + d * each, each)]
                    start += rows
                    place += each
            if place < LAST_ROWS[k]:
                for d in range(4):
                    out[d, pl.ds(place, LAST_ROWS[k] - place)] = jnp.zeros(
                        (LAST_ROWS[k] - place, 128), F32
                    )
            axis = ORDERS[k][2]
            for by in (1, 2, 3):
                to = lax.rem(spot[axis] + by, 4)
                go(out.at[to], got3[k].at[by - 1], k, 17 + by, axis, by)
        for k in (1, 0, 2):
            for j in (18, 19, 20):
                sent[k][j].wait_recv()
            total = last[k][spot[ORDERS[k][2]]] + got3[k][0] + got3[k][1] + got3[k][2]
            out_o[pl.ds(FIRST_ROWS[k], LAST_ROWS[k]), :] = total
        for copy in halo + shares + pairs:
            copy.wait_send()
        for k in range(3):
            for copy in sent[k].values():
                copy.wait_send()

    pl.run_scoped(backward, *[pltpu.VMEM((4, 4, n, 128), F32) for n in PART_ROWS])


BIG = (
    (2 * FRAMES, D), (D, FF), (FF, D), (2 * 513, D), (WIDE1, NFFT), (NFFT, WIDE1),
    (NFFT // 2, WIDE2), (2, 384, D), (2, 576, FF // 2), (2, 384, D),
)


def step_call(small, big):
    wide = [full(*((2,) if p else ()), *a.shape) for a, p in zip(OPERANDS, PICKED)]
    edge = full(1, HALO * HOP)
    rows = PART_ROWS
    cuts = [halves_of(n)[0].size for n in rows]

    def each(make):
        return [pltpu.VMEM(make(k), F32) for k in range(3)]

    return pl.pallas_call(
        step_kernel,
        out_shape=full(sum(LAST_ROWS), 128),
        in_specs=[spec(pltpu.VMEM)] * len(small) + [spec(pl.ANY)] * len(big),
        out_specs=spec(pltpu.VMEM),
        scratch_shapes=vmem([full(*BIG[i], dtype=BF16) for i in (1, 2, 3, 4, 5, 6, 9)])
        + vmem(SAVED)
        + vmem(wide)
        + vmem([*OPERANDS, IDS])
        + vmem([edge, edge, IDS, IDS])
        + [
            pltpu.VMEM((ROWS, FF), BF16),
            pltpu.VMEM((8, 128), F32),
            pltpu.VMEM((8, 8, 128), F32),
            pltpu.VMEM((ROWS, NFFT), BF16),
            pltpu.VMEM((ROWS, CHUNKS1 * 128), F32),
            pltpu.VMEM((ROWS, 1152), BF16),
            pltpu.VMEM((ROWS, FF), BF16),
            pltpu.VMEM((128, D), F32),
        ]
        + each(lambda k: (2, 2, rows[k], 128))
        + each(lambda k: (4, rows[k], 128))
        + each(lambda k: (4, rows[k], 128))
        + each(lambda k: (3, cuts[k], 128))
        + each(lambda k: (3, rows[k] - cuts[k], 128))
        + each(lambda k: (4, LAST_ROWS[k], 128))
        + each(lambda k: (3, LAST_ROWS[k], 128))
        + [pltpu.SemaphoreType.DMA((n,)) for n in (len(big), 4, 4, 7, 7, 9, 9)]
        + [pltpu.SemaphoreType.DMA((3, 21))] * 2,
        compiler_params=pltpu.CompilerParams(
            collective_id=0, has_side_effects=True, vmem_limit_bytes=64 * MB
        ),
        name="train_step",
    )(*small, *big)


def finish_kernel(sums, loss_o, table_o, kern_o, up_o, down_o, scale_o, head_o):
    for k, (out, count, each) in enumerate(((up_o, 18, 6), (down_o, 6, 18), (table_o, 6, 16))):
        start, blocks = HEAD_BLOCKS[k]
        for c in range(blocks):
            rows = FIRST_ROWS[k] + 6 * c
            values = sums[rows : rows + 6, :]
            if start + c < 8:
                head_o[:, 128 * (start + c) : 128 * (start + c + 1)] = values
            else:
                head_o[:, 1024:1026] = values[:, 0:2]
                tail = jnp.transpose(jnp.concatenate([values, jnp.zeros((122, 128), F32)], axis=0))
                kern_o[...] = tail[2:9, 0:6]
                scale_o[...] = tail[9:10, 0:6]
                pieces = values[0:1, 10:14]
                loss_o[...] = jnp.sum(pieces, axis=1, keepdims=True) * (0.5 / CLIPS)
        for c in range(count):
            rows = FIRST_ROWS[k] + 6 * blocks + each * c
            out[:, 128 * c : 128 * (c + 1)] = sums[rows : rows + each, :]


def finish_call(sums):
    loss, table, kern, up, down, scale, head = pl.pallas_call(
        finish_kernel,
        out_shape=[
            full(1, 1), full(16, D), full(7, 6), full(6, FF), full(18, D), full(1, 6), full(6, 1026),
        ],
        in_specs=[spec(pltpu.VMEM)],
        out_specs=[spec(pltpu.VMEM)] * 7,
        name="finish",
    )(sums)
    return loss.reshape(()), table, kern, up, down, scale.reshape(6), head


def body(
    code_ids, code_table, kernel, up_weight, down_weight, layer_scale, head_weight, target, loss_scale
):
    syn, a1, a2, win = make_constants()
    pick_n, pick_h, pick_k, turn1, turn2, row_id = make_orders()
    ids = jnp.swapaxes(code_ids, 1, 2).reshape(2, OWN)
    head_t = head_weight.T
    sums = step_call(
        (target, ids, kernel, layer_scale, win, loss_scale.reshape(1, 1), turn1, turn2, row_id),
        (
            code_table, up_weight, down_weight, head_t, syn, a1, a2, pick_n, pick_h, pick_k,
        ),
    )
    return finish_call(sums)


def solution(mesh):
    in_specs = (P("dp", "tm", None), P(), P(), P(), P(), P(), P(), P("dp", "tm"), P())
    out_specs = (
        P(),
        P(("dp", "tm"), None),
        P(None, ("dp", "tm")),
        P(("dp", "tm"), None),
        P(("dp", "tm"), None),
        P(("dp", "tm")),
        P(("dp", "tm"), None),
    )
    return jax.shard_map(body, mesh=mesh, in_specs=in_specs, out_specs=out_specs, check_vma=False)
```

```python
import jax
import jax.numpy as jnp
import ml_dtypes
import numpy as np
from jax import lax
from jax.experimental import pallas as pl
from jax.experimental.pallas import tpu as pltpu
from jax.sharding import PartitionSpec as P

F32, BF16 = jnp.float32, jnp.bfloat16
MESH = pl.DeviceIdType.MESH
D, FF = 768, 2304
HOP, NFFT = 256, 1024
FRAMES, OWN, HALO = 1024, 128, 16
ROWS = OWN + 2 * HALO
CHUNKS1, CHUNKS2 = 5, 3
WIDE1, WIDE2 = CHUNKS1 * 256, CHUNKS2 * 256
CLIPS = 16
MB = 1 << 20
ORDERS = ("xyz", "yzx", "zxy")
BLOCKS = (
    (("head", 0, 3, 24), ("up", 0, 15, 24)),
    (("head", 3, 2, 24), ("down", 0, 6, 72), ("up", 15, 3, 24)),
    (("head", 5, 3, 24), ("table", 0, 6, 64), ("head", 8, 1, 24)),
)
RANGES = (
    ((0, 72), (72, 264), (264, 432)),
    ((0, 264), (264, 480), (480, 552)),
    ((0, 72), (72, 264), (264, 480)),
)
PART_ROWS = (432, 552, 480)
LAST_ROWS = (112, 144, 120)
FIRST_ROWS = (0, 112, 256)


def bf(array):
    return np.asarray(array, np.float32).astype(ml_dtypes.bfloat16)


def hann(length):
    return 0.5 - 0.5 * np.cos(2.0 * np.pi * np.arange(length) / length)


def angles(length):
    product = np.arange(length // 2 + 1)[:, None] * np.arange(length)[None, :] % length
    return 2.0 * np.pi * product / length


def interleave(real, imag, chunks):
    bins, width = real.shape
    out = np.zeros((chunks, 2, 128, width), np.float64)
    for half, part in enumerate((real, imag)):
        padded = np.zeros((chunks * 128, width), np.float64)
        padded[:bins] = part
        out[:, half] = padded.reshape(chunks, 128, width)
    return out.reshape(chunks * 256, width)


def make_constants():
    ang = angles(NFFT)
    bins = np.arange(NFFT // 2 + 1)
    factor = np.where((bins == 0) | (bins == NFFT // 2), 1.0, 2.0)[:, None] / NFFT
    window = hann(NFFT)[None, :]
    synthesis = bf(interleave(factor * np.cos(ang) * window, -factor * np.sin(ang) * window, CHUNKS1))
    analysis1 = bf(interleave(np.cos(ang), -np.sin(ang), CHUNKS1).T)
    ang = angles(NFFT // 2)
    analysis2 = bf(interleave(np.cos(ang), -np.sin(ang), CHUNKS2).T)
    win = np.zeros((8, NFFT), np.float32)
    win[0] = hann(NFFT)
    win[1] = hann(NFFT) ** 2
    win[2, : NFFT // 2] = hann(NFFT // 2)
    return synthesis, analysis1, analysis2, win


def device_index(x, y, z, core):
    return ((y * 2 + z // 2) * 2 + core) * 8 + x * 2 + z % 2


def shard_order(order, core):
    places = []
    for a in range(4):
        for b in range(4):
            for c in range(4):
                at = dict(zip(order, (a, b, c)))
                places.append(device_index(at["x"], at["y"], at["z"], core))
    return np.array(places)


def columns_of(order, core, each):
    return (shard_order(order, core)[:, None] * each + np.arange(each)[None, :]).reshape(-1)


def one_hot_columns(sources, size):
    out = np.zeros((size, sources.size), np.float32)
    out[sources, np.arange(sources.size)] = 1.0
    return bf(out)


def make_orders():
    pick_n = np.stack([one_hot_columns(columns_of(ORDERS[0], c, 6), D).T for c in (0, 1)])
    half = [columns_of(ORDERS[1], c, 18)[: 4 * 4 * 2 * 18] for c in (0, 1)]
    pick_h = np.stack([one_hot_columns(h, FF // 2).T for h in half])
    pick_k = np.stack([one_hot_columns(columns_of(ORDERS[2], c, 6), D).T for c in (0, 1)])
    first = columns_of(ORDERS[0], 0, 6)
    where = {col: i for i, col in enumerate(first)}
    turns = []
    for k in (1, 2):
        sources = np.array([where[col] for col in columns_of(ORDERS[k], 0, 6)])
        turns.append(one_hot_columns(sources, 384).T)
    row_id = columns_of(ORDERS[2], 0, 16).astype(np.int32)[:, None]
    return pick_n, pick_h, pick_k, turns[0], turns[1], row_id


def mm(a, b):
    return jnp.dot(a, b, preferred_element_type=F32)


def mm_bt(a, b):
    return lax.dot_general(a, b, (((1,), (1,)), ((), ())), preferred_element_type=F32)


def mm_at(a, b):
    return lax.dot_general(a, b, (((0,), (0,)), ((), ())), preferred_element_type=F32)


def shift(values, by):
    by = by % values.shape[0]
    return values if by == 0 else pltpu.roll(values, by, 0)


def norm(values):
    centre = values - jnp.mean(values, axis=-1, keepdims=True)
    rstd = lax.rsqrt(jnp.mean(centre * centre, axis=-1, keepdims=True) + 1e-6)
    return centre * rstd, rstd


def norm_back(grad, y, rstd):
    mean_g = jnp.mean(grad, axis=-1, keepdims=True)
    mean_gy = jnp.mean(grad * y, axis=-1, keepdims=True)
    return rstd * (grad - mean_g - y * mean_gy)


def frame_places():
    first = lax.axis_index("tm") * OWN - HALO
    return (lax.broadcasted_iota(jnp.int32, (ROWS, 1), 0) + first).astype(F32)


def sin_cos(x):
    turns = jnp.round(x * 0.6366197723675814)
    r = x - turns * 1.5703125
    r = r - turns * 4.837512969970703125e-4
    r = r - turns * 7.549789954891882e-8
    z = r * r
    sine = r + r * z * (-1.6666654611e-1 + z * (8.3321608736e-3 + z * -1.9515295891e-4))
    cosine = (4.166664568298827e-2 + z * (-1.388731625493765e-3 + z * 2.443315711809948e-5)) * (z * z)
    cosine = cosine - 0.5 * z + 1.0
    quarter = turns.astype(jnp.int32)
    odd = (quarter & 1) == 1
    first, second = jnp.where(odd, cosine, sine), jnp.where(odd, sine, cosine)
    first = jnp.where((quarter & 2) == 2, -first, first)
    second = jnp.where(((quarter + 1) & 2) == 2, -second, second)
    return first, second


def inside(places):
    return (places >= 0.0) & (places < float(FRAMES))


def envelope(places, win):
    total = jnp.zeros((ROWS, HOP), F32)
    for p in range(4):
        total = total + jnp.where(inside(places + float(2 - p)), win[1:2, HOP * p : HOP * (p + 1)], 0.0)
    return jnp.where(inside(places), total, 1.0)


def spec(space):
    return pl.BlockSpec(memory_space=space)


def full(*shape, dtype=F32):
    return jax.ShapeDtypeStruct(shape, dtype)


def ids_column(ids):
    padded = jnp.concatenate([ids.astype(F32), jnp.zeros((126, OWN), F32)], axis=0)
    return jnp.transpose(padded)[:, :2]


OPERANDS = (
    full(384, OWN), full(1152, OWN), full(384, OWN), full(OWN, FF), full(OWN, D),
    full(OWN, 1152), full(OWN, D), full(384, 128),
)
PICKED = (True, True, True, False, False, False, False, True)
IDS = full(2, OWN, dtype=jnp.int32)
SAVED = (
    full(ROWS, D), full(ROWS, 128), full(ROWS, D), full(ROWS, FF),
    full(ROWS, D), full(ROWS, D), full(ROWS, CHUNKS1 * 128), full(ROWS, CHUNKS1 * 128),
    full(ROWS, WIDE1), full(ROWS, WIDE1), full(2 * ROWS, WIDE2), full(2 * ROWS, WIDE2),
)


def vmem(shapes):
    return [pltpu.VMEM(a.shape, a.dtype) for a in shapes]


def put(out, first, values, rows):
    for block in range(values.shape[1] // 128):
        part = values[:, 128 * block : 128 * (block + 1)].reshape(4, 4, rows, 128)
        out[:, :, first + rows * block : first + rows * (block + 1), :] = part


def halves_of(first, end):
    middle = first + ((end - first) // 2 + 7) // 8 * 8
    return pl.ds(first, middle - first), pl.ds(middle, end - middle)


def step_kernel(target, ids, kern, scale_i, win, loss_scale, turn1, turn2, row_id, *refs):
    big_h, out_o, refs = refs[:10], refs[10], refs[11:]
    (up_v, down_v, head_v, syn_v, a1_v, a2_v, pick_k), refs = refs[:7], refs[7:]
    (sin_o, rstd_o, y1_o, gp_o, down_o, y2_o, re_o, im_o, d1_o, q1_o, d2_o, q2_o) = refs[:12]
    refs = refs[12:]
    here, there, refs = refs[:8], refs[8:17], refs[17:]
    (nrm_o, hid_o, onm_o, dup_o, ddn_o, dhd_o, dem_o, kg_o) = here
    (left_t, right_t, left_i, right_i, hid_v, stat_o, slots), refs = refs[:7], refs[7:]
    (dfr, dphase, dhead, dup, small), refs = refs[:5], refs[5:]
    through, from_left, from_right, got2, last, got3 = (refs[3 * i : 3 * i + 3] for i in range(6))
    (
        sems, halo_send, halo_recv, stat_send, stat_recv, pair_send, pair_recv, send, recv,
    ) = refs[18:]

    dp, tm = lax.axis_index("dp"), lax.axis_index("tm")
    core = lax.rem(dp, 2)
    other = 1 - core
    partner = {"dp": dp + 1 - 2 * core, "tm": tm}
    others = [{"dp": dp, "tm": lax.rem(tm + j, 8)} for j in range(1, 8)]
    spot = {"x": tm // 2, "y": dp // 4, "z": lax.rem(dp // 2, 2) * 2 + lax.rem(tm, 2)}

    def device(axis, by):
        to = dict(spot)
        to[axis] = lax.rem(spot[axis] + by, 4)
        return {
            "dp": (to["y"] * 2 + to["z"] // 2) * 2 + core,
            "tm": to["x"] * 2 + lax.rem(to["z"], 2),
        }

    barrier = pltpu.get_barrier_semaphore()
    around_me = [device(axis, by) for axis in "xyz" for by in (1, 2, 3)]
    for place in others + [partner] + around_me:
        pl.semaphore_signal(barrier, inc=1, device_id=place, device_id_type=MESH)

    def remote(src, dst, send, recv, place):
        return pltpu.make_async_remote_copy(
            src_ref=src, dst_ref=dst, send_sem=send, recv_sem=recv,
            device_id=place, device_id_type=MESH,
        )

    edge = HALO * HOP
    right, left = others[0], others[6]
    halo = [
        remote(src, dst, halo_send.at[i], halo_recv.at[i], place)
        for i, (src, dst, place) in enumerate(
            (
                (ids, left_i, right),
                (ids, right_i, left),
                (target.at[:, pl.ds(OWN * HOP - edge, edge)], left_t, right),
                (target.at[:, pl.ds(0, edge)], right_t, left),
            )
        )
    ]
    shares = [
        remote(stat_o, slots.at[tm], stat_send.at[j], stat_recv.at[j], place)
        for j, place in enumerate(others)
    ]
    pairs = [
        remote(ref.at[other] if picked else ref, there[i], pair_send.at[i], pair_recv.at[i], partner)
        for i, (ref, picked) in enumerate(zip((*here, ids), (*PICKED, False)))
    ]

    def give(i):
        pairs[i].start()

    own = slice(HALO, HALO + OWN)
    scale = scale_i[...].reshape(1, D)
    places = frame_places()
    valid = inside(places)

    def forward(table_v, pick_n, pick_h, goal, codes, head_s, spec_v, seg1, seg2):
        big_v = (table_v, up_v, down_v, head_v, syn_v, a1_v, a2_v, pick_n, pick_h, pick_k)
        copies = [
            pltpu.make_async_copy(h, v, sems.at[i]) for i, (h, v) in enumerate(zip(big_h, big_v))
        ]
        for copy in copies:
            copy.start()
        pl.semaphore_wait(barrier, 17)
        for copy in halo:
            copy.start()
        give(8)
        codes[HALO : HALO + OWN, :] = ids_column(ids[...])
        for source, first, count in (
            (target, HALO, OWN), (left_t, 0, HALO), (right_t, HALO + OWN, HALO),
        ):
            if source is left_t:
                for copy in halo:
                    copy.wait_recv()
            for r in range(count):
                goal[first + r : first + r + 1, :] = source[:, HOP * r : HOP * (r + 1)]
        codes[0:HALO, :] = ids_column(left_i[...])[OWN - HALO :]
        codes[HALO + OWN :, :] = ids_column(right_i[...])[:HALO]
        lane = lax.broadcasted_iota(jnp.int32, (ROWS, 2 * FRAMES), 1).astype(F32)
        hot = (lane == codes[:, 0:1]) | (lane == codes[:, 1:2] + 1024.0)
        hot = jnp.where(hot, 1.0, 0.0).astype(BF16)
        copies[0].wait()
        y0, rstd0 = norm(mm(hot, table_v[...]))
        y0 = jnp.where(valid, y0, 0.0)
        sin_o[...] = y0
        mixture = kern[0:1, :] * shift(y0, 3)
        for k in range(1, 7):
            mixture = mixture + kern[k : k + 1, :] * shift(y0, 3 - k)
        y1, rstd1 = norm(mixture)
        y1_o[...] = y1
        normed = y1.astype(BF16)
        copies[1].wait()
        for c in range(FF // 256):
            at = slice(256 * c, 256 * (c + 1))
            up = mm(normed, up_v[:, at])
            cdf = 0.5 * (1.0 + lax.erf(up * 0.7071067811865476))
            hid_v[:, at] = (up * cdf).astype(BF16)
            gp_o[:, at] = cdf + up * (0.3989422804014327 * jnp.exp(-0.5 * up * up))
        copies[2].wait()
        down = mm(hid_v[...], down_v[...])
        down_o[...] = down
        y2, rstd2 = norm(y0 + scale * down)
        y2_o[...] = y2
        places128 = lax.broadcasted_iota(jnp.int32, (ROWS, 128), 1)
        rstd_o[...] = jnp.where(places128 == 0, rstd0, jnp.where(places128 == 1, rstd1, rstd2))
        onorm = y2.astype(BF16)
        copies[3].wait()
        head_s[:, 1024:] = jnp.zeros((ROWS, 128), F32)
        for c in range(4):
            head_s[:, 256 * c : 256 * (c + 1)] = mm_bt(onorm, head_v[256 * c : 256 * (c + 1), :])
        head_s[:, 1024:1026] = mm_bt(onorm, head_v[1024:1026, :])
        phases = pltpu.roll(head_s[:, 512:], CHUNKS1 * 128 - 1, 1)
        for c in range(CHUNKS1):
            logmag = head_s[:, 128 * c : 128 * (c + 1)]
            if c == 4:
                logmag = jnp.where(places128 == 0, logmag, 0.0)
            mag = jnp.exp(logmag)
            phase = phases[:, 128 * c : 128 * (c + 1)]
            sine, cosine = sin_cos(phase)
            re, im = mag * cosine, mag * sine
            re_o[:, 128 * c : 128 * (c + 1)] = re
            im_o[:, 128 * c : 128 * (c + 1)] = im
            spec_v[:, 256 * c : 256 * c + 128] = re.astype(BF16)
            spec_v[:, 256 * c + 128 : 256 * (c + 1)] = im.astype(BF16)
        copies[4].wait()
        pred = jnp.zeros((ROWS, HOP), F32)
        for p in range(4):
            piece = jnp.where(valid, mm(spec_v[...], syn_v[:, HOP * p : HOP * (p + 1)]), 0.0)
            pred = pred + shift(piece, p - 2)
        pred = jnp.where(valid, pred / envelope(places, win), 0.0)
        for s, x in enumerate((pred, jnp.where(valid, goal[...], 0.0))):
            r1 = slice(ROWS * s, ROWS * (s + 1))
            for p in range(4):
                at = slice(HOP * p, HOP * (p + 1))
                seg1[r1, at] = (shift(x, 2 - p) * win[0:1, at]).astype(BF16)
            even = slice(2 * ROWS * s, 2 * ROWS * s + ROWS)
            odd = slice(2 * ROWS * s + ROWS, 2 * ROWS * (s + 1))
            before, after = shift(x, 1), shift(x, -1)
            seg2[even, 0:256] = (before * win[2:3, 0:256]).astype(BF16)
            seg2[even, 256:512] = (x * win[2:3, 256:512]).astype(BF16)
            seg2[odd, 0:128] = (before[:, 128:] * win[2:3, 0:128]).astype(BF16)
            seg2[odd, 128:384] = (x * win[2:3, 128:384]).astype(BF16)
            seg2[odd, 384:512] = (after[:, :128] * win[2:3, 384:512]).astype(BF16)
        for level in range(2):
            seg, table, chunks = ((seg1, a1_v, CHUNKS1), (seg2, a2_v, CHUNKS2))[level]
            d_o, q_o = ((d1_o, q1_o), (d2_o, q2_o))[level]
            copies[5 + level].wait()
            sums = [jnp.zeros((OWN, 128), F32) for _ in range(3)]
            for c in range(chunks):
                spectra = mm(seg[...], table[:, 256 * c : 256 * (c + 1)])
                for sub in range(level + 1):
                    rows_p = slice(ROWS * sub, ROWS * (sub + 1))
                    base = ROWS * (level + 1)
                    rows_g = slice(base + ROWS * sub, base + ROWS * (sub + 1))
                    sp, sg = spectra[rows_p], spectra[rows_g]
                    diff = sp - sg
                    pr, pi, gr, gi = sp[:, :128], sp[:, 128:], sg[:, :128], sg[:, 128:]
                    power_p, power_g = pr * pr + pi * pi, gr * gr + gi * gi
                    gap = jnp.log1p(power_p) - jnp.log1p(power_g)
                    slope = jnp.where(valid, 4.0 * gap / (1.0 + power_p), 0.0)
                    d_o[rows_p, 256 * c : 256 * (c + 1)] = jnp.where(valid, diff, 0.0)
                    q_o[rows_p, 256 * c : 256 * c + 128] = slope * pr
                    q_o[rows_p, 256 * c + 128 : 256 * (c + 1)] = slope * pi
                    dr, di = diff[own, :128], diff[own, 128:]
                    sums[0] = sums[0] + dr * dr + di * di
                    sums[1] = sums[1] + power_g[own]
                    sums[2] = sums[2] + gap[own] * gap[own]
            for i in range(3):
                total = jnp.sum(jnp.sum(sums[i], axis=0, keepdims=True), axis=1, keepdims=True)
                stat_o[3 * level + i : 3 * level + i + 1, :] = jnp.broadcast_to(total, (1, 128))
        stat_o[6:8, :] = jnp.zeros((2, 128), F32)
        for share in shares:
            share.start()
        slots[tm] = stat_o[...]

        copies[7].wait()
        copies[8].wait()
        normed = y1_o[own, :].astype(BF16)
        onorm = y2_o[own, :].astype(BF16)
        for c in range(2):
            nrm_o[c] = mm_bt(pick_n[c], normed)
            onm_o[c] = mm_bt(pick_n[c], onorm)
            for h in range(2):
                out = slice(576 * h, 576 * (h + 1))
                hid_o[c, out, :] = mm_bt(pick_h[c], hid_v[own, 1152 * h : 1152 * (h + 1)])
        for i in (0, 2, 1):
            give(i)
        copies[9].wait()

    pl.run_scoped(
        forward,
        *vmem([full(*shape, dtype=BF16) for shape in (BIG[0], BIG[7], BIG[8])]),
        pltpu.VMEM((ROWS, HOP), F32),
        pltpu.VMEM((ROWS, 2), F32),
        pltpu.VMEM((ROWS, 1152), F32),
        pltpu.VMEM((ROWS, WIDE1), BF16),
        pltpu.VMEM((2 * ROWS, NFFT), BF16),
        pltpu.VMEM((4 * ROWS, NFFT // 2), BF16),
    )

    def need(*which):
        for i in which:
            pairs[i].wait_recv()

    def lhs(i):
        return jnp.concatenate([here[i][core], there[i][...]], axis=1).astype(BF16)

    def rhs(i, cols):
        return jnp.concatenate([here[i][:, cols], there[i][:, cols]], axis=0).astype(BF16)

    def head_block(onorm, block):
        return mm(onorm, rhs(5, slice(128 * block, 128 * (block + 1))))

    def around(axis):
        i = spot[axis]
        return i, lax.rem(i + 1, 4), lax.rem(i + 2, 4), lax.rem(i + 3, 4)

    def backward(*parts):
        sent = [{}, {}, {}]

        def go(src, dst, k, slot, axis, by):
            sent[k][slot] = remote(src, dst, send.at[k, slot], recv.at[k, slot], device(axis, by))
            sent[k][slot].start()

        low, high = pl.ds(0, 2), pl.ds(2, 2)

        def phase1(k, s):
            axis, p = ORDERS[k][0], parts[k]
            i, right, opposite, left = around(axis)
            first, end = RANGES[k][s]
            rows = pl.ds(first, end - first)
            go(p.at[opposite, low, rows], through[k].at[0, :, rows], k, 6 * s, axis, 1)
            go(p.at[opposite, high, rows], through[k].at[1, :, rows], k, 6 * s + 1, axis, 3)
            go(p.at[right, high, rows], from_left[k].at[high, rows], k, 6 * s + 2, axis, 1)
            go(p.at[left, low, rows], from_right[k].at[low, rows], k, 6 * s + 3, axis, 3)

        def combine(k, s):
            axis, p = ORDERS[k][0], parts[k]
            i, right, opposite, left = around(axis)
            first, end = RANGES[k][s]
            rows = pl.ds(first, end - first)
            sent[k][6 * s].wait_recv()
            p[right, low, rows] += through[k][0, :, rows]
            go(p.at[right, low, rows], from_left[k].at[low, rows], k, 6 * s + 4, axis, 1)
            sent[k][6 * s + 1].wait_recv()
            p[left, high, rows] += through[k][1, :, rows]
            go(p.at[left, high, rows], from_right[k].at[high, rows], k, 6 * s + 5, axis, 3)

        def phase2(k, s):
            mine, axis, p, g = spot[ORDERS[k][0]], ORDERS[k][1], parts[k], got2[k]
            i, right, opposite, left = around(axis)
            first, end = RANGES[k][s]
            rows = pl.ds(first, end - first)
            upper, lower = halves_of(first, end)
            slot = 18 + 6 * s
            for j in (2, 3, 4, 5):
                sent[k][6 * s + j].wait_recv()

            def add(j):
                p[mine, j, rows] += from_left[k][j, rows] + from_right[k][j, rows]

            add(opposite)
            go(p.at[mine, opposite, upper], g.at[0, upper], k, slot, axis, 1)
            go(p.at[mine, opposite, lower], g.at[0, lower], k, slot + 1, axis, 3)
            add(right)
            go(p.at[mine, right, lower], g.at[1, lower], k, slot + 2, axis, 1)
            add(left)
            go(p.at[mine, left, upper], g.at[2, upper], k, slot + 3, axis, 3)
            add(i)

        def forward2(k, s):
            mine, axis, p, g = spot[ORDERS[k][0]], ORDERS[k][1], parts[k], got2[k]
            i, right, opposite, left = around(axis)
            upper, lower = halves_of(*RANGES[k][s])
            slot = 18 + 6 * s
            sent[k][slot].wait_recv()
            p[mine, right, upper] += g[0, upper]
            go(p.at[mine, right, upper], g.at[1, upper], k, slot + 4, axis, 1)
            sent[k][slot + 1].wait_recv()
            p[mine, left, lower] += g[0, lower]
            go(p.at[mine, left, lower], g.at[2, lower], k, slot + 5, axis, 3)

        for share in shares:
            share.wait_recv()
        total = slots[0]
        for j in range(1, 8):
            total = total + slots[j]

        factor = loss_scale[...] * (0.5 / CLIPS)
        loss = jnp.zeros((1, 1), F32)
        cots = []
        for level in range(2):
            count = ((FRAMES * 513), (2 * FRAMES * 257))[level]
            sum_a = total[3 * level : 3 * level + 1, 0:1]
            sum_b = total[3 * level + 1 : 3 * level + 2, 0:1]
            sum_g = total[3 * level + 2 : 3 * level + 3, 0:1]
            root_a, root_b = jnp.sqrt(sum_a + 1e-6), jnp.sqrt(sum_b + 1e-6)
            loss = loss + root_a / root_b + sum_g * (1.0 / count)
            cots.append((factor / (root_a * root_b), factor * (1.0 / count)))
        loss = jnp.where(lax.axis_index("tm") == 0, loss, 0.0)

        dx = jnp.zeros((ROWS, HOP), F32)
        ds1 = (cots[0][0] * d1_o[...] + cots[0][1] * q1_o[...]).astype(BF16)
        for p in range(4):
            at = slice(HOP * p, HOP * (p + 1))
            piece = mm_bt(ds1, a1_v[at, :]).astype(BF16).astype(F32) * win[0:1, at]
            dx = dx + shift(piece, p - 2)
        ds2 = (cots[1][0] * d2_o[...] + cots[1][1] * q2_o[...]).astype(BF16)
        dseg = mm_bt(ds2, a2_v[...]).astype(BF16).astype(F32) * win[2:3, : NFFT // 2]
        even, odd = dseg[:ROWS], dseg[ROWS:]
        dx = dx + shift(even[:, :256], -1) + even[:, 256:] + odd[:, 128:384]
        dx = dx + jnp.concatenate([shift(odd[:, 384:], 1), shift(odd[:, :128], -1)], axis=1)
        dx = jnp.where(valid, dx / envelope(places, win), 0.0)
        for p in range(4):
            piece = jnp.where(valid, shift(dx, 2 - p), 0.0)
            dfr[:, HOP * p : HOP * (p + 1)] = piece.astype(BF16)

        for c in range(CHUNKS1):
            dsp = mm_bt(dfr[...], syn_v[256 * c : 256 * (c + 1), :]).astype(BF16).astype(F32)
            dre, dim = dsp[:, :128], dsp[:, 128:]
            re, im = re_o[:, 128 * c : 128 * (c + 1)], im_o[:, 128 * c : 128 * (c + 1)]
            dlog, dph = dre * re + dim * im, dim * re - dre * im
            if c < 4:
                dhead[:, 128 * c : 128 * (c + 1)] = dlog.astype(BF16)
            dphase[:, 128 * c : 128 * (c + 1)] = dph
        moved = pltpu.roll(dphase[...], 1, 1)
        dhead[:, 512:640] = (moved[:, :128] + dlog).astype(BF16)
        dhead[:, 640:] = moved[:, 128:].astype(BF16)
        dhd_o[...] = dhead[own, :].astype(F32)
        give(5)
        don = mm(dhead[:, :1026], head_v[...]).astype(BF16).astype(F32)
        dstream = norm_back(don, y2_o[...], rstd_o[:, 2:3])

        scale_grad = jnp.sum(dstream[own] * down_o[own, :], axis=0, keepdims=True)
        ddn = (scale * dstream).astype(BF16)
        ddn_o[...] = ddn[own].astype(F32)
        give(4)
        for c in range(FF // 256):
            at = slice(256 * c, 256 * (c + 1))
            dh = mm_bt(ddn, down_v[at, :]).astype(BF16).astype(F32)
            dup[:, at] = (dh * gp_o[:, at]).astype(BF16)
        dup_o[...] = dup[own, :].astype(F32)
        give(3)

        need(2, 5)
        onorm = [lhs(2)]
        onorm += [mm(turn[...], onorm[0]).astype(BF16) for turn in (turn1, turn2)]
        for k in range(3):
            start, blocks = BLOCKS[k][0][1:3]
            for b in range(blocks):
                put(parts[k], 24 * b, head_block(onorm[k], start + b), 24)
        phase1(0, 0)
        phase1(2, 0)
        need(1, 4)
        hidden = lhs(1)
        for c in range(3):
            put(parts[1], 48 + 144 * c, mm(hidden, rhs(4, slice(256 * c, 256 * (c + 1)))), 72)
            if c == 1:
                phase1(1, 0)
        phase1(1, 1)

        dnorm = mm_bt(dup[...], up_v[...]).astype(BF16).astype(F32)
        dmix = norm_back(dnorm, y1_o[...], rstd_o[:, 1:2])
        dmix = jnp.where(valid, dmix, 0.0)
        y0 = sin_o[...]
        dsin = dstream
        small[...] = jnp.zeros((128, D), F32)
        for k in range(7):
            dsin = dsin + kern[k : k + 1, :] * shift(dmix, k - 3)
            taps = dmix * shift(y0, 3 - k)
            small[2 + k : 3 + k, :] = jnp.sum(taps[own], axis=0, keepdims=True)
        demb = norm_back(dsin, y0, rstd_o[:, 0:1])
        dem_o[...] = demb[own].astype(BF16).astype(F32)
        give(6)

        small[9:10, :] = scale_grad
        rest = loss
        for i, grid in enumerate((65536.0, 1.0, 1.0 / 65536.0, 1.0 / 65536.0 / 65536.0)):
            piece = jnp.floor(rest * (1.0 / grid)) * grid
            rest = rest - piece
            small[10 + i : 11 + i, :] = jnp.broadcast_to(piece, (1, D))

        small0 = small[...].astype(BF16)
        rest = small[...] - small0.astype(F32)
        small1 = rest.astype(BF16)
        small2 = (rest - small1.astype(F32)).astype(BF16)
        for c in range(2):
            kg_o[c] = sum(mm_bt(pick_k[c], part) for part in (small0, small1, small2))
        give(7)

        combine(0, 0)
        combine(2, 0)
        need(8, 6)
        both_ids = jnp.concatenate([ids[...], there[8][...]], axis=1)
        code_rows = row_id[...] + OWN * core
        hot = (code_rows == both_ids[0:1, :]) | (code_rows == both_ids[1:2, :] + 1024)
        hot = jnp.where(hot, 1.0, 0.0).astype(BF16)
        put(parts[2], 72, mm(hot, rhs(6, slice(0, 384))), 64)
        phase1(2, 1)
        need(7)
        put(parts[2], 264, mm(hot, rhs(6, slice(384, 768))), 64)
        put(parts[2], 456, head_block(onorm[2], 8) + here[7][core] + there[7][...], 24)
        phase1(2, 2)
        need(0, 3)
        normed = lhs(0)
        for c in range(5):
            put(parts[0], 72 + 72 * c, mm(normed, rhs(3, slice(384 * c, 384 * (c + 1)))), 24)
            if c == 2:
                phase1(0, 1)
        phase1(0, 2)
        normed = mm(turn1[...], normed).astype(BF16)
        put(parts[1], 480, mm(normed, rhs(3, slice(1920, 2304))), 24)
        phase1(1, 2)
        phase2(0, 0)
        phase2(2, 0)
        combine(1, 0)
        forward2(0, 0)
        forward2(2, 0)
        combine(2, 1)
        combine(0, 1)
        combine(1, 1)
        phase2(1, 0)
        combine(2, 2)
        combine(0, 2)
        combine(1, 2)
        phase2(2, 1)
        phase2(0, 1)
        forward2(1, 0)
        phase2(1, 1)
        forward2(2, 1)
        forward2(0, 1)
        phase2(2, 2)
        phase2(0, 2)
        phase2(1, 2)
        for k, t in ((1, 1), (2, 2), (0, 2), (1, 2)):
            forward2(k, t)
        for k in (1, 2, 0):
            mine = spot[ORDERS[k][0]]
            i = spot[ORDERS[k][1]]
            p, g, out = parts[k], got2[k], last[k]
            for t in range(3):
                for j in (2, 3, 4, 5):
                    sent[k][18 + 6 * t + j].wait_recv()
            p[mine, i] += g[1] + g[2]
            start, place = 0, 0
            for _, _, count, rows in BLOCKS[k]:
                each = rows // 4
                for _ in range(count):
                    for d in range(4):
                        out[d, pl.ds(place, each)] = p[mine, i, pl.ds(start + d * each, each)]
                    start += rows
                    place += each
            if place < LAST_ROWS[k]:
                for d in range(4):
                    out[d, pl.ds(place, LAST_ROWS[k] - place)] = jnp.zeros(
                        (LAST_ROWS[k] - place, 128), F32
                    )
            axis = ORDERS[k][2]
            for by in (1, 2, 3):
                to = lax.rem(spot[axis] + by, 4)
                go(out.at[to], got3[k].at[by - 1], k, 35 + by, axis, by)
        for k in (1, 2, 0):
            for j in (36, 37, 38):
                sent[k][j].wait_recv()
            total = last[k][spot[ORDERS[k][2]]] + got3[k][0] + got3[k][1] + got3[k][2]
            out_o[pl.ds(FIRST_ROWS[k], LAST_ROWS[k]), :] = total
        for copy in halo + shares + pairs:
            copy.wait_send()
        for k in range(3):
            for copy in sent[k].values():
                copy.wait_send()

    pl.run_scoped(backward, *[pltpu.VMEM((4, 4, n, 128), F32) for n in PART_ROWS])


BIG = (
    (2 * FRAMES, D), (D, FF), (FF, D), (2 * 513, D), (WIDE1, NFFT), (NFFT, WIDE1),
    (NFFT // 2, WIDE2), (2, 384, D), (2, 576, FF // 2), (2, 384, D),
)


def step_call(small, big):
    wide = [full(*((2,) if p else ()), *a.shape) for a, p in zip(OPERANDS, PICKED)]
    edge = full(1, HALO * HOP)
    rows = PART_ROWS

    def each(make):
        return [pltpu.VMEM(make(k), F32) for k in range(3)]

    return pl.pallas_call(
        step_kernel,
        out_shape=full(sum(LAST_ROWS), 128),
        in_specs=[spec(pltpu.VMEM)] * len(small) + [spec(pl.ANY)] * len(big),
        out_specs=spec(pltpu.VMEM),
        scratch_shapes=vmem([full(*BIG[i], dtype=BF16) for i in (1, 2, 3, 4, 5, 6, 9)])
        + vmem(SAVED)
        + vmem(wide)
        + vmem([*OPERANDS, IDS])
        + vmem([edge, edge, IDS, IDS])
        + [
            pltpu.VMEM((ROWS, FF), BF16),
            pltpu.VMEM((8, 128), F32),
            pltpu.VMEM((8, 8, 128), F32),
            pltpu.VMEM((ROWS, NFFT), BF16),
            pltpu.VMEM((ROWS, CHUNKS1 * 128), F32),
            pltpu.VMEM((ROWS, 1152), BF16),
            pltpu.VMEM((ROWS, FF), BF16),
            pltpu.VMEM((128, D), F32),
        ]
        + each(lambda k: (2, 2, rows[k], 128))
        + each(lambda k: (4, rows[k], 128))
        + each(lambda k: (4, rows[k], 128))
        + each(lambda k: (3, rows[k], 128))
        + each(lambda k: (4, LAST_ROWS[k], 128))
        + each(lambda k: (3, LAST_ROWS[k], 128))
        + [pltpu.SemaphoreType.DMA((n,)) for n in (len(big), 4, 4, 7, 7, 9, 9)]
        + [pltpu.SemaphoreType.DMA((3, 39))] * 2,
        compiler_params=pltpu.CompilerParams(
            collective_id=0, has_side_effects=True, vmem_limit_bytes=64 * MB
        ),
        name="train_step",
    )(*small, *big)


def finish_kernel(sums, loss_o, table_o, kern_o, up_o, down_o, scale_o, head_o):
    outs = {"up": up_o, "down": down_o, "table": table_o, "head": head_o}
    for k in range(3):
        rows = FIRST_ROWS[k]
        for name, start, count, block in BLOCKS[k]:
            for c in range(start, start + count):
                values = sums[rows : rows + block // 4, :]
                rows += block // 4
                if (name, c) != ("head", 8):
                    outs[name][:, 128 * c : 128 * (c + 1)] = values
                    continue
                head_o[:, 1024:1026] = values[:, 0:2]
                tail = jnp.transpose(jnp.concatenate([values, jnp.zeros((122, 128), F32)], axis=0))
                kern_o[...] = tail[2:9, 0:6]
                scale_o[...] = tail[9:10, 0:6]
                pieces = values[0:1, 10:14]
                loss_o[...] = jnp.sum(pieces, axis=1, keepdims=True) * (0.5 / CLIPS)


def finish_call(sums):
    loss, table, kern, up, down, scale, head = pl.pallas_call(
        finish_kernel,
        out_shape=[
            full(1, 1), full(16, D), full(7, 6), full(6, FF), full(18, D), full(1, 6), full(6, 1026),
        ],
        in_specs=[spec(pltpu.VMEM)],
        out_specs=[spec(pltpu.VMEM)] * 7,
        name="finish",
    )(sums)
    return loss.reshape(()), table, kern, up, down, scale.reshape(6), head


def body(
    code_ids, code_table, kernel, up_weight, down_weight, layer_scale, head_weight, target, loss_scale
):
    syn, a1, a2, win = make_constants()
    pick_n, pick_h, pick_k, turn1, turn2, row_id = make_orders()
    ids = jnp.swapaxes(code_ids, 1, 2).reshape(2, OWN)
    head_t = head_weight.T
    sums = step_call(
        (target, ids, kernel, layer_scale, win, loss_scale.reshape(1, 1), turn1, turn2, row_id),
        (
            code_table, up_weight, down_weight, head_t, syn, a1, a2, pick_n, pick_h, pick_k,
        ),
    )
    return finish_call(sums)


def solution(mesh):
    in_specs = (P("dp", "tm", None), P(), P(), P(), P(), P(), P(), P("dp", "tm"), P())
    out_specs = (
        P(),
        P(("dp", "tm"), None),
        P(None, ("dp", "tm")),
        P(("dp", "tm"), None),
        P(("dp", "tm"), None),
        P(("dp", "tm")),
        P(("dp", "tm"), None),
    )
    return jax.shard_map(body, mesh=mesh, in_specs=in_specs, out_specs=out_specs, check_vma=False)
```

```python
import jax
import jax.numpy as jnp
import ml_dtypes
import numpy as np
from jax import lax
from jax.experimental import pallas as pl
from jax.experimental.pallas import tpu as pltpu
from jax.sharding import PartitionSpec as P

F32, BF16 = jnp.float32, jnp.bfloat16
MESH = pl.DeviceIdType.MESH
D, FF = 768, 2304
HOP, NFFT = 256, 1024
FRAMES, OWN, HALO = 1024, 128, 16
ROWS = OWN + 2 * HALO
CHUNKS1, CHUNKS2 = 5, 3
WIDE1, WIDE2 = CHUNKS1 * 256, CHUNKS2 * 256
CLIPS = 16
MB = 1 << 20
ORDERS = ("xyz", "yzx", "zxy")
BLOCKS = (
    (("head", 0, 3, 24), ("up", 0, 15, 24)),
    (("head", 3, 2, 24), ("down", 0, 6, 72), ("up", 15, 3, 24)),
    (("head", 5, 4, 24), ("table", 0, 6, 64)),
)
RANGES = (((0, 72), (72, 432)), ((0, 480), (480, 552)), ((0, 72), (72, 480)))
PART_ROWS = (432, 552, 480)
LAST_ROWS = (112, 144, 120)
FIRST_ROWS = (0, 112, 256)


def bf(array):
    return np.asarray(array, np.float32).astype(ml_dtypes.bfloat16)


def hann(length):
    return 0.5 - 0.5 * np.cos(2.0 * np.pi * np.arange(length) / length)


def angles(length):
    product = np.arange(length // 2 + 1)[:, None] * np.arange(length)[None, :] % length
    return 2.0 * np.pi * product / length


def interleave(real, imag, chunks):
    bins, width = real.shape
    out = np.zeros((chunks, 2, 128, width), np.float64)
    for half, part in enumerate((real, imag)):
        padded = np.zeros((chunks * 128, width), np.float64)
        padded[:bins] = part
        out[:, half] = padded.reshape(chunks, 128, width)
    return out.reshape(chunks * 256, width)


def make_constants():
    ang = angles(NFFT)
    bins = np.arange(NFFT // 2 + 1)
    factor = np.where((bins == 0) | (bins == NFFT // 2), 1.0, 2.0)[:, None] / NFFT
    window = hann(NFFT)[None, :]
    synthesis = bf(interleave(factor * np.cos(ang) * window, -factor * np.sin(ang) * window, CHUNKS1))
    analysis1 = bf(interleave(np.cos(ang), -np.sin(ang), CHUNKS1).T)
    ang = angles(NFFT // 2)
    analysis2 = bf(interleave(np.cos(ang), -np.sin(ang), CHUNKS2).T)
    win = np.zeros((8, NFFT), np.float32)
    win[0] = hann(NFFT)
    win[1] = hann(NFFT) ** 2
    win[2, : NFFT // 2] = hann(NFFT // 2)
    return synthesis, analysis1, analysis2, win


def device_index(x, y, z, core):
    return ((y * 2 + z // 2) * 2 + core) * 8 + x * 2 + z % 2


def shard_order(order, core):
    places = []
    for a in range(4):
        for b in range(4):
            for c in range(4):
                at = dict(zip(order, (a, b, c)))
                places.append(device_index(at["x"], at["y"], at["z"], core))
    return np.array(places)


def columns_of(order, core, each):
    return (shard_order(order, core)[:, None] * each + np.arange(each)[None, :]).reshape(-1)


def one_hot_columns(sources, size):
    out = np.zeros((size, sources.size), np.float32)
    out[sources, np.arange(sources.size)] = 1.0
    return bf(out)


def make_orders():
    pick_n = np.stack([one_hot_columns(columns_of(ORDERS[0], c, 6), D).T for c in (0, 1)])
    half = [columns_of(ORDERS[1], c, 18)[: 4 * 4 * 2 * 18] for c in (0, 1)]
    pick_h = np.stack([one_hot_columns(h, FF // 2).T for h in half])
    pick_k = np.stack([one_hot_columns(columns_of(ORDERS[2], c, 6), D).T for c in (0, 1)])
    first = columns_of(ORDERS[0], 0, 6)
    where = {col: i for i, col in enumerate(first)}
    turns = []
    for k in (1, 2):
        sources = np.array([where[col] for col in columns_of(ORDERS[k], 0, 6)])
        turns.append(one_hot_columns(sources, 384).T)
    row_id = columns_of(ORDERS[2], 0, 16).astype(np.int32)[:, None]
    return pick_n, pick_h, pick_k, turns[0], turns[1], row_id


def mm(a, b):
    return jnp.dot(a, b, preferred_element_type=F32)


def mm_bt(a, b):
    return lax.dot_general(a, b, (((1,), (1,)), ((), ())), preferred_element_type=F32)


def mm_at(a, b):
    return lax.dot_general(a, b, (((0,), (0,)), ((), ())), preferred_element_type=F32)


def shift(values, by):
    by = by % values.shape[0]
    return values if by == 0 else pltpu.roll(values, by, 0)


def norm(values):
    centre = values - jnp.mean(values, axis=-1, keepdims=True)
    rstd = lax.rsqrt(jnp.mean(centre * centre, axis=-1, keepdims=True) + 1e-6)
    return centre * rstd, rstd


def norm_back(grad, y, rstd):
    mean_g = jnp.mean(grad, axis=-1, keepdims=True)
    mean_gy = jnp.mean(grad * y, axis=-1, keepdims=True)
    return rstd * (grad - mean_g - y * mean_gy)


def frame_places():
    first = lax.axis_index("tm") * OWN - HALO
    return (lax.broadcasted_iota(jnp.int32, (ROWS, 1), 0) + first).astype(F32)


def sin_cos(x):
    turns = jnp.round(x * 0.6366197723675814)
    r = x - turns * 1.5703125
    r = r - turns * 4.837512969970703125e-4
    r = r - turns * 7.549789954891882e-8
    z = r * r
    sine = r + r * z * (-1.6666654611e-1 + z * (8.3321608736e-3 + z * -1.9515295891e-4))
    cosine = (4.166664568298827e-2 + z * (-1.388731625493765e-3 + z * 2.443315711809948e-5)) * (z * z)
    cosine = cosine - 0.5 * z + 1.0
    quarter = turns.astype(jnp.int32)
    odd = (quarter & 1) == 1
    first, second = jnp.where(odd, cosine, sine), jnp.where(odd, sine, cosine)
    first = jnp.where((quarter & 2) == 2, -first, first)
    second = jnp.where(((quarter + 1) & 2) == 2, -second, second)
    return first, second


def inside(places):
    return (places >= 0.0) & (places < float(FRAMES))


def envelope(places, win):
    total = jnp.zeros((ROWS, HOP), F32)
    for p in range(4):
        total = total + jnp.where(inside(places + float(2 - p)), win[1:2, HOP * p : HOP * (p + 1)], 0.0)
    return jnp.where(inside(places), total, 1.0)


def spec(space):
    return pl.BlockSpec(memory_space=space)


def full(*shape, dtype=F32):
    return jax.ShapeDtypeStruct(shape, dtype)


def ids_column(ids):
    padded = jnp.concatenate([ids.astype(F32), jnp.zeros((126, OWN), F32)], axis=0)
    return jnp.transpose(padded)[:, :2]


OPERANDS = (
    full(384, OWN), full(1152, OWN), full(384, OWN), full(OWN, FF), full(OWN, D),
    full(OWN, 1152), full(OWN, D), full(384, 128),
)
PICKED = (True, True, True, False, False, False, False, True)
IDS = full(2, OWN, dtype=jnp.int32)
SAVED = (
    full(ROWS, D), full(ROWS, 128), full(ROWS, D), full(ROWS, FF),
    full(ROWS, D), full(ROWS, D), full(ROWS, CHUNKS1 * 128), full(ROWS, CHUNKS1 * 128),
    full(ROWS, WIDE1), full(ROWS, WIDE1), full(2 * ROWS, WIDE2), full(2 * ROWS, WIDE2),
)


def vmem(shapes):
    return [pltpu.VMEM(a.shape, a.dtype) for a in shapes]


def put(out, first, values, rows):
    for block in range(values.shape[1] // 128):
        part = values[:, 128 * block : 128 * (block + 1)].reshape(4, 4, rows, 128)
        out[:, :, first + rows * block : first + rows * (block + 1), :] = part


def halves_of(rows):
    upper = (rows // 2 + 7) // 8 * 8
    return pl.ds(0, upper), pl.ds(upper, rows - upper)


def step_kernel(target, ids, kern, scale_i, win, loss_scale, turn1, turn2, row_id, *refs):
    big_h, out_o, refs = refs[:10], refs[10], refs[11:]
    (up_v, down_v, head_v, syn_v, a1_v, a2_v, pick_k), refs = refs[:7], refs[7:]
    (sin_o, rstd_o, y1_o, gp_o, down_o, y2_o, re_o, im_o, d1_o, q1_o, d2_o, q2_o) = refs[:12]
    refs = refs[12:]
    here, there, refs = refs[:8], refs[8:17], refs[17:]
    (nrm_o, hid_o, onm_o, dup_o, ddn_o, dhd_o, dem_o, kg_o) = here
    (left_t, right_t, left_i, right_i, hid_v, stat_o, slots), refs = refs[:7], refs[7:]
    (dfr, dphase, dhead, dup, small), refs = refs[:5], refs[5:]
    through, from_left, from_right, got2a, got2b, last, got3 = (
        refs[3 * i : 3 * i + 3] for i in range(7)
    )
    (
        sems, halo_send, halo_recv, stat_send, stat_recv, pair_send, pair_recv, send, recv,
    ) = refs[21:]

    dp, tm = lax.axis_index("dp"), lax.axis_index("tm")
    core = lax.rem(dp, 2)
    other = 1 - core
    partner = {"dp": dp + 1 - 2 * core, "tm": tm}
    others = [{"dp": dp, "tm": lax.rem(tm + j, 8)} for j in range(1, 8)]
    spot = {"x": tm // 2, "y": dp // 4, "z": lax.rem(dp // 2, 2) * 2 + lax.rem(tm, 2)}

    def device(axis, by):
        to = dict(spot)
        to[axis] = lax.rem(spot[axis] + by, 4)
        return {
            "dp": (to["y"] * 2 + to["z"] // 2) * 2 + core,
            "tm": to["x"] * 2 + lax.rem(to["z"], 2),
        }

    barrier = pltpu.get_barrier_semaphore()
    around_me = [device(axis, by) for axis in "xyz" for by in (1, 2, 3)]
    for place in others + [partner] + around_me:
        pl.semaphore_signal(barrier, inc=1, device_id=place, device_id_type=MESH)

    def remote(src, dst, send, recv, place):
        return pltpu.make_async_remote_copy(
            src_ref=src, dst_ref=dst, send_sem=send, recv_sem=recv,
            device_id=place, device_id_type=MESH,
        )

    edge = HALO * HOP
    right, left = others[0], others[6]
    halo = [
        remote(src, dst, halo_send.at[i], halo_recv.at[i], place)
        for i, (src, dst, place) in enumerate(
            (
                (ids, left_i, right),
                (ids, right_i, left),
                (target.at[:, pl.ds(OWN * HOP - edge, edge)], left_t, right),
                (target.at[:, pl.ds(0, edge)], right_t, left),
            )
        )
    ]
    shares = [
        remote(stat_o, slots.at[tm], stat_send.at[j], stat_recv.at[j], place)
        for j, place in enumerate(others)
    ]
    pairs = [
        remote(ref.at[other] if picked else ref, there[i], pair_send.at[i], pair_recv.at[i], partner)
        for i, (ref, picked) in enumerate(zip((*here, ids), (*PICKED, False)))
    ]

    def give(i):
        pairs[i].start()

    own = slice(HALO, HALO + OWN)
    scale = scale_i[...].reshape(1, D)
    places = frame_places()
    valid = inside(places)

    def forward(table_v, pick_n, pick_h, goal, codes, head_s, spec_v, seg1, seg2):
        big_v = (table_v, up_v, down_v, head_v, syn_v, a1_v, a2_v, pick_n, pick_h, pick_k)
        copies = [
            pltpu.make_async_copy(h, v, sems.at[i]) for i, (h, v) in enumerate(zip(big_h, big_v))
        ]
        for copy in copies:
            copy.start()
        pl.semaphore_wait(barrier, 17)
        for copy in halo:
            copy.start()
        give(8)
        codes[HALO : HALO + OWN, :] = ids_column(ids[...])
        for source, first, count in (
            (target, HALO, OWN), (left_t, 0, HALO), (right_t, HALO + OWN, HALO),
        ):
            if source is left_t:
                for copy in halo:
                    copy.wait_recv()
            for r in range(count):
                goal[first + r : first + r + 1, :] = source[:, HOP * r : HOP * (r + 1)]
        codes[0:HALO, :] = ids_column(left_i[...])[OWN - HALO :]
        codes[HALO + OWN :, :] = ids_column(right_i[...])[:HALO]
        lane = lax.broadcasted_iota(jnp.int32, (ROWS, 2 * FRAMES), 1).astype(F32)
        hot = (lane == codes[:, 0:1]) | (lane == codes[:, 1:2] + 1024.0)
        hot = jnp.where(hot, 1.0, 0.0).astype(BF16)
        copies[0].wait()
        y0, rstd0 = norm(mm(hot, table_v[...]))
        y0 = jnp.where(valid, y0, 0.0)
        sin_o[...] = y0
        mixture = kern[0:1, :] * shift(y0, 3)
        for k in range(1, 7):
            mixture = mixture + kern[k : k + 1, :] * shift(y0, 3 - k)
        y1, rstd1 = norm(mixture)
        y1_o[...] = y1
        normed = y1.astype(BF16)
        copies[1].wait()
        for c in range(FF // 256):
            at = slice(256 * c, 256 * (c + 1))
            up = mm(normed, up_v[:, at])
            cdf = 0.5 * (1.0 + lax.erf(up * 0.7071067811865476))
            hid_v[:, at] = (up * cdf).astype(BF16)
            gp_o[:, at] = cdf + up * (0.3989422804014327 * jnp.exp(-0.5 * up * up))
        copies[2].wait()
        down = mm(hid_v[...], down_v[...])
        down_o[...] = down
        y2, rstd2 = norm(y0 + scale * down)
        y2_o[...] = y2
        places128 = lax.broadcasted_iota(jnp.int32, (ROWS, 128), 1)
        rstd_o[...] = jnp.where(places128 == 0, rstd0, jnp.where(places128 == 1, rstd1, rstd2))
        onorm = y2.astype(BF16)
        copies[3].wait()
        head_s[:, 1024:] = jnp.zeros((ROWS, 128), F32)
        for c in range(4):
            head_s[:, 256 * c : 256 * (c + 1)] = mm_bt(onorm, head_v[256 * c : 256 * (c + 1), :])
        head_s[:, 1024:1026] = mm_bt(onorm, head_v[1024:1026, :])
        phases = pltpu.roll(head_s[:, 512:], CHUNKS1 * 128 - 1, 1)
        for c in range(CHUNKS1):
            logmag = head_s[:, 128 * c : 128 * (c + 1)]
            if c == 4:
                logmag = jnp.where(places128 == 0, logmag, 0.0)
            mag = jnp.exp(logmag)
            phase = phases[:, 128 * c : 128 * (c + 1)]
            sine, cosine = sin_cos(phase)
            re, im = mag * cosine, mag * sine
            re_o[:, 128 * c : 128 * (c + 1)] = re
            im_o[:, 128 * c : 128 * (c + 1)] = im
            spec_v[:, 256 * c : 256 * c + 128] = re.astype(BF16)
            spec_v[:, 256 * c + 128 : 256 * (c + 1)] = im.astype(BF16)
        copies[4].wait()
        pred = jnp.zeros((ROWS, HOP), F32)
        for p in range(4):
            piece = jnp.where(valid, mm(spec_v[...], syn_v[:, HOP * p : HOP * (p + 1)]), 0.0)
            pred = pred + shift(piece, p - 2)
        pred = jnp.where(valid, pred / envelope(places, win), 0.0)
        for s, x in enumerate((pred, jnp.where(valid, goal[...], 0.0))):
            r1 = slice(ROWS * s, ROWS * (s + 1))
            for p in range(4):
                at = slice(HOP * p, HOP * (p + 1))
                seg1[r1, at] = (shift(x, 2 - p) * win[0:1, at]).astype(BF16)
            even = slice(2 * ROWS * s, 2 * ROWS * s + ROWS)
            odd = slice(2 * ROWS * s + ROWS, 2 * ROWS * (s + 1))
            before, after = shift(x, 1), shift(x, -1)
            seg2[even, 0:256] = (before * win[2:3, 0:256]).astype(BF16)
            seg2[even, 256:512] = (x * win[2:3, 256:512]).astype(BF16)
            seg2[odd, 0:128] = (before[:, 128:] * win[2:3, 0:128]).astype(BF16)
            seg2[odd, 128:384] = (x * win[2:3, 128:384]).astype(BF16)
            seg2[odd, 384:512] = (after[:, :128] * win[2:3, 384:512]).astype(BF16)
        for level in range(2):
            seg, table, chunks = ((seg1, a1_v, CHUNKS1), (seg2, a2_v, CHUNKS2))[level]
            d_o, q_o = ((d1_o, q1_o), (d2_o, q2_o))[level]
            copies[5 + level].wait()
            sums = [jnp.zeros((OWN, 128), F32) for _ in range(3)]
            for c in range(chunks):
                for sub in range(level + 1):
                    rows_p = slice(ROWS * sub, ROWS * (sub + 1))
                    base = ROWS * (level + 1)
                    rows_g = slice(base + ROWS * sub, base + ROWS * (sub + 1))
                    weights = table[:, 256 * c : 256 * (c + 1)]
                    sp, sg = mm(seg[rows_p, :], weights), mm(seg[rows_g, :], weights)
                    diff = sp - sg
                    pr, pi, gr, gi = sp[:, :128], sp[:, 128:], sg[:, :128], sg[:, 128:]
                    power_p, power_g = pr * pr + pi * pi, gr * gr + gi * gi
                    gap = jnp.log1p(power_p) - jnp.log1p(power_g)
                    slope = jnp.where(valid, 4.0 * gap / (1.0 + power_p), 0.0)
                    d_o[rows_p, 256 * c : 256 * (c + 1)] = jnp.where(valid, diff, 0.0)
                    q_o[rows_p, 256 * c : 256 * c + 128] = slope * pr
                    q_o[rows_p, 256 * c + 128 : 256 * (c + 1)] = slope * pi
                    dr, di = diff[own, :128], diff[own, 128:]
                    sums[0] = sums[0] + dr * dr + di * di
                    sums[1] = sums[1] + power_g[own]
                    sums[2] = sums[2] + gap[own] * gap[own]
            for i in range(3):
                total = jnp.sum(jnp.sum(sums[i], axis=0, keepdims=True), axis=1, keepdims=True)
                stat_o[3 * level + i : 3 * level + i + 1, :] = jnp.broadcast_to(total, (1, 128))
        stat_o[6:8, :] = jnp.zeros((2, 128), F32)
        for share in shares:
            share.start()
        slots[tm] = stat_o[...]

        copies[7].wait()
        copies[8].wait()
        normed = y1_o[own, :].astype(BF16)
        onorm = y2_o[own, :].astype(BF16)
        for c in range(2):
            nrm_o[c] = mm_bt(pick_n[c], normed)
            onm_o[c] = mm_bt(pick_n[c], onorm)
            for h in range(2):
                out = slice(576 * h, 576 * (h + 1))
                hid_o[c, out, :] = mm_bt(pick_h[c], hid_v[own, 1152 * h : 1152 * (h + 1)])
        for i in (0, 2, 1):
            give(i)
        copies[9].wait()

    pl.run_scoped(
        forward,
        *vmem([full(*shape, dtype=BF16) for shape in (BIG[0], BIG[7], BIG[8])]),
        pltpu.VMEM((ROWS, HOP), F32),
        pltpu.VMEM((ROWS, 2), F32),
        pltpu.VMEM((ROWS, 1152), F32),
        pltpu.VMEM((ROWS, WIDE1), BF16),
        pltpu.VMEM((2 * ROWS, NFFT), BF16),
        pltpu.VMEM((4 * ROWS, NFFT // 2), BF16),
    )

    def need(*which):
        for i in which:
            pairs[i].wait_recv()

    def lhs(i):
        return jnp.concatenate([here[i][core], there[i][...]], axis=1).astype(BF16)

    def rhs(i, cols):
        return jnp.concatenate([here[i][:, cols], there[i][:, cols]], axis=0).astype(BF16)

    def head_block(onorm, block):
        return mm(onorm, rhs(5, slice(128 * block, 128 * (block + 1))))

    def around(axis):
        i = spot[axis]
        return i, lax.rem(i + 1, 4), lax.rem(i + 2, 4), lax.rem(i + 3, 4)

    def backward(*parts):
        sent = [{}, {}, {}]

        def go(src, dst, k, slot, axis, by):
            sent[k][slot] = remote(src, dst, send.at[k, slot], recv.at[k, slot], device(axis, by))
            sent[k][slot].start()

        low, high = pl.ds(0, 2), pl.ds(2, 2)

        def phase1(k, s):
            axis, p = ORDERS[k][0], parts[k]
            i, right, opposite, left = around(axis)
            first, end = RANGES[k][s]
            rows = pl.ds(first, end - first)
            go(p.at[opposite, low, rows], through[k].at[0, :, rows], k, 6 * s, axis, 1)
            go(p.at[opposite, high, rows], through[k].at[1, :, rows], k, 6 * s + 1, axis, 3)
            go(p.at[right, high, rows], from_left[k].at[high, rows], k, 6 * s + 2, axis, 1)
            go(p.at[left, low, rows], from_right[k].at[low, rows], k, 6 * s + 3, axis, 3)

        def combine(k, s):
            axis, p = ORDERS[k][0], parts[k]
            i, right, opposite, left = around(axis)
            first, end = RANGES[k][s]
            rows = pl.ds(first, end - first)
            sent[k][6 * s].wait_recv()
            p[right, low, rows] += through[k][0, :, rows]
            go(p.at[right, low, rows], from_left[k].at[low, rows], k, 6 * s + 4, axis, 1)
            sent[k][6 * s + 1].wait_recv()
            p[left, high, rows] += through[k][1, :, rows]
            go(p.at[left, high, rows], from_right[k].at[high, rows], k, 6 * s + 5, axis, 3)

        for share in shares:
            share.wait_recv()
        total = slots[0]
        for j in range(1, 8):
            total = total + slots[j]

        factor = loss_scale[...] * (0.5 / CLIPS)
        loss = jnp.zeros((1, 1), F32)
        cots = []
        for level in range(2):
            count = ((FRAMES * 513), (2 * FRAMES * 257))[level]
            sum_a = total[3 * level : 3 * level + 1, 0:1]
            sum_b = total[3 * level + 1 : 3 * level + 2, 0:1]
            sum_g = total[3 * level + 2 : 3 * level + 3, 0:1]
            root_a, root_b = jnp.sqrt(sum_a + 1e-6), jnp.sqrt(sum_b + 1e-6)
            loss = loss + root_a / root_b + sum_g * (1.0 / count)
            cots.append((factor / (root_a * root_b), factor * (1.0 / count)))
        loss = jnp.where(lax.axis_index("tm") == 0, loss, 0.0)

        dx = jnp.zeros((ROWS, HOP), F32)
        ds1 = (cots[0][0] * d1_o[...] + cots[0][1] * q1_o[...]).astype(BF16)
        for p in range(4):
            at = slice(HOP * p, HOP * (p + 1))
            piece = mm_bt(ds1, a1_v[at, :]).astype(BF16).astype(F32) * win[0:1, at]
            dx = dx + shift(piece, p - 2)
        ds2 = (cots[1][0] * d2_o[...] + cots[1][1] * q2_o[...]).astype(BF16)
        dseg = mm_bt(ds2, a2_v[...]).astype(BF16).astype(F32) * win[2:3, : NFFT // 2]
        even, odd = dseg[:ROWS], dseg[ROWS:]
        dx = dx + shift(even[:, :256], -1) + even[:, 256:] + odd[:, 128:384]
        dx = dx + jnp.concatenate([shift(odd[:, 384:], 1), shift(odd[:, :128], -1)], axis=1)
        dx = jnp.where(valid, dx / envelope(places, win), 0.0)
        for p in range(4):
            piece = jnp.where(valid, shift(dx, 2 - p), 0.0)
            dfr[:, HOP * p : HOP * (p + 1)] = piece.astype(BF16)

        for c in range(CHUNKS1):
            dsp = mm_bt(dfr[...], syn_v[256 * c : 256 * (c + 1), :]).astype(BF16).astype(F32)
            dre, dim = dsp[:, :128], dsp[:, 128:]
            re, im = re_o[:, 128 * c : 128 * (c + 1)], im_o[:, 128 * c : 128 * (c + 1)]
            dlog, dph = dre * re + dim * im, dim * re - dre * im
            if c < 4:
                dhead[:, 128 * c : 128 * (c + 1)] = dlog.astype(BF16)
            dphase[:, 128 * c : 128 * (c + 1)] = dph
        moved = pltpu.roll(dphase[...], 1, 1)
        dhead[:, 512:640] = (moved[:, :128] + dlog).astype(BF16)
        dhead[:, 640:] = moved[:, 128:].astype(BF16)
        dhd_o[...] = dhead[own, :].astype(F32)
        give(5)
        don = mm(dhead[:, :1026], head_v[...]).astype(BF16).astype(F32)
        dstream = norm_back(don, y2_o[...], rstd_o[:, 2:3])

        scale_grad = jnp.sum(dstream[own] * down_o[own, :], axis=0, keepdims=True)
        ddn = (scale * dstream).astype(BF16)
        ddn_o[...] = ddn[own].astype(F32)
        give(4)
        for c in range(FF // 256):
            at = slice(256 * c, 256 * (c + 1))
            dh = mm_bt(ddn, down_v[at, :]).astype(BF16).astype(F32)
            dup[:, at] = (dh * gp_o[:, at]).astype(BF16)
        dup_o[...] = dup[own, :].astype(F32)
        give(3)

        need(2, 5)
        onorm = [lhs(2)]
        onorm += [mm(turn[...], onorm[0]).astype(BF16) for turn in (turn1, turn2)]
        for k in range(3):
            start, blocks = BLOCKS[k][0][1:3]
            for b in range(min(blocks, 8 - start)):
                put(parts[k], 24 * b, head_block(onorm[k], start + b), 24)
        phase1(0, 0)
        phase1(2, 0)
        need(1, 4)
        hidden = lhs(1)
        for c in range(3):
            put(parts[1], 48 + 144 * c, mm(hidden, rhs(4, slice(256 * c, 256 * (c + 1)))), 72)
        phase1(1, 0)

        dnorm = mm_bt(dup[...], up_v[...]).astype(BF16).astype(F32)
        dmix = norm_back(dnorm, y1_o[...], rstd_o[:, 1:2])
        dmix = jnp.where(valid, dmix, 0.0)
        y0 = sin_o[...]
        dsin = dstream
        small[...] = jnp.zeros((16, D), F32)
        for k in range(7):
            dsin = dsin + kern[k : k + 1, :] * shift(dmix, k - 3)
            taps = dmix * shift(y0, 3 - k)
            small[2 + k : 3 + k, :] = jnp.sum(taps[own], axis=0, keepdims=True)
        demb = norm_back(dsin, y0, rstd_o[:, 0:1])
        dem_o[...] = demb[own].astype(BF16).astype(F32)
        give(6)

        small[9:10, :] = scale_grad
        rest = loss
        for i, grid in enumerate((65536.0, 1.0, 1.0 / 65536.0, 1.0 / 65536.0 / 65536.0)):
            piece = jnp.floor(rest * (1.0 / grid)) * grid
            rest = rest - piece
            small[10 + i : 11 + i, :] = jnp.broadcast_to(piece, (1, D))

        small0 = small[...].astype(BF16)
        rest = small[...] - small0.astype(F32)
        small1 = rest.astype(BF16)
        small2 = (rest - small1.astype(F32)).astype(BF16)
        pieces = jnp.concatenate([small0, small1, small2], axis=0)
        for c in range(2):
            picked = mm_bt(pieces, pick_k[c])
            picked = picked[0:16] + picked[16:32] + picked[32:48]
            picked = jnp.concatenate([picked, jnp.zeros((112, 384), F32)], axis=0)
            kg_o[c] = jnp.transpose(picked)
        give(7)

        combine(0, 0)
        combine(2, 0)
        need(8, 6)
        both_ids = jnp.concatenate([ids[...], there[8][...]], axis=1)
        code_rows = row_id[...] + OWN * core
        hot = (code_rows == both_ids[0:1, :]) | (code_rows == both_ids[1:2, :] + 1024)
        hot = jnp.where(hot, 1.0, 0.0).astype(BF16)
        for c in range(3):
            put(parts[2], 96 + 128 * c, mm(hot, rhs(6, slice(256 * c, 256 * (c + 1)))), 64)
        need(7)
        put(parts[2], 72, head_block(onorm[2], 8) + here[7][core] + there[7][...], 24)
        phase1(2, 1)
        need(0, 3)
        normed = lhs(0)
        for c in range(5):
            put(parts[0], 72 + 72 * c, mm(normed, rhs(3, slice(384 * c, 384 * (c + 1)))), 24)
        phase1(0, 1)
        normed = mm(turn1[...], normed).astype(BF16)
        put(parts[1], 480, mm(normed, rhs(3, slice(1920, 2304))), 24)
        phase1(1, 1)
        combine(1, 0)
        combine(2, 1)
        combine(0, 1)
        combine(1, 1)

        for k in (1, 2, 0):
            mine = spot[ORDERS[k][0]]
            axis, p, a, b = ORDERS[k][1], parts[k], got2a[k], got2b[k]
            i, right, opposite, left = around(axis)
            upper, lower = halves_of(PART_ROWS[k])
            for s in range(len(RANGES[k])):
                for j in (2, 3, 4, 5):
                    sent[k][6 * s + j].wait_recv()
            p[mine, opposite] += from_left[k][opposite] + from_right[k][opposite]
            go(p.at[mine, opposite, upper], a.at[0], k, 12, axis, 1)
            go(p.at[mine, opposite, lower], b.at[0], k, 13, axis, 3)
            p[mine, right] += from_left[k][right] + from_right[k][right]
            go(p.at[mine, right, lower], b.at[1], k, 14, axis, 1)
            p[mine, left] += from_left[k][left] + from_right[k][left]
            go(p.at[mine, left, upper], a.at[1], k, 15, axis, 3)
            p[mine, i] += from_left[k][i] + from_right[k][i]
        for k in (1, 2, 0):
            mine = spot[ORDERS[k][0]]
            axis, p, a, b = ORDERS[k][1], parts[k], got2a[k], got2b[k]
            i, right, opposite, left = around(axis)
            upper, lower = halves_of(PART_ROWS[k])
            sent[k][12].wait_recv()
            p[mine, right, upper] += a[0]
            go(p.at[mine, right, upper], a.at[2], k, 16, axis, 1)
            sent[k][13].wait_recv()
            p[mine, left, lower] += b[0]
            go(p.at[mine, left, lower], b.at[2], k, 17, axis, 3)
        for k in (1, 2, 0):
            mine = spot[ORDERS[k][0]]
            i = spot[ORDERS[k][1]]
            p, a, b, out = parts[k], got2a[k], got2b[k], last[k]
            upper, lower = halves_of(PART_ROWS[k])
            for j in (14, 15, 16, 17):
                sent[k][j].wait_recv()
            p[mine, i, upper] += a[1] + a[2]
            p[mine, i, lower] += b[1] + b[2]
            start, place = 0, 0
            for _, _, count, rows in BLOCKS[k]:
                each = rows // 4
                for _ in range(count):
                    for d in range(4):
                        out[d, pl.ds(place, each)] = p[mine, i, pl.ds(start + d * each, each)]
                    start += rows
                    place += each
            if place < LAST_ROWS[k]:
                for d in range(4):
                    out[d, pl.ds(place, LAST_ROWS[k] - place)] = jnp.zeros(
                        (LAST_ROWS[k] - place, 128), F32
                    )
            axis = ORDERS[k][2]
            for by in (1, 2, 3):
                to = lax.rem(spot[axis] + by, 4)
                go(out.at[to], got3[k].at[by - 1], k, 17 + by, axis, by)
        for k in (1, 2, 0):
            for j in (18, 19, 20):
                sent[k][j].wait_recv()
            total = last[k][spot[ORDERS[k][2]]] + got3[k][0] + got3[k][1] + got3[k][2]
            out_o[pl.ds(FIRST_ROWS[k], LAST_ROWS[k]), :] = total
        for copy in halo + shares + pairs:
            copy.wait_send()
        for k in range(3):
            for copy in sent[k].values():
                copy.wait_send()

    pl.run_scoped(backward, *[pltpu.VMEM((4, 4, n, 128), F32) for n in PART_ROWS])


BIG = (
    (2 * FRAMES, D), (D, FF), (FF, D), (2 * 513, D), (WIDE1, NFFT), (NFFT, WIDE1),
    (NFFT // 2, WIDE2), (2, 384, D), (2, 576, FF // 2), (2, 384, D),
)


def step_call(small, big):
    wide = [full(*((2,) if p else ()), *a.shape) for a, p in zip(OPERANDS, PICKED)]
    edge = full(1, HALO * HOP)
    rows = PART_ROWS
    cuts = [halves_of(n)[0].size for n in rows]

    def each(make):
        return [pltpu.VMEM(make(k), F32) for k in range(3)]

    return pl.pallas_call(
        step_kernel,
        out_shape=full(sum(LAST_ROWS), 128),
        in_specs=[spec(pltpu.VMEM)] * len(small) + [spec(pl.ANY)] * len(big),
        out_specs=spec(pltpu.VMEM),
        scratch_shapes=vmem([full(*BIG[i], dtype=BF16) for i in (1, 2, 3, 4, 5, 6, 9)])
        + vmem(SAVED)
        + vmem(wide)
        + vmem([*OPERANDS, IDS])
        + vmem([edge, edge, IDS, IDS])
        + [
            pltpu.VMEM((ROWS, FF), BF16),
            pltpu.VMEM((8, 128), F32),
            pltpu.VMEM((8, 8, 128), F32),
            pltpu.VMEM((ROWS, NFFT), BF16),
            pltpu.VMEM((ROWS, CHUNKS1 * 128), F32),
            pltpu.VMEM((ROWS, 1152), BF16),
            pltpu.VMEM((ROWS, FF), BF16),
            pltpu.VMEM((16, D), F32),
        ]
        + each(lambda k: (2, 2, rows[k], 128))
        + each(lambda k: (4, rows[k], 128))
        + each(lambda k: (4, rows[k], 128))
        + each(lambda k: (3, cuts[k], 128))
        + each(lambda k: (3, rows[k] - cuts[k], 128))
        + each(lambda k: (4, LAST_ROWS[k], 128))
        + each(lambda k: (3, LAST_ROWS[k], 128))
        + [pltpu.SemaphoreType.DMA((n,)) for n in (len(big), 4, 4, 7, 7, 9, 9)]
        + [pltpu.SemaphoreType.DMA((3, 21))] * 2,
        compiler_params=pltpu.CompilerParams(
            collective_id=0, has_side_effects=True, vmem_limit_bytes=64 * MB
        ),
        name="train_step",
    )(*small, *big)


def finish_kernel(sums, loss_o, table_o, kern_o, up_o, down_o, scale_o, head_o):
    outs = {"up": up_o, "down": down_o, "table": table_o, "head": head_o}
    for k in range(3):
        rows = FIRST_ROWS[k]
        for name, start, count, block in BLOCKS[k]:
            for c in range(start, start + count):
                values = sums[rows : rows + block // 4, :]
                rows += block // 4
                if (name, c) != ("head", 8):
                    outs[name][:, 128 * c : 128 * (c + 1)] = values
                    continue
                head_o[:, 1024:1026] = values[:, 0:2]
                tail = jnp.transpose(jnp.concatenate([values, jnp.zeros((122, 128), F32)], axis=0))
                kern_o[...] = tail[2:9, 0:6]
                scale_o[...] = tail[9:10, 0:6]
                pieces = values[0:1, 10:14]
                loss_o[...] = jnp.sum(pieces, axis=1, keepdims=True) * (0.5 / CLIPS)


def finish_call(sums):
    loss, table, kern, up, down, scale, head = pl.pallas_call(
        finish_kernel,
        out_shape=[
            full(1, 1), full(16, D), full(7, 6), full(6, FF), full(18, D), full(1, 6), full(6, 1026),
        ],
        in_specs=[spec(pltpu.VMEM)],
        out_specs=[spec(pltpu.VMEM)] * 7,
        name="finish",
    )(sums)
    return loss.reshape(()), table, kern, up, down, scale.reshape(6), head


def body(
    code_ids, code_table, kernel, up_weight, down_weight, layer_scale, head_weight, target, loss_scale
):
    syn, a1, a2, win = make_constants()
    pick_n, pick_h, pick_k, turn1, turn2, row_id = make_orders()
    ids = jnp.swapaxes(code_ids, 1, 2).reshape(2, OWN)
    head_t = head_weight.T
    sums = step_call(
        (target, ids, kernel, layer_scale, win, loss_scale.reshape(1, 1), turn1, turn2, row_id),
        (
            code_table, up_weight, down_weight, head_t, syn, a1, a2, pick_n, pick_h, pick_k,
        ),
    )
    return finish_call(sums)


def solution(mesh):
    in_specs = (P("dp", "tm", None), P(), P(), P(), P(), P(), P(), P("dp", "tm"), P())
    out_specs = (
        P(),
        P(("dp", "tm"), None),
        P(None, ("dp", "tm")),
        P(("dp", "tm"), None),
        P(("dp", "tm"), None),
        P(("dp", "tm")),
        P(("dp", "tm"), None),
    )
    return jax.shard_map(body, mesh=mesh, in_specs=in_specs, out_specs=out_specs, check_vma=False)
```

```python
import jax
import jax.numpy as jnp
import ml_dtypes
import numpy as np
from jax import lax
from jax.experimental import pallas as pl
from jax.experimental.pallas import tpu as pltpu
from jax.sharding import PartitionSpec as P

F32, BF16 = jnp.float32, jnp.bfloat16
MESH = pl.DeviceIdType.MESH
D, FF = 768, 2304
HOP, NFFT = 256, 1024
FRAMES, OWN, HALO = 1024, 128, 16
ROWS = OWN + 2 * HALO
CHUNKS1, CHUNKS2 = 5, 3
WIDE1, WIDE2 = CHUNKS1 * 256, CHUNKS2 * 256
CLIPS = 16
MB = 1 << 20
ORDERS = ("xyz", "yzx", "zxy")
HEAD_BLOCKS = ((0, 3), (3, 2), (5, 4))
MAIN_BLOCKS = ((18, 24), (6, 72), (6, 64))
RANGES = (((0, 72), (72, 504)), ((0, 480),), ((0, 72), (72, 480)))
PART_ROWS = (504, 480, 480)
LAST_ROWS = (128, 120, 120)
FIRST_ROWS = (0, 128, 248)


def bf(array):
    return np.asarray(array, np.float32).astype(ml_dtypes.bfloat16)


def hann(length):
    return 0.5 - 0.5 * np.cos(2.0 * np.pi * np.arange(length) / length)


def angles(length):
    product = np.arange(length // 2 + 1)[:, None] * np.arange(length)[None, :] % length
    return 2.0 * np.pi * product / length


def interleave(real, imag, chunks):
    bins, width = real.shape
    out = np.zeros((chunks, 2, 128, width), np.float64)
    for half, part in enumerate((real, imag)):
        padded = np.zeros((chunks * 128, width), np.float64)
        padded[:bins] = part
        out[:, half] = padded.reshape(chunks, 128, width)
    return out.reshape(chunks * 256, width)


def make_constants():
    ang = angles(NFFT)
    bins = np.arange(NFFT // 2 + 1)
    factor = np.where((bins == 0) | (bins == NFFT // 2), 1.0, 2.0)[:, None] / NFFT
    window = hann(NFFT)[None, :]
    synthesis = bf(interleave(factor * np.cos(ang) * window, -factor * np.sin(ang) * window, CHUNKS1))
    analysis1 = bf(interleave(np.cos(ang), -np.sin(ang), CHUNKS1).T)
    ang = angles(NFFT // 2)
    analysis2 = bf(interleave(np.cos(ang), -np.sin(ang), CHUNKS2).T)
    win = np.zeros((8, NFFT), np.float32)
    win[0] = hann(NFFT)
    win[1] = hann(NFFT) ** 2
    win[2, : NFFT // 2] = hann(NFFT // 2)
    return synthesis, analysis1, analysis2, win


def device_index(x, y, z, core):
    return ((y * 2 + z // 2) * 2 + core) * 8 + x * 2 + z % 2


def shard_order(order, core):
    places = []
    for a in range(4):
        for b in range(4):
            for c in range(4):
                at = dict(zip(order, (a, b, c)))
                places.append(device_index(at["x"], at["y"], at["z"], core))
    return np.array(places)


def columns_of(order, core, each):
    return (shard_order(order, core)[:, None] * each + np.arange(each)[None, :]).reshape(-1)


def one_hot_columns(sources, size):
    out = np.zeros((size, sources.size), np.float32)
    out[sources, np.arange(sources.size)] = 1.0
    return bf(out)


def make_orders():
    pick_n = np.stack([one_hot_columns(columns_of(ORDERS[0], c, 6), D).T for c in (0, 1)])
    half = [columns_of(ORDERS[1], c, 18)[: 4 * 4 * 2 * 18] for c in (0, 1)]
    pick_h = np.stack([one_hot_columns(h, FF // 2).T for h in half])
    pick_k = np.stack([one_hot_columns(columns_of(ORDERS[2], c, 6), D).T for c in (0, 1)])
    first = columns_of(ORDERS[0], 0, 6)
    where = {col: i for i, col in enumerate(first)}
    turns = []
    for k in (1, 2):
        sources = np.array([where[col] for col in columns_of(ORDERS[k], 0, 6)])
        turns.append(one_hot_columns(sources, 384).T)
    row_id = columns_of(ORDERS[2], 0, 16).astype(np.int32)[:, None]
    return pick_n, pick_h, pick_k, turns[0], turns[1], row_id


def mm(a, b):
    return jnp.dot(a, b, preferred_element_type=F32)


def mm_bt(a, b):
    return lax.dot_general(a, b, (((1,), (1,)), ((), ())), preferred_element_type=F32)


def mm_at(a, b):
    return lax.dot_general(a, b, (((0,), (0,)), ((), ())), preferred_element_type=F32)


def shift(values, by):
    by = by % values.shape[0]
    return values if by == 0 else pltpu.roll(values, by, 0)


def norm(values):
    centre = values - jnp.mean(values, axis=-1, keepdims=True)
    rstd = lax.rsqrt(jnp.mean(centre * centre, axis=-1, keepdims=True) + 1e-6)
    return centre * rstd, rstd


def norm_back(grad, y, rstd):
    mean_g = jnp.mean(grad, axis=-1, keepdims=True)
    mean_gy = jnp.mean(grad * y, axis=-1, keepdims=True)
    return rstd * (grad - mean_g - y * mean_gy)


def frame_places():
    first = lax.axis_index("tm") * OWN - HALO
    return (lax.broadcasted_iota(jnp.int32, (ROWS, 1), 0) + first).astype(F32)


def sin_cos(x):
    turns = jnp.round(x * 0.6366197723675814)
    r = x - turns * 1.5703125
    r = r - turns * 4.837512969970703125e-4
    r = r - turns * 7.549789954891882e-8
    z = r * r
    sine = r + r * z * (-1.6666654611e-1 + z * (8.3321608736e-3 + z * -1.9515295891e-4))
    cosine = (4.166664568298827e-2 + z * (-1.388731625493765e-3 + z * 2.443315711809948e-5)) * (z * z)
    cosine = cosine - 0.5 * z + 1.0
    quarter = turns.astype(jnp.int32)
    odd = (quarter & 1) == 1
    first, second = jnp.where(odd, cosine, sine), jnp.where(odd, sine, cosine)
    first = jnp.where((quarter & 2) == 2, -first, first)
    second = jnp.where(((quarter + 1) & 2) == 2, -second, second)
    return first, second


def inside(places):
    return (places >= 0.0) & (places < float(FRAMES))


def envelope(places, win):
    total = jnp.zeros((ROWS, HOP), F32)
    for p in range(4):
        total = total + jnp.where(inside(places + float(2 - p)), win[1:2, HOP * p : HOP * (p + 1)], 0.0)
    return jnp.where(inside(places), total, 1.0)


def spec(space):
    return pl.BlockSpec(memory_space=space)


def full(*shape, dtype=F32):
    return jax.ShapeDtypeStruct(shape, dtype)


def ids_column(ids):
    padded = jnp.concatenate([ids.astype(F32), jnp.zeros((126, OWN), F32)], axis=0)
    return jnp.transpose(padded)[:, :2]


OPERANDS = (
    full(384, OWN), full(1152, OWN), full(384, OWN), full(OWN, FF), full(OWN, D),
    full(OWN, 1152), full(OWN, D), full(384, 128),
)
PICKED = (True, True, True, False, False, False, False, True)
IDS = full(2, OWN, dtype=jnp.int32)
SAVED = (
    full(ROWS, D), full(ROWS, 128), full(ROWS, D), full(ROWS, FF),
    full(ROWS, D), full(ROWS, D), full(ROWS, CHUNKS1 * 128), full(ROWS, CHUNKS1 * 128),
    full(ROWS, WIDE1), full(ROWS, WIDE1), full(2 * ROWS, WIDE2), full(2 * ROWS, WIDE2),
)


def vmem(shapes):
    return [pltpu.VMEM(a.shape, a.dtype) for a in shapes]


def put(out, first, values, rows):
    for block in range(values.shape[1] // 128):
        part = values[:, 128 * block : 128 * (block + 1)].reshape(4, 4, rows, 128)
        out[:, :, first + rows * block : first + rows * (block + 1), :] = part


def halves_of(rows):
    upper = (rows // 2 + 7) // 8 * 8
    return pl.ds(0, upper), pl.ds(upper, rows - upper)


def step_kernel(target, ids, kern, scale_i, win, loss_scale, turn1, turn2, row_id, *refs):
    big_h, out_o, refs = refs[:10], refs[10], refs[11:]
    (up_v, down_v, head_v, syn_v, a1_v, a2_v, pick_k), refs = refs[:7], refs[7:]
    (sin_o, rstd_o, y1_o, gp_o, down_o, y2_o, re_o, im_o, d1_o, q1_o, d2_o, q2_o) = refs[:12]
    refs = refs[12:]
    here, there, refs = refs[:8], refs[8:17], refs[17:]
    (nrm_o, hid_o, onm_o, dup_o, ddn_o, dhd_o, dem_o, kg_o) = here
    (left_t, right_t, left_i, right_i, hid_v, stat_o, slots), refs = refs[:7], refs[7:]
    (dfr, dphase, dhead, dup, small), refs = refs[:5], refs[5:]
    through, from_left, from_right, got2a, got2b, last, got3 = (
        refs[3 * i : 3 * i + 3] for i in range(7)
    )
    (
        sems, halo_send, halo_recv, stat_send, stat_recv, pair_send, pair_recv, send, recv,
    ) = refs[21:]

    dp, tm = lax.axis_index("dp"), lax.axis_index("tm")
    core = lax.rem(dp, 2)
    other = 1 - core
    partner = {"dp": dp + 1 - 2 * core, "tm": tm}
    others = [{"dp": dp, "tm": lax.rem(tm + j, 8)} for j in range(1, 8)]
    spot = {"x": tm // 2, "y": dp // 4, "z": lax.rem(dp // 2, 2) * 2 + lax.rem(tm, 2)}

    def device(axis, by):
        to = dict(spot)
        to[axis] = lax.rem(spot[axis] + by, 4)
        return {
            "dp": (to["y"] * 2 + to["z"] // 2) * 2 + core,
            "tm": to["x"] * 2 + lax.rem(to["z"], 2),
        }

    barrier = pltpu.get_barrier_semaphore()
    around_me = [device(axis, by) for axis in "xyz" for by in (1, 2, 3)]
    for place in others + [partner] + around_me:
        pl.semaphore_signal(barrier, inc=1, device_id=place, device_id_type=MESH)

    def remote(src, dst, send, recv, place):
        return pltpu.make_async_remote_copy(
            src_ref=src, dst_ref=dst, send_sem=send, recv_sem=recv,
            device_id=place, device_id_type=MESH,
        )

    edge = HALO * HOP
    right, left = others[0], others[6]
    halo = [
        remote(src, dst, halo_send.at[i], halo_recv.at[i], place)
        for i, (src, dst, place) in enumerate(
            (
                (ids, left_i, right),
                (ids, right_i, left),
                (target.at[:, pl.ds(OWN * HOP - edge, edge)], left_t, right),
                (target.at[:, pl.ds(0, edge)], right_t, left),
            )
        )
    ]
    shares = [
        remote(stat_o, slots.at[tm], stat_send.at[j], stat_recv.at[j], place)
        for j, place in enumerate(others)
    ]
    pairs = [
        remote(ref.at[other] if picked else ref, there[i], pair_send.at[i], pair_recv.at[i], partner)
        for i, (ref, picked) in enumerate(zip((*here, ids), (*PICKED, False)))
    ]

    def give(i):
        pairs[i].start()

    own = slice(HALO, HALO + OWN)
    scale = scale_i[...].reshape(1, D)
    places = frame_places()
    valid = inside(places)

    def forward(table_v, pick_n, pick_h, goal, codes, head_s, spec_v, seg1, seg2):
        big_v = (table_v, up_v, down_v, head_v, syn_v, a1_v, a2_v, pick_n, pick_h, pick_k)
        copies = [
            pltpu.make_async_copy(h, v, sems.at[i]) for i, (h, v) in enumerate(zip(big_h, big_v))
        ]
        for copy in copies:
            copy.start()
        pl.semaphore_wait(barrier, 17)
        for copy in halo:
            copy.start()
        give(8)
        codes[HALO : HALO + OWN, :] = ids_column(ids[...])
        for source, first, count in (
            (target, HALO, OWN), (left_t, 0, HALO), (right_t, HALO + OWN, HALO),
        ):
            if source is left_t:
                for copy in halo:
                    copy.wait_recv()
            for r in range(count):
                goal[first + r : first + r + 1, :] = source[:, HOP * r : HOP * (r + 1)]
        codes[0:HALO, :] = ids_column(left_i[...])[OWN - HALO :]
        codes[HALO + OWN :, :] = ids_column(right_i[...])[:HALO]
        lane = lax.broadcasted_iota(jnp.int32, (ROWS, 2 * FRAMES), 1).astype(F32)
        hot = (lane == codes[:, 0:1]) | (lane == codes[:, 1:2] + 1024.0)
        hot = jnp.where(hot, 1.0, 0.0).astype(BF16)
        copies[0].wait()
        y0, rstd0 = norm(mm(hot, table_v[...]))
        y0 = jnp.where(valid, y0, 0.0)
        sin_o[...] = y0
        mixture = kern[0:1, :] * shift(y0, 3)
        for k in range(1, 7):
            mixture = mixture + kern[k : k + 1, :] * shift(y0, 3 - k)
        y1, rstd1 = norm(mixture)
        y1_o[...] = y1
        normed = y1.astype(BF16)
        copies[1].wait()
        for c in range(FF // 256):
            at = slice(256 * c, 256 * (c + 1))
            up = mm(normed, up_v[:, at])
            cdf = 0.5 * (1.0 + lax.erf(up * 0.7071067811865476))
            hid_v[:, at] = (up * cdf).astype(BF16)
            gp_o[:, at] = cdf + up * (0.3989422804014327 * jnp.exp(-0.5 * up * up))
        copies[2].wait()
        down = mm(hid_v[...], down_v[...])
        down_o[...] = down
        y2, rstd2 = norm(y0 + scale * down)
        y2_o[...] = y2
        places128 = lax.broadcasted_iota(jnp.int32, (ROWS, 128), 1)
        rstd_o[...] = jnp.where(places128 == 0, rstd0, jnp.where(places128 == 1, rstd1, rstd2))
        onorm = y2.astype(BF16)
        copies[3].wait()
        head_s[:, 1024:] = jnp.zeros((ROWS, 128), F32)
        for c in range(4):
            head_s[:, 256 * c : 256 * (c + 1)] = mm_bt(onorm, head_v[256 * c : 256 * (c + 1), :])
        head_s[:, 1024:1026] = mm_bt(onorm, head_v[1024:1026, :])
        phases = pltpu.roll(head_s[:, 512:], CHUNKS1 * 128 - 1, 1)
        for c in range(CHUNKS1):
            logmag = head_s[:, 128 * c : 128 * (c + 1)]
            if c == 4:
                logmag = jnp.where(places128 == 0, logmag, 0.0)
            mag = jnp.exp(logmag)
            phase = phases[:, 128 * c : 128 * (c + 1)]
            sine, cosine = sin_cos(phase)
            re, im = mag * cosine, mag * sine
            re_o[:, 128 * c : 128 * (c + 1)] = re
            im_o[:, 128 * c : 128 * (c + 1)] = im
            spec_v[:, 256 * c : 256 * c + 128] = re.astype(BF16)
            spec_v[:, 256 * c + 128 : 256 * (c + 1)] = im.astype(BF16)
        copies[4].wait()
        pred = jnp.zeros((ROWS, HOP), F32)
        for p in range(4):
            piece = jnp.where(valid, mm(spec_v[...], syn_v[:, HOP * p : HOP * (p + 1)]), 0.0)
            pred = pred + shift(piece, p - 2)
        pred = jnp.where(valid, pred / envelope(places, win), 0.0)
        for s, x in enumerate((pred, jnp.where(valid, goal[...], 0.0))):
            r1 = slice(ROWS * s, ROWS * (s + 1))
            for p in range(4):
                at = slice(HOP * p, HOP * (p + 1))
                seg1[r1, at] = (shift(x, 2 - p) * win[0:1, at]).astype(BF16)
            even = slice(2 * ROWS * s, 2 * ROWS * s + ROWS)
            odd = slice(2 * ROWS * s + ROWS, 2 * ROWS * (s + 1))
            before, after = shift(x, 1), shift(x, -1)
            seg2[even, 0:256] = (before * win[2:3, 0:256]).astype(BF16)
            seg2[even, 256:512] = (x * win[2:3, 256:512]).astype(BF16)
            seg2[odd, 0:128] = (before[:, 128:] * win[2:3, 0:128]).astype(BF16)
            seg2[odd, 128:384] = (x * win[2:3, 128:384]).astype(BF16)
            seg2[odd, 384:512] = (after[:, :128] * win[2:3, 384:512]).astype(BF16)
        for level in range(2):
            seg, table, chunks = ((seg1, a1_v, CHUNKS1), (seg2, a2_v, CHUNKS2))[level]
            d_o, q_o = ((d1_o, q1_o), (d2_o, q2_o))[level]
            copies[5 + level].wait()
            sums = [jnp.zeros((OWN, 128), F32) for _ in range(3)]
            for c in range(chunks):
                for sub in range(level + 1):
                    rows_p = slice(ROWS * sub, ROWS * (sub + 1))
                    base = ROWS * (level + 1)
                    rows_g = slice(base + ROWS * sub, base + ROWS * (sub + 1))
                    weights = table[:, 256 * c : 256 * (c + 1)]
                    sp, sg = mm(seg[rows_p, :], weights), mm(seg[rows_g, :], weights)
                    diff = sp - sg
                    pr, pi, gr, gi = sp[:, :128], sp[:, 128:], sg[:, :128], sg[:, 128:]
                    power_p, power_g = pr * pr + pi * pi, gr * gr + gi * gi
                    gap = jnp.log1p(power_p) - jnp.log1p(power_g)
                    slope = jnp.where(valid, 4.0 * gap / (1.0 + power_p), 0.0)
                    d_o[rows_p, 256 * c : 256 * (c + 1)] = jnp.where(valid, diff, 0.0)
                    q_o[rows_p, 256 * c : 256 * c + 128] = slope * pr
                    q_o[rows_p, 256 * c + 128 : 256 * (c + 1)] = slope * pi
                    dr, di = diff[own, :128], diff[own, 128:]
                    sums[0] = sums[0] + dr * dr + di * di
                    sums[1] = sums[1] + power_g[own]
                    sums[2] = sums[2] + gap[own] * gap[own]
            for i in range(3):
                total = jnp.sum(jnp.sum(sums[i], axis=0, keepdims=True), axis=1, keepdims=True)
                stat_o[3 * level + i : 3 * level + i + 1, :] = jnp.broadcast_to(total, (1, 128))
        stat_o[6:8, :] = jnp.zeros((2, 128), F32)
        for share in shares:
            share.start()
        slots[tm] = stat_o[...]

        copies[7].wait()
        copies[8].wait()
        normed = y1_o[own, :].astype(BF16)
        onorm = y2_o[own, :].astype(BF16)
        for c in range(2):
            nrm_o[c] = mm_bt(pick_n[c], normed)
            onm_o[c] = mm_bt(pick_n[c], onorm)
            for h in range(2):
                out = slice(576 * h, 576 * (h + 1))
                hid_o[c, out, :] = mm_bt(pick_h[c], hid_v[own, 1152 * h : 1152 * (h + 1)])
        for i in (0, 2, 1):
            give(i)
        copies[9].wait()

    pl.run_scoped(
        forward,
        *vmem([full(*shape, dtype=BF16) for shape in (BIG[0], BIG[7], BIG[8])]),
        pltpu.VMEM((ROWS, HOP), F32),
        pltpu.VMEM((ROWS, 2), F32),
        pltpu.VMEM((ROWS, 1152), F32),
        pltpu.VMEM((ROWS, WIDE1), BF16),
        pltpu.VMEM((2 * ROWS, NFFT), BF16),
        pltpu.VMEM((4 * ROWS, NFFT // 2), BF16),
    )

    def need(*which):
        for i in which:
            pairs[i].wait_recv()

    def lhs(i):
        return jnp.concatenate([here[i][core], there[i][...]], axis=1).astype(BF16)

    def rhs(i, cols):
        return jnp.concatenate([here[i][:, cols], there[i][:, cols]], axis=0).astype(BF16)

    def head_block(onorm, block):
        return mm(onorm, rhs(5, slice(128 * block, 128 * (block + 1))))

    def around(axis):
        i = spot[axis]
        return i, lax.rem(i + 1, 4), lax.rem(i + 2, 4), lax.rem(i + 3, 4)

    def backward(*parts):
        sent = [{}, {}, {}]

        def go(src, dst, k, slot, axis, by):
            sent[k][slot] = remote(src, dst, send.at[k, slot], recv.at[k, slot], device(axis, by))
            sent[k][slot].start()

        low, high = pl.ds(0, 2), pl.ds(2, 2)

        def phase1(k, s):
            axis, p = ORDERS[k][0], parts[k]
            i, right, opposite, left = around(axis)
            first, end = RANGES[k][s]
            rows = pl.ds(first, end - first)
            go(p.at[opposite, low, rows], through[k].at[0, :, rows], k, 6 * s, axis, 1)
            go(p.at[opposite, high, rows], through[k].at[1, :, rows], k, 6 * s + 1, axis, 3)
            go(p.at[right, high, rows], from_left[k].at[high, rows], k, 6 * s + 2, axis, 1)
            go(p.at[left, low, rows], from_right[k].at[low, rows], k, 6 * s + 3, axis, 3)

        def combine(k, s):
            axis, p = ORDERS[k][0], parts[k]
            i, right, opposite, left = around(axis)
            first, end = RANGES[k][s]
            rows = pl.ds(first, end - first)
            sent[k][6 * s].wait_recv()
            p[right, low, rows] += through[k][0, :, rows]
            go(p.at[right, low, rows], from_left[k].at[low, rows], k, 6 * s + 4, axis, 1)
            sent[k][6 * s + 1].wait_recv()
            p[left, high, rows] += through[k][1, :, rows]
            go(p.at[left, high, rows], from_right[k].at[high, rows], k, 6 * s + 5, axis, 3)

        for share in shares:
            share.wait_recv()
        total = slots[0]
        for j in range(1, 8):
            total = total + slots[j]

        factor = loss_scale[...] * (0.5 / CLIPS)
        loss = jnp.zeros((1, 1), F32)
        cots = []
        for level in range(2):
            count = ((FRAMES * 513), (2 * FRAMES * 257))[level]
            sum_a = total[3 * level : 3 * level + 1, 0:1]
            sum_b = total[3 * level + 1 : 3 * level + 2, 0:1]
            sum_g = total[3 * level + 2 : 3 * level + 3, 0:1]
            root_a, root_b = jnp.sqrt(sum_a + 1e-6), jnp.sqrt(sum_b + 1e-6)
            loss = loss + root_a / root_b + sum_g * (1.0 / count)
            cots.append((factor / (root_a * root_b), factor * (1.0 / count)))
        loss = jnp.where(lax.axis_index("tm") == 0, loss, 0.0)

        dx = jnp.zeros((ROWS, HOP), F32)
        ds1 = (cots[0][0] * d1_o[...] + cots[0][1] * q1_o[...]).astype(BF16)
        for p in range(4):
            at = slice(HOP * p, HOP * (p + 1))
            piece = mm_bt(ds1, a1_v[at, :]).astype(BF16).astype(F32) * win[0:1, at]
            dx = dx + shift(piece, p - 2)
        ds2 = (cots[1][0] * d2_o[...] + cots[1][1] * q2_o[...]).astype(BF16)
        dseg = mm_bt(ds2, a2_v[...]).astype(BF16).astype(F32) * win[2:3, : NFFT // 2]
        even, odd = dseg[:ROWS], dseg[ROWS:]
        dx = dx + shift(even[:, :256], -1) + even[:, 256:] + odd[:, 128:384]
        dx = dx + jnp.concatenate([shift(odd[:, 384:], 1), shift(odd[:, :128], -1)], axis=1)
        dx = jnp.where(valid, dx / envelope(places, win), 0.0)
        for p in range(4):
            piece = jnp.where(valid, shift(dx, 2 - p), 0.0)
            dfr[:, HOP * p : HOP * (p + 1)] = piece.astype(BF16)

        for c in range(CHUNKS1):
            dsp = mm_bt(dfr[...], syn_v[256 * c : 256 * (c + 1), :]).astype(BF16).astype(F32)
            dre, dim = dsp[:, :128], dsp[:, 128:]
            re, im = re_o[:, 128 * c : 128 * (c + 1)], im_o[:, 128 * c : 128 * (c + 1)]
            dlog, dph = dre * re + dim * im, dim * re - dre * im
            if c < 4:
                dhead[:, 128 * c : 128 * (c + 1)] = dlog.astype(BF16)
            dphase[:, 128 * c : 128 * (c + 1)] = dph
        moved = pltpu.roll(dphase[...], 1, 1)
        dhead[:, 512:640] = (moved[:, :128] + dlog).astype(BF16)
        dhead[:, 640:] = moved[:, 128:].astype(BF16)
        dhd_o[...] = dhead[own, :].astype(F32)
        give(5)
        don = mm(dhead[:, :1026], head_v[...]).astype(BF16).astype(F32)
        dstream = norm_back(don, y2_o[...], rstd_o[:, 2:3])

        scale_grad = jnp.sum(dstream[own] * down_o[own, :], axis=0, keepdims=True)
        ddn = (scale * dstream).astype(BF16)
        ddn_o[...] = ddn[own].astype(F32)
        give(4)
        for c in range(FF // 256):
            at = slice(256 * c, 256 * (c + 1))
            dh = mm_bt(ddn, down_v[at, :]).astype(BF16).astype(F32)
            dup[:, at] = (dh * gp_o[:, at]).astype(BF16)
        dup_o[...] = dup[own, :].astype(F32)
        give(3)

        need(2, 5)
        onorm = [lhs(2)]
        onorm += [mm(turn[...], onorm[0]).astype(BF16) for turn in (turn1, turn2)]
        for k in range(3):
            start, blocks = HEAD_BLOCKS[k]
            for b in range(min(blocks, 8 - start)):
                put(parts[k], 24 * b, head_block(onorm[k], start + b), 24)
        phase1(0, 0)
        phase1(2, 0)
        need(1, 4)
        hidden = lhs(1)
        for c in range(3):
            put(parts[1], 48 + 144 * c, mm(hidden, rhs(4, slice(256 * c, 256 * (c + 1)))), 72)
        phase1(1, 0)
        need(0, 3)
        normed = lhs(0)
        for c in range(FF // 256):
            put(parts[0], 72 + 48 * c, mm(normed, rhs(3, slice(256 * c, 256 * (c + 1)))), 24)
        phase1(0, 1)

        dnorm = mm_bt(dup[...], up_v[...]).astype(BF16).astype(F32)
        dmix = norm_back(dnorm, y1_o[...], rstd_o[:, 1:2])
        dmix = jnp.where(valid, dmix, 0.0)
        y0 = sin_o[...]
        dsin = dstream
        for k in range(7):
            dsin = dsin + kern[k : k + 1, :] * shift(dmix, k - 3)
        demb = norm_back(dsin, y0, rstd_o[:, 0:1])
        dem_o[...] = demb[own].astype(BF16).astype(F32)
        give(6)
        small[...] = jnp.zeros((16, D), F32)
        for k in range(7):
            taps = dmix * shift(y0, 3 - k)
            small[2 + k : 3 + k, :] = jnp.sum(taps[own], axis=0, keepdims=True)

        small[9:10, :] = scale_grad
        rest = loss
        for i, grid in enumerate((65536.0, 1.0, 1.0 / 65536.0, 1.0 / 65536.0 / 65536.0)):
            piece = jnp.floor(rest * (1.0 / grid)) * grid
            rest = rest - piece
            small[10 + i : 11 + i, :] = jnp.broadcast_to(piece, (1, D))

        small0 = small[...].astype(BF16)
        rest = small[...] - small0.astype(F32)
        small1 = rest.astype(BF16)
        small2 = (rest - small1.astype(F32)).astype(BF16)
        pieces = jnp.concatenate([small0, small1, small2], axis=0)
        for c in range(2):
            picked = mm_bt(pieces, pick_k[c])
            picked = picked[0:16] + picked[16:32] + picked[32:48]
            picked = jnp.concatenate([picked, jnp.zeros((112, 384), F32)], axis=0)
            kg_o[c] = jnp.transpose(picked)
        give(7)

        combine(0, 0)
        combine(2, 0)
        need(8, 6)
        both_ids = jnp.concatenate([ids[...], there[8][...]], axis=1)
        code_rows = row_id[...] + OWN * core
        hot = (code_rows == both_ids[0:1, :]) | (code_rows == both_ids[1:2, :] + 1024)
        hot = jnp.where(hot, 1.0, 0.0).astype(BF16)
        for c in range(3):
            put(parts[2], 96 + 128 * c, mm(hot, rhs(6, slice(256 * c, 256 * (c + 1)))), 64)
        need(7)
        put(parts[2], 72, head_block(onorm[2], 8) + here[7][core] + there[7][...], 24)
        phase1(2, 1)
        combine(1, 0)
        combine(0, 1)
        combine(2, 1)

        for k in (1, 0, 2):
            mine = spot[ORDERS[k][0]]
            axis, p, a, b = ORDERS[k][1], parts[k], got2a[k], got2b[k]
            i, right, opposite, left = around(axis)
            upper, lower = halves_of(PART_ROWS[k])
            for s in range(len(RANGES[k])):
                for j in (2, 3, 4, 5):
                    sent[k][6 * s + j].wait_recv()
            p[mine, opposite] += from_left[k][opposite] + from_right[k][opposite]
            go(p.at[mine, opposite, upper], a.at[0], k, 12, axis, 1)
            go(p.at[mine, opposite, lower], b.at[0], k, 13, axis, 3)
            p[mine, right] += from_left[k][right] + from_right[k][right]
            go(p.at[mine, right, lower], b.at[1], k, 14, axis, 1)
            p[mine, left] += from_left[k][left] + from_right[k][left]
            go(p.at[mine, left, upper], a.at[1], k, 15, axis, 3)
            p[mine, i] += from_left[k][i] + from_right[k][i]
        for k in (1, 0, 2):
            mine = spot[ORDERS[k][0]]
            axis, p, a, b = ORDERS[k][1], parts[k], got2a[k], got2b[k]
            i, right, opposite, left = around(axis)
            upper, lower = halves_of(PART_ROWS[k])
            sent[k][12].wait_recv()
            p[mine, right, upper] += a[0]
            go(p.at[mine, right, upper], a.at[2], k, 16, axis, 1)
            sent[k][13].wait_recv()
            p[mine, left, lower] += b[0]
            go(p.at[mine, left, lower], b.at[2], k, 17, axis, 3)
        for k in (1, 0, 2):
            mine = spot[ORDERS[k][0]]
            i = spot[ORDERS[k][1]]
            p, a, b, out = parts[k], got2a[k], got2b[k], last[k]
            upper, lower = halves_of(PART_ROWS[k])
            for j in (14, 15, 16, 17):
                sent[k][j].wait_recv()
            p[mine, i, upper] += a[1] + a[2]
            p[mine, i, lower] += b[1] + b[2]
            start, place = 0, 0
            for count, rows in ((HEAD_BLOCKS[k][1], 24), MAIN_BLOCKS[k]):
                each = rows // 4
                for _ in range(count):
                    for d in range(4):
                        out[d, pl.ds(place, each)] = p[mine, i, pl.ds(start + d * each, each)]
                    start += rows
                    place += each
            if place < LAST_ROWS[k]:
                for d in range(4):
                    out[d, pl.ds(place, LAST_ROWS[k] - place)] = jnp.zeros(
                        (LAST_ROWS[k] - place, 128), F32
                    )
            axis = ORDERS[k][2]
            for by in (1, 2, 3):
                to = lax.rem(spot[axis] + by, 4)
                go(out.at[to], got3[k].at[by - 1], k, 17 + by, axis, by)
        for k in (1, 0, 2):
            for j in (18, 19, 20):
                sent[k][j].wait_recv()
            total = last[k][spot[ORDERS[k][2]]] + got3[k][0] + got3[k][1] + got3[k][2]
            out_o[pl.ds(FIRST_ROWS[k], LAST_ROWS[k]), :] = total
        for copy in halo + shares + pairs:
            copy.wait_send()
        for k in range(3):
            for copy in sent[k].values():
                copy.wait_send()

    pl.run_scoped(backward, *[pltpu.VMEM((4, 4, n, 128), F32) for n in PART_ROWS])


BIG = (
    (2 * FRAMES, D), (D, FF), (FF, D), (2 * 513, D), (WIDE1, NFFT), (NFFT, WIDE1),
    (NFFT // 2, WIDE2), (2, 384, D), (2, 576, FF // 2), (2, 384, D),
)


def step_call(small, big):
    wide = [full(*((2,) if p else ()), *a.shape) for a, p in zip(OPERANDS, PICKED)]
    edge = full(1, HALO * HOP)
    rows = PART_ROWS
    cuts = [halves_of(n)[0].size for n in rows]

    def each(make):
        return [pltpu.VMEM(make(k), F32) for k in range(3)]

    return pl.pallas_call(
        step_kernel,
        out_shape=full(sum(LAST_ROWS), 128),
        in_specs=[spec(pltpu.VMEM)] * len(small) + [spec(pl.ANY)] * len(big),
        out_specs=spec(pltpu.VMEM),
        scratch_shapes=vmem([full(*BIG[i], dtype=BF16) for i in (1, 2, 3, 4, 5, 6, 9)])
        + vmem(SAVED)
        + vmem(wide)
        + vmem([*OPERANDS, IDS])
        + vmem([edge, edge, IDS, IDS])
        + [
            pltpu.VMEM((ROWS, FF), BF16),
            pltpu.VMEM((8, 128), F32),
            pltpu.VMEM((8, 8, 128), F32),
            pltpu.VMEM((ROWS, NFFT), BF16),
            pltpu.VMEM((ROWS, CHUNKS1 * 128), F32),
            pltpu.VMEM((ROWS, 1152), BF16),
            pltpu.VMEM((ROWS, FF), BF16),
            pltpu.VMEM((16, D), F32),
        ]
        + each(lambda k: (2, 2, rows[k], 128))
        + each(lambda k: (4, rows[k], 128))
        + each(lambda k: (4, rows[k], 128))
        + each(lambda k: (3, cuts[k], 128))
        + each(lambda k: (3, rows[k] - cuts[k], 128))
        + each(lambda k: (4, LAST_ROWS[k], 128))
        + each(lambda k: (3, LAST_ROWS[k], 128))
        + [pltpu.SemaphoreType.DMA((n,)) for n in (len(big), 4, 4, 7, 7, 9, 9)]
        + [pltpu.SemaphoreType.DMA((3, 21))] * 2,
        compiler_params=pltpu.CompilerParams(
            collective_id=0, has_side_effects=True, vmem_limit_bytes=64 * MB
        ),
        name="train_step",
    )(*small, *big)


def finish_kernel(sums, loss_o, table_o, kern_o, up_o, down_o, scale_o, head_o):
    for k, (out, count, each) in enumerate(((up_o, 18, 6), (down_o, 6, 18), (table_o, 6, 16))):
        start, blocks = HEAD_BLOCKS[k]
        for c in range(blocks):
            rows = FIRST_ROWS[k] + 6 * c
            values = sums[rows : rows + 6, :]
            if start + c < 8:
                head_o[:, 128 * (start + c) : 128 * (start + c + 1)] = values
            else:
                head_o[:, 1024:1026] = values[:, 0:2]
                tail = jnp.transpose(jnp.concatenate([values, jnp.zeros((122, 128), F32)], axis=0))
                kern_o[...] = tail[2:9, 0:6]
                scale_o[...] = tail[9:10, 0:6]
                pieces = values[0:1, 10:14]
                loss_o[...] = jnp.sum(pieces, axis=1, keepdims=True) * (0.5 / CLIPS)
        for c in range(count):
            rows = FIRST_ROWS[k] + 6 * blocks + each * c
            out[:, 128 * c : 128 * (c + 1)] = sums[rows : rows + each, :]


def finish_call(sums):
    loss, table, kern, up, down, scale, head = pl.pallas_call(
        finish_kernel,
        out_shape=[
            full(1, 1), full(16, D), full(7, 6), full(6, FF), full(18, D), full(1, 6), full(6, 1026),
        ],
        in_specs=[spec(pltpu.VMEM)],
        out_specs=[spec(pltpu.VMEM)] * 7,
        name="finish",
    )(sums)
    return loss.reshape(()), table, kern, up, down, scale.reshape(6), head


def body(
    code_ids, code_table, kernel, up_weight, down_weight, layer_scale, head_weight, target, loss_scale
):
    syn, a1, a2, win = make_constants()
    pick_n, pick_h, pick_k, turn1, turn2, row_id = make_orders()
    ids = jnp.swapaxes(code_ids, 1, 2).reshape(2, OWN)
    head_t = head_weight.T
    sums = step_call(
        (target, ids, kernel, layer_scale, win, loss_scale.reshape(1, 1), turn1, turn2, row_id),
        (
            code_table, up_weight, down_weight, head_t, syn, a1, a2, pick_n, pick_h, pick_k,
        ),
    )
    return finish_call(sums)


def solution(mesh):
    in_specs = (P("dp", "tm", None), P(), P(), P(), P(), P(), P(), P("dp", "tm"), P())
    out_specs = (
        P(),
        P(("dp", "tm"), None),
        P(None, ("dp", "tm")),
        P(("dp", "tm"), None),
        P(("dp", "tm"), None),
        P(("dp", "tm")),
        P(("dp", "tm"), None),
    )
    return jax.shard_map(body, mesh=mesh, in_specs=in_specs, out_specs=out_specs, check_vma=False)
```

```python
import jax
import jax.numpy as jnp
import ml_dtypes
import numpy as np
from jax import lax
from jax.experimental import pallas as pl
from jax.experimental.pallas import tpu as pltpu
from jax.sharding import PartitionSpec as P

F32, BF16 = jnp.float32, jnp.bfloat16
MESH = pl.DeviceIdType.MESH
D, FF = 768, 2304
HOP, NFFT = 256, 1024
FRAMES, OWN, HALO = 1024, 128, 16
ROWS = OWN + 2 * HALO
CHUNKS1, CHUNKS2 = 5, 3
WIDE1, WIDE2 = CHUNKS1 * 256, CHUNKS2 * 256
CLIPS = 16
MB = 1 << 20
ORDERS = ("xyz", "yzx", "zxy")
HEAD_BLOCKS = ((0, 3), (3, 2), (5, 4))
MAIN_BLOCKS = ((18, 24), (6, 72), (6, 64))
RANGES = (((0, 72), (72, 504)), ((0, 480),), ((0, 72), (72, 480)))
PART_ROWS = (504, 480, 480)
LAST_ROWS = (128, 120, 120)
FIRST_ROWS = (0, 128, 248)


def bf(array):
    return np.asarray(array, np.float32).astype(ml_dtypes.bfloat16)


def hann(length):
    return 0.5 - 0.5 * np.cos(2.0 * np.pi * np.arange(length) / length)


def angles(length):
    product = np.arange(length // 2 + 1)[:, None] * np.arange(length)[None, :] % length
    return 2.0 * np.pi * product / length


def interleave(real, imag, chunks):
    bins, width = real.shape
    out = np.zeros((chunks, 2, 128, width), np.float64)
    for half, part in enumerate((real, imag)):
        padded = np.zeros((chunks * 128, width), np.float64)
        padded[:bins] = part
        out[:, half] = padded.reshape(chunks, 128, width)
    return out.reshape(chunks * 256, width)


def make_constants():
    ang = angles(NFFT)
    bins = np.arange(NFFT // 2 + 1)
    factor = np.where((bins == 0) | (bins == NFFT // 2), 1.0, 2.0)[:, None] / NFFT
    window = hann(NFFT)[None, :]
    synthesis = bf(interleave(factor * np.cos(ang) * window, -factor * np.sin(ang) * window, CHUNKS1))
    analysis1 = bf(interleave(np.cos(ang), -np.sin(ang), CHUNKS1).T)
    ang = angles(NFFT // 2)
    analysis2 = bf(interleave(np.cos(ang), -np.sin(ang), CHUNKS2).T)
    win = np.zeros((8, NFFT), np.float32)
    win[0] = hann(NFFT)
    win[1] = hann(NFFT) ** 2
    win[2, : NFFT // 2] = hann(NFFT // 2)
    return synthesis, analysis1, analysis2, win


def device_index(x, y, z, core):
    return ((y * 2 + z // 2) * 2 + core) * 8 + x * 2 + z % 2


def shard_order(order, core):
    places = []
    for a in range(4):
        for b in range(4):
            for c in range(4):
                at = dict(zip(order, (a, b, c)))
                places.append(device_index(at["x"], at["y"], at["z"], core))
    return np.array(places)


def columns_of(order, core, each):
    return (shard_order(order, core)[:, None] * each + np.arange(each)[None, :]).reshape(-1)


def one_hot_columns(sources, size):
    out = np.zeros((size, sources.size), np.float32)
    out[sources, np.arange(sources.size)] = 1.0
    return bf(out)


def make_orders():
    pick_n = np.stack([one_hot_columns(columns_of(ORDERS[0], c, 6), D).T for c in (0, 1)])
    half = [columns_of(ORDERS[1], c, 18)[: 4 * 4 * 2 * 18] for c in (0, 1)]
    pick_h = np.stack([one_hot_columns(h, FF // 2).T for h in half])
    pick_k = np.stack([one_hot_columns(columns_of(ORDERS[2], c, 6), D).T for c in (0, 1)])
    first = columns_of(ORDERS[0], 0, 6)
    where = {col: i for i, col in enumerate(first)}
    turns = []
    for k in (1, 2):
        sources = np.array([where[col] for col in columns_of(ORDERS[k], 0, 6)])
        turns.append(one_hot_columns(sources, 384).T)
    row_id = columns_of(ORDERS[2], 0, 16).astype(np.int32)[:, None]
    return pick_n, pick_h, pick_k, turns[0], turns[1], row_id


def mm(a, b):
    return jnp.dot(a, b, preferred_element_type=F32)


def mm_bt(a, b):
    return lax.dot_general(a, b, (((1,), (1,)), ((), ())), preferred_element_type=F32)


def mm_at(a, b):
    return lax.dot_general(a, b, (((0,), (0,)), ((), ())), preferred_element_type=F32)


def shift(values, by):
    by = by % values.shape[0]
    return values if by == 0 else pltpu.roll(values, by, 0)


def norm(values):
    centre = values - jnp.mean(values, axis=-1, keepdims=True)
    rstd = lax.rsqrt(jnp.mean(centre * centre, axis=-1, keepdims=True) + 1e-6)
    return centre * rstd, rstd


def norm_back(grad, y, rstd):
    mean_g = jnp.mean(grad, axis=-1, keepdims=True)
    mean_gy = jnp.mean(grad * y, axis=-1, keepdims=True)
    return rstd * (grad - mean_g - y * mean_gy)


def frame_places():
    first = lax.axis_index("tm") * OWN - HALO
    return (lax.broadcasted_iota(jnp.int32, (ROWS, 1), 0) + first).astype(F32)


def sin_cos(x):
    turns = jnp.round(x * 0.6366197723675814)
    r = x - turns * 1.5703125
    r = r - turns * 4.837512969970703125e-4
    r = r - turns * 7.549789954891882e-8
    z = r * r
    sine = r + r * z * (-1.6666654611e-1 + z * (8.3321608736e-3 + z * -1.9515295891e-4))
    cosine = (4.166664568298827e-2 + z * (-1.388731625493765e-3 + z * 2.443315711809948e-5)) * (z * z)
    cosine = cosine - 0.5 * z + 1.0
    quarter = turns.astype(jnp.int32)
    odd = (quarter & 1) == 1
    first, second = jnp.where(odd, cosine, sine), jnp.where(odd, sine, cosine)
    first = jnp.where((quarter & 2) == 2, -first, first)
    second = jnp.where(((quarter + 1) & 2) == 2, -second, second)
    return first, second


def inside(places):
    return (places >= 0.0) & (places < float(FRAMES))


def envelope(places, win):
    total = jnp.zeros((ROWS, HOP), F32)
    for p in range(4):
        total = total + jnp.where(inside(places + float(2 - p)), win[1:2, HOP * p : HOP * (p + 1)], 0.0)
    return jnp.where(inside(places), total, 1.0)


def spec(space):
    return pl.BlockSpec(memory_space=space)


def full(*shape, dtype=F32):
    return jax.ShapeDtypeStruct(shape, dtype)


def ids_column(ids):
    padded = jnp.concatenate([ids.astype(F32), jnp.zeros((126, OWN), F32)], axis=0)
    return jnp.transpose(padded)[:, :2]


OPERANDS = (
    full(384, OWN), full(1152, OWN), full(384, OWN), full(OWN, FF), full(OWN, D),
    full(OWN, 1152), full(OWN, D), full(384, 128),
)
PICKED = (True, True, True, False, False, False, False, True)
IDS = full(2, OWN, dtype=jnp.int32)
SAVED = (
    full(ROWS, D), full(ROWS, 128), full(ROWS, D), full(ROWS, FF),
    full(ROWS, D), full(ROWS, D), full(ROWS, CHUNKS1 * 128), full(ROWS, CHUNKS1 * 128),
    full(ROWS, WIDE1), full(ROWS, WIDE1), full(2 * ROWS, WIDE2), full(2 * ROWS, WIDE2),
)


def vmem(shapes):
    return [pltpu.VMEM(a.shape, a.dtype) for a in shapes]


def put(out, first, values, rows):
    for block in range(values.shape[1] // 128):
        part = values[:, 128 * block : 128 * (block + 1)].reshape(4, 4, rows, 128)
        out[:, :, first + rows * block : first + rows * (block + 1), :] = part


def halves_of(rows):
    upper = (rows // 2 + 7) // 8 * 8
    return pl.ds(0, upper), pl.ds(upper, rows - upper)


def step_kernel(target, ids, kern, scale_i, win, loss_scale, turn1, turn2, row_id, *refs):
    big_h, out_o, refs = refs[:10], refs[10], refs[11:]
    (up_v, down_v, head_v, syn_v, a1_v, a2_v, pick_k), refs = refs[:7], refs[7:]
    (sin_o, rstd_o, y1_o, gp_o, down_o, y2_o, re_o, im_o, d1_o, q1_o, d2_o, q2_o) = refs[:12]
    refs = refs[12:]
    here, there, refs = refs[:8], refs[8:17], refs[17:]
    (nrm_o, hid_o, onm_o, dup_o, ddn_o, dhd_o, dem_o, kg_o) = here
    (left_t, right_t, left_i, right_i, hid_v, stat_o, slots), refs = refs[:7], refs[7:]
    (dfr, dphase, dhead, dup, small), refs = refs[:5], refs[5:]
    through, from_left, from_right, got2a, got2b, last, got3 = (
        refs[3 * i : 3 * i + 3] for i in range(7)
    )
    (
        sems, halo_send, halo_recv, stat_send, stat_recv, pair_send, pair_recv, send, recv,
    ) = refs[21:]

    dp, tm = lax.axis_index("dp"), lax.axis_index("tm")
    core = lax.rem(dp, 2)
    other = 1 - core
    partner = {"dp": dp + 1 - 2 * core, "tm": tm}
    others = [{"dp": dp, "tm": lax.rem(tm + j, 8)} for j in range(1, 8)]
    spot = {"x": tm // 2, "y": dp // 4, "z": lax.rem(dp // 2, 2) * 2 + lax.rem(tm, 2)}

    def device(axis, by):
        to = dict(spot)
        to[axis] = lax.rem(spot[axis] + by, 4)
        return {
            "dp": (to["y"] * 2 + to["z"] // 2) * 2 + core,
            "tm": to["x"] * 2 + lax.rem(to["z"], 2),
        }

    barrier = pltpu.get_barrier_semaphore()
    around_me = [device(axis, by) for axis in "xyz" for by in (1, 2, 3)]
    for place in others + [partner] + around_me:
        pl.semaphore_signal(barrier, inc=1, device_id=place, device_id_type=MESH)

    def remote(src, dst, send, recv, place):
        return pltpu.make_async_remote_copy(
            src_ref=src, dst_ref=dst, send_sem=send, recv_sem=recv,
            device_id=place, device_id_type=MESH,
        )

    edge = HALO * HOP
    right, left = others[0], others[6]
    halo = [
        remote(src, dst, halo_send.at[i], halo_recv.at[i], place)
        for i, (src, dst, place) in enumerate(
            (
                (ids, left_i, right),
                (ids, right_i, left),
                (target.at[:, pl.ds(OWN * HOP - edge, edge)], left_t, right),
                (target.at[:, pl.ds(0, edge)], right_t, left),
            )
        )
    ]
    shares = [
        remote(stat_o, slots.at[tm], stat_send.at[j], stat_recv.at[j], place)
        for j, place in enumerate(others)
    ]
    pairs = [
        remote(ref.at[other] if picked else ref, there[i], pair_send.at[i], pair_recv.at[i], partner)
        for i, (ref, picked) in enumerate(zip((*here, ids), (*PICKED, False)))
    ]

    def give(i):
        pairs[i].start()

    own = slice(HALO, HALO + OWN)
    scale = scale_i[...].reshape(1, D)
    places = frame_places()
    valid = inside(places)

    def forward(table_v, pick_n, pick_h, goal, codes, head_s, spec_v, seg1, seg2):
        big_v = (table_v, up_v, down_v, head_v, syn_v, a1_v, a2_v, pick_n, pick_h, pick_k)
        copies = [
            pltpu.make_async_copy(h, v, sems.at[i]) for i, (h, v) in enumerate(zip(big_h, big_v))
        ]
        for copy in copies:
            copy.start()
        pl.semaphore_wait(barrier, 17)
        for copy in halo:
            copy.start()
        give(8)
        codes[HALO : HALO + OWN, :] = ids_column(ids[...])
        for source, first, count in (
            (target, HALO, OWN), (left_t, 0, HALO), (right_t, HALO + OWN, HALO),
        ):
            if source is left_t:
                for copy in halo:
                    copy.wait_recv()
            for r in range(count):
                goal[first + r : first + r + 1, :] = source[:, HOP * r : HOP * (r + 1)]
        codes[0:HALO, :] = ids_column(left_i[...])[OWN - HALO :]
        codes[HALO + OWN :, :] = ids_column(right_i[...])[:HALO]
        lane = lax.broadcasted_iota(jnp.int32, (ROWS, 2 * FRAMES), 1).astype(F32)
        hot = (lane == codes[:, 0:1]) | (lane == codes[:, 1:2] + 1024.0)
        hot = jnp.where(hot, 1.0, 0.0).astype(BF16)
        copies[0].wait()
        y0, rstd0 = norm(mm(hot, table_v[...]))
        y0 = jnp.where(valid, y0, 0.0)
        sin_o[...] = y0
        mixture = kern[0:1, :] * shift(y0, 3)
        for k in range(1, 7):
            mixture = mixture + kern[k : k + 1, :] * shift(y0, 3 - k)
        y1, rstd1 = norm(mixture)
        y1_o[...] = y1
        normed = y1.astype(BF16)
        copies[1].wait()
        for c in range(FF // 256):
            at = slice(256 * c, 256 * (c + 1))
            up = mm(normed, up_v[:, at])
            cdf = 0.5 * (1.0 + lax.erf(up * 0.7071067811865476))
            hid_v[:, at] = (up * cdf).astype(BF16)
            gp_o[:, at] = cdf + up * (0.3989422804014327 * jnp.exp(-0.5 * up * up))
        copies[2].wait()
        down = mm(hid_v[...], down_v[...])
        down_o[...] = down
        y2, rstd2 = norm(y0 + scale * down)
        y2_o[...] = y2
        places128 = lax.broadcasted_iota(jnp.int32, (ROWS, 128), 1)
        rstd_o[...] = jnp.where(places128 == 0, rstd0, jnp.where(places128 == 1, rstd1, rstd2))
        onorm = y2.astype(BF16)
        copies[3].wait()
        head_s[:, 1024:] = jnp.zeros((ROWS, 128), F32)
        for c in range(4):
            head_s[:, 256 * c : 256 * (c + 1)] = mm_bt(onorm, head_v[256 * c : 256 * (c + 1), :])
        head_s[:, 1024:1026] = mm_bt(onorm, head_v[1024:1026, :])
        phases = pltpu.roll(head_s[:, 512:], CHUNKS1 * 128 - 1, 1)
        for c in range(CHUNKS1):
            logmag = head_s[:, 128 * c : 128 * (c + 1)]
            if c == 4:
                logmag = jnp.where(places128 == 0, logmag, 0.0)
            mag = jnp.exp(logmag)
            phase = phases[:, 128 * c : 128 * (c + 1)]
            sine, cosine = sin_cos(phase)
            re, im = mag * cosine, mag * sine
            re_o[:, 128 * c : 128 * (c + 1)] = re
            im_o[:, 128 * c : 128 * (c + 1)] = im
            spec_v[:, 256 * c : 256 * c + 128] = re.astype(BF16)
            spec_v[:, 256 * c + 128 : 256 * (c + 1)] = im.astype(BF16)
        copies[4].wait()
        pred = jnp.zeros((ROWS, HOP), F32)
        for p in range(4):
            piece = jnp.where(valid, mm(spec_v[...], syn_v[:, HOP * p : HOP * (p + 1)]), 0.0)
            pred = pred + shift(piece, p - 2)
        pred = jnp.where(valid, pred / envelope(places, win), 0.0)
        for s, x in enumerate((pred, jnp.where(valid, goal[...], 0.0))):
            r1 = slice(ROWS * s, ROWS * (s + 1))
            for p in range(4):
                at = slice(HOP * p, HOP * (p + 1))
                seg1[r1, at] = (shift(x, 2 - p) * win[0:1, at]).astype(BF16)
            even = slice(2 * ROWS * s, 2 * ROWS * s + ROWS)
            odd = slice(2 * ROWS * s + ROWS, 2 * ROWS * (s + 1))
            before, after = shift(x, 1), shift(x, -1)
            seg2[even, 0:256] = (before * win[2:3, 0:256]).astype(BF16)
            seg2[even, 256:512] = (x * win[2:3, 256:512]).astype(BF16)
            seg2[odd, 0:128] = (before[:, 128:] * win[2:3, 0:128]).astype(BF16)
            seg2[odd, 128:384] = (x * win[2:3, 128:384]).astype(BF16)
            seg2[odd, 384:512] = (after[:, :128] * win[2:3, 384:512]).astype(BF16)
        for level in range(2):
            seg, table, chunks = ((seg1, a1_v, CHUNKS1), (seg2, a2_v, CHUNKS2))[level]
            d_o, q_o = ((d1_o, q1_o), (d2_o, q2_o))[level]
            copies[5 + level].wait()
            sums = [jnp.zeros((OWN, 128), F32) for _ in range(3)]
            for c in range(chunks):
                for sub in range(level + 1):
                    rows_p = slice(ROWS * sub, ROWS * (sub + 1))
                    base = ROWS * (level + 1)
                    rows_g = slice(base + ROWS * sub, base + ROWS * (sub + 1))
                    weights = table[:, 256 * c : 256 * (c + 1)]
                    sp, sg = mm(seg[rows_p, :], weights), mm(seg[rows_g, :], weights)
                    diff = sp - sg
                    pr, pi, gr, gi = sp[:, :128], sp[:, 128:], sg[:, :128], sg[:, 128:]
                    power_p, power_g = pr * pr + pi * pi, gr * gr + gi * gi
                    gap = jnp.log1p(power_p) - jnp.log1p(power_g)
                    slope = jnp.where(valid, 4.0 * gap / (1.0 + power_p), 0.0)
                    d_o[rows_p, 256 * c : 256 * (c + 1)] = jnp.where(valid, diff, 0.0)
                    q_o[rows_p, 256 * c : 256 * c + 128] = slope * pr
                    q_o[rows_p, 256 * c + 128 : 256 * (c + 1)] = slope * pi
                    dr, di = diff[own, :128], diff[own, 128:]
                    sums[0] = sums[0] + dr * dr + di * di
                    sums[1] = sums[1] + power_g[own]
                    sums[2] = sums[2] + gap[own] * gap[own]
            for i in range(3):
                total = jnp.sum(jnp.sum(sums[i], axis=0, keepdims=True), axis=1, keepdims=True)
                stat_o[3 * level + i : 3 * level + i + 1, :] = jnp.broadcast_to(total, (1, 128))
        stat_o[6:8, :] = jnp.zeros((2, 128), F32)
        for share in shares:
            share.start()
        slots[tm] = stat_o[...]

        copies[7].wait()
        copies[8].wait()
        normed = y1_o[own, :].astype(BF16)
        onorm = y2_o[own, :].astype(BF16)
        for c in range(2):
            nrm_o[c] = mm_bt(pick_n[c], normed)
            onm_o[c] = mm_bt(pick_n[c], onorm)
            for h in range(2):
                out = slice(576 * h, 576 * (h + 1))
                hid_o[c, out, :] = mm_bt(pick_h[c], hid_v[own, 1152 * h : 1152 * (h + 1)])
        for i in (0, 2, 1):
            give(i)
        copies[9].wait()

    pl.run_scoped(
        forward,
        *vmem([full(*shape, dtype=BF16) for shape in (BIG[0], BIG[7], BIG[8])]),
        pltpu.VMEM((ROWS, HOP), F32),
        pltpu.VMEM((ROWS, 2), F32),
        pltpu.VMEM((ROWS, 1152), F32),
        pltpu.VMEM((ROWS, WIDE1), BF16),
        pltpu.VMEM((2 * ROWS, NFFT), BF16),
        pltpu.VMEM((4 * ROWS, NFFT // 2), BF16),
    )

    def need(*which):
        for i in which:
            pairs[i].wait_recv()

    def lhs(i):
        return jnp.concatenate([here[i][core], there[i][...]], axis=1).astype(BF16)

    def rhs(i, cols):
        return jnp.concatenate([here[i][:, cols], there[i][:, cols]], axis=0).astype(BF16)

    def head_block(onorm, block):
        return mm(onorm, rhs(5, slice(128 * block, 128 * (block + 1))))

    def around(axis):
        i = spot[axis]
        return i, lax.rem(i + 1, 4), lax.rem(i + 2, 4), lax.rem(i + 3, 4)

    def backward(*parts):
        sent = [{}, {}, {}]

        def go(src, dst, k, slot, axis, by):
            sent[k][slot] = remote(src, dst, send.at[k, slot], recv.at[k, slot], device(axis, by))
            sent[k][slot].start()

        low, high = pl.ds(0, 2), pl.ds(2, 2)

        def phase1(k, s):
            axis, p = ORDERS[k][0], parts[k]
            i, right, opposite, left = around(axis)
            first, end = RANGES[k][s]
            rows = pl.ds(first, end - first)
            go(p.at[opposite, 0, rows], through[k].at[0, 0, rows], k, 6 * s, axis, 1)
            go(p.at[opposite, 1, rows], through[k].at[0, 1, rows], k, 21 + 2 * s, axis, 1)
            go(p.at[opposite, 2, rows], through[k].at[1, 0, rows], k, 6 * s + 1, axis, 3)
            go(p.at[opposite, 3, rows], through[k].at[1, 1, rows], k, 22 + 2 * s, axis, 3)
            go(p.at[right, high, rows], from_left[k].at[high, rows], k, 6 * s + 2, axis, 1)
            go(p.at[left, low, rows], from_right[k].at[low, rows], k, 6 * s + 3, axis, 3)

        def combine(k, s):
            axis, p = ORDERS[k][0], parts[k]
            i, right, opposite, left = around(axis)
            first, end = RANGES[k][s]
            rows = pl.ds(first, end - first)
            sent[k][6 * s].wait_recv()
            sent[k][21 + 2 * s].wait_recv()
            p[right, low, rows] += through[k][0, :, rows]
            go(p.at[right, low, rows], from_left[k].at[low, rows], k, 6 * s + 4, axis, 1)
            sent[k][6 * s + 1].wait_recv()
            sent[k][22 + 2 * s].wait_recv()
            p[left, high, rows] += through[k][1, :, rows]
            go(p.at[left, high, rows], from_right[k].at[high, rows], k, 6 * s + 5, axis, 3)

        for share in shares:
            share.wait_recv()
        total = slots[0]
        for j in range(1, 8):
            total = total + slots[j]

        factor = loss_scale[...] * (0.5 / CLIPS)
        loss = jnp.zeros((1, 1), F32)
        cots = []
        for level in range(2):
            count = ((FRAMES * 513), (2 * FRAMES * 257))[level]
            sum_a = total[3 * level : 3 * level + 1, 0:1]
            sum_b = total[3 * level + 1 : 3 * level + 2, 0:1]
            sum_g = total[3 * level + 2 : 3 * level + 3, 0:1]
            root_a, root_b = jnp.sqrt(sum_a + 1e-6), jnp.sqrt(sum_b + 1e-6)
            loss = loss + root_a / root_b + sum_g * (1.0 / count)
            cots.append((factor / (root_a * root_b), factor * (1.0 / count)))
        loss = jnp.where(lax.axis_index("tm") == 0, loss, 0.0)

        dx = jnp.zeros((ROWS, HOP), F32)
        ds1 = (cots[0][0] * d1_o[...] + cots[0][1] * q1_o[...]).astype(BF16)
        for p in range(4):
            at = slice(HOP * p, HOP * (p + 1))
            piece = mm_bt(ds1, a1_v[at, :]).astype(BF16).astype(F32) * win[0:1, at]
            dx = dx + shift(piece, p - 2)
        ds2 = (cots[1][0] * d2_o[...] + cots[1][1] * q2_o[...]).astype(BF16)
        dseg = mm_bt(ds2, a2_v[...]).astype(BF16).astype(F32) * win[2:3, : NFFT // 2]
        even, odd = dseg[:ROWS], dseg[ROWS:]
        dx = dx + shift(even[:, :256], -1) + even[:, 256:] + odd[:, 128:384]
        dx = dx + jnp.concatenate([shift(odd[:, 384:], 1), shift(odd[:, :128], -1)], axis=1)
        dx = jnp.where(valid, dx / envelope(places, win), 0.0)
        for p in range(4):
            piece = jnp.where(valid, shift(dx, 2 - p), 0.0)
            dfr[:, HOP * p : HOP * (p + 1)] = piece.astype(BF16)

        for c in range(CHUNKS1):
            dsp = mm_bt(dfr[...], syn_v[256 * c : 256 * (c + 1), :]).astype(BF16).astype(F32)
            dre, dim = dsp[:, :128], dsp[:, 128:]
            re, im = re_o[:, 128 * c : 128 * (c + 1)], im_o[:, 128 * c : 128 * (c + 1)]
            dlog, dph = dre * re + dim * im, dim * re - dre * im
            if c < 4:
                dhead[:, 128 * c : 128 * (c + 1)] = dlog.astype(BF16)
            dphase[:, 128 * c : 128 * (c + 1)] = dph
        moved = pltpu.roll(dphase[...], 1, 1)
        dhead[:, 512:640] = (moved[:, :128] + dlog).astype(BF16)
        dhead[:, 640:] = moved[:, 128:].astype(BF16)
        dhd_o[...] = dhead[own, :].astype(F32)
        give(5)
        don = mm(dhead[:, :1026], head_v[...]).astype(BF16).astype(F32)
        dstream = norm_back(don, y2_o[...], rstd_o[:, 2:3])

        scale_grad = jnp.sum(dstream[own] * down_o[own, :], axis=0, keepdims=True)
        ddn = (scale * dstream).astype(BF16)
        ddn_o[...] = ddn[own].astype(F32)
        give(4)
        for c in range(FF // 256):
            at = slice(256 * c, 256 * (c + 1))
            dh = mm_bt(ddn, down_v[at, :]).astype(BF16).astype(F32)
            dup[:, at] = (dh * gp_o[:, at]).astype(BF16)
        dup_o[...] = dup[own, :].astype(F32)
        give(3)

        need(2, 5)
        onorm = [lhs(2)]
        onorm += [mm(turn[...], onorm[0]).astype(BF16) for turn in (turn1, turn2)]
        for k in range(3):
            start, blocks = HEAD_BLOCKS[k]
            for b in range(min(blocks, 8 - start)):
                put(parts[k], 24 * b, head_block(onorm[k], start + b), 24)
        phase1(0, 0)
        phase1(2, 0)
        need(1, 4)
        hidden = lhs(1)
        for c in range(3):
            put(parts[1], 48 + 144 * c, mm(hidden, rhs(4, slice(256 * c, 256 * (c + 1)))), 72)
        phase1(1, 0)
        need(0, 3)
        normed = lhs(0)
        for c in range(FF // 256):
            put(parts[0], 72 + 48 * c, mm(normed, rhs(3, slice(256 * c, 256 * (c + 1)))), 24)
        phase1(0, 1)

        dnorm = mm_bt(dup[...], up_v[...]).astype(BF16).astype(F32)
        dmix = norm_back(dnorm, y1_o[...], rstd_o[:, 1:2])
        dmix = jnp.where(valid, dmix, 0.0)
        y0 = sin_o[...]
        dsin = dstream
        for k in range(7):
            dsin = dsin + kern[k : k + 1, :] * shift(dmix, k - 3)
        demb = norm_back(dsin, y0, rstd_o[:, 0:1])
        dem_o[...] = demb[own].astype(BF16).astype(F32)
        give(6)
        small[...] = jnp.zeros((16, D), F32)
        for k in range(7):
            taps = dmix * shift(y0, 3 - k)
            small[2 + k : 3 + k, :] = jnp.sum(taps[own], axis=0, keepdims=True)

        small[9:10, :] = scale_grad
        rest = loss
        for i, grid in enumerate((65536.0, 1.0, 1.0 / 65536.0, 1.0 / 65536.0 / 65536.0)):
            piece = jnp.floor(rest * (1.0 / grid)) * grid
            rest = rest - piece
            small[10 + i : 11 + i, :] = jnp.broadcast_to(piece, (1, D))

        small0 = small[...].astype(BF16)
        rest = small[...] - small0.astype(F32)
        small1 = rest.astype(BF16)
        small2 = (rest - small1.astype(F32)).astype(BF16)
        pieces = jnp.concatenate([small0, small1, small2], axis=0)
        for c in range(2):
            picked = mm_bt(pieces, pick_k[c])
            picked = picked[0:16] + picked[16:32] + picked[32:48]
            picked = jnp.concatenate([picked, jnp.zeros((112, 384), F32)], axis=0)
            kg_o[c] = jnp.transpose(picked)
        give(7)

        combine(0, 0)
        combine(2, 0)
        need(8, 6)
        both_ids = jnp.concatenate([ids[...], there[8][...]], axis=1)
        code_rows = row_id[...] + OWN * core
        hot = (code_rows == both_ids[0:1, :]) | (code_rows == both_ids[1:2, :] + 1024)
        hot = jnp.where(hot, 1.0, 0.0).astype(BF16)
        for c in range(3):
            put(parts[2], 96 + 128 * c, mm(hot, rhs(6, slice(256 * c, 256 * (c + 1)))), 64)
        need(7)
        put(parts[2], 72, head_block(onorm[2], 8) + here[7][core] + there[7][...], 24)
        phase1(2, 1)
        combine(1, 0)
        combine(0, 1)
        combine(2, 1)

        for k in (1, 0, 2):
            mine = spot[ORDERS[k][0]]
            axis, p, a, b = ORDERS[k][1], parts[k], got2a[k], got2b[k]
            i, right, opposite, left = around(axis)
            upper, lower = halves_of(PART_ROWS[k])
            for s in range(len(RANGES[k])):
                for j in (2, 3, 4, 5):
                    sent[k][6 * s + j].wait_recv()
            p[mine, opposite] += from_left[k][opposite] + from_right[k][opposite]
            go(p.at[mine, opposite, upper], a.at[0], k, 12, axis, 1)
            go(p.at[mine, opposite, lower], b.at[0], k, 13, axis, 3)
            p[mine, right] += from_left[k][right] + from_right[k][right]
            go(p.at[mine, right, lower], b.at[1], k, 14, axis, 1)
            p[mine, left] += from_left[k][left] + from_right[k][left]
            go(p.at[mine, left, upper], a.at[1], k, 15, axis, 3)
            p[mine, i] += from_left[k][i] + from_right[k][i]
        for k in (1, 0, 2):
            mine = spot[ORDERS[k][0]]
            axis, p, a, b = ORDERS[k][1], parts[k], got2a[k], got2b[k]
            i, right, opposite, left = around(axis)
            upper, lower = halves_of(PART_ROWS[k])
            sent[k][12].wait_recv()
            p[mine, right, upper] += a[0]
            go(p.at[mine, right, upper], a.at[2], k, 16, axis, 1)
            sent[k][13].wait_recv()
            p[mine, left, lower] += b[0]
            go(p.at[mine, left, lower], b.at[2], k, 17, axis, 3)
        for k in (1, 0, 2):
            mine = spot[ORDERS[k][0]]
            i = spot[ORDERS[k][1]]
            p, a, b, out = parts[k], got2a[k], got2b[k], last[k]
            upper, lower = halves_of(PART_ROWS[k])
            for j in (14, 15, 16, 17):
                sent[k][j].wait_recv()
            p[mine, i, upper] += a[1] + a[2]
            p[mine, i, lower] += b[1] + b[2]
            start, place = 0, 0
            for count, rows in ((HEAD_BLOCKS[k][1], 24), MAIN_BLOCKS[k]):
                each = rows // 4
                for _ in range(count):
                    for d in range(4):
                        out[d, pl.ds(place, each)] = p[mine, i, pl.ds(start + d * each, each)]
                    start += rows
                    place += each
            if place < LAST_ROWS[k]:
                for d in range(4):
                    out[d, pl.ds(place, LAST_ROWS[k] - place)] = jnp.zeros(
                        (LAST_ROWS[k] - place, 128), F32
                    )
            axis = ORDERS[k][2]
            for by in (1, 2, 3):
                to = lax.rem(spot[axis] + by, 4)
                go(out.at[to], got3[k].at[by - 1], k, 17 + by, axis, by)
        for k in (1, 0, 2):
            for j in (18, 19, 20):
                sent[k][j].wait_recv()
            total = last[k][spot[ORDERS[k][2]]] + got3[k][0] + got3[k][1] + got3[k][2]
            out_o[pl.ds(FIRST_ROWS[k], LAST_ROWS[k]), :] = total
        for copy in halo + shares + pairs:
            copy.wait_send()
        for k in range(3):
            for copy in sent[k].values():
                copy.wait_send()

    pl.run_scoped(backward, *[pltpu.VMEM((4, 4, n, 128), F32) for n in PART_ROWS])


BIG = (
    (2 * FRAMES, D), (D, FF), (FF, D), (2 * 513, D), (WIDE1, NFFT), (NFFT, WIDE1),
    (NFFT // 2, WIDE2), (2, 384, D), (2, 576, FF // 2), (2, 384, D),
)


def step_call(small, big):
    wide = [full(*((2,) if p else ()), *a.shape) for a, p in zip(OPERANDS, PICKED)]
    edge = full(1, HALO * HOP)
    rows = PART_ROWS
    cuts = [halves_of(n)[0].size for n in rows]

    def each(make):
        return [pltpu.VMEM(make(k), F32) for k in range(3)]

    return pl.pallas_call(
        step_kernel,
        out_shape=full(sum(LAST_ROWS), 128),
        in_specs=[spec(pltpu.VMEM)] * len(small) + [spec(pl.ANY)] * len(big),
        out_specs=spec(pltpu.VMEM),
        scratch_shapes=vmem([full(*BIG[i], dtype=BF16) for i in (1, 2, 3, 4, 5, 6, 9)])
        + vmem(SAVED)
        + vmem(wide)
        + vmem([*OPERANDS, IDS])
        + vmem([edge, edge, IDS, IDS])
        + [
            pltpu.VMEM((ROWS, FF), BF16),
            pltpu.VMEM((8, 128), F32),
            pltpu.VMEM((8, 8, 128), F32),
            pltpu.VMEM((ROWS, NFFT), BF16),
            pltpu.VMEM((ROWS, CHUNKS1 * 128), F32),
            pltpu.VMEM((ROWS, 1152), BF16),
            pltpu.VMEM((ROWS, FF), BF16),
            pltpu.VMEM((16, D), F32),
        ]
        + each(lambda k: (2, 2, rows[k], 128))
        + each(lambda k: (4, rows[k], 128))
        + each(lambda k: (4, rows[k], 128))
        + each(lambda k: (3, cuts[k], 128))
        + each(lambda k: (3, rows[k] - cuts[k], 128))
        + each(lambda k: (4, LAST_ROWS[k], 128))
        + each(lambda k: (3, LAST_ROWS[k], 128))
        + [pltpu.SemaphoreType.DMA((n,)) for n in (len(big), 4, 4, 7, 7, 9, 9)]
        + [pltpu.SemaphoreType.DMA((3, 25))] * 2,
        compiler_params=pltpu.CompilerParams(
            collective_id=0, has_side_effects=True, vmem_limit_bytes=64 * MB
        ),
        name="train_step",
    )(*small, *big)


def finish_kernel(sums, loss_o, table_o, kern_o, up_o, down_o, scale_o, head_o):
    for k, (out, count, each) in enumerate(((up_o, 18, 6), (down_o, 6, 18), (table_o, 6, 16))):
        start, blocks = HEAD_BLOCKS[k]
        for c in range(blocks):
            rows = FIRST_ROWS[k] + 6 * c
            values = sums[rows : rows + 6, :]
            if start + c < 8:
                head_o[:, 128 * (start + c) : 128 * (start + c + 1)] = values
            else:
                head_o[:, 1024:1026] = values[:, 0:2]
                tail = jnp.transpose(jnp.concatenate([values, jnp.zeros((122, 128), F32)], axis=0))
                kern_o[...] = tail[2:9, 0:6]
                scale_o[...] = tail[9:10, 0:6]
                pieces = values[0:1, 10:14]
                loss_o[...] = jnp.sum(pieces, axis=1, keepdims=True) * (0.5 / CLIPS)
        for c in range(count):
            rows = FIRST_ROWS[k] + 6 * blocks + each * c
            out[:, 128 * c : 128 * (c + 1)] = sums[rows : rows + each, :]


def finish_call(sums):
    loss, table, kern, up, down, scale, head = pl.pallas_call(
        finish_kernel,
        out_shape=[
            full(1, 1), full(16, D), full(7, 6), full(6, FF), full(18, D), full(1, 6), full(6, 1026),
        ],
        in_specs=[spec(pltpu.VMEM)],
        out_specs=[spec(pltpu.VMEM)] * 7,
        name="finish",
    )(sums)
    return loss.reshape(()), table, kern, up, down, scale.reshape(6), head


def body(
    code_ids, code_table, kernel, up_weight, down_weight, layer_scale, head_weight, target, loss_scale
):
    syn, a1, a2, win = make_constants()
    pick_n, pick_h, pick_k, turn1, turn2, row_id = make_orders()
    ids = jnp.swapaxes(code_ids, 1, 2).reshape(2, OWN)
    head_t = head_weight.T
    sums = step_call(
        (target, ids, kernel, layer_scale, win, loss_scale.reshape(1, 1), turn1, turn2, row_id),
        (
            code_table, up_weight, down_weight, head_t, syn, a1, a2, pick_n, pick_h, pick_k,
        ),
    )
    return finish_call(sums)


def solution(mesh):
    in_specs = (P("dp", "tm", None), P(), P(), P(), P(), P(), P(), P("dp", "tm"), P())
    out_specs = (
        P(),
        P(("dp", "tm"), None),
        P(None, ("dp", "tm")),
        P(("dp", "tm"), None),
        P(("dp", "tm"), None),
        P(("dp", "tm")),
        P(("dp", "tm"), None),
    )
    return jax.shard_map(body, mesh=mesh, in_specs=in_specs, out_specs=out_specs, check_vma=False)
```
